32 devices in a mesh: gx: 8 (over z, y), gy: 4 (over x, core).
Axes of the slice: x: 2, y: 2, z: 4, core: 2. Of those that a mesh axis runs over, the one named last changes fastest.
Arguments:
- warm_start: float32 [8, 16, 128, 512], P(None, None, 'gx', 'gy'), may hold values from 0 to 39.36
- slowness: float32 [16, 128, 512], P(None, 'gx', 'gy'), may hold values from 0.02 to 0.05
- anisotropy: float32 [3, 16, 128, 512], P(None, None, 'gx', 'gy'), may hold values from 0.5 to 1.5
- observed: float32 [8, 512], P(None, ('gx', 'gy')), may hold values from 0 to 25
- station_cell: int32 [512], replicated, may hold values from 0 to 65535
- source_cell: int32 [8], replicated, may hold values from 0 to 1048575
Outputs:
- traveltime: float32 [8, 16, 128, 512], P(None, None, 'gx', 'gy')
- kernel: float32 [16, 128, 512], P(None, 'gx', 'gy')
The draws below stay inside these ranges and needn't reach their ends.
All inputs are finite; a program needn't handle non-finite values.
Results may differ from the reference program's by a relative error of at most 0.0003.
Values sent between devices are 32-bit elements; how exact they have to be, the bound alone decides.
No kernel may reach another device: no remote copies, remote signals or barrier semaphores. Data moves between devices by JAX's collectives and lax.ppermute only.
A program may use at most 128 MiB of HBM per device.

```python
import math
import jax
import jax.numpy as jnp
import numpy as np
from jax import lax

E = 8
Z = 16
NX = 128
NY = 512
NS = 512


def quake_nodes(key):
    nodes = jax.random.randint(jax.random.fold_in(key, 11), (E,), 0, Z * NX * NY)
    nodes = nodes.at[0].set(0)
    nodes = nodes.at[E - 1].set(Z * NX * NY - 1)
    return nodes.astype(jnp.int32)


def draw_source_cell(key, part):
    nodes = quake_nodes(key)
    return nodes.astype(jnp.int32)


def draw_warm_start(key, part):
    nodes = quake_nodes(key)
    key = jax.random.fold_in(key, 5)
    noise_key = jax.random.fold_in(key, 1)
    depth_node = nodes // (NX * NY)
    row_node = nodes // NY % NX
    col_node = nodes % NY
    shape = (E, Z, NX, NY)
    depth_gap = (lax.broadcasted_iota(jnp.int32, shape, 1) - depth_node[:, None, None, None]).astype(jnp.float32)
    row_gap = (lax.broadcasted_iota(jnp.int32, shape, 2) - row_node[:, None, None, None]).astype(jnp.float32)
    col_gap = (lax.broadcasted_iota(jnp.int32, shape, 3) - col_node[:, None, None, None]).astype(jnp.float32)
    distance = jnp.sqrt(depth_gap * depth_gap + row_gap * row_gap + col_gap * col_gap)
    factor = 1.3
    noise = jax.random.uniform(noise_key, shape, jnp.float32, 0.97, 1.03)
    return (0.035 * factor * distance * noise).astype(jnp.float32)


def place_ends(entries, own_key, smallest, high):
    longest = entries.shape.index(max(entries.shape))
    spots = []
    for shift in (0, 1):
        where = [jax.random.randint(jax.random.fold_in(own_key, axis), (), 0, length) for axis, length in enumerate(entries.shape)]
        where[longest] = (where[longest] + shift) % entries.shape[longest]
        spots.append(tuple(where))
    return entries.at[spots[0]].set(smallest).at[spots[1]].set(high)


def block_scale(stream_key, dims, shards, low, top_value):
    def one(axis_at, parts):
        heights = jax.random.uniform(jax.random.fold_in(jax.random.fold_in(stream_key, 6), axis_at), (parts,), jnp.float32, low / len(shards), top_value / len(shards))
        return jnp.repeat(jnp.exp(heights), dims[axis_at] // parts).reshape((-1,) + (1,) * (len(dims) - axis_at - 1))

    loudness = one(*shards[0])
    for cut in shards[1:]:
        loudness = loudness * one(*cut)
    return loudness


def cumulative_ranks(count, slope):
    weights = [(1 << 20) // math.isqrt(grade ** slope) + 1 for grade in range(1, count + 1)]
    scale = 1 + sum(weights) // (1 << 30)
    return np.cumsum(np.array([max(1, weight // scale) for weight in weights]))


def ranked(rng, shape, number_of, skew):
    grid = cumulative_ranks(number_of, skew)
    lot = jax.random.randint(jax.random.fold_in(rng, 1), shape, 0, int(grid[number_of - 1]))
    grade = jnp.searchsorted(jnp.asarray(grid, jnp.int32), lot, side="right")
    return jax.random.permutation(jax.random.fold_in(rng, 2), number_of)[grade].astype(jnp.int32)


def setup_inputs(seed: int = 0) -> dict:
    streams_of = jax.random.split(jax.random.key(seed), 7)
    warm_start = draw_warm_start(jax.random.fold_in(streams_of[6], 71), 0)
    slowness = jnp.clip(0.02 + 0.030000001 * jax.random.uniform(streams_of[1], (Z, NX, NY), jnp.float32) ** block_scale(streams_of[1], (Z, NX, NY), ((1, 8), (2, 4)), -0.2, 0.2), 0.02, 0.05)
    anisotropy = jnp.clip(1.0 + 0.1 * jax.random.normal(streams_of[2], (3, Z, NX, NY), jnp.float32), 0.5, 1.5)
    observed = jnp.clip(25.0 * jax.random.uniform(streams_of[3], (E, NS), jnp.float32) ** block_scale(streams_of[3], (E, NS), ((1, 32),), -0.2, 0.2), 0.0, 25.0)
    station_cell = place_ends(ranked(streams_of[4], (NS,), NX * NY, 2), jax.random.fold_in(streams_of[4], 3), 0, (NX * NY) - 1).astype(jnp.int32)
    source_cell = draw_source_cell(jax.random.fold_in(streams_of[6], 71), 0)
    return {"warm_start": warm_start, "slowness": slowness, "anisotropy": anisotropy, "observed": observed, "station_cell": station_cell, "source_cell": source_cell}


TAU = 0.05
BIG = 10000.0
ADJ_SCALE = 0.1

def soft_pair(first, second):
    return -TAU * jnp.logaddexp(-first / TAU, -second / TAU)

def transverse(field, cost_y, cost_z):
    below = jnp.pad(field, ((0, 0), (0, 0), (1, 0)), constant_values=BIG)[:, :, :-1]
    above = jnp.pad(field, ((0, 0), (0, 0), (0, 1)), constant_values=BIG)[:, :, 1:]
    lower = jnp.pad(field, ((1, 0), (0, 0), (0, 0)), constant_values=BIG)[:-1]
    upper = jnp.pad(field, ((0, 1), (0, 0), (0, 0)), constant_values=BIG)[1:]
    values = jnp.stack([field, below + cost_y, above + cost_y, lower + cost_z, upper + cost_z])
    return -TAU * jax.scipy.special.logsumexp(-values / TAU, axis=0)

def along_x(levels, cost_x, backward):

    def advance(carry, inputs):
        fresh = soft_pair(inputs[0], carry + inputs[1])
        return (fresh, fresh)
    initial = jnp.full((levels.shape[0], levels.shape[2]), BIG, levels.dtype)
    finish, swept = lax.scan(advance, initial, (jnp.moveaxis(levels, 1, 0), jnp.moveaxis(cost_x, 1, 0)), reverse=backward)
    return jnp.moveaxis(swept, 0, 1)

def forward(slowness, anisotropy, start):
    cost_x = slowness * anisotropy[0]
    cost_y = slowness * anisotropy[1]
    cost_z = slowness * anisotropy[2]
    first = along_x(transverse(start, cost_y, cost_z), cost_x, False)
    return along_x(transverse(first, cost_y, cost_z), cost_x, True)

def reference(warm_start, slowness, anisotropy, observed, station_cell, source_cell):
    shape = (Z, NX, NY)
    flat = lax.broadcasted_iota(jnp.int32, shape, 0) * (NX * NY) + lax.broadcasted_iota(jnp.int32, shape, 1) * NY + lax.broadcasted_iota(jnp.int32, shape, 2)

    def quake(kernel, inputs):
        start_field, source, record = inputs
        start = jnp.where(flat == source, jnp.zeros_like(start_field), start_field)
        final, pullback = jax.vjp(lambda slow: forward(slow, anisotropy, start), slowness)
        picks = final[0].reshape(-1)[station_cell]
        misfit = ADJ_SCALE * (picks - record)
        injected_field = jnp.zeros((NX * NY,), final.dtype).at[station_cell].add(misfit).reshape(NX, NY)
        cotangent = jnp.zeros_like(final).at[0].set(injected_field)
        return (kernel + pullback(cotangent)[0], final)
    kernel, final = lax.scan(quake, jnp.zeros_like(slowness), (warm_start, source_cell, observed))
    return (final, kernel)
```

```python
import jax
import jax.numpy as jnp
from jax import lax
from jax.sharding import PartitionSpec as P

TAU = 0.05
BIG = 10000.0
ADJ_SCALE = 0.1


def extended(block, sides, width):
    for axis, dim in sides:
        count = lax.axis_size(axis)
        forward = [(i, i + 1) for i in range(count - 1)]
        backward = [(target, source) for source, target in forward]
        low = lax.ppermute(
            lax.slice_in_dim(block, block.shape[dim] - width, None, axis=dim), axis, forward
        )
        high = lax.ppermute(lax.slice_in_dim(block, 0, width, axis=dim), axis, backward)
        block = jnp.concatenate([low, block, high], axis=dim)
    return block


def shifted(value, axis, by):
    count = lax.axis_size(axis)
    pairs = [(i, i + by) for i in range(count) if 0 <= i + by < count]
    return lax.ppermute(value, axis, pairs)


def entering_exchanged(reach, total, axis, reverse):
    count = lax.axis_size(axis)
    quakes = reach.shape[0]
    spare = -quakes % count
    reach = jnp.pad(reach, ((0, spare), (0, 0), (0, 0)), constant_values=BIG)
    total = jnp.broadcast_to(total, reach.shape)
    both = jnp.stack([reach, total], 1)
    both = lax.all_to_all(both, axis, 0, 0, tiled=True)
    per = (quakes + spare) // count
    both = both.reshape((count, per) + both.shape[1:])
    state = jnp.full(both.shape[1:2] + both.shape[3:], BIG, jnp.float32)
    entering = [None] * count
    for lap in range(count):
        device = count - 1 - lap if reverse else lap
        entering[device] = state
        state = soft_pair(both[device, :, 0], state + both[device, :, 1])
    entering = jnp.concatenate(entering, 0)
    return lax.all_to_all(entering, axis, 0, 0, tiled=True)[:quakes]


def entering_tree(reach, total, axis, reverse):
    count = lax.axis_size(axis)
    place = lax.axis_index(axis)
    sign = -1 if reverse else 1
    ahead = count - 1 - place if reverse else place
    both = jnp.concatenate([reach, total[None]], 0)

    def joined(early, late):
        return jnp.concatenate([soft_pair(late[:-1], early[:-1] + late[-1:]), early[-1:] + late[-1:]], 0)

    def received(value, span):
        came = shifted(value, axis, sign * span)
        blank = jnp.concatenate([jnp.full_like(came[:-1], BIG), jnp.zeros_like(came[-1:])], 0)
        return jnp.where(ahead >= span, came, blank)

    one, two = received(both, 1), received(both, 2)
    before = joined(two, one)
    block = joined(before, both)
    span = 3
    while span - 1 < count - 1:
        near, far = received(block, span), received(block, 2 * span)
        prior = joined(far, near)
        before = joined(prior, before)
        block = joined(prior, block)
        span *= 3
    return before[:-1]


def entering_linear(part, axis, reverse):
    count = lax.axis_size(axis)
    sign = -1 if reverse else 1
    place = lax.axis_index(axis)
    ahead = count - 1 - place if reverse else place
    both = jnp.stack(part)
    value = jnp.zeros_like(part[0])
    factor = jnp.ones_like(part[1])
    for by in range(1, count):
        came = shifted(both, axis, sign * by)
        value = value + factor * jnp.where(ahead >= by, came[0], 0.0)
        factor = factor * jnp.where(ahead >= by, came[1], 1.0)
    return value


def soft_pair(first, second):
    return -TAU * jnp.logaddexp(-first / TAU, -second / TAU)


def transverse(field, cost_y, cost_z, lower_edge, upper_edge):
    padded = extended(field, (("gy", 3),), 1)
    column = lax.broadcasted_iota(jnp.int32, field.shape, 3)
    last_col = field.shape[3] - 1
    below = jnp.where(lower_edge & (column == 0), BIG, padded[..., :-2])
    above = jnp.where(upper_edge & (column == last_col), BIG, padded[..., 2:])
    border = jnp.full_like(field[:, :1], BIG)
    lower = jnp.concatenate([border, field[:, :-1]], 1)
    upper = jnp.concatenate([field[:, 1:], border], 1)
    values = jnp.stack([field, below + cost_y, above + cost_y, lower + cost_z, upper + cost_z])
    levels = -TAU * jax.scipy.special.logsumexp(-values / TAU, axis=0)
    weights = jnp.exp((levels - values) / TAU)
    return (levels, weights)


def along_x(levels, cost_x, direction):
    backward = direction < 0
    column_levels = jnp.moveaxis(levels, 2, 0)
    column_cost = jnp.moveaxis(cost_x, 1, 0)

    def advance(carry, inputs):
        reach = soft_pair(inputs[0], carry[0] + inputs[1])
        total = carry[1] + inputs[1]
        return ((reach, total), (reach, total))

    initial = (
        jnp.full(column_levels.shape[1:], BIG, jnp.float32),
        jnp.zeros(column_cost.shape[1:], jnp.float32),
    )
    block, running = lax.scan(advance, initial, (column_levels, column_cost), reverse=backward)
    block_reach, block_total = block
    reaches, totals = running
    carry = entering_tree if backward else entering_exchanged
    entering = carry(block_reach, block_total, "gx", backward)
    times = soft_pair(reaches, entering[None] + totals[:, None])
    if backward:
        prior = jnp.concatenate([times[1:], entering[None]], 0)
    else:
        prior = jnp.concatenate([entering[None], times[:-1]], 0)
    slope = jnp.exp((times - prior - column_cost[:, None]) / TAU)
    keeping = jnp.exp((times - column_levels) / TAU)
    return (jnp.moveaxis(times, 0, 2), jnp.moveaxis(slope, 0, 2), jnp.moveaxis(keeping, 0, 2))


def adjoint_x(source_term, slope, direction):
    backward = direction > 0
    column_source = jnp.moveaxis(source_term, 2, 0)
    column_slope = jnp.moveaxis(slope, 2, 0)

    def retreat(carry, inputs):
        fresh = (inputs[1] * (inputs[0] + carry[0]), inputs[1] * carry[1])
        return (fresh, carry)

    initial = (
        jnp.zeros(column_source.shape[1:], jnp.float32),
        jnp.ones(column_source.shape[1:], jnp.float32),
    )
    block, running = lax.scan(retreat, initial, (column_source, column_slope), reverse=backward)
    arriving = entering_linear(block, "gx", backward)
    total = column_source + running[0] + running[1] * arriving[None]
    return jnp.moveaxis(total, 0, 2)


def kernel_terms(adjoint, slope, keeping, weights, anisotropy):
    through_levels = keeping * adjoint
    sideways = anisotropy[1] * (weights[1] + weights[2]) + anisotropy[2] * (weights[3] + weights[4])
    terms = adjoint * slope * anisotropy[0] + through_levels * sideways
    return (jnp.sum(terms, axis=0), through_levels)


def spread_back(through_levels, weights):
    outgoing = jnp.stack([through_levels * weights[1], through_levels * weights[2]])
    padded = extended(outgoing, (("gy", 4),), 1)
    from_above = padded[0, ..., 2:]
    from_below = padded[1, ..., :-2]
    level = through_levels * weights[0] + from_above + from_below
    return jnp.concatenate([level, through_levels * weights[4]], 1)


def body(warm_start, slowness, anisotropy, observed, station_cell, source_cell):
    quakes, depth, width_x, width_y = warm_start.shape
    count_y = lax.axis_size("gy")
    index_x = lax.axis_index("gx")
    index_y = lax.axis_index("gy")
    span_x = width_x * lax.axis_size("gx")
    span_y = width_y * count_y
    anchor_x = index_x * width_x
    anchor_y = index_y * width_y
    shape = (depth, width_x, width_y)
    flat = (
        lax.broadcasted_iota(jnp.int32, shape, 0) * (span_x * span_y)
        + (lax.broadcasted_iota(jnp.int32, shape, 1) + anchor_x) * span_y
        + lax.broadcasted_iota(jnp.int32, shape, 2)
        + anchor_y
    )
    start = jnp.where(flat[None] == source_cell[:, None, None, None], 0.0, warm_start)
    cost_x = slowness * anisotropy[0]
    cost_y = slowness * anisotropy[1]
    cost_z = slowness * anisotropy[2]
    lower_edge = index_y == 0
    upper_edge = index_y == count_y - 1
    levels_one, weights_one = transverse(start, cost_y, cost_z, lower_edge, upper_edge)
    times_one, slope_one, keep_one = along_x(levels_one, cost_x, 1)
    levels_two, weights_two = transverse(times_one, cost_y, cost_z, lower_edge, upper_edge)
    times_two, slope_two, keep_two = along_x(levels_two, cost_x, -1)
    records = lax.all_gather(observed, ("gx", "gy"), axis=1, tiled=True)
    station_row = station_cell // span_y
    station_col = station_cell % span_y
    owned = (
        (station_row >= anchor_x)
        & (station_row < anchor_x + width_x)
        & (station_col >= anchor_y)
        & (station_col < anchor_y + width_y)
    )
    local_cell = jnp.where(owned, (station_row - anchor_x) * width_y + (station_col - anchor_y), 0)
    surface = times_two[:, 0].reshape(quakes, width_x * width_y)
    picked = jnp.take(surface, local_cell, axis=1)
    misfit = jnp.where(owned[None], ADJ_SCALE * (picked - records), 0.0)
    injected = jnp.zeros((quakes, width_x * width_y), jnp.float32).at[:, local_cell].add(misfit)
    top = slice(0, 1)
    near = slice(0, 2)
    source_two = injected.reshape(quakes, 1, width_x, width_y)
    adjoint_two = adjoint_x(source_two, slope_two[:, top], -1)
    kernel_two, through_two = kernel_terms(
        adjoint_two, slope_two[:, top], keep_two[:, top], weights_two[:, :, top], anisotropy[:, top]
    )
    source_one = spread_back(through_two, weights_two[:, :, top])
    adjoint_one = adjoint_x(source_one, slope_one[:, near], 1)
    kernel_one, through_one = kernel_terms(
        adjoint_one, slope_one[:, near], keep_one[:, near], weights_one[:, :, near], anisotropy[:, near]
    )
    rest = jnp.zeros((depth - 2, width_x, width_y), jnp.float32)
    kernel = jnp.concatenate([kernel_one[:1] + kernel_two, kernel_one[1:], rest], 0)
    return (times_two, kernel)


def solution(mesh):
    return jax.shard_map(
        body,
        mesh=mesh,
        in_specs=(
            P(None, None, "gx", "gy"),
            P(None, "gx", "gy"),
            P(None, None, "gx", "gy"),
            P(None, ("gx", "gy")),
            P(),
            P(),
        ),
        out_specs=(P(None, None, "gx", "gy"), P(None, "gx", "gy")),
        check_vma=False,
    )
```

```python
import functools
import math

import jax
import jax.numpy as jnp
from jax import lax
from jax.experimental import pallas as pl
from jax.experimental.pallas import tpu as pltpu
from jax.sharding import PartitionSpec as P

TAU = 0.05
BIG = 10000.0
ADJ_SCALE = 0.1
RATE = math.log2(math.e) / TAU
VMEM = pl.BlockSpec(memory_space=pltpu.VMEM)
SMEM = pl.BlockSpec(memory_space=pltpu.SMEM)
PARAMS = pltpu.CompilerParams(vmem_limit_bytes=48 * 1024 * 1024)


def weight(gap):
    return jnp.exp2(gap * RATE)


def soft_pair(first, second):
    return jnp.minimum(first, second) - TAU * jnp.log(1.0 + weight(-jnp.abs(first - second)))


def split_pair(first, second):
    gap = weight(-jnp.abs(first - second))
    share = 1.0 / (1.0 + gap)
    less = gap * share
    nearer = first <= second
    return jnp.where(nearer, share, less), jnp.where(nearer, less, share)


def lanes(shape):
    return lax.broadcasted_iota(jnp.int32, shape, len(shape) - 1)


def row(ref, index, x, like):
    return jnp.broadcast_to(ref[index, pl.ds(x, 1), :], like)


def gather_edge(edges, values, x):
    here = (lanes(values[0].shape) >> 1) == x
    return [jnp.where(here, pltpu.roll(v, 2 * x + 1, 1), a) for a, v in zip(edges, values)]


def edge_rows(edges, count):
    return jnp.transpose(jnp.concatenate(edges, 0))[:count]


def pack_kernel(place, source, warm, observed, start, edge):
    width_x, depth, quakes, width_y = start.shape
    tile = (quakes, width_y)
    quake = lax.broadcasted_iota(jnp.int32, tile, 0)
    span_y = place[2]
    plane = place[3]
    base = lanes(tile) + place[0] * span_y + place[1]
    cell = jnp.zeros(tile, jnp.int32)
    for e in range(quakes):
        cell = jnp.where(quake == e, source[e], cell)
    cell = cell - base

    def one(x, edges):
        levels = []
        for z in range(depth):
            value = warm[pl.ds(z * width_x + x, quakes, stride=depth * width_x), :]
            value = jnp.where(cell == z * plane + x * span_y, 0.0, value)
            start[x, z] = value
            levels.append(value)
        return gather_edge(edges, levels, x)

    edges = lax.fori_loop(0, width_x, one, [jnp.zeros(tile, jnp.float32)] * depth)
    edge[: 2 * width_x, :] = edge_rows(edges, 2 * width_x)
    edge[2 * width_x :, :] = jnp.zeros((quakes, width_y), jnp.float32)
    edge[2 * width_x :, : observed.shape[1]] = observed[...]


def halo_columns(place, from_left, from_right, width_x, depth):
    left = jnp.where(place[4] == 1, BIG, pltpu.roll(from_left[: 2 * width_x, :], 1, 0))
    right = jnp.where(place[5] == 1, BIG, pltpu.roll(from_right[: 2 * width_x, :], 2 * width_x - 1, 0))
    odd = lax.broadcasted_iota(jnp.int32, left.shape, 0) % 2 == 1
    both = jnp.where(odd, left, right)
    rest = jnp.zeros((left.shape[1] - 2 * width_x, left.shape[1]), jnp.float32)
    return jnp.transpose(jnp.concatenate([both, rest], 0))


def sweep(direction, near, place, field, from_left, from_right, slowness, anisotropy, halo, keep_level):
    width_x, depth, quakes, width_y = field.shape
    tile = (quakes, width_y)
    lane = lanes(tile)
    halo[...] = halo_columns(place, from_left, from_right, width_x, depth).reshape(depth, quakes, width_y)

    def one(step, state):
        x = step if direction > 0 else width_x - 1 - step
        out = []
        for z in range(depth):
            u = field[x, z]
            slow = row(slowness, z, x, tile)
            cost_x = slow * row(anisotropy, z, x, tile)
            cost_y = slow * row(anisotropy, depth + z, x, tile)
            cost_z = slow * row(anisotropy, 2 * depth + z, x, tile)
            edge = pltpu.roll(halo[z], width_y - 1 - 2 * x, 1)
            below = jnp.where(lane == 0, edge, pltpu.roll(u, 1, 1)) + cost_y
            above = jnp.where(lane == width_y - 1, edge, pltpu.roll(u, width_y - 1, 1)) + cost_y
            values = [u, below, above]
            values.append(field[x, z - 1] + cost_z if z > 0 else None)
            values.append(field[x, z + 1] + cost_z if z < depth - 1 else None)
            least = functools.reduce(jnp.minimum, [v for v in values if v is not None])
            parts = [None if v is None else weight(least - v) for v in values]
            total = functools.reduce(jnp.add, [p for p in parts if p is not None])
            level = least - TAU * jnp.log(total)
            if z < near:
                scale = 1.0 / total
                keep_level(x, z, level, [None if p is None else p * scale for p in parts])
            out.append((level, state[z] + cost_x))
        return [soft_pair(level, reach) for level, reach in out]

    return one


def first_sweep_kernel(
    count, place, field, from_left, from_right, far, slowness, anisotropy, local, levels, sides, message, halo, block
):
    width_x, depth, quakes, width_y = field.shape
    tile = (quakes, width_y)

    def keep_level(x, z, level, w):
        levels[x, z] = level
        sideways = row(anisotropy, depth + z, x, tile) * (w[1] + w[2])
        vertical = w[4] if w[3] is None else w[3] + w[4]
        sides[x, z] = sideways + row(anisotropy, 2 * depth + z, x, tile) * vertical

    one = sweep(1, levels.shape[1], place, field, from_left, from_right, slowness, anisotropy, halo, keep_level)

    def step(x, state):
        state = one(x, state)
        for z in range(depth):
            local[x, z] = state[z]
        return state

    state = lax.fori_loop(0, width_x, step, [jnp.full(tile, BIG, jnp.float32)] * depth)
    for z in range(depth):
        total = jnp.sum(slowness[z] * anisotropy[z], axis=0, keepdims=True)
        block[z : z + 1, :] = total
    per = message.shape[1] - 2
    owners = depth // per
    records = far[...]
    for p in range(count):
        for k in range(per):
            message[p, k] = state[p * per + k] if p < owners else jnp.zeros(tile, jnp.float32)
        message[p, per] = jnp.zeros(tile, jnp.float32)
        if p < owners:
            message[p, per, :per, :] = block[p * per : (p + 1) * per, :]
        message[p, per + 1] = records


def second_sweep_kernel(
    count, place, field, from_left, from_right, slowness, anisotropy, local, levels, shares, message, halo
):
    width_x, depth, quakes, width_y = field.shape
    tile = (quakes, width_y)

    def keep_level(x, z, level, w):
        levels[x] = level
        shares[0, x] = w[0]
        shares[1, x] = w[1]
        shares[2, x] = w[2]
        shares[3, x] = w[4]

    one = sweep(-1, 1, place, field, from_left, from_right, slowness, anisotropy, halo, keep_level)

    def step(lap, state):
        state = one(lap, state)
        for z in range(depth):
            local[width_x - 1 - lap, z] = state[z]
        return state

    state = lax.fori_loop(0, width_x, step, [jnp.full(tile, BIG, jnp.float32)] * depth)
    per = message.shape[1]
    owners = depth // per
    for p in range(count):
        for k in range(per):
            message[p, k] = state[p * per + k] if p < owners else jnp.zeros(tile, jnp.float32)


def blocks_kernel(count, per, backward, reach, total, entering):
    tile = entering.shape[2:]
    state = [jnp.full(tile, BIG, jnp.float32)] * per
    for lap in range(count):
        device = count - 1 - lap if backward else lap
        for k in range(per):
            entering[device, k] = state[k]
            passed = state[k] + jnp.broadcast_to(total[device, per, k : k + 1, :], tile)
            state[k] = soft_pair(reach[device, k], passed)


def first_finish_kernel(local, entering, slowness, anisotropy, levels, sides, times, edge, slopes, gains):
    width_x, depth, quakes, width_y = local.shape
    tile = (quakes, width_y)
    near = levels.shape[1]

    def one(x, carry):
        running, prior, edges = carry
        sums, values = [], []
        for z in range(depth):
            cost = row(slowness, z, x, tile) * row(anisotropy, z, x, tile)
            sums.append(running[z] + cost)
            value = soft_pair(local[x, z], entering[z] + sums[z])
            times[x, z] = value
            values.append(value)
            if z < near:
                keep, slope = split_pair(levels[x, z], prior[z] + cost)
                slopes[x, z] = slope
                gains[x, z] = slope * row(anisotropy, z, x, tile) + keep * sides[x, z]
        return sums, values[:near], gather_edge(edges, values, x)

    blank = [jnp.zeros(tile, jnp.float32)] * depth
    carry = (blank, [entering[z] for z in range(near)], blank)
    _, _, edges = lax.fori_loop(0, width_x, one, carry)
    edge[...] = edge_rows(edges, edge.shape[0])


def records_kernel(count, rows_of, place, cell, message, sums, counts):
    width_x, quakes, width_y = sums.shape
    per = message.shape[1] - 2
    span_y = place[2]
    many = place[6]
    lane = lanes((quakes, width_y))
    column = lax.broadcasted_iota(jnp.int32, (width_y, width_y), 0)
    total = [jnp.zeros((width_x * quakes, width_y), jnp.float32) for _ in range(3)]
    tally = jnp.zeros((width_x, width_y), jnp.float32)
    share = width_y // rows_of
    for chunk in range(cell.shape[0]):
        records = jnp.zeros((quakes, width_y), jnp.float32)
        for part in range(share):
            piece = message[chunk * share + part, per + 1]
            moved = pltpu.roll(piece, part * rows_of, 1) if part else piece
            records = jnp.where(lane // rows_of == part, moved, records)
        cells = cell[chunk : chunk + 1, :]
        station_x = lax.shift_right_logical(cells, many) - place[0]
        station_y = (cells & (span_y - 1)) - place[1]
        at_y = (column == jnp.broadcast_to(station_y, column.shape)).astype(jnp.float32).astype(jnp.bfloat16)
        one_x = lax.broadcasted_iota(jnp.int32, (width_x, width_y), 0)
        at_x = (one_x == jnp.broadcast_to(station_x, one_x.shape)).astype(jnp.float32)
        high = records.astype(jnp.bfloat16).astype(jnp.float32)
        middle = (records - high).astype(jnp.bfloat16).astype(jnp.float32)
        low = records - high - middle
        dims = (((1,), (1,)), ((), ()))
        for i, piece in enumerate((high, middle, low)):
            spread = jnp.concatenate(
                [piece * jnp.broadcast_to(at_x[x : x + 1], piece.shape) for x in range(width_x)], 0
            ).astype(jnp.bfloat16)
            total[i] += lax.dot_general(spread, at_y, dims, preferred_element_type=jnp.float32)
        tally += lax.dot_general(at_x.astype(jnp.bfloat16), at_y, dims, preferred_element_type=jnp.float32)
    sums[...] = (total[0] + total[1] + total[2]).reshape(sums.shape)
    counts[...] = tally


def second_finish_kernel(
    count, local, entering, slowness, anisotropy, levels, sums, counts, times, slopes, keeps, misfits, message
):
    width_x, depth, quakes, width_y = local.shape
    tile = (quakes, width_y)

    def one(lap, carry):
        x = width_x - 1 - lap
        running, prior = carry
        out = []
        for z in range(depth):
            cost = row(slowness, z, x, tile) * row(anisotropy, z, x, tile)
            out.append(running[z] + cost)
            value = soft_pair(local[x, z], entering[z] + out[z])
            times[pl.ds(z * width_x + x, quakes, stride=depth * width_x), :] = value
            if z == 0:
                keep, slope = split_pair(levels[x], prior + cost)
                slopes[x] = slope
                keeps[x] = keep
                tally = jnp.broadcast_to(counts[pl.ds(x, 1), :], tile)
                misfits[x] = ADJ_SCALE * (tally * value - sums[x])
                top = value
        return out, top

    lax.fori_loop(0, width_x, one, ([jnp.zeros(tile, jnp.float32)] * depth, entering[0]))
    leaving = jnp.zeros(tile, jnp.float32)
    through = jnp.ones(tile, jnp.float32)
    for x in range(width_x):
        leaving = slopes[x] * (misfits[x] + leaving)
        through = slopes[x] * through
    for p in range(count):
        message[p, 0] = leaving
        message[p, 1] = through


def linear_carry(count, me, backward, message, loc, factor, tile):
    state = jnp.zeros(tile, jnp.float32)
    for lap in range(count):
        device = count - 1 - lap if backward else lap
        ahead = device > me if backward else device < me
        state = jnp.where(ahead, message[device, loc] + message[device, factor] * state, state)
    return state


def second_adjoint_kernel(count, place, blocks, slopes, keeps, misfits, shares, anisotropy, through, kernel, edge):
    width_x, quakes, width_y = slopes.shape
    tile = (quakes, width_y)
    depth = anisotropy.shape[0] // 3
    lane = lanes(tile)
    state = linear_carry(count, place[7], False, blocks, 0, 1, tile)
    edges = jnp.zeros(tile, jnp.float32)
    for x in range(width_x):
        total = misfits[x] + state
        state = slopes[x] * total
        passed = keeps[x] * total
        through[x] = passed
        sideways = row(anisotropy, depth, x, tile) * (shares[1, x] + shares[2, x])
        sideways = sideways + row(anisotropy, 2 * depth, x, tile) * shares[3, x]
        terms = state * row(anisotropy, 0, x, tile) + passed * sideways
        kernel[x : x + 1, :] = jnp.sum(terms, axis=0, keepdims=True)
        outgoing = passed * jnp.where(lane == 0, shares[1, x], shares[2, x])
        (edges,) = gather_edge([edges], [outgoing], x)
    edge[...] = edges


def first_adjoint_kernel(count, place, through, shares, from_left, from_right, slopes, entries, message):
    width_x, near, quakes, width_y = slopes.shape
    tile = (quakes, width_y)
    lane = lanes(tile)
    left = jnp.where(place[4] == 1, 0.0, from_left[...])
    right = jnp.where(place[5] == 1, 0.0, from_right[...])
    leaving = [jnp.zeros(tile, jnp.float32)] * near
    factor = [jnp.ones(tile, jnp.float32)] * near
    for x in reversed(range(width_x)):
        passed = through[x]
        above = pltpu.roll(passed * shares[1, x], width_y - 1, 1)
        above = jnp.where(lane == width_y - 1, pltpu.roll(right, width_y - 2 - 2 * x, 1), above)
        below = pltpu.roll(passed * shares[2, x], 1, 1)
        below = jnp.where(lane == 0, pltpu.roll(left, (width_y - 2 * x) % width_y, 1), below)
        entry = (passed * shares[0, x] + above + below, passed * shares[3, x])
        for z in range(near):
            entries[x, z] = entry[z]
            leaving[z] = slopes[x, z] * (entry[z] + leaving[z])
            factor[z] = slopes[x, z] * factor[z]
    for p in range(count):
        for z in range(near):
            message[p, z] = leaving[z]
            message[p, near + z] = factor[z]


def kernel_kernel(count, place, blocks, entries, slopes, gains, top, kernel):
    width_x, near, quakes, width_y = slopes.shape
    tile = (quakes, width_y)
    state = [linear_carry(count, place[7], True, blocks, z, near + z, tile) for z in range(near)]
    for x in reversed(range(width_x)):
        for z in range(near):
            total = entries[x, z] + state[z]
            state[z] = slopes[x, z] * total
            value = jnp.sum(total * gains[x, z], axis=0, keepdims=True)
            if z == 0:
                value = value + top[x : x + 1, :]
            kernel[z, x : x + 1, :] = value
    for z in range(near, kernel.shape[0]):
        kernel[z] = jnp.zeros(kernel.shape[1:], jnp.float32)


def call(kernel, shapes, specs, operands, scratch=()):
    many = isinstance(shapes, list)
    out = [jax.ShapeDtypeStruct(s, jnp.float32) for s in (shapes if many else [shapes])]
    result = pl.pallas_call(
        kernel,
        out_shape=out,
        in_specs=specs,
        out_specs=[VMEM] * len(out),
        scratch_shapes=list(scratch),
        compiler_params=PARAMS,
    )(*operands)
    return result if many else result[0]


def traded(message):
    return lax.all_to_all(message, "gx", 0, 0, tiled=True)


def rotated(value, axis, by):
    count = lax.axis_size(axis)
    return lax.ppermute(value, axis, [(i, (i + by) % count) for i in range(count)])


def body(warm_start, slowness, anisotropy, observed, station_cell, source_cell):
    quakes, depth, width_x, width_y = warm_start.shape
    count_x, count_y = lax.axis_size("gx"), lax.axis_size("gy")
    index_x, index_y = lax.axis_index("gx"), lax.axis_index("gy")
    span_x, span_y = width_x * count_x, width_y * count_y
    near = 2
    per = max(1, depth // count_x)
    owners = depth // per
    tile = (quakes, width_y)
    field = (width_x, depth) + tile
    place = jnp.stack(
        [
            index_x * width_x,
            index_y * width_y,
            jnp.int32(span_y),
            jnp.int32(span_x * span_y),
            (index_y == 0).astype(jnp.int32),
            (index_y == count_y - 1).astype(jnp.int32),
            jnp.int32(span_y.bit_length() - 1),
            index_x,
        ]
    ).astype(jnp.int32)
    anis = anisotropy.reshape(3 * depth, width_x, width_y)
    local_records = observed.shape[1]

    start, edge = call(
        pack_kernel,
        [field, (2 * width_x + quakes, width_y)],
        [SMEM, SMEM, VMEM, VMEM],
        [place, source_cell, warm_start.reshape(quakes * depth * width_x, width_y), observed],
    )
    from_left = rotated(edge, "gy", 1)
    from_right = rotated(edge, "gy", -1)
    far = {0: observed, 1: from_left[2 * width_x :, :local_records]}
    far[count_y - 1] = from_right[2 * width_x :, :local_records]
    for by in range(2, count_y - 1):
        far[by] = rotated(observed, "gy", by)
    pile = jnp.stack([far[by] for by in range(count_y)])
    records = jnp.concatenate([pile[(index_y - j) % count_y] for j in range(count_y)], 1)
    rows_of = records.shape[1]
    records = jnp.pad(records, ((0, 0), (0, width_y - rows_of)))

    near_field = (width_x, near) + tile
    local, levels, sides, message = call(
        functools.partial(first_sweep_kernel, count_x),
        [field, near_field, near_field, (count_x, per + 2) + tile],
        [SMEM] + [VMEM] * 6,
        [place, start, from_left, from_right, records, slowness, anis],
        [pltpu.VMEM((depth,) + tile, jnp.float32), pltpu.VMEM((depth, width_y), jnp.float32)],
    )
    blocks_one = traded(message)

    def entering_of(reach, backward):
        entering = call(
            functools.partial(blocks_kernel, count_x, per, backward),
            (count_x, per) + tile,
            [VMEM, VMEM],
            [reach, blocks_one],
        )
        return traded(entering).reshape((count_x * per,) + tile)[:depth]

    entering = entering_of(blocks_one, False)
    sums, counts = call(
        functools.partial(records_kernel, count_x, rows_of),
        [(width_x,) + tile, (width_x, width_y)],
        [SMEM, VMEM, VMEM],
        [place, station_cell.reshape(-1, width_y), blocks_one],
    )
    times_one, edge, slopes_one, gains_one = call(
        first_finish_kernel,
        [field, (2 * width_x, width_y), near_field, near_field],
        [VMEM] * 6,
        [local, entering, slowness, anis, levels, sides],
    )
    from_left = rotated(edge, "gy", 1)
    from_right = rotated(edge, "gy", -1)
    top_field = (width_x,) + tile
    local, levels, shares, message = call(
        functools.partial(second_sweep_kernel, count_x),
        [field, top_field, (4,) + top_field, (count_x, per) + tile],
        [SMEM] + [VMEM] * 5,
        [place, times_one, from_left, from_right, slowness, anis],
        [pltpu.VMEM((depth,) + tile, jnp.float32)],
    )
    entering = entering_of(traded(message), True)
    times_two, slopes_two, keeps_two, misfits, message = call(
        functools.partial(second_finish_kernel, count_x),
        [(quakes * depth * width_x, width_y), top_field, top_field, top_field, (count_x, 2) + tile],
        [VMEM] * 7,
        [local, entering, slowness, anis, levels, sums, counts],
    )
    through, kernel_two, edge = call(
        functools.partial(second_adjoint_kernel, count_x),
        [top_field, (width_x, width_y), tile],
        [SMEM] + [VMEM] * 6,
        [place, traded(message), slopes_two, keeps_two, misfits, shares, anis],
    )
    from_left = rotated(edge, "gy", 1)
    from_right = rotated(edge, "gy", -1)
    entries, message = call(
        functools.partial(first_adjoint_kernel, count_x),
        [near_field, (count_x, 2 * near) + tile],
        [SMEM] + [VMEM] * 5,
        [place, through, shares, from_left, from_right, slopes_one],
    )
    kernel = call(
        functools.partial(kernel_kernel, count_x),
        (depth, width_x, width_y),
        [SMEM] + [VMEM] * 5,
        [place, traded(message), entries, slopes_one, gains_one, kernel_two],
    )
    return (times_two.reshape(warm_start.shape), kernel)


def solution(mesh):
    return jax.shard_map(
        body,
        mesh=mesh,
        in_specs=(
            P(None, None, "gx", "gy"),
            P(None, "gx", "gy"),
            P(None, None, "gx", "gy"),
            P(None, ("gx", "gy")),
            P(),
            P(),
        ),
        out_specs=(P(None, None, "gx", "gy"), P(None, "gx", "gy")),
        check_vma=False,
    )
```

```python
import functools
import math

import jax
import jax.numpy as jnp
from jax import lax
from jax.experimental import pallas as pl
from jax.experimental.pallas import tpu as pltpu
from jax.sharding import PartitionSpec as P

TAU = 0.05
BIG = 10000.0
ADJ_SCALE = 0.1
RATE = math.log2(math.e) / TAU
VMEM = pl.BlockSpec(memory_space=pltpu.VMEM)
SMEM = pl.BlockSpec(memory_space=pltpu.SMEM)
PARAMS = pltpu.CompilerParams(vmem_limit_bytes=48 * 1024 * 1024)


def weight(gap):
    return jnp.exp2(gap * RATE)


def soft_pair(first, second):
    return jnp.minimum(first, second) - TAU * jnp.log(1.0 + weight(-jnp.abs(first - second)))


def split_pair(first, second):
    gap = weight(-jnp.abs(first - second))
    share = 1.0 / (1.0 + gap)
    less = gap * share
    nearer = first <= second
    return jnp.where(nearer, share, less), jnp.where(nearer, less, share)


def lanes(shape):
    return lax.broadcasted_iota(jnp.int32, shape, len(shape) - 1)


def row(ref, index, x, like):
    return jnp.broadcast_to(ref[index, pl.ds(x, 1), :], like)


def gather_edge(edges, values, x):
    here = (lanes(values[0].shape) >> 1) == x
    return [jnp.where(here, pltpu.roll(v, 2 * x + 1, 1), a) for a, v in zip(edges, values)]


def edge_rows(edges, count):
    return jnp.transpose(jnp.concatenate(edges, 0))[:count]


def pack_kernel(place, source, warm, observed, start, edge):
    width_x, depth, quakes, width_y = start.shape
    tile = (quakes, width_y)
    quake = lax.broadcasted_iota(jnp.int32, tile, 0)
    span_y = place[2]
    plane = place[3]
    base = lanes(tile) + place[0] * span_y + place[1]
    cell = jnp.zeros(tile, jnp.int32)
    for e in range(quakes):
        cell = jnp.where(quake == e, source[e], cell)
    cell = cell - base

    def one(x, edges):
        levels = []
        for z in range(depth):
            value = warm[pl.ds(z * width_x + x, quakes, stride=depth * width_x), :]
            value = jnp.where(cell == z * plane + x * span_y, 0.0, value)
            start[x, z] = value
            levels.append(value)
        return gather_edge(edges, levels, x)

    edges = lax.fori_loop(0, width_x, one, [jnp.zeros(tile, jnp.float32)] * depth)
    edge[: 2 * width_x, :] = edge_rows(edges, 2 * width_x)
    edge[2 * width_x :, :] = jnp.zeros((quakes, width_y), jnp.float32)
    edge[2 * width_x :, : observed.shape[1]] = observed[...]


def halo_columns(place, from_left, from_right, width_x, depth):
    left = jnp.where(place[4] == 1, BIG, pltpu.roll(from_left[: 2 * width_x, :], 1, 0))
    right = jnp.where(place[5] == 1, BIG, pltpu.roll(from_right[: 2 * width_x, :], 2 * width_x - 1, 0))
    odd = lax.broadcasted_iota(jnp.int32, left.shape, 0) % 2 == 1
    both = jnp.where(odd, left, right)
    rest = jnp.zeros((left.shape[1] - 2 * width_x, left.shape[1]), jnp.float32)
    return jnp.transpose(jnp.concatenate([both, rest], 0))


def sweep(direction, near, place, field, from_left, from_right, slowness, anisotropy, halo, keep_level):
    width_x, depth, quakes, width_y = field.shape
    tile = (quakes, width_y)
    lane = lanes(tile)
    halo[...] = halo_columns(place, from_left, from_right, width_x, depth).reshape(depth, quakes, width_y)

    def one(step, state):
        x = step if direction > 0 else width_x - 1 - step
        out = []
        for z in range(depth):
            u = field[x, z]
            slow = row(slowness, z, x, tile)
            cost_x = slow * row(anisotropy, z, x, tile)
            cost_y = slow * row(anisotropy, depth + z, x, tile)
            cost_z = slow * row(anisotropy, 2 * depth + z, x, tile)
            edge = pltpu.roll(halo[z], width_y - 1 - 2 * x, 1)
            below = jnp.where(lane == 0, edge, pltpu.roll(u, 1, 1)) + cost_y
            above = jnp.where(lane == width_y - 1, edge, pltpu.roll(u, width_y - 1, 1)) + cost_y
            values = [u, below, above]
            values.append(field[x, z - 1] + cost_z if z > 0 else None)
            values.append(field[x, z + 1] + cost_z if z < depth - 1 else None)
            least = functools.reduce(jnp.minimum, [v for v in values if v is not None])
            parts = [None if v is None else weight(least - v) for v in values]
            total = functools.reduce(jnp.add, [p for p in parts if p is not None])
            level = least - TAU * jnp.log(total)
            if z < near:
                scale = 1.0 / total
                keep_level(x, z, level, [None if p is None else p * scale for p in parts])
            out.append((level, state[z] + cost_x))
        return [soft_pair(level, reach) for level, reach in out]

    return one


def owned(me, turn, count, per, depth):
    return jnp.minimum(lax.rem(me + turn, count) * per, depth - per)


def first_sweep_kernel(
    count, place, field, from_left, from_right, far, slowness, anisotropy, local, levels, sides, *rest
):
    messages, (halo, block, leaving) = rest[:count], rest[count:]
    width_x, depth, quakes, width_y = field.shape
    tile = (quakes, width_y)

    def keep_level(x, z, level, w):
        levels[x, z] = level
        sideways = row(anisotropy, depth + z, x, tile) * (w[1] + w[2])
        vertical = w[4] if w[3] is None else w[3] + w[4]
        sides[x, z] = sideways + row(anisotropy, 2 * depth + z, x, tile) * vertical

    one = sweep(1, levels.shape[1], place, field, from_left, from_right, slowness, anisotropy, halo, keep_level)

    def step(x, state):
        state = one(x, state)
        for z in range(depth):
            local[x, z] = state[z]
        return state

    state = lax.fori_loop(0, width_x, step, [jnp.full(tile, BIG, jnp.float32)] * depth)
    for z in range(depth):
        total = jnp.sum(slowness[z] * anisotropy[z], axis=0, keepdims=True)
        block[z] = jnp.broadcast_to(total, tile)
        leaving[z] = state[z]
    per = messages[0].shape[0] - 2
    quake = lax.broadcasted_iota(jnp.int32, tile, 0)
    records = far[...]
    for turn, message in enumerate(messages):
        first = owned(place[7], turn, count, per, depth)
        totals = jnp.zeros(tile, jnp.float32)
        for k in range(per):
            message[k] = leaving[first + k]
            totals = jnp.where(quake == k, block[first + k], totals)
        message[per] = totals
        message[per + 1] = records


def second_sweep_kernel(
    count, place, field, from_left, from_right, slowness, anisotropy, local, levels, shares, *rest
):
    messages, (halo, leaving) = rest[:count], rest[count:]
    width_x, depth, quakes, width_y = field.shape
    tile = (quakes, width_y)

    def keep_level(x, z, level, w):
        levels[x] = level
        shares[0, x] = w[0]
        shares[1, x] = w[1]
        shares[2, x] = w[2]
        shares[3, x] = w[4]

    one = sweep(-1, 1, place, field, from_left, from_right, slowness, anisotropy, halo, keep_level)

    def step(lap, state):
        state = one(lap, state)
        for z in range(depth):
            local[width_x - 1 - lap, z] = state[z]
        return state

    state = lax.fori_loop(0, width_x, step, [jnp.full(tile, BIG, jnp.float32)] * depth)
    for z in range(depth):
        leaving[z] = state[z]
    per = messages[0].shape[0]
    for turn, message in enumerate(messages):
        first = owned(place[7], turn, count, per, depth)
        for k in range(per):
            message[k] = leaving[first + k]


def sender(me, turn, count):
    return lax.rem(me + count - turn, count)


def blocks_kernel(count, per, backward, place, *rest):
    if backward:
        received, totals, entering = rest[:count], rest[count], rest[count + 1 : -1]
    else:
        received, entering, totals = rest[:count], rest[count : 2 * count], rest[-2]
    blocks = rest[-1]
    tile = blocks.shape[2:]
    me = place[7]
    for turn, message in enumerate(received):
        device = sender(me, turn, count)
        for k in range(per):
            blocks[device, k] = message[k]
        if not backward:
            totals[device] = message[per]
    state = [jnp.full(tile, BIG, jnp.float32)] * per
    for lap in range(count):
        device = count - 1 - lap if backward else lap
        for k in range(per):
            reach = blocks[device, k]
            blocks[device, k] = state[k]
            passed = state[k] + jnp.broadcast_to(totals[device, k : k + 1, :], tile)
            state[k] = soft_pair(reach, passed)
    for turn, message in enumerate(entering):
        device = lax.rem(me + turn, count)
        for k in range(per):
            message[k] = blocks[device, k]


def placed(me, received, count, depth, entering):
    per = received[0].shape[0]
    for turn, message in enumerate(received):
        device = sender(me, turn, count)

        @pl.when(device * per < depth)
        def _(device=device, message=message):
            for k in range(per):
                entering[device * per + k] = message[k]


def first_finish_kernel(count, place, local, slowness, anisotropy, levels, sides, *rest):
    received, (times, edge, slopes, gains, entering) = rest[:count], rest[count:]
    placed(place[7], received, count, local.shape[1], entering)
    width_x, depth, quakes, width_y = local.shape
    tile = (quakes, width_y)
    near = levels.shape[1]

    def one(x, carry):
        running, prior, edges = carry
        sums, values = [], []
        for z in range(depth):
            cost = row(slowness, z, x, tile) * row(anisotropy, z, x, tile)
            sums.append(running[z] + cost)
            value = soft_pair(local[x, z], entering[z] + sums[z])
            times[x, z] = value
            values.append(value)
            if z < near:
                keep, slope = split_pair(levels[x, z], prior[z] + cost)
                slopes[x, z] = slope
                gains[x, z] = slope * row(anisotropy, z, x, tile) + keep * sides[x, z]
        return sums, values[:near], gather_edge(edges, values, x)

    blank = [jnp.zeros(tile, jnp.float32)] * depth
    carry = (blank, [entering[z] for z in range(near)], blank)
    _, _, edges = lax.fori_loop(0, width_x, one, carry)
    edge[...] = edge_rows(edges, edge.shape[0])


def records_kernel(count, rows_of, place, cell, *rest):
    received, (sums, counts, pieces) = rest[:count], rest[count:]
    for turn, message in enumerate(received):
        pieces[sender(place[7], turn, count)] = message[message.shape[0] - 1]
    width_x, quakes, width_y = sums.shape
    span_y = place[2]
    many = place[6]
    lane = lanes((quakes, width_y))
    column = lax.broadcasted_iota(jnp.int32, (width_y, width_y), 0)
    total = [jnp.zeros((width_x * quakes, width_y), jnp.float32) for _ in range(3)]
    tally = jnp.zeros((width_x, width_y), jnp.float32)
    share = width_y // rows_of
    for chunk in range(cell.shape[0]):
        records = jnp.zeros((quakes, width_y), jnp.float32)
        for part in range(share):
            piece = pieces[chunk * share + part]
            moved = pltpu.roll(piece, part * rows_of, 1) if part else piece
            records = jnp.where(lane // rows_of == part, moved, records)
        cells = cell[chunk : chunk + 1, :]
        station_x = lax.shift_right_logical(cells, many) - place[0]
        station_y = (cells & (span_y - 1)) - place[1]
        at_y = (column == jnp.broadcast_to(station_y, column.shape)).astype(jnp.float32).astype(jnp.bfloat16)
        one_x = lax.broadcasted_iota(jnp.int32, (width_x, width_y), 0)
        at_x = (one_x == jnp.broadcast_to(station_x, one_x.shape)).astype(jnp.float32)
        high = records.astype(jnp.bfloat16).astype(jnp.float32)
        middle = (records - high).astype(jnp.bfloat16).astype(jnp.float32)
        low = records - high - middle
        dims = (((1,), (1,)), ((), ()))
        for i, piece in enumerate((high, middle, low)):
            spread = jnp.concatenate(
                [piece * jnp.broadcast_to(at_x[x : x + 1], piece.shape) for x in range(width_x)], 0
            ).astype(jnp.bfloat16)
            total[i] += lax.dot_general(spread, at_y, dims, preferred_element_type=jnp.float32)
        tally += lax.dot_general(at_x.astype(jnp.bfloat16), at_y, dims, preferred_element_type=jnp.float32)
    sums[...] = (total[0] + total[1] + total[2]).reshape(sums.shape)
    counts[...] = tally


def second_finish_kernel(
    count, place, local, slowness, anisotropy, levels, sums, counts, *rest
):
    received, (times, slopes, keeps, misfits, message, entering) = rest[:count], rest[count:]
    placed(place[7], received, count, local.shape[1], entering)
    width_x, depth, quakes, width_y = local.shape
    tile = (quakes, width_y)

    def one(lap, carry):
        x = width_x - 1 - lap
        running, prior = carry
        out = []
        for z in range(depth):
            cost = row(slowness, z, x, tile) * row(anisotropy, z, x, tile)
            out.append(running[z] + cost)
            value = soft_pair(local[x, z], entering[z] + out[z])
            times[pl.ds(z * width_x + x, quakes, stride=depth * width_x), :] = value
            if z == 0:
                keep, slope = split_pair(levels[x], prior + cost)
                slopes[x] = slope
                keeps[x] = keep
                tally = jnp.broadcast_to(counts[pl.ds(x, 1), :], tile)
                misfits[x] = ADJ_SCALE * (tally * value - sums[x])
                top = value
        return out, top

    lax.fori_loop(0, width_x, one, ([jnp.zeros(tile, jnp.float32)] * depth, entering[0]))
    leaving = jnp.zeros(tile, jnp.float32)
    through = jnp.ones(tile, jnp.float32)
    for x in range(width_x):
        leaving = slopes[x] * (misfits[x] + leaving)
        through = slopes[x] * through
    message[0] = leaving
    message[1] = through


def linear_carry(count, me, backward, message, loc, factor, tile):
    state = jnp.zeros(tile, jnp.float32)
    for lap in range(count):
        device = count - 1 - lap if backward else lap
        ahead = device > me if backward else device < me
        state = jnp.where(ahead, message[device, loc] + message[device, factor] * state, state)
    return state


def second_adjoint_kernel(count, place, slopes, keeps, misfits, shares, anisotropy, *rest):
    received, (through, kernel, edge, blocks) = rest[: count - 1], rest[count - 1 :]
    for turn, message in enumerate(received):
        blocks[sender(place[7], turn + 1, count)] = message[...]
    width_x, quakes, width_y = slopes.shape
    tile = (quakes, width_y)
    depth = anisotropy.shape[0] // 3
    lane = lanes(tile)
    state = linear_carry(count, place[7], False, blocks, 0, 1, tile)
    edges = jnp.zeros(tile, jnp.float32)
    for x in range(width_x):
        total = misfits[x] + state
        state = slopes[x] * total
        passed = keeps[x] * total
        through[x] = passed
        sideways = row(anisotropy, depth, x, tile) * (shares[1, x] + shares[2, x])
        sideways = sideways + row(anisotropy, 2 * depth, x, tile) * shares[3, x]
        terms = state * row(anisotropy, 0, x, tile) + passed * sideways
        kernel[x : x + 1, :] = jnp.sum(terms, axis=0, keepdims=True)
        outgoing = passed * jnp.where(lane == 0, shares[1, x], shares[2, x])
        (edges,) = gather_edge([edges], [outgoing], x)
    edge[...] = edges


def first_adjoint_kernel(place, through, shares, from_left, from_right, slopes, entries, message):
    width_x, near, quakes, width_y = slopes.shape
    tile = (quakes, width_y)
    lane = lanes(tile)
    left = jnp.where(place[4] == 1, 0.0, from_left[...])
    right = jnp.where(place[5] == 1, 0.0, from_right[...])
    leaving = [jnp.zeros(tile, jnp.float32)] * near
    factor = [jnp.ones(tile, jnp.float32)] * near
    for x in reversed(range(width_x)):
        passed = through[x]
        above = pltpu.roll(passed * shares[1, x], width_y - 1, 1)
        above = jnp.where(lane == width_y - 1, pltpu.roll(right, width_y - 2 - 2 * x, 1), above)
        below = pltpu.roll(passed * shares[2, x], 1, 1)
        below = jnp.where(lane == 0, pltpu.roll(left, (width_y - 2 * x) % width_y, 1), below)
        entry = (passed * shares[0, x] + above + below, passed * shares[3, x])
        for z in range(near):
            entries[x, z] = entry[z]
            leaving[z] = slopes[x, z] * (entry[z] + leaving[z])
            factor[z] = slopes[x, z] * factor[z]
    for z in range(near):
        message[z] = leaving[z]
        message[near + z] = factor[z]


def kernel_kernel(count, place, entries, slopes, gains, top, *rest):
    received, (kernel, blocks) = rest[: count - 1], rest[count - 1 :]
    for turn, message in enumerate(received):
        blocks[sender(place[7], turn + 1, count)] = message[...]
    width_x, near, quakes, width_y = slopes.shape
    tile = (quakes, width_y)
    state = [linear_carry(count, place[7], True, blocks, z, near + z, tile) for z in range(near)]
    for x in reversed(range(width_x)):
        for z in range(near):
            total = entries[x, z] + state[z]
            state[z] = slopes[x, z] * total
            value = jnp.sum(total * gains[x, z], axis=0, keepdims=True)
            if z == 0:
                value = value + top[x : x + 1, :]
            kernel[z, x : x + 1, :] = value
    for z in range(near, kernel.shape[0]):
        kernel[z] = jnp.zeros(kernel.shape[1:], jnp.float32)


def call(kernel, shapes, specs, operands, scratch=()):
    many = isinstance(shapes, list)
    out = [jax.ShapeDtypeStruct(s, jnp.float32) for s in (shapes if many else [shapes])]
    result = pl.pallas_call(
        kernel,
        out_shape=out,
        in_specs=specs,
        out_specs=[VMEM] * len(out),
        scratch_shapes=list(scratch),
        compiler_params=PARAMS,
    )(*operands)
    return result if many else result[0]


def rotated(value, axis, by):
    count = lax.axis_size(axis)
    return lax.ppermute(value, axis, [(i, (i + by) % count) for i in range(count)])


def traded(messages):
    return [m if by == 0 else rotated(m, "gx", by) for by, m in enumerate(messages)]


def body(warm_start, slowness, anisotropy, observed, station_cell, source_cell):
    quakes, depth, width_x, width_y = warm_start.shape
    count_x, count_y = lax.axis_size("gx"), lax.axis_size("gy")
    index_x, index_y = lax.axis_index("gx"), lax.axis_index("gy")
    span_x, span_y = width_x * count_x, width_y * count_y
    near = 2
    per = max(1, depth // count_x)
    owners = depth // per
    tile = (quakes, width_y)
    field = (width_x, depth) + tile
    place = jnp.stack(
        [
            index_x * width_x,
            index_y * width_y,
            jnp.int32(span_y),
            jnp.int32(span_x * span_y),
            (index_y == 0).astype(jnp.int32),
            (index_y == count_y - 1).astype(jnp.int32),
            jnp.int32(span_y.bit_length() - 1),
            index_x,
        ]
    ).astype(jnp.int32)
    anis = anisotropy.reshape(3 * depth, width_x, width_y)
    local_records = observed.shape[1]

    start, edge = call(
        pack_kernel,
        [field, (2 * width_x + quakes, width_y)],
        [SMEM, SMEM, VMEM, VMEM],
        [place, source_cell, warm_start.reshape(quakes * depth * width_x, width_y), observed],
    )
    from_left = rotated(edge, "gy", 1)
    from_right = rotated(edge, "gy", -1)
    far = {0: observed, 1: from_left[2 * width_x :, :local_records]}
    far[count_y - 1] = from_right[2 * width_x :, :local_records]
    for by in range(2, count_y - 1):
        far[by] = rotated(observed, "gy", by)
    pile = jnp.stack([far[by] for by in range(count_y)])
    records = jnp.concatenate([pile[(index_y - j) % count_y] for j in range(count_y)], 1)
    rows_of = records.shape[1]
    records = jnp.pad(records, ((0, 0), (0, width_y - rows_of)))

    near_field = (width_x, near) + tile
    top_field = (width_x,) + tile
    level_field = pltpu.VMEM((depth,) + tile, jnp.float32)
    outs = call(
        functools.partial(first_sweep_kernel, count_x),
        [field, near_field, near_field] + [(per + 2,) + tile] * count_x,
        [SMEM] + [VMEM] * 6,
        [place, start, from_left, from_right, records, slowness, anis],
        [level_field] * 3,
    )
    local, levels, sides = outs[:3]
    blocks_one = traded(outs[3:])
    share = (per,) + tile
    outs = call(
        functools.partial(blocks_kernel, count_x, per, False),
        [share] * count_x + [(count_x,) + tile],
        [SMEM] + [VMEM] * count_x,
        [place] + blocks_one,
        [pltpu.VMEM((count_x,) + share, jnp.float32)],
    )
    totals = outs[-1]
    entering = traded(outs[:-1])
    sums, counts = call(
        functools.partial(records_kernel, count_x, rows_of),
        [top_field, (width_x, width_y)],
        [SMEM, VMEM] + [VMEM] * count_x,
        [place, station_cell.reshape(-1, width_y)] + blocks_one,
        [pltpu.VMEM((count_x,) + tile, jnp.float32)],
    )
    times_one, edge, slopes_one, gains_one = call(
        functools.partial(first_finish_kernel, count_x),
        [field, (2 * width_x, width_y), near_field, near_field],
        [SMEM] + [VMEM] * (5 + count_x),
        [place, local, slowness, anis, levels, sides] + entering,
        [level_field],
    )
    from_left = rotated(edge, "gy", 1)
    from_right = rotated(edge, "gy", -1)
    outs = call(
        functools.partial(second_sweep_kernel, count_x),
        [field, top_field, (4,) + top_field] + [share] * count_x,
        [SMEM] + [VMEM] * 5,
        [place, times_one, from_left, from_right, slowness, anis],
        [level_field] * 2,
    )
    local, levels, shares = outs[:3]
    entering = call(
        functools.partial(blocks_kernel, count_x, per, True),
        [share] * count_x,
        [SMEM] + [VMEM] * (count_x + 1),
        [place] + traded(outs[3:]) + [totals],
        [pltpu.VMEM((count_x,) + share, jnp.float32)],
    )
    times_two, slopes_two, keeps_two, misfits, message = call(
        functools.partial(second_finish_kernel, count_x),
        [(quakes * depth * width_x, width_y), top_field, top_field, top_field, (2,) + tile],
        [SMEM] + [VMEM] * (6 + count_x),
        [place, local, slowness, anis, levels, sums, counts] + traded(entering),
        [level_field],
    )
    through, kernel_two, edge = call(
        functools.partial(second_adjoint_kernel, count_x),
        [top_field, (width_x, width_y), tile],
        [SMEM] + [VMEM] * (4 + count_x),
        [place, slopes_two, keeps_two, misfits, shares, anis] + traded([message] * count_x)[1:],
        [pltpu.VMEM((count_x, 2) + tile, jnp.float32)],
    )
    from_left = rotated(edge, "gy", 1)
    from_right = rotated(edge, "gy", -1)
    entries, message = call(
        first_adjoint_kernel,
        [near_field, (2 * near,) + tile],
        [SMEM] + [VMEM] * 5,
        [place, through, shares, from_left, from_right, slopes_one],
    )
    kernel = call(
        functools.partial(kernel_kernel, count_x),
        (depth, width_x, width_y),
        [SMEM] + [VMEM] * (3 + count_x),
        [place, entries, slopes_one, gains_one, kernel_two] + traded([message] * count_x)[1:],
        [pltpu.VMEM((count_x, 2 * near) + tile, jnp.float32)],
    )
    return (times_two.reshape(warm_start.shape), kernel)


def solution(mesh):
    return jax.shard_map(
        body,
        mesh=mesh,
        in_specs=(
            P(None, None, "gx", "gy"),
            P(None, "gx", "gy"),
            P(None, None, "gx", "gy"),
            P(None, ("gx", "gy")),
            P(),
            P(),
        ),
        out_specs=(P(None, None, "gx", "gy"), P(None, "gx", "gy")),
        check_vma=False,
    )
```

```python
import functools
import math

import jax
import jax.numpy as jnp
from jax import lax
from jax.experimental import pallas as pl
from jax.experimental.pallas import tpu as pltpu
from jax.sharding import PartitionSpec as P

TAU = 0.05
ADJ_SCALE = 0.1
LOG2E = math.log2(math.e)
RATE = LOG2E / TAU
BIG = 10000.0 * RATE
UNROLL = 4
VMEM = pl.BlockSpec(memory_space=pltpu.VMEM)
SMEM = pl.BlockSpec(memory_space=pltpu.SMEM)
PARAMS = pltpu.CompilerParams(vmem_limit_bytes=48 * 1024 * 1024)


def softmin(values):
    least = functools.reduce(jnp.minimum, values)
    parts = [jnp.exp2(least - v) for v in values]
    total = functools.reduce(jnp.add, parts)
    return least - LOG2E * jnp.log(total), parts, total


def soft_pair(first, second):
    return jnp.minimum(first, second) - LOG2E * jnp.log(1.0 + jnp.exp2(-jnp.abs(first - second)))


def split_pair(first, second):
    gap = jnp.exp2(-jnp.abs(first - second))
    share = 1.0 / (1.0 + gap)
    less = gap * share
    nearer = first <= second
    return jnp.where(nearer, share, less), jnp.where(nearer, less, share)


def iota(shape, axis):
    return lax.broadcasted_iota(jnp.int32, shape, axis)


def row(ref, index, x, like):
    return jnp.broadcast_to(ref[index, pl.ds(x, 1), :], like)


def by_steps(count, step, carry):
    def group(i, carry):
        for j in range(UNROLL):
            carry = step(i * UNROLL + j, carry)
        return carry

    return lax.fori_loop(0, count // UNROLL, group, carry)


def packed(left, right):
    return jnp.where(iota(left.shape, 0) < 5, left, pltpu.roll(right, 2, 0))


def merged(left, right):
    return jnp.where(iota(left.shape, 0) < 4, left, right)


def shifted_down(tile, by):
    return pltpu.roll(tile, tile.shape[0] - by, 0)


def exact_parts(value):
    high = value.astype(jnp.bfloat16).astype(jnp.float32)
    middle = (value - high).astype(jnp.bfloat16).astype(jnp.float32)
    low = value - high - middle
    return [p.astype(jnp.bfloat16) for p in (high, middle, low)]


def pack_kernel(place, source, warm, observed, slowness, anisotropy, start, costs, edge):
    width_x, depth, quakes, width_y = start.shape
    tile = (quakes, width_y)
    quake = iota(tile, 0)
    lane = iota(tile, 1)
    span_y = place[2]
    plane = place[3]
    cell = jnp.zeros(tile, jnp.int32)
    for e in range(quakes):
        cell = jnp.where(quake == e, source[e], cell)
    cell = cell - (lane + place[0] * span_y + place[1])

    def one(x, edges):
        here = (lane >> 3) == x
        out = []
        for z in range(depth):
            value = warm[pl.ds(z * width_x + x, quakes, stride=depth * width_x), :] * RATE
            value = jnp.where(cell == z * plane + x * span_y, 0.0, value)
            start[x, z] = value
            out.append(jnp.where(here, pltpu.roll(value, 8 * x + 4, 1), edges[z]))
        return out

    edges = by_steps(width_x, one, [jnp.zeros(tile, jnp.float32)] * depth)
    rows = width_x * 8
    edge[:rows, :] = jnp.transpose(jnp.concatenate(edges, 0))
    wide = (width_x, width_y)
    group = iota(wide, 1) >> 3
    for k in range(3):
        columns = jnp.zeros(wide, jnp.float32)
        for z in range(depth):
            cost = slowness[z] * anisotropy[k * depth + z] * RATE
            costs[k * depth + z] = cost
            columns = jnp.where(group == z, pltpu.roll(cost, 8 * z + 4, 1), columns)
        edge[rows : rows + width_x, :] = columns
        rows += width_x
    edge[rows:, :] = jnp.zeros(tile, jnp.float32)
    edge[rows:, : observed.shape[1]] = observed[...]


def halo_columns(left, right):
    rows = []
    for l, r in zip(left, right):
        rows.append(jnp.where(iota(l.shape, 0) == 4, r, pltpu.roll(l, 2, 0)))
    return jnp.transpose(jnp.concatenate(rows, 0))


def strip_costs(own, from_left, from_right, out, width_x, depth):
    tile = own.shape[1]
    base = width_x * 8
    lane = iota((8, tile), 1)
    low = (lane & 7) < 4
    mine = (lane & 7) == iota((8, tile), 0)
    spread = ((iota((tile, tile), 0) >> 3) == (iota((tile, tile), 1) >> 3)).astype(jnp.float32)
    spread = spread.astype(jnp.bfloat16)
    for side in range(2):
        for k in range(3):
            rows = []
            for x in range(width_x):
                at = slice(base + k * width_x + x, base + k * width_x + x + 1)
                here = jnp.broadcast_to(own[at, :], lane.shape)
                there = jnp.broadcast_to((from_right if side else from_left)[at, :], lane.shape)
                value = jnp.where(low, here, there) if side else jnp.where(low, there, here)
                rows.append(jnp.where(mine, value, 0.0))
            whole = jnp.concatenate(rows, 0)
            total = 0.0
            for part in reversed(exact_parts(whole)):
                total = total + lax.dot_general(
                    part, spread, (((1,), (0,)), ((), ())), preferred_element_type=jnp.float32
                )
            out[3 * side + k] = total.reshape(width_x, 8, tile)


def sweep_step(x, near, field, strip, costs, edge_costs, halo, state, strip_state, keep, keep_strip):
    depth = field.shape[1]
    tile = field.shape[2:]
    width_y = tile[1]
    lane = iota(tile, 1)
    sub = iota(tile, 0)
    out = []
    for z in range(depth):
        u = field[x, z]
        cost_x = row(costs, z, x, tile)
        cost_y = row(costs, depth + z, x, tile)
        cost_z = row(costs, 2 * depth + z, x, tile)
        edge = pltpu.roll(halo[z], width_y - 5 - 8 * x, 1)
        values = [u]
        values.append(jnp.where(lane == 0, edge, pltpu.roll(u, 1, 1)) + cost_y)
        values.append(jnp.where(lane == width_y - 1, edge, pltpu.roll(u, width_y - 1, 1)) + cost_y)
        if z > 0:
            values.append(field[x, z - 1] + cost_z)
        if z < depth - 1:
            values.append(field[x, z + 1] + cost_z)
        level, parts, total = softmin(values)
        if z < near:
            scale = 1.0 / total
            keep(x, z, level, [p * scale for p in parts])
        out.append(soft_pair(level, state[z] + cost_x))
    strips, levels, weights = [], [], []
    for side in range(2):
        u = strip[x, side]
        cost_y = edge_costs[3 * side + 1, x]
        cost_z = edge_costs[3 * side + 2, x]
        values = [u, pltpu.roll(u, 1, 0) + cost_y, pltpu.roll(u, 7, 0) + cost_y]
        values.append(jnp.where(lane < 8, BIG, pltpu.roll(u, 8, 1)) + cost_z)
        values.append(jnp.where(lane >= width_y - 8, BIG, pltpu.roll(u, width_y - 8, 1)) + cost_z)
        level, parts, total = softmin(values)
        strips.append(soft_pair(level, strip_state[side] + edge_costs[3 * side, x]))
        levels.append(level)
        weights.append(parts[2 - side] / total)
    if keep_strip is not None:
        keep_strip(x, merged(*levels), merged(*weights))
    return out, strips


def trade_messages(messages, state, extras, depth):
    count = messages.shape[0]
    per = messages.shape[1] - len(extras)
    tile = messages.shape[2:]
    for p in range(count):
        for k in range(per):
            z = p * per + k
            messages[p, k] = state[z] if z < depth else jnp.zeros(tile, jnp.float32)
        for i, extra in enumerate(extras):
            messages[p, per + i] = extra(p) if callable(extra) else extra


def first_sweep_kernel(
    place, field, own, from_left, from_right, costs, anisotropy,
    local, local_strip, edge_costs, levels, sides, message, halo, strip,
):
    width_x, depth, quakes, width_y = field.shape
    tile = (quakes, width_y)
    low = iota(tile, 0) < 4
    left, right = [], []
    for x in range(width_x):
        at = slice(8 * x, 8 * x + 8)
        before = jnp.where(place[4] == 1, BIG, from_left[at, :])
        after = jnp.where(place[5] == 1, BIG, from_right[at, :])
        left.append(jnp.where(low, before, own[at, :]))
        right.append(jnp.where(low, own[at, :], after))
        strip[x, 0] = left[x]
        strip[x, 1] = right[x]
    halo[...] = halo_columns(left, right).reshape(halo.shape)
    strip_costs(own, from_left, from_right, edge_costs, width_x, depth)

    def keep(x, z, level, w):
        levels[x, z] = level
        vertical = w[3] if z == 0 else w[3] + w[4]
        sideways = row(anisotropy, depth + z, x, tile) * (w[1] + w[2])
        sides[x, z] = sideways + row(anisotropy, 2 * depth + z, x, tile) * vertical

    def step(x, carry):
        state, strips = sweep_step(
            x, levels.shape[1], field, strip, costs, edge_costs, halo, *carry, keep, None
        )
        for z in range(depth):
            local[x, z] = state[z]
        for side in range(2):
            local_strip[x, side] = strips[side]
        return state, strips

    blank = jnp.full(tile, BIG, jnp.float32)
    state, strips = by_steps(width_x, step, ([blank] * depth, [blank] * 2))
    totals = [jnp.sum(costs[z], axis=0, keepdims=True) for z in range(depth)]
    strip_total = packed(jnp.sum(edge_costs[0], axis=0), jnp.sum(edge_costs[3], axis=0))
    reach = packed(*strips)
    per = message.shape[1] - 2
    sub = iota(tile, 0)

    def with_totals(p):
        value = reach
        for k in range(per):
            if p * per + k < depth:
                value = jnp.where(sub == k, jnp.broadcast_to(totals[p * per + k], tile), value)
        return value

    trade_messages(message, state, [with_totals, strip_total], depth)


def blocks_kernel(count, per, backward, place, received, totals, entering, entering_strip):
    tile = entering.shape[2:]
    me = place[6]
    state = [jnp.full(tile, BIG, jnp.float32)] * per
    strip = jnp.full(tile, BIG, jnp.float32)
    for lap in range(count):
        device = count - 1 - lap if backward else lap
        for k in range(per):
            entering[device, k] = state[k]
            passed = state[k] + jnp.broadcast_to(totals[device, per, k : k + 1, :], tile)
            state[k] = soft_pair(received[device, k], passed)
        ahead = device > me if backward else device < me
        passed = soft_pair(received[device, per], strip + totals[device, per + 1])
        strip = jnp.where(ahead, passed, strip)
    entering_strip[...] = strip


def second_sweep_kernel(
    place, first, first_strip, entering, entering_strip, costs, edge_costs, anisotropy, levels_one, sides, records,
    local, local_strip, levels, levels_strip, shares, shares_strip, slopes, gains, message, field, strip, halo,
):
    width_x, depth, quakes, width_y = first.shape
    tile = (quakes, width_y)
    near = levels_one.shape[1]
    sub = iota(tile, 0)
    outside = [(place[4] == 1) & (sub < 4), (place[5] == 1) & (sub >= 4)]
    strip_in = entering_strip[...]
    strips_in = [strip_in, shifted_down(strip_in, 2)]

    def finish(x, carry):
        running, strip_running, prior = carry
        sums, values = [], []
        for z in range(depth):
            cost = row(costs, z, x, tile)
            sums.append(running[z] + cost)
            value = soft_pair(first[x, z], entering[z] + sums[z])
            field[x, z] = value
            if z < near:
                values.append(value)
                keep, slope = split_pair(levels_one[x, z], prior[z] + cost)
                slopes[x, z] = slope
                gains[x, z] = slope * row(anisotropy, z, x, tile) + keep * sides[x, z]
        strip_sums = []
        for side in range(2):
            strip_sums.append(strip_running[side] + edge_costs[3 * side, x])
            value = soft_pair(first_strip[x, side], strips_in[side] + strip_sums[side])
            strip[x, side] = jnp.where(outside[side], BIG, value)
        return sums, strip_sums, values

    blank = jnp.zeros(tile, jnp.float32)
    by_steps(width_x, finish, ([blank] * depth, [blank] * 2, [entering[z] for z in range(near)]))
    edges = [[strip[x, side] for x in range(width_x)] for side in range(2)]
    halo[...] = halo_columns(*edges).reshape(halo.shape)

    def keep(x, z, level, w):
        levels[x] = level
        for i in range(4):
            shares[i, x] = w[i]

    def keep_strip(x, level, w):
        levels_strip[x] = level
        shares_strip[x] = w

    def step(lap, carry):
        x = width_x - 1 - lap
        state, strips = sweep_step(x, 1, field, strip, costs, edge_costs, halo, *carry, keep, keep_strip)
        for z in range(depth):
            local[x, z] = state[z]
        local_strip[x] = merged(*strips)
        return state, strips

    blank = jnp.full(tile, BIG, jnp.float32)
    state, strips = by_steps(width_x, step, ([blank] * depth, [blank] * 2))
    trade_messages(message, state, [packed(*strips), records[...]], depth)


def records_kernel(rows_of, place, cell, received, sums, counts, sums_strip, counts_strip):
    width_x, quakes, width_y = sums.shape
    last = received.shape[1] - 1
    span_y = place[2]
    lane = iota((quakes, width_y), 1)
    column = iota((width_y, width_y), 0)
    strip_column = iota((8, width_y), 0)
    strip_column = jnp.where(strip_column == 3, -1, jnp.where(strip_column == 4, width_y, -2))
    share = width_y // rows_of
    dims = (((1,), (1,)), ((), ()))
    one_x = iota((width_x, width_y), 0)
    parts = [[], [], [], []]
    at, at_strip = [], []
    for chunk in range(cell.shape[0]):
        records = jnp.zeros((quakes, width_y), jnp.float32)
        for part in range(share):
            piece = received[chunk * share + part, last]
            moved = pltpu.roll(piece, part * rows_of, 1) if part else piece
            records = jnp.where(lane // rows_of == part, moved, records)
        cells = cell[chunk : chunk + 1, :]
        station_x = lax.shift_right_logical(cells, place[7]) - place[0]
        station_y = (cells & (span_y - 1)) - place[1]
        at_x = (one_x == jnp.broadcast_to(station_x, one_x.shape)).astype(jnp.float32)
        pieces = [p.astype(jnp.float32) for p in exact_parts(records)] + [jnp.ones((quakes, width_y), jnp.float32)]
        for out, piece in zip(parts, pieces):
            spread = [piece * jnp.broadcast_to(at_x[x : x + 1], piece.shape) for x in range(width_x)]
            out.append(jnp.concatenate(spread, 0).astype(jnp.bfloat16))
        hit = column == jnp.broadcast_to(station_y, column.shape)
        at.append(hit.astype(jnp.float32).astype(jnp.bfloat16))
        hit = strip_column == jnp.broadcast_to(station_y, strip_column.shape)
        at_strip.append(hit.astype(jnp.float32).astype(jnp.bfloat16))
    at = jnp.concatenate(at, 1)
    at_strip = jnp.concatenate(at_strip, 1)
    parts = [jnp.concatenate(p, 1) for p in parts]
    main = [lax.dot_general(p, at, dims, preferred_element_type=jnp.float32) for p in parts]
    side = [lax.dot_general(at_strip, p, dims, preferred_element_type=jnp.float32) for p in parts]
    sums[...] = (main[0] + main[1] + main[2]).reshape(sums.shape)
    counts[...] = main[3].reshape(counts.shape)
    sums_strip[...] = side[0] + side[1] + side[2]
    counts_strip[...] = side[3]


def surface_kernel(
    local, local_strip, entering, entering_strip, costs, edge_costs, levels, levels_strip,
    sums, counts, sums_strip, counts_strip, slopes, slopes_strip, keeps, keeps_strip, misfits, misfits_strip, message,
):
    width_x, quakes, width_y = levels.shape
    tile = (quakes, width_y)
    strip_in = entering_strip[...]
    strip_in = merged(strip_in, shifted_down(strip_in, 2))
    running = jnp.zeros(tile, jnp.float32)
    strip_running = jnp.zeros(tile, jnp.float32)
    prior, strip_prior = entering[0], strip_in
    for x in reversed(range(width_x)):
        cost = row(costs, 0, x, tile)
        running = running + cost
        value = soft_pair(local[x, 0], entering[0] + running)
        keeps[x], slopes[x] = split_pair(levels[x], prior + cost)
        misfits[x] = ADJ_SCALE * (counts[x] * (value * (1.0 / RATE)) - sums[x])
        prior = value
        cost = merged(edge_costs[0, x], edge_costs[3, x])
        strip_running = strip_running + cost
        value = soft_pair(local_strip[x], strip_in + strip_running)
        keeps_strip[x], slopes_strip[x] = split_pair(levels_strip[x], strip_prior + cost)
        turn = (width_y - 8 * x) % width_y
        tally = pltpu.roll(counts_strip[...], turn, 1) if turn else counts_strip[...]
        total = pltpu.roll(sums_strip[...], turn, 1) if turn else sums_strip[...]
        misfits_strip[x] = ADJ_SCALE * (tally * (value * (1.0 / RATE)) - total)
        strip_prior = value
    leaving, strip_leaving = jnp.zeros(tile, jnp.float32), jnp.zeros(tile, jnp.float32)
    through, strip_through = jnp.ones(tile, jnp.float32), jnp.ones(tile, jnp.float32)
    for x in range(width_x):
        leaving = slopes[x] * (misfits[x] + leaving)
        through = slopes[x] * through
        strip_leaving = slopes_strip[x] * (misfits_strip[x] + strip_leaving)
        strip_through = slopes_strip[x] * strip_through
    both = jnp.where(iota(tile, 0) < 5, strip_leaving, pltpu.roll(strip_through, 2, 0))
    for p in range(message.shape[0]):
        message[p, 0] = leaving
        message[p, 1] = through
        message[p, 2] = both


def times_kernel(local, entering, costs, times):
    width_x, depth, quakes, width_y = local.shape
    tile = (quakes, width_y)

    def step(lap, running):
        x = width_x - 1 - lap
        sums = []
        for z in range(depth):
            sums.append(running[z] + row(costs, z, x, tile))
            value = soft_pair(local[x, z], entering[z] + sums[z]) * (1.0 / RATE)
            times[pl.ds(z * width_x + x, quakes, stride=depth * width_x), :] = value
        return sums

    by_steps(width_x, step, [jnp.zeros(tile, jnp.float32)] * depth)


def linear_carry(me, backward, blocks, tile):
    count, block = blocks
    state = jnp.zeros(tile, jnp.float32)
    for lap in range(count):
        device = count - 1 - lap if backward else lap
        ahead = device > me if backward else device < me
        own, factor = block(device)
        state = jnp.where(ahead, own + factor * state, state)
    return state


def adjoint_kernel(
    place, received, slopes, slopes_strip, keeps, keeps_strip, misfits, misfits_strip,
    shares, shares_strip, anisotropy, slopes_one, entries, kernel, message, through,
):
    width_x, quakes, width_y = slopes.shape
    tile = (quakes, width_y)
    depth = anisotropy.shape[0] // 3
    near = slopes_one.shape[1]
    count = received.shape[0]
    lane = iota(tile, 1)
    me = place[6]
    state = linear_carry(me, False, (count, lambda d: (received[d, 0], received[d, 1])), tile)
    strip = linear_carry(
        me, False, (count, lambda d: (received[d, 2], shifted_down(received[d, 2], 2))), tile
    )
    outgoing = jnp.zeros(tile, jnp.float32)
    for x in range(width_x):
        total = misfits[x] + state
        state = slopes[x] * total
        passed = keeps[x] * total
        through[x] = passed
        sideways = row(anisotropy, depth, x, tile) * (shares[1, x] + shares[2, x])
        sideways = sideways + row(anisotropy, 2 * depth, x, tile) * shares[3, x]
        terms = state * row(anisotropy, 0, x, tile) + passed * sideways
        kernel[x : x + 1, :] = jnp.sum(terms, axis=0, keepdims=True)
        total = misfits_strip[x] + strip
        strip = slopes_strip[x] * total
        sent = keeps_strip[x] * total * shares_strip[x]
        outgoing = jnp.where((lane >> 3) == x, pltpu.roll(sent, 8 * x, 1) if x else sent, outgoing)
    first, last = shifted_down(outgoing, 3), pltpu.roll(outgoing, 3, 0)
    halo = jnp.transpose(jnp.concatenate([first] * (width_y // 16) + [last] * (width_y // 16), 0))
    leaving = [jnp.zeros(tile, jnp.float32)] * near
    factor = [jnp.ones(tile, jnp.float32)] * near
    for x in reversed(range(width_x)):
        passed = through[x]
        edge = halo[8 * x : 8 * x + 8]
        above = jnp.where(lane == width_y - 1, edge, pltpu.roll(passed * shares[1, x], width_y - 1, 1))
        below = jnp.where(lane == 0, edge, pltpu.roll(passed * shares[2, x], 1, 1))
        entry = (passed * shares[0, x] + above + below, passed * shares[3, x])
        for z in range(near):
            entries[x, z] = entry[z]
            leaving[z] = slopes_one[x, z] * (entry[z] + leaving[z])
            factor[z] = slopes_one[x, z] * factor[z]
    for p in range(count):
        for z in range(near):
            message[p, z] = leaving[z]
            message[p, near + z] = factor[z]


def kernel_kernel(place, received, entries, slopes, gains, top, kernel):
    width_x, near, quakes, width_y = slopes.shape
    tile = (quakes, width_y)
    count = received.shape[0]
    state = [
        linear_carry(place[6], True, (count, lambda d, z=z: (received[d, z], received[d, near + z])), tile)
        for z in range(near)
    ]
    for x in reversed(range(width_x)):
        for z in range(near):
            total = entries[x, z] + state[z]
            state[z] = slopes[x, z] * total
            value = jnp.sum(total * gains[x, z], axis=0, keepdims=True)
            if z == 0:
                value = value + top[x : x + 1, :]
            kernel[z, x : x + 1, :] = value
    for z in range(near, kernel.shape[0]):
        kernel[z] = jnp.zeros(kernel.shape[1:], jnp.float32)


def call(kernel, shapes, operands, scratch=(), scalars=0):
    many = isinstance(shapes, list)
    out = [jax.ShapeDtypeStruct(s, jnp.float32) for s in (shapes if many else [shapes])]
    result = pl.pallas_call(
        kernel,
        out_shape=out,
        in_specs=[SMEM] * scalars + [VMEM] * (len(operands) - scalars),
        out_specs=[VMEM] * len(out),
        scratch_shapes=[pltpu.VMEM(s, jnp.float32) for s in scratch],
        compiler_params=PARAMS,
    )(*operands)
    return result if many else result[0]


def traded(message):
    return lax.all_to_all(message, "gx", 0, 0, tiled=True)


def rotated(value, axis, by):
    count = lax.axis_size(axis)
    return lax.ppermute(value, axis, [(i, (i + by) % count) for i in range(count)])


def body(warm_start, slowness, anisotropy, observed, station_cell, source_cell):
    quakes, depth, width_x, width_y = warm_start.shape
    count_x, count_y = lax.axis_size("gx"), lax.axis_size("gy")
    index_x, index_y = lax.axis_index("gx"), lax.axis_index("gy")
    span_x, span_y = width_x * count_x, width_y * count_y
    near = 2
    per = max(1, depth // count_x)
    tile = (quakes, width_y)
    top = (width_x,) + tile
    close = (width_x, near) + tile
    field = (width_x, depth) + tile
    place = jnp.stack(
        [
            index_x * width_x,
            index_y * width_y,
            jnp.int32(span_y),
            jnp.int32(span_x * span_y),
            (index_y == 0).astype(jnp.int32),
            (index_y == count_y - 1).astype(jnp.int32),
            index_x,
            jnp.int32(span_y.bit_length() - 1),
        ]
    ).astype(jnp.int32)
    anis = anisotropy.reshape(3 * depth, width_x, width_y)
    local_records = observed.shape[1]
    flat = (quakes * depth * width_x, width_y)

    base = width_x * 11
    start, costs, edge = call(
        pack_kernel,
        [field, anis.shape, (base + quakes, width_y)],
        [place, source_cell, warm_start.reshape(flat), observed, slowness, anis],
        scalars=2,
    )
    from_left = rotated(edge, "gy", 1)
    from_right = rotated(edge, "gy", -1)
    far = {0: observed, 1: from_left[base:, :local_records]}
    far[count_y - 1] = from_right[base:, :local_records]
    for by in range(2, count_y - 1):
        far[by] = rotated(observed, "gy", by)
    pile = jnp.stack([far[by] for by in range(count_y)])
    records = jnp.concatenate([pile[(index_y - j) % count_y] for j in range(count_y)], 1)
    rows_of = records.shape[1]
    records = jnp.pad(records, ((0, 0), (0, width_y - rows_of)))

    traded_shape = (count_x, per + 2) + tile
    first, first_strip, edge_costs, levels_one, sides, message = call(
        first_sweep_kernel,
        [field, (width_x, 2) + tile, (6,) + top, close, close, traded_shape],
        [place, start, edge, from_left, from_right, costs, anis],
        [(depth,) + tile, (width_x, 2) + tile],
        scalars=1,
    )
    totals = traded(message)

    def entering_of(reach, backward):
        entering, strip = call(
            functools.partial(blocks_kernel, count_x, per, backward),
            [(count_x, per) + tile, tile],
            [place, reach, totals],
            scalars=1,
        )
        return traded(entering).reshape((count_x * per,) + tile)[:depth], strip

    entering, entering_strip = entering_of(totals, False)
    second, second_strip, levels, levels_strip, shares, shares_strip, slopes_one, gains, message = call(
        second_sweep_kernel,
        [field, top, top, top, (4,) + top, top, close, close, traded_shape],
        [place, first, first_strip, entering, entering_strip, costs, edge_costs, anis, levels_one, sides, records],
        [field, (width_x, 2) + tile, (depth,) + tile],
        scalars=1,
    )
    reach = traded(message)
    sums, counts, sums_strip, counts_strip = call(
        functools.partial(records_kernel, rows_of),
        [top, top, tile, tile],
        [place, station_cell.reshape(-1, width_y), reach],
        scalars=1,
    )
    entering, entering_strip = entering_of(reach, True)
    slopes, slopes_strip, keeps, keeps_strip, misfits, misfits_strip, message = call(
        surface_kernel,
        [top] * 6 + [(count_x, 3) + tile],
        [second, second_strip, entering, entering_strip, costs, edge_costs, levels, levels_strip]
        + [sums, counts, sums_strip, counts_strip],
    )
    received = traded(message)
    times = call(times_kernel, flat, [second, entering, costs])
    entries, kernel_two, message = call(
        adjoint_kernel,
        [close, (width_x, width_y), (count_x, 2 * near) + tile],
        [place, received, slopes, slopes_strip, keeps, keeps_strip, misfits, misfits_strip]
        + [shares, shares_strip, anis, slopes_one],
        [top],
        scalars=1,
    )
    kernel = call(
        kernel_kernel,
        (depth, width_x, width_y),
        [place, traded(message), entries, slopes_one, gains, kernel_two],
        scalars=1,
    )
    return (times.reshape(warm_start.shape), kernel)


def solution(mesh):
    return jax.shard_map(
        body,
        mesh=mesh,
        in_specs=(
            P(None, None, "gx", "gy"),
            P(None, "gx", "gy"),
            P(None, None, "gx", "gy"),
            P(None, ("gx", "gy")),
            P(),
            P(),
        ),
        out_specs=(P(None, None, "gx", "gy"), P(None, "gx", "gy")),
        check_vma=False,
    )
```

```python
import functools
import math

import jax
import jax.numpy as jnp
from jax import lax
from jax.experimental import pallas as pl
from jax.experimental.pallas import tpu as pltpu
from jax.sharding import PartitionSpec as P

TAU = 0.05
ADJ_SCALE = 0.1
LOG2E = math.log2(math.e)
RATE = LOG2E / TAU
BIG = 10000.0 * RATE
UNROLL = 4
VMEM = pl.BlockSpec(memory_space=pltpu.VMEM)
FAR = pl.BlockSpec(memory_space=pltpu.HBM)
SMEM = pl.BlockSpec(memory_space=pltpu.SMEM)
PARAMS = pltpu.CompilerParams(vmem_limit_bytes=16 * 1024 * 1024)


def softmin(values):
    least = functools.reduce(jnp.minimum, values)
    parts = [jnp.exp2(least - v) for v in values]
    total = functools.reduce(jnp.add, parts)
    return least - LOG2E * jnp.log(total), parts, total


def soft_pair(first, second):
    return jnp.minimum(first, second) - LOG2E * jnp.log(1.0 + jnp.exp2(-jnp.abs(first - second)))


def split_pair(first, second):
    gap = jnp.exp2(-jnp.abs(first - second))
    share = 1.0 / (1.0 + gap)
    less = gap * share
    nearer = first <= second
    return jnp.where(nearer, share, less), jnp.where(nearer, less, share)


def iota(shape, axis):
    return lax.broadcasted_iota(jnp.int32, shape, axis)


def row(ref, index, x, like):
    return jnp.broadcast_to(ref[index, pl.ds(x, 1), :], like)


def by_steps(count, step, carry):
    def group(i, carry):
        for j in range(UNROLL):
            carry = step(i * UNROLL + j, carry)
        return carry

    return lax.fori_loop(0, count // UNROLL, group, carry)


def packed(left, right):
    return jnp.where(iota(left.shape, 0) < 5, left, pltpu.roll(right, 2, 0))


def merged(left, right):
    return jnp.where(iota(left.shape, 0) < 4, left, right)


def shifted_down(tile, by):
    return pltpu.roll(tile, tile.shape[0] - by, 0)


def exact_parts(value):
    high = value.astype(jnp.bfloat16).astype(jnp.float32)
    middle = (value - high).astype(jnp.bfloat16).astype(jnp.float32)
    low = value - high - middle
    return [p.astype(jnp.bfloat16) for p in (high, middle, low)]


def pack_kernel(
    place, source, warm_far, observed_far, slowness_far, anisotropy_far, start, costs, near, edge, records,
    warm, observed, slowness, anisotropy, arrived,
):
    pairs = ((slowness_far, slowness), (anisotropy_far, anisotropy), (warm_far, warm), (observed_far, observed))
    copies = [pltpu.make_async_copy(a, b, arrived.at[i]) for i, (a, b) in enumerate(pairs)]
    for copy in copies:
        copy.start()
    width_x, depth, quakes, width_y = start.shape
    tile = (quakes, width_y)
    quake = iota(tile, 0)
    lane = iota(tile, 1)
    span_y = place[2]
    plane = place[3]
    cell = jnp.zeros(tile, jnp.int32)
    for e in range(quakes):
        cell = jnp.where(quake == e, source[e], cell)
    cell = cell - (lane + place[0] * span_y + place[1])

    def one(x, edges):
        here = (lane >> 3) == x
        out = []
        for z in range(depth):
            value = warm[pl.ds(z * width_x + x, quakes, stride=depth * width_x), :] * RATE
            value = jnp.where(cell == z * plane + x * span_y, 0.0, value)
            start[x, z] = value
            out.append(jnp.where(here, pltpu.roll(value, 8 * x + 4, 1), edges[z]))
        return out

    rows = width_x * 8
    wide = (width_x, width_y)
    group = iota(wide, 1) >> 3
    copies[0].wait()
    copies[1].wait()
    for k in range(3):
        columns = jnp.zeros(wide, jnp.float32)
        for z in range(depth):
            cost = slowness[z] * anisotropy[k * depth + z] * RATE
            costs[k * depth + z] = cost
            columns = jnp.where(group == z, pltpu.roll(cost, 8 * z + 4, 1), columns)
        edge[rows : rows + width_x, :] = columns
        rows += width_x
        for z in range(near.shape[0] // 3):
            near[k * (near.shape[0] // 3) + z] = anisotropy[k * depth + z]
    copies[2].wait()
    edges = by_steps(width_x, one, [jnp.zeros(tile, jnp.float32)] * depth)
    edge[: width_x * 8, :] = jnp.transpose(jnp.concatenate(edges, 0))
    copies[3].wait()
    records[...] = jnp.zeros(tile, jnp.float32)
    records[:, : observed.shape[1]] = observed[...]
    edge[rows:, :] = records[...]


def halo_columns(left, right):
    rows = []
    for l, r in zip(left, right):
        rows.append(jnp.where(iota(l.shape, 0) == 4, r, pltpu.roll(l, 2, 0)))
    return jnp.transpose(jnp.concatenate(rows, 0))


def strip_costs(own, from_left, from_right, out, width_x, depth):
    tile = own.shape[1]
    base = width_x * 8
    lane = iota((8, tile), 1)
    low = (lane & 7) < 4
    mine = (lane & 7) == iota((8, tile), 0)
    spread = ((iota((tile, tile), 0) >> 3) == (iota((tile, tile), 1) >> 3)).astype(jnp.float32)
    spread = spread.astype(jnp.bfloat16)
    for side in range(2):
        for k in range(3):
            rows = []
            for x in range(width_x):
                at = slice(base + k * width_x + x, base + k * width_x + x + 1)
                here = jnp.broadcast_to(own[at, :], lane.shape)
                there = jnp.broadcast_to((from_right if side else from_left)[at, :], lane.shape)
                value = jnp.where(low, here, there) if side else jnp.where(low, there, here)
                rows.append(jnp.where(mine, value, 0.0))
            whole = jnp.concatenate(rows, 0)
            total = 0.0
            for part in reversed(exact_parts(whole)):
                total = total + lax.dot_general(
                    part, spread, (((1,), (0,)), ((), ())), preferred_element_type=jnp.float32
                )
            out[3 * side + k] = total.reshape(width_x, 8, tile)


def sweep_step(x, near, field, strip, costs, edge_costs, halo, state, strip_state, keep, keep_strip):
    depth = field.shape[1]
    tile = field.shape[2:]
    width_y = tile[1]
    lane = iota(tile, 1)
    sub = iota(tile, 0)
    out = []
    for z in range(depth):
        u = field[x, z]
        cost_x = row(costs, z, x, tile)
        cost_y = row(costs, depth + z, x, tile)
        cost_z = row(costs, 2 * depth + z, x, tile)
        edge = pltpu.roll(halo[z], width_y - 5 - 8 * x, 1)
        values = [u]
        values.append(jnp.where(lane == 0, edge, pltpu.roll(u, 1, 1)) + cost_y)
        values.append(jnp.where(lane == width_y - 1, edge, pltpu.roll(u, width_y - 1, 1)) + cost_y)
        if z > 0:
            values.append(field[x, z - 1] + cost_z)
        if z < depth - 1:
            values.append(field[x, z + 1] + cost_z)
        level, parts, total = softmin(values)
        if z < near:
            scale = 1.0 / total
            keep(x, z, level, [p * scale for p in parts])
        out.append(soft_pair(level, state[z] + cost_x))
    strips, levels, weights = [], [], []
    for side in range(2):
        u = strip[x, side]
        cost_y = edge_costs[3 * side + 1, x]
        cost_z = edge_costs[3 * side + 2, x]
        values = [u, pltpu.roll(u, 1, 0) + cost_y, pltpu.roll(u, 7, 0) + cost_y]
        values.append(jnp.where(lane < 8, BIG, pltpu.roll(u, 8, 1)) + cost_z)
        values.append(jnp.where(lane >= width_y - 8, BIG, pltpu.roll(u, width_y - 8, 1)) + cost_z)
        level, parts, total = softmin(values)
        strips.append(soft_pair(level, strip_state[side] + edge_costs[3 * side, x]))
        levels.append(level)
        weights.append(parts[2 - side] / total)
    if keep_strip is not None:
        keep_strip(x, merged(*levels), merged(*weights))
    return out, strips


def trade_messages(messages, state, extras, depth):
    count = messages.shape[0]
    per = messages.shape[1] - len(extras)
    tile = messages.shape[2:]
    for p in range(count):
        for k in range(per):
            z = p * per + k
            messages[p, k] = state[z] if z < depth else jnp.zeros(tile, jnp.float32)
        for i, extra in enumerate(extras):
            messages[p, per + i] = extra(p) if callable(extra) else extra


def first_sweep_kernel(
    rows_of, count_y, place, field, own, from_left, from_right, costs, anisotropy, *rest
):
    others = rest[: count_y - 3]
    local, local_strip, edge_costs, levels, sides, message, records, halo, strip = rest[count_y - 3 :]
    width_x, depth, quakes, width_y = field.shape
    tile = (quakes, width_y)
    low = iota(tile, 0) < 4
    near = levels.shape[1]
    last = 11 * width_x
    far = [own[last:, :], from_left[last:, :]] + [o[...] for o in others] + [from_right[last:, :]]
    total = jnp.zeros(tile, jnp.float32)
    for by, piece in enumerate(far):
        owner = lax.rem(place[8] + count_y - by, count_y)
        total = total + pltpu.roll(piece, owner * rows_of, 1)
    records[...] = total
    left, right = [], []
    for x in range(width_x):
        at = slice(8 * x, 8 * x + 8)
        before = jnp.where(place[4] == 1, BIG, from_left[at, :])
        after = jnp.where(place[5] == 1, BIG, from_right[at, :])
        left.append(jnp.where(low, before, own[at, :]))
        right.append(jnp.where(low, own[at, :], after))
        strip[x, 0] = left[x]
        strip[x, 1] = right[x]
    halo[...] = halo_columns(left, right).reshape(halo.shape)
    strip_costs(own, from_left, from_right, edge_costs, width_x, depth)

    def keep(x, z, level, w):
        levels[x, z] = level
        vertical = w[3] if z == 0 else w[3] + w[4]
        sideways = row(anisotropy, near + z, x, tile) * (w[1] + w[2])
        sides[x, z] = sideways + row(anisotropy, 2 * near + z, x, tile) * vertical

    def step(x, carry):
        state, strips = sweep_step(
            x, near, field, strip, costs, edge_costs, halo, *carry, keep, None
        )
        for z in range(depth):
            local[x, z] = state[z]
        for side in range(2):
            local_strip[x, side] = strips[side]
        return state, strips

    blank = jnp.full(tile, BIG, jnp.float32)
    state, strips = by_steps(width_x, step, ([blank] * depth, [blank] * 2))
    totals = [jnp.sum(costs[z], axis=0, keepdims=True) for z in range(depth)]
    strip_total = packed(jnp.sum(edge_costs[0], axis=0), jnp.sum(edge_costs[3], axis=0))
    reach = packed(*strips)
    per = message.shape[1] - 2
    sub = iota(tile, 0)

    def with_totals(p):
        value = reach
        for k in range(per):
            if p * per + k < depth:
                value = jnp.where(sub == k, jnp.broadcast_to(totals[p * per + k], tile), value)
        return value

    trade_messages(message, state, [with_totals, strip_total], depth)


def blocks_kernel(count, per, backward, place, received, totals, entering, entering_strip):
    tile = entering.shape[2:]
    me = place[6]
    state = [jnp.full(tile, BIG, jnp.float32)] * per
    strip = jnp.full(tile, BIG, jnp.float32)
    for lap in range(count):
        device = count - 1 - lap if backward else lap
        for k in range(per):
            entering[device, k] = state[k]
            passed = state[k] + jnp.broadcast_to(totals[device, per, k : k + 1, :], tile)
            state[k] = soft_pair(received[device, k], passed)
        ahead = device > me if backward else device < me
        passed = soft_pair(received[device, per], strip + totals[device, per + 1])
        strip = jnp.where(ahead, passed, strip)
    entering_strip[...] = strip


def second_sweep_kernel(
    place, first, first_strip, entering, entering_strip, costs, edge_costs, anisotropy, levels_one, sides, records,
    local, local_strip, levels, levels_strip, shares, shares_strip, slopes, gains, message, field, strip, halo,
):
    width_x, depth, quakes, width_y = first.shape
    tile = (quakes, width_y)
    near = levels_one.shape[1]
    sub = iota(tile, 0)
    outside = [(place[4] == 1) & (sub < 4), (place[5] == 1) & (sub >= 4)]
    strip_in = entering_strip[...]
    strips_in = [strip_in, shifted_down(strip_in, 2)]

    def finish(x, carry):
        running, strip_running, prior = carry
        sums, values = [], []
        for z in range(depth):
            cost = row(costs, z, x, tile)
            sums.append(running[z] + cost)
            value = soft_pair(first[x, z], entering[z] + sums[z])
            field[x, z] = value
            if z < near:
                values.append(value)
                keep, slope = split_pair(levels_one[x, z], prior[z] + cost)
                slopes[x, z] = slope
                gains[x, z] = slope * row(anisotropy, z, x, tile) + keep * sides[x, z]
        strip_sums = []
        for side in range(2):
            strip_sums.append(strip_running[side] + edge_costs[3 * side, x])
            value = soft_pair(first_strip[x, side], strips_in[side] + strip_sums[side])
            strip[x, side] = jnp.where(outside[side], BIG, value)
        return sums, strip_sums, values

    blank = jnp.zeros(tile, jnp.float32)
    by_steps(width_x, finish, ([blank] * depth, [blank] * 2, [entering[z] for z in range(near)]))
    edges = [[strip[x, side] for x in range(width_x)] for side in range(2)]
    halo[...] = halo_columns(*edges).reshape(halo.shape)

    def keep(x, z, level, w):
        levels[x] = level
        for i in range(4):
            shares[i, x] = w[i]

    def keep_strip(x, level, w):
        levels_strip[x] = level
        shares_strip[x] = w

    def step(lap, carry):
        x = width_x - 1 - lap
        state, strips = sweep_step(x, 1, field, strip, costs, edge_costs, halo, *carry, keep, keep_strip)
        for z in range(depth):
            local[x, z] = state[z]
        local_strip[x] = merged(*strips)
        return state, strips

    blank = jnp.full(tile, BIG, jnp.float32)
    state, strips = by_steps(width_x, step, ([blank] * depth, [blank] * 2))
    trade_messages(message, state, [packed(*strips), records[...]], depth)


def records_kernel(rows_of, place, cell, received, sums, counts, sums_strip, counts_strip):
    width_x, quakes, width_y = sums.shape
    last = received.shape[1] - 1
    span_y = place[2]
    lane = iota((quakes, width_y), 1)
    column = iota((width_y, width_y), 0)
    strip_column = iota((8, width_y), 0)
    strip_column = jnp.where(strip_column == 3, -1, jnp.where(strip_column == 4, width_y, -2))
    share = width_y // rows_of
    dims = (((1,), (1,)), ((), ()))
    one_x = iota((width_x, width_y), 0)
    parts = [[], [], [], []]
    at, at_strip = [], []
    for chunk in range(cell.shape[0]):
        records = jnp.zeros((quakes, width_y), jnp.float32)
        for part in range(share):
            piece = received[chunk * share + part, last]
            moved = pltpu.roll(piece, part * rows_of, 1) if part else piece
            records = jnp.where(lane // rows_of == part, moved, records)
        cells = cell[chunk : chunk + 1, :]
        station_x = lax.shift_right_logical(cells, place[7]) - place[0]
        station_y = (cells & (span_y - 1)) - place[1]
        at_x = (one_x == jnp.broadcast_to(station_x, one_x.shape)).astype(jnp.float32)
        pieces = [p.astype(jnp.float32) for p in exact_parts(records)] + [jnp.ones((quakes, width_y), jnp.float32)]
        for out, piece in zip(parts, pieces):
            spread = [piece * jnp.broadcast_to(at_x[x : x + 1], piece.shape) for x in range(width_x)]
            out.append(jnp.concatenate(spread, 0).astype(jnp.bfloat16))
        hit = column == jnp.broadcast_to(station_y, column.shape)
        at.append(hit.astype(jnp.float32).astype(jnp.bfloat16))
        hit = strip_column == jnp.broadcast_to(station_y, strip_column.shape)
        at_strip.append(hit.astype(jnp.float32).astype(jnp.bfloat16))
    at = jnp.concatenate(at, 1)
    at_strip = jnp.concatenate(at_strip, 1)
    parts = [jnp.concatenate(p, 1) for p in parts]
    main = [lax.dot_general(p, at, dims, preferred_element_type=jnp.float32) for p in parts]
    side = [lax.dot_general(at_strip, p, dims, preferred_element_type=jnp.float32) for p in parts]
    sums[...] = (main[0] + main[1] + main[2]).reshape(sums.shape)
    counts[...] = main[3].reshape(counts.shape)
    sums_strip[...] = side[0] + side[1] + side[2]
    counts_strip[...] = side[3]


def surface_kernel(
    local, local_strip, entering, entering_strip, costs, edge_costs, levels, levels_strip,
    sums, counts, sums_strip, counts_strip, slopes, slopes_strip, keeps, keeps_strip, misfits, misfits_strip, message,
):
    width_x, quakes, width_y = levels.shape
    tile = (quakes, width_y)
    strip_in = entering_strip[...]
    strip_in = merged(strip_in, shifted_down(strip_in, 2))
    running = jnp.zeros(tile, jnp.float32)
    strip_running = jnp.zeros(tile, jnp.float32)
    prior, strip_prior = entering[0], strip_in
    for x in reversed(range(width_x)):
        cost = row(costs, 0, x, tile)
        running = running + cost
        value = soft_pair(local[x, 0], entering[0] + running)
        keeps[x], slopes[x] = split_pair(levels[x], prior + cost)
        misfits[x] = ADJ_SCALE * (counts[x] * (value * (1.0 / RATE)) - sums[x])
        prior = value
        cost = merged(edge_costs[0, x], edge_costs[3, x])
        strip_running = strip_running + cost
        value = soft_pair(local_strip[x], strip_in + strip_running)
        keeps_strip[x], slopes_strip[x] = split_pair(levels_strip[x], strip_prior + cost)
        turn = (width_y - 8 * x) % width_y
        tally = pltpu.roll(counts_strip[...], turn, 1) if turn else counts_strip[...]
        total = pltpu.roll(sums_strip[...], turn, 1) if turn else sums_strip[...]
        misfits_strip[x] = ADJ_SCALE * (tally * (value * (1.0 / RATE)) - total)
        strip_prior = value
    leaving, strip_leaving = jnp.zeros(tile, jnp.float32), jnp.zeros(tile, jnp.float32)
    through, strip_through = jnp.ones(tile, jnp.float32), jnp.ones(tile, jnp.float32)
    for x in range(width_x):
        leaving = slopes[x] * (misfits[x] + leaving)
        through = slopes[x] * through
        strip_leaving = slopes_strip[x] * (misfits_strip[x] + strip_leaving)
        strip_through = slopes_strip[x] * strip_through
    both = jnp.where(iota(tile, 0) < 5, strip_leaving, pltpu.roll(strip_through, 2, 0))
    for p in range(message.shape[0]):
        message[p, 0] = leaving
        message[p, 1] = through
        message[p, 2] = both


def times_kernel(local, entering, costs, times):
    width_x, depth, quakes, width_y = local.shape
    tile = (quakes, width_y)

    def step(lap, running):
        x = width_x - 1 - lap
        sums = []
        for z in range(depth):
            sums.append(running[z] + row(costs, z, x, tile))
            value = soft_pair(local[x, z], entering[z] + sums[z]) * (1.0 / RATE)
            times[pl.ds(z * width_x + x, quakes, stride=depth * width_x), :] = value
        return sums

    by_steps(width_x, step, [jnp.zeros(tile, jnp.float32)] * depth)


def linear_carry(me, backward, blocks, tile):
    count, block = blocks
    state = jnp.zeros(tile, jnp.float32)
    for lap in range(count):
        device = count - 1 - lap if backward else lap
        ahead = device > me if backward else device < me
        own, factor = block(device)
        state = jnp.where(ahead, own + factor * state, state)
    return state


def adjoint_kernel(
    place, received, slopes, slopes_strip, keeps, keeps_strip, misfits, misfits_strip,
    shares, shares_strip, anisotropy, slopes_one, entries, kernel, message, through,
):
    width_x, quakes, width_y = slopes.shape
    tile = (quakes, width_y)
    near = slopes_one.shape[1]
    count = received.shape[0]
    lane = iota(tile, 1)
    me = place[6]
    state = linear_carry(me, False, (count, lambda d: (received[d, 0], received[d, 1])), tile)
    strip = linear_carry(
        me, False, (count, lambda d: (received[d, 2], shifted_down(received[d, 2], 2))), tile
    )
    outgoing = jnp.zeros(tile, jnp.float32)
    for x in range(width_x):
        total = misfits[x] + state
        state = slopes[x] * total
        passed = keeps[x] * total
        through[x] = passed
        sideways = row(anisotropy, near, x, tile) * (shares[1, x] + shares[2, x])
        sideways = sideways + row(anisotropy, 2 * near, x, tile) * shares[3, x]
        terms = state * row(anisotropy, 0, x, tile) + passed * sideways
        kernel[x : x + 1, :] = jnp.sum(terms, axis=0, keepdims=True)
        total = misfits_strip[x] + strip
        strip = slopes_strip[x] * total
        sent = keeps_strip[x] * total * shares_strip[x]
        outgoing = jnp.where((lane >> 3) == x, pltpu.roll(sent, 8 * x, 1) if x else sent, outgoing)
    first, last = shifted_down(outgoing, 3), pltpu.roll(outgoing, 3, 0)
    halo = jnp.transpose(jnp.concatenate([first] * (width_y // 16) + [last] * (width_y // 16), 0))
    leaving = [jnp.zeros(tile, jnp.float32)] * near
    factor = [jnp.ones(tile, jnp.float32)] * near
    for x in reversed(range(width_x)):
        passed = through[x]
        edge = halo[8 * x : 8 * x + 8]
        above = jnp.where(lane == width_y - 1, edge, pltpu.roll(passed * shares[1, x], width_y - 1, 1))
        below = jnp.where(lane == 0, edge, pltpu.roll(passed * shares[2, x], 1, 1))
        entry = (passed * shares[0, x] + above + below, passed * shares[3, x])
        for z in range(near):
            entries[x, z] = entry[z]
            leaving[z] = slopes_one[x, z] * (entry[z] + leaving[z])
            factor[z] = slopes_one[x, z] * factor[z]
    for p in range(count):
        for z in range(near):
            message[p, z] = leaving[z]
            message[p, near + z] = factor[z]


def kernel_kernel(place, received, entries, slopes, gains, top, kernel):
    width_x, near, quakes, width_y = slopes.shape
    tile = (quakes, width_y)
    count = received.shape[0]
    state = [
        linear_carry(place[6], True, (count, lambda d, z=z: (received[d, z], received[d, near + z])), tile)
        for z in range(near)
    ]
    for x in reversed(range(width_x)):
        for z in range(near):
            total = entries[x, z] + state[z]
            state[z] = slopes[x, z] * total
            value = jnp.sum(total * gains[x, z], axis=0, keepdims=True)
            if z == 0:
                value = value + top[x : x + 1, :]
            kernel[z, x : x + 1, :] = value
    for z in range(near, kernel.shape[0]):
        kernel[z] = jnp.zeros(kernel.shape[1:], jnp.float32)


def call(kernel, shapes, operands, scratch=(), scalars=0, far=0):
    many = isinstance(shapes, list)
    out = [jax.ShapeDtypeStruct(s, jnp.float32) for s in (shapes if many else [shapes])]
    result = pl.pallas_call(
        kernel,
        out_shape=out,
        in_specs=[SMEM] * scalars + [FAR] * far + [VMEM] * (len(operands) - scalars - far),
        out_specs=[VMEM] * len(out),
        scratch_shapes=[pltpu.VMEM(s, jnp.float32) if isinstance(s, tuple) else s for s in scratch],
        compiler_params=PARAMS,
    )(*operands)
    return result if many else result[0]


def traded(message):
    return lax.all_to_all(message, "gx", 0, 0, tiled=True)


def rotated(value, axis, by):
    count = lax.axis_size(axis)
    return lax.ppermute(value, axis, [(i, (i + by) % count) for i in range(count)])


def body(warm_start, slowness, anisotropy, observed, station_cell, source_cell):
    quakes, depth, width_x, width_y = warm_start.shape
    count_x, count_y = lax.axis_size("gx"), lax.axis_size("gy")
    index_x, index_y = lax.axis_index("gx"), lax.axis_index("gy")
    span_x, span_y = width_x * count_x, width_y * count_y
    near = 2
    per = max(1, depth // count_x)
    tile = (quakes, width_y)
    top = (width_x,) + tile
    close = (width_x, near) + tile
    field = (width_x, depth) + tile
    place = jnp.stack(
        [
            index_x * width_x,
            index_y * width_y,
            jnp.int32(span_y),
            jnp.int32(span_x * span_y),
            (index_y == 0).astype(jnp.int32),
            (index_y == count_y - 1).astype(jnp.int32),
            index_x,
            jnp.int32(span_y.bit_length() - 1),
            index_y,
        ]
    ).astype(jnp.int32)
    anis = anisotropy.reshape(3 * depth, width_x, width_y)
    local_records = observed.shape[1]
    flat = (quakes * depth * width_x, width_y)

    base = width_x * 11
    sources = [warm_start.reshape(flat), observed, slowness, anis]
    start, costs, anis, edge, records = call(
        pack_kernel,
        [field, anis.shape, (3 * near, width_x, width_y), (base + quakes, width_y), tile],
        [place, source_cell] + sources,
        [sources[i].shape for i in range(4)] + [pltpu.SemaphoreType.DMA((4,))],
        scalars=2,
        far=4,
    )
    from_left = rotated(edge, "gy", 1)
    from_right = rotated(edge, "gy", -1)
    others = [rotated(records, "gy", by) for by in range(2, count_y - 1)]

    traded_shape = (count_x, per + 2) + tile
    first, first_strip, edge_costs, levels_one, sides, message, records = call(
        functools.partial(first_sweep_kernel, local_records, count_y),
        [field, (width_x, 2) + tile, (6,) + top, close, close, traded_shape, tile],
        [place, start, edge, from_left, from_right, costs, anis] + others,
        [(depth,) + tile, (width_x, 2) + tile],
        scalars=1,
    )
    totals = traded(message)

    def entering_of(reach, backward):
        entering, strip = call(
            functools.partial(blocks_kernel, count_x, per, backward),
            [(count_x, per) + tile, tile],
            [place, reach, totals],
            scalars=1,
        )
        return traded(entering).reshape((count_x * per,) + tile)[:depth], strip

    entering, entering_strip = entering_of(totals, False)
    second, second_strip, levels, levels_strip, shares, shares_strip, slopes_one, gains, message = call(
        second_sweep_kernel,
        [field, top, top, top, (4,) + top, top, close, close, traded_shape],
        [place, first, first_strip, entering, entering_strip, costs, edge_costs, anis, levels_one, sides, records],
        [field, (width_x, 2) + tile, (depth,) + tile],
        scalars=1,
    )
    reach = traded(message)
    sums, counts, sums_strip, counts_strip = call(
        functools.partial(records_kernel, local_records * count_y),
        [top, top, tile, tile],
        [place, station_cell.reshape(-1, width_y), reach],
        scalars=1,
    )
    entering, entering_strip = entering_of(reach, True)
    slopes, slopes_strip, keeps, keeps_strip, misfits, misfits_strip, message = call(
        surface_kernel,
        [top] * 6 + [(count_x, 3) + tile],
        [second, second_strip, entering, entering_strip, costs, edge_costs, levels, levels_strip]
        + [sums, counts, sums_strip, counts_strip],
    )
    received = traded(message)
    times = call(times_kernel, flat, [second, entering, costs])
    entries, kernel_two, message = call(
        adjoint_kernel,
        [close, (width_x, width_y), (count_x, 2 * near) + tile],
        [place, received, slopes, slopes_strip, keeps, keeps_strip, misfits, misfits_strip]
        + [shares, shares_strip, anis, slopes_one],
        [top],
        scalars=1,
    )
    kernel = call(
        kernel_kernel,
        (depth, width_x, width_y),
        [place, traded(message), entries, slopes_one, gains, kernel_two],
        scalars=1,
    )
    return (times.reshape(warm_start.shape), kernel)


def solution(mesh):
    return jax.shard_map(
        body,
        mesh=mesh,
        in_specs=(
            P(None, None, "gx", "gy"),
            P(None, "gx", "gy"),
            P(None, None, "gx", "gy"),
            P(None, ("gx", "gy")),
            P(),
            P(),
        ),
        out_specs=(P(None, None, "gx", "gy"), P(None, "gx", "gy")),
        check_vma=False,
    )
```

```python
import functools
import math

import jax
import jax.numpy as jnp
from jax import lax
from jax.experimental import pallas as pl
from jax.experimental.pallas import tpu as pltpu
from jax.sharding import PartitionSpec as P

TAU = 0.05
ADJ_SCALE = 0.1
LOG2E = math.log2(math.e)
RATE = LOG2E / TAU
BIG = 10000.0 * RATE
UNROLL = 4
VMEM = pl.BlockSpec(memory_space=pltpu.VMEM)
FAR = pl.BlockSpec(memory_space=pl.ANY)
SMEM = pl.BlockSpec(memory_space=pltpu.SMEM)
PARAMS = pltpu.CompilerParams(vmem_limit_bytes=16 * 1024 * 1024)


def softmin(values):
    least = functools.reduce(jnp.minimum, values)
    parts = [jnp.exp2(least - v) for v in values]
    total = functools.reduce(jnp.add, parts)
    return least - LOG2E * jnp.log(total), parts, total


def soft_pair(first, second):
    return jnp.minimum(first, second) - LOG2E * jnp.log(1.0 + jnp.exp2(-jnp.abs(first - second)))


def split_pair(first, second):
    gap = jnp.exp2(-jnp.abs(first - second))
    share = 1.0 / (1.0 + gap)
    less = gap * share
    nearer = first <= second
    return jnp.where(nearer, share, less), jnp.where(nearer, less, share)


def iota(shape, axis):
    return lax.broadcasted_iota(jnp.int32, shape, axis)


def row(ref, index, x, like):
    return jnp.broadcast_to(ref[index, pl.ds(x, 1), :], like)


def by_steps(count, step, carry):
    def group(i, carry):
        for j in range(UNROLL):
            carry = step(i * UNROLL + j, carry)
        return carry

    return lax.fori_loop(0, count // UNROLL, group, carry)


def packed(left, right):
    return jnp.where(iota(left.shape, 0) < 5, left, pltpu.roll(right, 2, 0))


def merged(left, right):
    return jnp.where(iota(left.shape, 0) < 4, left, right)


def shifted_down(tile, by):
    return pltpu.roll(tile, tile.shape[0] - by, 0)


def exact_parts(value):
    high = value.astype(jnp.bfloat16).astype(jnp.float32)
    middle = (value - high).astype(jnp.bfloat16).astype(jnp.float32)
    low = value - high - middle
    return [p.astype(jnp.bfloat16) for p in (high, middle, low)]


def pack_kernel(
    place, source, warm_far, observed_far, slowness_far, anisotropy_far, start, costs, near, edge, records,
    warm, observed, slowness, anisotropy, arrived,
):
    pairs = [(slowness_far, slowness), (anisotropy_far, anisotropy), (observed_far, observed)]
    share = warm.shape[0] // 4
    pairs += [(warm_far.at[pl.ds(i * share, share)], warm.at[pl.ds(i * share, share)]) for i in range(4)]
    copies = [pltpu.make_async_copy(a, b, arrived.at[i]) for i, (a, b) in enumerate(pairs)]
    for copy in copies:
        copy.start()
    width_x, depth, quakes, width_y = start.shape
    tile = (quakes, width_y)
    quake = iota(tile, 0)
    lane = iota(tile, 1)
    span_y = place[2]
    plane = place[3]
    cell = jnp.zeros(tile, jnp.int32)
    for e in range(quakes):
        cell = jnp.where(quake == e, source[e], cell)
    cell = cell - (lane + place[0] * span_y + place[1])

    def one(x, edges):
        here = (lane >> 3) == x
        out = []
        for z in range(depth):
            value = warm[pl.ds(z * width_x + x, quakes, stride=depth * width_x), :] * RATE
            value = jnp.where(cell == z * plane + x * span_y, 0.0, value)
            start[x, z] = value
            out.append(jnp.where(here, pltpu.roll(value, 8 * x + 4, 1), edges[z]))
        return out

    rows = width_x * 8
    wide = (width_x, width_y)
    group = iota(wide, 1) >> 3
    copies[0].wait()
    copies[1].wait()
    for k in range(3):
        columns = jnp.zeros(wide, jnp.float32)
        for z in range(depth):
            cost = slowness[z] * anisotropy[k * depth + z] * RATE
            costs[k * depth + z] = cost
            columns = jnp.where(group == z, pltpu.roll(cost, 8 * z + 4, 1), columns)
        edge[rows : rows + width_x, :] = columns
        rows += width_x
        for z in range(near.shape[0] // 3):
            near[k * (near.shape[0] // 3) + z] = anisotropy[k * depth + z]
    for copy in copies[3:]:
        copy.wait()
    edges = by_steps(width_x, one, [jnp.zeros(tile, jnp.float32)] * depth)
    edge[: width_x * 8, :] = jnp.transpose(jnp.concatenate(edges, 0))
    copies[2].wait()
    records[...] = jnp.zeros(tile, jnp.float32)
    records[:, : observed.shape[1]] = observed[...]
    edge[rows:, :] = records[...]


def halo_columns(left, right):
    rows = []
    for l, r in zip(left, right):
        rows.append(jnp.where(iota(l.shape, 0) == 4, r, pltpu.roll(l, 2, 0)))
    return jnp.transpose(jnp.concatenate(rows, 0))


def strip_costs(own, from_left, from_right, out, width_x, depth):
    tile = own.shape[1]
    base = width_x * 8
    lane = iota((8, tile), 1)
    low = (lane & 7) < 4
    mine = (lane & 7) == iota((8, tile), 0)
    spread = ((iota((tile, tile), 0) >> 3) == (iota((tile, tile), 1) >> 3)).astype(jnp.float32)
    spread = spread.astype(jnp.bfloat16)
    for side in range(2):
        for k in range(3):
            rows = []
            for x in range(width_x):
                at = slice(base + k * width_x + x, base + k * width_x + x + 1)
                here = jnp.broadcast_to(own[at, :], lane.shape)
                there = jnp.broadcast_to((from_right if side else from_left)[at, :], lane.shape)
                value = jnp.where(low, here, there) if side else jnp.where(low, there, here)
                rows.append(jnp.where(mine, value, 0.0))
            whole = jnp.concatenate(rows, 0)
            total = 0.0
            for part in reversed(exact_parts(whole)):
                total = total + lax.dot_general(
                    part, spread, (((1,), (0,)), ((), ())), preferred_element_type=jnp.float32
                )
            out[3 * side + k] = total.reshape(width_x, 8, tile)


def running_sum(value):
    rows = iota(value.shape, 0)
    by = 1
    while by < value.shape[0]:
        value = value + jnp.where(rows >= by, pltpu.roll(value, by, 0), 0.0)
        by *= 2
    return value


def log_sum(exponents):
    return -LOG2E * jnp.log(functools.reduce(jnp.add, [jnp.exp2(-e) for e in exponents]))


def passages(costs, own, from_left, from_right, depth):
    width_x, width_y = costs.shape[1:]
    base = 8 * width_x
    at = slice(base, base + width_x)
    lane = iota((width_x, width_y), 1)
    beside = jnp.where((lane & 7) == 4, running_sum(from_right[at, :]), pltpu.roll(running_sum(from_left[at, :]), 2, 1))
    sums = [running_sum(costs[z]) for z in range(depth)]
    sub = iota((8, width_y), 0)
    tiles = []
    for z in range(depth):
        back = sums[z] - costs[z]
        edge = pltpu.roll(beside, width_y - 5 - 8 * z, 1)
        below = jnp.where(lane == 0, edge, pltpu.roll(sums[z], 1, 1))
        above = jnp.where(lane == width_y - 1, edge, pltpu.roll(sums[z], width_y - 1, 1))
        step_y = back + costs[depth + z]
        step_z = back + costs[2 * depth + z]
        paths = [sums[z] + back, below + step_y, above + step_y]
        paths.append(sums[z - 1] + step_z if z > 0 else None)
        paths.append(sums[z + 1] + step_z if z < depth - 1 else None)
        tile = jnp.broadcast_to(sums[z][width_x - 1 :, :], sub.shape)
        for j, path in enumerate(paths):
            if path is None:
                tile = jnp.where(sub == j + 1, BIG, tile)
            else:
                total = jnp.sum(jnp.exp2(-path), axis=0, keepdims=True)
                tile = jnp.where(sub == j + 1, -LOG2E * jnp.log(total), tile)
        tiles.append(tile)
    return tiles


def strip_passages(edge_costs, width_x):
    shape = edge_costs.shape[2:]
    lane = iota(shape, 1)
    sums = jnp.zeros(shape, jnp.float32)
    totals = [jnp.zeros(shape, jnp.float32)] * 5
    for x in range(width_x):
        cost, step_y, step_z = [packed(edge_costs[k, x], edge_costs[3 + k, x]) for k in range(3)]
        back = sums
        sums = sums + cost
        step_y, step_z = step_y + back, step_z + back
        paths = [sums + back, pltpu.roll(sums, 1, 0) + step_y, shifted_down(sums, 1) + step_y]
        paths.append(jnp.where(lane < 8, BIG, pltpu.roll(sums, 8, 1) + step_z))
        paths.append(jnp.where(lane >= shape[1] - 8, BIG, pltpu.roll(sums, shape[1] - 8, 1) + step_z))
        totals = [t + jnp.exp2(-p) for t, p in zip(totals, paths)]
    return sums, [-LOG2E * jnp.log(jnp.maximum(t, 1e-37)) for t in totals]


def sweep_step(x, near, field, strip, costs, edge_costs, halo, state, strip_state, keep, keep_strip):
    depth = field.shape[1]
    tile = field.shape[2:]
    width_y = tile[1]
    lane = iota(tile, 1)
    out = []
    for z in range(depth):
        u = field[x, z]
        cost_y = row(costs, depth + z, x, tile)
        cost_z = row(costs, 2 * depth + z, x, tile)
        edge = pltpu.roll(halo[z], width_y - 5 - 8 * x, 1)
        values = [u]
        values.append(jnp.where(lane == 0, edge, pltpu.roll(u, 1, 1)) + cost_y)
        values.append(jnp.where(lane == width_y - 1, edge, pltpu.roll(u, width_y - 1, 1)) + cost_y)
        if z > 0:
            values.append(field[x, z - 1] + cost_z)
        if z < depth - 1:
            values.append(field[x, z + 1] + cost_z)
        level, parts, total = softmin(values)
        passed = state[z] + row(costs, z, x, tile)
        if z < near:
            scale = 1.0 / total
            keep(x, z, level, [p * scale for p in parts], passed)
        out.append(soft_pair(level, passed))
    strips, levels, weights, passes = [], [], [], []
    for side in range(2):
        u = strip[x, side]
        cost_y = edge_costs[3 * side + 1, x]
        cost_z = edge_costs[3 * side + 2, x]
        values = [u, pltpu.roll(u, 1, 0) + cost_y, pltpu.roll(u, 7, 0) + cost_y]
        values.append(jnp.where(lane < 8, BIG, pltpu.roll(u, 8, 1)) + cost_z)
        values.append(jnp.where(lane >= width_y - 8, BIG, pltpu.roll(u, width_y - 8, 1)) + cost_z)
        level, parts, total = softmin(values)
        passes.append(strip_state[side] + edge_costs[3 * side, x])
        strips.append(soft_pair(level, passes[side]))
        levels.append(level)
        weights.append(parts[2 - side] / total)
    if keep_strip is not None:
        keep_strip(x, merged(*levels), merged(*weights), merged(*passes), merged(*strips))
    return out, strips


def outside_strips(place, shape):
    sub = iota(shape, 0)
    return [(place[4] == 1) & (sub < 4), (place[5] == 1) & (sub >= 4)]


def first_sweep_kernel(
    rows_of, count_y, place, field, own, from_left, from_right, costs, anisotropy, *rest
):
    others = rest[: count_y - 3]
    local, local_strip, edge_costs, levels, sides, message, halo, strip = rest[count_y - 3 :]
    width_x, depth, quakes, width_y = field.shape
    tile = (quakes, width_y)
    sub = iota(tile, 0)
    low = sub < 4
    near = levels.shape[1]
    last = 11 * width_x
    far = [own[last:, :], from_left[last:, :]] + [o[...] for o in others] + [from_right[last:, :]]
    records = jnp.zeros(tile, jnp.float32)
    for by, piece in enumerate(far):
        owner = lax.rem(place[8] + count_y - by, count_y)
        records = records + pltpu.roll(piece, owner * rows_of, 1)
    left, right = [], []
    for x in range(width_x):
        at = slice(8 * x, 8 * x + 8)
        before = jnp.where(place[4] == 1, BIG, from_left[at, :])
        after = jnp.where(place[5] == 1, BIG, from_right[at, :])
        left.append(jnp.where(low, before, own[at, :]))
        right.append(jnp.where(low, own[at, :], after))
        strip[x, 0] = left[x]
        strip[x, 1] = right[x]
    halo[...] = halo_columns(left, right).reshape(halo.shape)
    strip_costs(own, from_left, from_right, edge_costs, width_x, depth)
    outside = outside_strips(place, tile)

    def keep(x, z, level, w, passed):
        levels[x, z] = level
        vertical = w[3] if z == 0 else w[3] + w[4]
        sideways = row(anisotropy, near + z, x, tile) * (w[1] + w[2])
        sides[x, z] = sideways + row(anisotropy, 2 * near + z, x, tile) * vertical

    def step(x, carry):
        state, strips = sweep_step(x, near, field, strip, costs, edge_costs, halo, *carry, keep, None)
        for z in range(depth):
            local[x, z] = state[z]
        for side in range(2):
            local_strip[x, side] = jnp.where(outside[side], BIG, strips[side])
        return state, strips

    blank = jnp.full(tile, BIG, jnp.float32)
    state, strips = by_steps(width_x, step, ([blank] * depth, [blank] * 2))
    reach_strip = packed(*[jnp.where(o, BIG, s) for o, s in zip(outside, strips)])

    edges = [[local_strip[x, side] for x in range(width_x)] for side in range(2)]
    halo[...] = halo_columns(*edges).reshape(halo.shape)

    def again(lap, carry):
        x = width_x - 1 - lap
        return sweep_step(x, 0, local, local_strip, costs, edge_costs, halo, *carry, None, None)

    back, back_strips = by_steps(width_x, again, ([blank] * depth, [blank] * 2))
    tiles = passages(costs, own, from_left, from_right, depth)
    strip_total, strip_paths = strip_passages(edge_costs, width_x)

    def three(a, b, c):
        value = jnp.where((sub == 3) | (sub == 6), a, pltpu.roll(b, 1, 0))
        return jnp.where((sub == 5) | (sub == 0), pltpu.roll(c, 2, 0), value)

    strip_tiles = [
        reach_strip,
        strip_total,
        three(packed(*back_strips), strip_paths[0], strip_paths[1]),
        three(*strip_paths[2:]),
        records,
    ]
    count = message.shape[0]
    per = (message.shape[1] - 2 - len(strip_tiles)) // 3
    for p in range(count):
        first = min(p * per, depth - per)
        for k in range(per + 2):
            z = first + k - 1
            message[p, k] = state[z] if 0 <= z < depth else blank
        for k in range(per):
            message[p, per + 2 + k] = back[first + k]
            value = tiles[first + k]
            if k == 0 and first > 0:
                value = jnp.where(sub == 6, jnp.broadcast_to(tiles[first - 1][:1], tile), value)
            if k == 0 and first + per < depth:
                value = jnp.where(sub == 7, jnp.broadcast_to(tiles[first + per][:1], tile), value)
            message[p, 2 * per + 2 + k] = value
        for i, value in enumerate(strip_tiles):
            message[p, 3 * per + 2 + i] = value


def blocks_kernel(per, depth, place, received, entering, entering_strips, halo):
    count = received.shape[0]
    tile = entering.shape[2:]
    lane = iota(tile, 1)
    width_y = tile[1]
    me = place[6]
    blank = jnp.full(tile, BIG, jnp.float32)
    side = 3 * per + 2

    def rows(device, k, j):
        return jnp.broadcast_to(received[device, 2 * per + 2 + k, j : j + 1, :], tile)

    def total(device, k):
        if k < 0:
            return rows(device, 0, 6)
        return rows(device, k, 0) if k < per else rows(device, 0, 7)

    state = [blank] * (per + 2)
    strip = blank
    first, first_strip = [], []
    for device in range(count):
        first.append(state)
        first_strip.append(strip)
        state = [
            soft_pair(received[device, k], state[k] + total(device, k - 1)) for k in range(per + 2)
        ]
        strip = soft_pair(received[device, side], strip + received[device, side + 1])
    own = blank
    for device in range(count):
        own = jnp.where(device == me, first_strip[device], own)
        for k in range(per):
            entering[device, k] = first[device][k + 1]
    entering_strips[0] = own
    group = width_y // 8
    for at in range(0, count, group):
        some = first_strip[at : at + group]
        some = some + [blank] * (group - len(some))
        turned = halo_columns(some, [shifted_down(s, 2) for s in some])
        halo[at // group] = turned.reshape(halo.shape[1:])
    low = jnp.minimum(me * per, depth - per)
    edges = [[halo[i, low + k] for k in range(per)] for i in range(halo.shape[0])]
    state = [blank] * per
    strip = blank
    for device in reversed(range(count)):
        for k in range(per):
            entering[device, per + k] = state[k]
            u = first[device][k + 1]
            turn = (width_y - 5 - 8 * (device % group)) % width_y
            edge = pltpu.roll(edges[device // group][k], turn, 1)
            values = [received[device, per + 2 + k], u + rows(device, k, 1)]
            values.append(jnp.where(lane == 0, edge, pltpu.roll(u, 1, 1)) + rows(device, k, 2))
            values.append(jnp.where(lane == width_y - 1, edge, pltpu.roll(u, width_y - 1, 1)) + rows(device, k, 3))
            values.append(first[device][k] + rows(device, k, 4))
            values.append(first[device][k + 2] + rows(device, k, 5))
            state[k] = soft_pair(softmin(values)[0], state[k] + total(device, k))
        u = first_strip[device]
        one, two = received[device, side + 2], received[device, side + 3]
        values = [one, u + shifted_down(one, 1), pltpu.roll(u, 1, 0) + shifted_down(one, 2)]
        values.append(shifted_down(u, 1) + two)
        values.append(jnp.where(lane < 8, BIG, pltpu.roll(u, 8, 1)) + shifted_down(two, 1))
        values.append(jnp.where(lane >= width_y - 8, BIG, pltpu.roll(u, width_y - 8, 1)) + shifted_down(two, 2))
        passed = soft_pair(softmin(values)[0], strip + received[device, side + 1])
        strip = jnp.where(device > me, passed, strip)
    entering_strips[1] = strip


def second_sweep_kernel(
    place, first, first_strip, entering, entering_strips, costs, edge_costs, anisotropy, levels_one, sides,
    sums, counts, sums_strip, counts_strip,
    local, shares, shares_strip, slopes, slopes_strip, keeps, keeps_strip, misfits, misfits_strip,
    slopes_one, gains, message, field, strip, halo,
):
    width_x, depth, quakes, width_y = first.shape
    tile = (quakes, width_y)
    near = levels_one.shape[1]
    per = entering.shape[1] // 2
    outside = outside_strips(place, tile)
    strips_in = [[s, shifted_down(s, 2)] for s in (entering_strips[0], entering_strips[1])]
    carried = [[entering[z // per, k * per + z % per] for z in range(depth)] for k in range(2)]

    def finish(x, carry):
        running, strip_running, prior = carry
        sums_now, values = [], []
        for z in range(depth):
            cost = row(costs, z, x, tile)
            sums_now.append(running[z] + cost)
            value = soft_pair(first[x, z], entering[z // per, z % per] + sums_now[z])
            field[x, z] = value
            if z < near:
                values.append(value)
                keep, slope = split_pair(levels_one[x, z], prior[z] + cost)
                slopes_one[x, z] = slope
                gains[x, z] = slope * row(anisotropy, z, x, tile) + keep * sides[x, z]
        strip_sums = []
        for side in range(2):
            strip_sums.append(strip_running[side] + edge_costs[3 * side, x])
            value = soft_pair(first_strip[x, side], strips_in[0][side] + strip_sums[side])
            strip[x, side] = jnp.where(outside[side], BIG, value)
        return sums_now, strip_sums, values

    blank = jnp.zeros(tile, jnp.float32)
    by_steps(width_x, finish, ([blank] * depth, [blank] * 2, carried[0][:near]))
    edges = [[strip[x, side] for x in range(width_x)] for side in range(2)]
    halo[...] = halo_columns(*edges).reshape(halo.shape)

    def keep(x, z, level, w, passed):
        for i in range(4):
            shares[i, x] = w[i]
        keeps[x], slopes[x] = split_pair(level, passed)

    def keep_strip(x, level, w, passed, value):
        shares_strip[x] = w
        keeps_strip[x], slopes_strip[x] = split_pair(level, passed)
        tally = pltpu.roll(counts_strip[...], lax.rem(width_y - 8 * x, width_y), 1)
        total = pltpu.roll(sums_strip[...], lax.rem(width_y - 8 * x, width_y), 1)
        misfits_strip[x] = ADJ_SCALE * (tally * (value * (1.0 / RATE)) - total)

    def step(lap, carry):
        x = width_x - 1 - lap
        state, strips = sweep_step(x, 1, field, strip, costs, edge_costs, halo, *carry, keep, keep_strip)
        for z in range(depth):
            local[x, z] = state[z]
        misfits[x] = ADJ_SCALE * (counts[x] * (state[0] * (1.0 / RATE)) - sums[x])
        return state, strips

    by_steps(width_x, step, (carried[1], strips_in[1]))
    leaving, strip_leaving = jnp.zeros(tile, jnp.float32), jnp.zeros(tile, jnp.float32)
    through, strip_through = jnp.ones(tile, jnp.float32), jnp.ones(tile, jnp.float32)
    for x in range(width_x):
        leaving = slopes[x] * (misfits[x] + leaving)
        through = slopes[x] * through
        strip_leaving = slopes_strip[x] * (misfits_strip[x] + strip_leaving)
        strip_through = slopes_strip[x] * strip_through
    both = jnp.where(iota(tile, 0) < 5, strip_leaving, pltpu.roll(strip_through, 2, 0))
    for p in range(message.shape[0]):
        message[p, 0] = leaving
        message[p, 1] = through
        message[p, 2] = both


def records_kernel(rows_of, place, cell, received, sums, counts, sums_strip, counts_strip):
    width_x, quakes, width_y = sums.shape
    last = received.shape[1] - 1
    span_y = place[2]
    lane = iota((quakes, width_y), 1)
    column = iota((width_y, width_y), 0)
    strip_column = iota((8, width_y), 0)
    strip_column = jnp.where(strip_column == 3, -1, jnp.where(strip_column == 4, width_y, -2))
    share = width_y // rows_of
    dims = (((1,), (1,)), ((), ()))
    one_x = iota((width_x, width_y), 0)
    parts = [[], [], [], []]
    at, at_strip = [], []
    for chunk in range(cell.shape[0]):
        records = jnp.zeros((quakes, width_y), jnp.float32)
        for part in range(share):
            piece = received[chunk * share + part, last]
            moved = pltpu.roll(piece, part * rows_of, 1) if part else piece
            records = jnp.where(lane // rows_of == part, moved, records)
        cells = cell[chunk : chunk + 1, :]
        station_x = lax.shift_right_logical(cells, place[7]) - place[0]
        station_y = (cells & (span_y - 1)) - place[1]
        at_x = (one_x == jnp.broadcast_to(station_x, one_x.shape)).astype(jnp.float32)
        pieces = [p.astype(jnp.float32) for p in exact_parts(records)] + [jnp.ones((quakes, width_y), jnp.float32)]
        for out, piece in zip(parts, pieces):
            spread = [piece * jnp.broadcast_to(at_x[x : x + 1], piece.shape) for x in range(width_x)]
            out.append(jnp.concatenate(spread, 0).astype(jnp.bfloat16))
        hit = column == jnp.broadcast_to(station_y, column.shape)
        at.append(hit.astype(jnp.float32).astype(jnp.bfloat16))
        hit = strip_column == jnp.broadcast_to(station_y, strip_column.shape)
        at_strip.append(hit.astype(jnp.float32).astype(jnp.bfloat16))
    at = jnp.concatenate(at, 1)
    at_strip = jnp.concatenate(at_strip, 1)
    parts = [jnp.concatenate(p, 1) for p in parts]
    main = [lax.dot_general(p, at, dims, preferred_element_type=jnp.float32) for p in parts]
    side = [lax.dot_general(at_strip, p, dims, preferred_element_type=jnp.float32) for p in parts]
    sums[...] = (main[0] + main[1] + main[2]).reshape(sums.shape)
    counts[...] = main[3].reshape(counts.shape)
    sums_strip[...] = side[0] + side[1] + side[2]
    counts_strip[...] = side[3]


def times_kernel(local, times):
    width_x, depth, quakes, _ = local.shape

    def step(x, carry):
        for z in range(depth):
            times[pl.ds(z * width_x + x, quakes, stride=depth * width_x), :] = local[x, z] * (1.0 / RATE)
        return carry

    by_steps(width_x, step, 0)


def linear_carry(me, backward, blocks, tile):
    count, block = blocks
    state = jnp.zeros(tile, jnp.float32)
    for lap in range(count):
        device = count - 1 - lap if backward else lap
        ahead = device > me if backward else device < me
        own, factor = block(device)
        state = jnp.where(ahead, own + factor * state, state)
    return state


def adjoint_kernel(
    place, received, slopes, slopes_strip, keeps, keeps_strip, misfits, misfits_strip,
    shares, shares_strip, anisotropy, slopes_one, entries, kernel, message, through,
):
    width_x, quakes, width_y = slopes.shape
    tile = (quakes, width_y)
    near = slopes_one.shape[1]
    count = received.shape[0]
    lane = iota(tile, 1)
    me = place[6]
    state = linear_carry(me, False, (count, lambda d: (received[d, 0], received[d, 1])), tile)
    strip = linear_carry(
        me, False, (count, lambda d: (received[d, 2], shifted_down(received[d, 2], 2))), tile
    )
    outgoing = jnp.zeros(tile, jnp.float32)
    for x in range(width_x):
        total = misfits[x] + state
        state = slopes[x] * total
        passed = keeps[x] * total
        through[x] = passed
        sideways = row(anisotropy, near, x, tile) * (shares[1, x] + shares[2, x])
        sideways = sideways + row(anisotropy, 2 * near, x, tile) * shares[3, x]
        terms = state * row(anisotropy, 0, x, tile) + passed * sideways
        kernel[x : x + 1, :] = jnp.sum(terms, axis=0, keepdims=True)
        total = misfits_strip[x] + strip
        strip = slopes_strip[x] * total
        sent = keeps_strip[x] * total * shares_strip[x]
        outgoing = jnp.where((lane >> 3) == x, pltpu.roll(sent, 8 * x, 1) if x else sent, outgoing)
    first, last = shifted_down(outgoing, 3), pltpu.roll(outgoing, 3, 0)
    halo = jnp.transpose(jnp.concatenate([first] * (width_y // 16) + [last] * (width_y // 16), 0))
    leaving = [jnp.zeros(tile, jnp.float32)] * near
    factor = [jnp.ones(tile, jnp.float32)] * near
    for x in reversed(range(width_x)):
        passed = through[x]
        edge = halo[8 * x : 8 * x + 8]
        above = jnp.where(lane == width_y - 1, edge, pltpu.roll(passed * shares[1, x], width_y - 1, 1))
        below = jnp.where(lane == 0, edge, pltpu.roll(passed * shares[2, x], 1, 1))
        entry = (passed * shares[0, x] + above + below, passed * shares[3, x])
        for z in range(near):
            entries[x, z] = entry[z]
            leaving[z] = slopes_one[x, z] * (entry[z] + leaving[z])
            factor[z] = slopes_one[x, z] * factor[z]
    for p in range(count):
        for z in range(near):
            message[p, z] = leaving[z]
            message[p, near + z] = factor[z]


def kernel_kernel(place, received, entries, slopes, gains, top, kernel):
    width_x, near, quakes, width_y = slopes.shape
    tile = (quakes, width_y)
    count = received.shape[0]
    state = [
        linear_carry(place[6], True, (count, lambda d, z=z: (received[d, z], received[d, near + z])), tile)
        for z in range(near)
    ]
    for x in reversed(range(width_x)):
        for z in range(near):
            total = entries[x, z] + state[z]
            state[z] = slopes[x, z] * total
            value = jnp.sum(total * gains[x, z], axis=0, keepdims=True)
            if z == 0:
                value = value + top[x : x + 1, :]
            kernel[z, x : x + 1, :] = value
    for z in range(near, kernel.shape[0]):
        kernel[z] = jnp.zeros(kernel.shape[1:], jnp.float32)


def call(kernel, shapes, operands, scratch=(), scalars=0, far=0):
    many = isinstance(shapes, list)
    out = [jax.ShapeDtypeStruct(s, jnp.float32) for s in (shapes if many else [shapes])]
    result = pl.pallas_call(
        kernel,
        out_shape=out,
        in_specs=[SMEM] * scalars + [FAR] * far + [VMEM] * (len(operands) - scalars - far),
        out_specs=[VMEM] * len(out),
        scratch_shapes=[pltpu.VMEM(s, jnp.float32) if isinstance(s, tuple) else s for s in scratch],
        compiler_params=PARAMS,
    )(*operands)
    return result if many else result[0]


def traded(message):
    return lax.all_to_all(message, "gx", 0, 0, tiled=True)


def rotated(value, axis, by):
    count = lax.axis_size(axis)
    return lax.ppermute(value, axis, [(i, (i + by) % count) for i in range(count)])


def body(warm_start, slowness, anisotropy, observed, station_cell, source_cell):
    quakes, depth, width_x, width_y = warm_start.shape
    count_x, count_y = lax.axis_size("gx"), lax.axis_size("gy")
    index_x, index_y = lax.axis_index("gx"), lax.axis_index("gy")
    span_x, span_y = width_x * count_x, width_y * count_y
    near = 2
    per = max(1, depth // count_x)
    tile = (quakes, width_y)
    top = (width_x,) + tile
    close = (width_x, near) + tile
    field = (width_x, depth) + tile
    place = jnp.stack(
        [
            index_x * width_x,
            index_y * width_y,
            jnp.int32(span_y),
            jnp.int32(span_x * span_y),
            (index_y == 0).astype(jnp.int32),
            (index_y == count_y - 1).astype(jnp.int32),
            index_x,
            jnp.int32(span_y.bit_length() - 1),
            index_y,
        ]
    ).astype(jnp.int32)
    anis = anisotropy.reshape(3 * depth, width_x, width_y)
    local_records = observed.shape[1]
    flat = (quakes * depth * width_x, width_y)

    base = width_x * 11
    sources = [warm_start.reshape(flat), observed, slowness, anis]
    sources = [pltpu.with_memory_space_constraint(a, pltpu.HBM) for a in sources]
    start, costs, anis, edge, records = call(
        pack_kernel,
        [field, anis.shape, (3 * near, width_x, width_y), (base + quakes, width_y), tile],
        [place, source_cell] + sources,
        [sources[i].shape for i in range(4)] + [pltpu.SemaphoreType.DMA((7,))],
        scalars=2,
        far=4,
    )
    from_left = rotated(edge, "gy", 1)
    from_right = rotated(edge, "gy", -1)
    others = [rotated(records, "gy", by) for by in range(2, count_y - 1)]

    message_shape = (count_x, 3 * per + 7) + tile
    first, first_strip, edge_costs, levels_one, sides, message = call(
        functools.partial(first_sweep_kernel, local_records, count_y),
        [field, (width_x, 2) + tile, (6,) + top, close, close, message_shape],
        [place, start, edge, from_left, from_right, costs, anis] + others,
        [(depth,) + tile, (width_x, 2) + tile],
        scalars=1,
    )
    reach = traded(message)
    group = width_y // 8
    entering, entering_strips = call(
        functools.partial(blocks_kernel, per, depth),
        [(count_x, 2 * per) + tile, (2,) + tile],
        [place, reach],
        [(-(-count_x // group), depth) + tile],
        scalars=1,
    )
    entering = traded(entering)
    recorded = call(
        functools.partial(records_kernel, local_records * count_y),
        [top, top, tile, tile],
        [place, station_cell.reshape(-1, width_y), reach],
        scalars=1,
    )
    second, shares, shares_strip, *rest = call(
        second_sweep_kernel,
        [field, (4,) + top] + [top] * 7 + [close, close, (count_x, 3) + tile],
        [place, first, first_strip, entering, entering_strips, costs, edge_costs, anis, levels_one, sides]
        + list(recorded),
        [field, (width_x, 2) + tile, (depth,) + tile],
        scalars=1,
    )
    slopes, slopes_strip, keeps, keeps_strip, misfits, misfits_strip, slopes_one, gains, message = rest
    received = traded(message)
    times = call(times_kernel, flat, [second])
    entries, kernel_two, message = call(
        adjoint_kernel,
        [close, (width_x, width_y), (count_x, 2 * near) + tile],
        [place, received, slopes, slopes_strip, keeps, keeps_strip, misfits, misfits_strip]
        + [shares, shares_strip, anis, slopes_one],
        [top],
        scalars=1,
    )
    kernel = call(
        kernel_kernel,
        (depth, width_x, width_y),
        [place, traded(message), entries, slopes_one, gains, kernel_two],
        scalars=1,
    )
    return (times.reshape(warm_start.shape), kernel)


def solution(mesh):
    return jax.shard_map(
        body,
        mesh=mesh,
        in_specs=(
            P(None, None, "gx", "gy"),
            P(None, "gx", "gy"),
            P(None, None, "gx", "gy"),
            P(None, ("gx", "gy")),
            P(),
            P(),
        ),
        out_specs=(P(None, None, "gx", "gy"), P(None, "gx", "gy")),
        check_vma=False,
    )
```

```python
import functools
import math

import jax
import jax.numpy as jnp
from jax import lax
from jax.experimental import pallas as pl
from jax.experimental.pallas import tpu as pltpu
from jax.sharding import PartitionSpec as P

TAU = 0.05
ADJ_SCALE = 0.1
LOG2E = math.log2(math.e)
RATE = LOG2E / TAU
BIG = 10000.0 * RATE
UNROLL = 4
VMEM = pl.BlockSpec(memory_space=pltpu.VMEM)
FAR = pl.BlockSpec(memory_space=pl.ANY)
SMEM = pl.BlockSpec(memory_space=pltpu.SMEM)
PARAMS = pltpu.CompilerParams(vmem_limit_bytes=8 * 1024 * 1024)


def softmin(values):
    least = functools.reduce(jnp.minimum, values)
    parts = [jnp.exp2(least - v) for v in values]
    total = functools.reduce(jnp.add, parts)
    return least - LOG2E * jnp.log(total), parts, total


def soft_pair(first, second):
    return jnp.minimum(first, second) - LOG2E * jnp.log(1.0 + jnp.exp2(-jnp.abs(first - second)))


def split_pair(first, second):
    gap = jnp.exp2(-jnp.abs(first - second))
    share = 1.0 / (1.0 + gap)
    less = gap * share
    nearer = first <= second
    return jnp.where(nearer, share, less), jnp.where(nearer, less, share)


def iota(shape, axis):
    return lax.broadcasted_iota(jnp.int32, shape, axis)


def row(ref, index, x, like):
    return jnp.broadcast_to(ref[index, pl.ds(x, 1), :], like)


def by_steps(count, step, carry):
    def group(i, carry):
        for j in range(UNROLL):
            carry = step(i * UNROLL + j, carry)
        return carry

    return lax.fori_loop(0, count // UNROLL, group, carry)


def packed(left, right):
    return jnp.where(iota(left.shape, 0) < 5, left, pltpu.roll(right, 2, 0))


def merged(left, right):
    return jnp.where(iota(left.shape, 0) < 4, left, right)


def shifted_down(tile, by):
    return pltpu.roll(tile, tile.shape[0] - by, 0)


def exact_parts(value):
    high = value.astype(jnp.bfloat16).astype(jnp.float32)
    middle = (value - high).astype(jnp.bfloat16).astype(jnp.float32)
    low = value - high - middle
    return [p.astype(jnp.bfloat16) for p in (high, middle, low)]


def pack_kernel(
    place, source, warm_far, observed_far, slowness_far, anisotropy_far, start, costs, near, edge, records,
    warm, observed, slowness, anisotropy, arrived,
):
    pairs = [(slowness_far, slowness), (anisotropy_far, anisotropy), (observed_far, observed)]
    share = warm.shape[0] // 4
    pairs += [(warm_far.at[pl.ds(i * share, share)], warm.at[pl.ds(i * share, share)]) for i in range(4)]
    copies = [pltpu.make_async_copy(a, b, arrived.at[i]) for i, (a, b) in enumerate(pairs)]
    for copy in copies:
        copy.start()
    width_x, depth, quakes, width_y = start.shape
    tile = (quakes, width_y)
    quake = iota(tile, 0)
    lane = iota(tile, 1)
    span_y = place[2]
    plane = place[3]
    cell = jnp.zeros(tile, jnp.int32)
    for e in range(quakes):
        cell = jnp.where(quake == e, source[e], cell)
    cell = cell - (lane + place[0] * span_y + place[1])

    def one(x, edges):
        here = (lane >> 3) == x
        out = []
        for z in range(depth):
            value = warm[pl.ds(z * width_x + x, quakes, stride=depth * width_x), :] * RATE
            value = jnp.where(cell == z * plane + x * span_y, 0.0, value)
            start[x, z] = value
            out.append(jnp.where(here, pltpu.roll(value, 8 * x + 4, 1), edges[z]))
        return out

    rows = width_x * 8
    wide = (width_x, width_y)
    group = iota(wide, 1) >> 3
    copies[0].wait()
    copies[1].wait()
    for k in range(3):
        columns = jnp.zeros(wide, jnp.float32)
        for z in range(depth):
            cost = slowness[z] * anisotropy[k * depth + z] * RATE
            costs[k * depth + z] = cost
            columns = jnp.where(group == z, pltpu.roll(cost, 8 * z + 4, 1), columns)
        edge[rows : rows + width_x, :] = columns
        rows += width_x
        for z in range(near.shape[0] // 3):
            near[k * (near.shape[0] // 3) + z] = anisotropy[k * depth + z]
    for copy in copies[3:]:
        copy.wait()
    edges = by_steps(width_x, one, [jnp.zeros(tile, jnp.float32)] * depth)
    edge[: width_x * 8, :] = jnp.transpose(jnp.concatenate(edges, 0))
    copies[2].wait()
    records[...] = jnp.zeros(tile, jnp.float32)
    records[:, : observed.shape[1]] = observed[...]
    edge[rows:, :] = records[...]


def halo_columns(left, right):
    rows = []
    for l, r in zip(left, right):
        rows.append(jnp.where(iota(l.shape, 0) == 4, r, pltpu.roll(l, 2, 0)))
    return jnp.transpose(jnp.concatenate(rows, 0))


def strip_costs(own, from_left, from_right, out, width_x, depth):
    tile = own.shape[1]
    base = width_x * 8
    lane = iota((8, tile), 1)
    low = (lane & 7) < 4
    mine = (lane & 7) == iota((8, tile), 0)
    spread = ((iota((tile, tile), 0) >> 3) == (iota((tile, tile), 1) >> 3)).astype(jnp.float32)
    spread = spread.astype(jnp.bfloat16)
    for side in range(2):
        for k in range(3):
            rows = []
            for x in range(width_x):
                at = slice(base + k * width_x + x, base + k * width_x + x + 1)
                here = jnp.broadcast_to(own[at, :], lane.shape)
                there = jnp.broadcast_to((from_right if side else from_left)[at, :], lane.shape)
                value = jnp.where(low, here, there) if side else jnp.where(low, there, here)
                rows.append(jnp.where(mine, value, 0.0))
            whole = jnp.concatenate(rows, 0)
            total = 0.0
            for part in reversed(exact_parts(whole)):
                total = total + lax.dot_general(
                    part, spread, (((1,), (0,)), ((), ())), preferred_element_type=jnp.float32
                )
            out[3 * side + k] = total.reshape(width_x, 8, tile)


def running_sum(value):
    rows = iota(value.shape, 0)
    by = 1
    while by < value.shape[0]:
        value = value + jnp.where(rows >= by, pltpu.roll(value, by, 0), 0.0)
        by *= 2
    return value


def log_sum(exponents):
    return -LOG2E * jnp.log(functools.reduce(jnp.add, [jnp.exp2(-e) for e in exponents]))


def passages(costs, own, from_left, from_right, depth):
    width_x, width_y = costs.shape[1:]
    base = 8 * width_x
    at = slice(base, base + width_x)
    lane = iota((width_x, width_y), 1)
    beside = jnp.where((lane & 7) == 4, running_sum(from_right[at, :]), pltpu.roll(running_sum(from_left[at, :]), 2, 1))
    sums = [running_sum(costs[z]) for z in range(depth)]
    sub = iota((8, width_y), 0)
    tiles = []
    for z in range(depth):
        back = sums[z] - costs[z]
        edge = pltpu.roll(beside, width_y - 5 - 8 * z, 1)
        below = jnp.where(lane == 0, edge, pltpu.roll(sums[z], 1, 1))
        above = jnp.where(lane == width_y - 1, edge, pltpu.roll(sums[z], width_y - 1, 1))
        step_y = back + costs[depth + z]
        step_z = back + costs[2 * depth + z]
        paths = [sums[z] + back, below + step_y, above + step_y]
        paths.append(sums[z - 1] + step_z if z > 0 else None)
        paths.append(sums[z + 1] + step_z if z < depth - 1 else None)
        tile = jnp.broadcast_to(sums[z][width_x - 1 :, :], sub.shape)
        for j, path in enumerate(paths):
            if path is None:
                tile = jnp.where(sub == j + 1, BIG, tile)
            else:
                total = jnp.sum(jnp.exp2(-path), axis=0, keepdims=True)
                tile = jnp.where(sub == j + 1, -LOG2E * jnp.log(total), tile)
        tiles.append(tile)
    return tiles


def strip_passages(edge_costs, width_x):
    shape = edge_costs.shape[2:]
    lane = iota(shape, 1)
    sums = jnp.zeros(shape, jnp.float32)
    totals = [jnp.zeros(shape, jnp.float32)] * 5
    for x in range(width_x):
        cost, step_y, step_z = [packed(edge_costs[k, x], edge_costs[3 + k, x]) for k in range(3)]
        back = sums
        sums = sums + cost
        step_y, step_z = step_y + back, step_z + back
        paths = [sums + back, pltpu.roll(sums, 1, 0) + step_y, shifted_down(sums, 1) + step_y]
        paths.append(jnp.where(lane < 8, BIG, pltpu.roll(sums, 8, 1) + step_z))
        paths.append(jnp.where(lane >= shape[1] - 8, BIG, pltpu.roll(sums, shape[1] - 8, 1) + step_z))
        totals = [t + jnp.exp2(-p) for t, p in zip(totals, paths)]
    return sums, [-LOG2E * jnp.log(jnp.maximum(t, 1e-37)) for t in totals]


def shared_rows(total, paths):
    place = iota(total.shape, 1) & 7
    first, second = total, total
    for q in range(6):
        value = pltpu.roll(total, (4 - q) % 8, 0)
        first = jnp.where(place == q, value, first)
    for q, (path, at) in enumerate([(p, r) for p in paths for r in (3, 6)]):
        if q < 2:
            first = jnp.where(place == 6 + q, pltpu.roll(path, (6 - at) % 8, 0), first)
        else:
            second = jnp.where(place == q - 2, pltpu.roll(path, (7 - at) % 8, 0), second)
    return jnp.where(iota(total.shape, 0) == 6, first, second)


def spread_rows(tiles):
    shape = tiles[0].shape
    wide = shape[1]
    sub = iota(shape, 0)
    mine = (iota(shape, 1) & 7) == sub
    spread = ((iota((wide, wide), 0) >> 3) == (iota((wide, wide), 1) >> 3)).astype(jnp.float32)
    spread = spread.astype(jnp.bfloat16)
    rows = [jnp.where(mine, jnp.broadcast_to(t[r : r + 1], shape), 0.0) for t in tiles for r in (6, 7)]
    whole = jnp.concatenate(rows, 0)
    value = 0.0
    for part in reversed(exact_parts(whole)):
        value = value + lax.dot_general(part, spread, (((1,), (0,)), ((), ())), preferred_element_type=jnp.float32)
    out = []
    for i in range(len(tiles)):
        first, second = value[16 * i : 16 * i + 8], value[16 * i + 8 : 16 * i + 16]
        paths = [jnp.where(sub == 3, pltpu.roll(first, 5, 0), pltpu.roll(first, 7, 0))]
        for q in range(4):
            at_three = pltpu.roll(second, (3 - 2 * q) % 8, 0)
            at_six = pltpu.roll(second, (6 - 2 * q - 1) % 8, 0)
            paths.append(jnp.where(sub == 3, at_three, at_six))
        out.append((pltpu.roll(first, 2, 0), paths))
    return out


def sweep_step(x, near, field, strip, costs, edge_costs, halo, state, strip_state, keep, keep_strip):
    depth = field.shape[1]
    tile = field.shape[2:]
    width_y = tile[1]
    lane = iota(tile, 1)
    out = []
    for z in range(depth):
        u = field[x, z]
        cost_y = row(costs, depth + z, x, tile)
        cost_z = row(costs, 2 * depth + z, x, tile)
        edge = pltpu.roll(halo[z], width_y - 5 - 8 * x, 1)
        values = [u]
        values.append(jnp.where(lane == 0, edge, pltpu.roll(u, 1, 1)) + cost_y)
        values.append(jnp.where(lane == width_y - 1, edge, pltpu.roll(u, width_y - 1, 1)) + cost_y)
        if z > 0:
            values.append(field[x, z - 1] + cost_z)
        if z < depth - 1:
            values.append(field[x, z + 1] + cost_z)
        level, parts, total = softmin(values)
        passed = state[z] + row(costs, z, x, tile)
        if z < near:
            scale = 1.0 / total
            keep(x, z, level, [p * scale for p in parts], passed)
        out.append(soft_pair(level, passed))
    strips, levels, weights, passes = [], [], [], []
    for side in range(2):
        u = strip[x, side]
        cost_y = edge_costs[3 * side + 1, x]
        cost_z = edge_costs[3 * side + 2, x]
        values = [u, pltpu.roll(u, 1, 0) + cost_y, pltpu.roll(u, 7, 0) + cost_y]
        values.append(jnp.where(lane < 8, BIG, pltpu.roll(u, 8, 1)) + cost_z)
        values.append(jnp.where(lane >= width_y - 8, BIG, pltpu.roll(u, width_y - 8, 1)) + cost_z)
        level, parts, total = softmin(values)
        passes.append(strip_state[side] + edge_costs[3 * side, x])
        strips.append(soft_pair(level, passes[side]))
        levels.append(level)
        weights.append(parts[2 - side] / total)
    if keep_strip is not None:
        keep_strip(x, merged(*levels), merged(*weights), merged(*passes), merged(*strips))
    return out, strips


def outside_strips(place, shape):
    sub = iota(shape, 0)
    return [(place[4] == 1) & (sub < 4), (place[5] == 1) & (sub >= 4)]


def first_sweep_kernel(
    rows_of, count_y, place, field, own, from_left, from_right, costs, anisotropy, *rest
):
    others = rest[: count_y - 3]
    local, local_strip, edge_costs, levels, sides, message, halo, strip = rest[count_y - 3 :]
    width_x, depth, quakes, width_y = field.shape
    tile = (quakes, width_y)
    sub = iota(tile, 0)
    low = sub < 4
    near = levels.shape[1]
    last = 11 * width_x
    far = [own[last:, :], from_left[last:, :]] + [o[...] for o in others] + [from_right[last:, :]]
    records = jnp.zeros(tile, jnp.float32)
    for by, piece in enumerate(far):
        owner = lax.rem(place[8] + count_y - by, count_y)
        records = records + pltpu.roll(piece, owner * rows_of, 1)
    left, right = [], []
    for x in range(width_x):
        at = slice(8 * x, 8 * x + 8)
        before = jnp.where(place[4] == 1, BIG, from_left[at, :])
        after = jnp.where(place[5] == 1, BIG, from_right[at, :])
        left.append(jnp.where(low, before, own[at, :]))
        right.append(jnp.where(low, own[at, :], after))
        strip[x, 0] = left[x]
        strip[x, 1] = right[x]
    halo[...] = halo_columns(left, right).reshape(halo.shape)
    strip_costs(own, from_left, from_right, edge_costs, width_x, depth)
    outside = outside_strips(place, tile)

    def keep(x, z, level, w, passed):
        levels[x, z] = level
        vertical = w[3] if z == 0 else w[3] + w[4]
        sideways = row(anisotropy, near + z, x, tile) * (w[1] + w[2])
        sides[x, z] = sideways + row(anisotropy, 2 * near + z, x, tile) * vertical

    def step(x, carry):
        state, strips = sweep_step(x, near, field, strip, costs, edge_costs, halo, *carry, keep, None)
        for z in range(depth):
            local[x, z] = state[z]
        for side in range(2):
            local_strip[x, side] = jnp.where(outside[side], BIG, strips[side])
        return state, strips

    blank = jnp.full(tile, BIG, jnp.float32)
    state, strips = by_steps(width_x, step, ([blank] * depth, [blank] * 2))
    reach_strip = packed(*[jnp.where(o, BIG, s) for o, s in zip(outside, strips)])

    edges = [[local_strip[x, side] for x in range(width_x)] for side in range(2)]
    halo[...] = halo_columns(*edges).reshape(halo.shape)

    def again(lap, carry):
        x = width_x - 1 - lap
        return sweep_step(x, 0, local, local_strip, costs, edge_costs, halo, *carry, None, None)

    back, back_strips = by_steps(width_x, again, ([blank] * depth, [blank] * 2))
    tiles = passages(costs, own, from_left, from_right, depth)
    strip_total, strip_paths = strip_passages(edge_costs, width_x)

    back_strip = packed(*back_strips)
    reach_strip = jnp.where(sub == 0, shifted_down(back_strip, 3), reach_strip)
    reach_strip = jnp.where(sub == 1, shifted_down(back_strip, 5), reach_strip)
    shared = shared_rows(strip_total, strip_paths)
    count = message.shape[0]
    per = message.shape[1] // 3 - 1
    for p in range(count):
        first = min(p * per, depth - per)
        for k in range(per + 2):
            z = first + k - 1
            message[p, k] = state[z] if 0 <= z < depth else blank
        for k in range(per):
            message[p, per + 2 + k] = back[first + k]
            value = tiles[first + k]
            if k == 0 and first > 0:
                value = jnp.where(sub == 6, jnp.broadcast_to(tiles[first - 1][:1], tile), value)
            if k == 0 and first + per < depth:
                value = jnp.where(sub == 7, jnp.broadcast_to(tiles[first + per][:1], tile), value)
            if per > 1 and k == 1:
                value = jnp.where(sub < 6, value, shared)
            message[p, 2 * per + 2 + k] = value
        message[p, 3 * per + 2] = reach_strip
        message[p, 3 * per + 3] = records
        if per == 1:
            message[p, 3 * per + 4] = shared


def blocks_kernel(per, depth, place, received, entering, entering_strips, halo):
    count = received.shape[0]
    tile = entering.shape[2:]
    lane = iota(tile, 1)
    width_y = tile[1]
    me = place[6]
    blank = jnp.full(tile, BIG, jnp.float32)
    side = 3 * per + 2

    def rows(device, k, j):
        return jnp.broadcast_to(received[device, 2 * per + 2 + k, j : j + 1, :], tile)

    def total(device, k):
        if k < 0:
            return rows(device, 0, 6)
        return rows(device, k, 0) if k < per else rows(device, 0, 7)

    shared = [received[d, 2 * per + 3] if per > 1 else received[d, 3 * per + 4] for d in range(count)]
    shared = spread_rows(shared)
    state = [blank] * (per + 2)
    strip = blank
    first, first_strip = [], []
    for device in range(count):
        first.append(state)
        first_strip.append(strip)
        state = [
            soft_pair(received[device, k], state[k] + total(device, k - 1)) for k in range(per + 2)
        ]
        strip = soft_pair(received[device, side], strip + shared[device][0])
    own = blank
    for device in range(count):
        own = jnp.where(device == me, first_strip[device], own)
        for k in range(per):
            entering[device, k] = first[device][k + 1]
    entering_strips[0] = own
    group = width_y // 8
    for at in range(0, count, group):
        some = first_strip[at : at + group]
        some = some + [blank] * (group - len(some))
        turned = halo_columns(some, [shifted_down(s, 2) for s in some])
        halo[at // group] = turned.reshape(halo.shape[1:])
    low = jnp.minimum(me * per, depth - per)
    edges = [[halo[i, low + k] for k in range(per)] for i in range(halo.shape[0])]
    state = [blank] * per
    strip = blank
    for device in reversed(range(count)):
        for k in range(per):
            entering[device, per + k] = state[k]
            u = first[device][k + 1]
            turn = (width_y - 5 - 8 * (device % group)) % width_y
            edge = pltpu.roll(edges[device // group][k], turn, 1)
            values = [received[device, per + 2 + k], u + rows(device, k, 1)]
            values.append(jnp.where(lane == 0, edge, pltpu.roll(u, 1, 1)) + rows(device, k, 2))
            values.append(jnp.where(lane == width_y - 1, edge, pltpu.roll(u, width_y - 1, 1)) + rows(device, k, 3))
            values.append(first[device][k] + rows(device, k, 4))
            values.append(first[device][k + 2] + rows(device, k, 5))
            state[k] = soft_pair(softmin(values)[0], state[k] + total(device, k))
        u = first_strip[device]
        back = received[device, side]
        back = jnp.where(iota(tile, 0) == 3, pltpu.roll(back, 3, 0), pltpu.roll(back, 5, 0))
        paths = shared[device][1]
        values = [back, u + paths[0], pltpu.roll(u, 1, 0) + paths[1], shifted_down(u, 1) + paths[2]]
        values.append(jnp.where(lane < 8, BIG, pltpu.roll(u, 8, 1)) + paths[3])
        values.append(jnp.where(lane >= width_y - 8, BIG, pltpu.roll(u, width_y - 8, 1)) + paths[4])
        passed = soft_pair(softmin(values)[0], strip + shared[device][0])
        strip = jnp.where(device > me, passed, strip)
    entering_strips[1] = strip


def second_sweep_kernel(
    place, first, first_strip, entering, entering_strips, costs, edge_costs, anisotropy, levels_one, sides,
    sums, counts, sums_strip, counts_strip,
    local, shares, shares_strip, slopes, slopes_strip, keeps, keeps_strip, misfits, misfits_strip,
    slopes_one, gains, message, field, strip, halo,
):
    width_x, depth, quakes, width_y = first.shape
    tile = (quakes, width_y)
    near = levels_one.shape[1]
    per = entering.shape[1] // 2
    outside = outside_strips(place, tile)
    strips_in = [[s, shifted_down(s, 2)] for s in (entering_strips[0], entering_strips[1])]
    carried = [[entering[z // per, k * per + z % per] for z in range(depth)] for k in range(2)]

    def finish(x, carry):
        running, strip_running, prior = carry
        sums_now, values = [], []
        for z in range(depth):
            cost = row(costs, z, x, tile)
            sums_now.append(running[z] + cost)
            value = soft_pair(first[x, z], entering[z // per, z % per] + sums_now[z])
            field[x, z] = value
            if z < near:
                values.append(value)
                keep, slope = split_pair(levels_one[x, z], prior[z] + cost)
                slopes_one[x, z] = slope
                gains[x, z] = slope * row(anisotropy, z, x, tile) + keep * sides[x, z]
        strip_sums = []
        for side in range(2):
            strip_sums.append(strip_running[side] + edge_costs[3 * side, x])
            value = soft_pair(first_strip[x, side], strips_in[0][side] + strip_sums[side])
            strip[x, side] = jnp.where(outside[side], BIG, value)
        return sums_now, strip_sums, values

    blank = jnp.zeros(tile, jnp.float32)
    by_steps(width_x, finish, ([blank] * depth, [blank] * 2, carried[0][:near]))
    edges = [[strip[x, side] for x in range(width_x)] for side in range(2)]
    halo[...] = halo_columns(*edges).reshape(halo.shape)

    def keep(x, z, level, w, passed):
        for i in range(4):
            shares[i, x] = w[i]
        keeps[x], slopes[x] = split_pair(level, passed)

    def keep_strip(x, level, w, passed, value):
        shares_strip[x] = w
        keeps_strip[x], slopes_strip[x] = split_pair(level, passed)
        tally = pltpu.roll(counts_strip[...], lax.rem(width_y - 8 * x, width_y), 1)
        total = pltpu.roll(sums_strip[...], lax.rem(width_y - 8 * x, width_y), 1)
        misfits_strip[x] = ADJ_SCALE * (tally * (value * (1.0 / RATE)) - total)

    def step(lap, carry):
        x = width_x - 1 - lap
        state, strips = sweep_step(x, 1, field, strip, costs, edge_costs, halo, *carry, keep, keep_strip)
        for z in range(depth):
            local[x, z] = state[z]
        misfits[x] = ADJ_SCALE * (counts[x] * (state[0] * (1.0 / RATE)) - sums[x])
        return state, strips

    by_steps(width_x, step, (carried[1], strips_in[1]))
    leaving, strip_leaving = jnp.zeros(tile, jnp.float32), jnp.zeros(tile, jnp.float32)
    through, strip_through = jnp.ones(tile, jnp.float32), jnp.ones(tile, jnp.float32)
    for x in range(width_x):
        leaving = slopes[x] * (misfits[x] + leaving)
        through = slopes[x] * through
        strip_leaving = slopes_strip[x] * (misfits_strip[x] + strip_leaving)
        strip_through = slopes_strip[x] * strip_through
    both = jnp.where(iota(tile, 0) < 5, strip_leaving, pltpu.roll(strip_through, 2, 0))
    for p in range(message.shape[0]):
        message[p, 0] = leaving
        message[p, 1] = through
        message[p, 2] = both


def records_kernel(rows_of, tile_of, place, cell, received, sums, counts, sums_strip, counts_strip):
    width_x, quakes, width_y = sums.shape
    last = tile_of
    span_y = place[2]
    lane = iota((quakes, width_y), 1)
    column = iota((width_y, width_y), 0)
    strip_column = iota((8, width_y), 0)
    strip_column = jnp.where(strip_column == 3, -1, jnp.where(strip_column == 4, width_y, -2))
    share = width_y // rows_of
    dims = (((1,), (1,)), ((), ()))
    one_x = iota((width_x, width_y), 0)
    parts = [[], [], [], []]
    at, at_strip = [], []
    for chunk in range(cell.shape[0]):
        records = jnp.zeros((quakes, width_y), jnp.float32)
        for part in range(share):
            piece = received[chunk * share + part, last]
            moved = pltpu.roll(piece, part * rows_of, 1) if part else piece
            records = jnp.where(lane // rows_of == part, moved, records)
        cells = cell[chunk : chunk + 1, :]
        station_x = lax.shift_right_logical(cells, place[7]) - place[0]
        station_y = (cells & (span_y - 1)) - place[1]
        at_x = (one_x == jnp.broadcast_to(station_x, one_x.shape)).astype(jnp.float32)
        pieces = [p.astype(jnp.float32) for p in exact_parts(records)] + [jnp.ones((quakes, width_y), jnp.float32)]
        for out, piece in zip(parts, pieces):
            spread = [piece * jnp.broadcast_to(at_x[x : x + 1], piece.shape) for x in range(width_x)]
            out.append(jnp.concatenate(spread, 0).astype(jnp.bfloat16))
        hit = column == jnp.broadcast_to(station_y, column.shape)
        at.append(hit.astype(jnp.float32).astype(jnp.bfloat16))
        hit = strip_column == jnp.broadcast_to(station_y, strip_column.shape)
        at_strip.append(hit.astype(jnp.float32).astype(jnp.bfloat16))
    at = jnp.concatenate(at, 1)
    at_strip = jnp.concatenate(at_strip, 1)
    parts = [jnp.concatenate(p, 1) for p in parts]
    main = [lax.dot_general(p, at, dims, preferred_element_type=jnp.float32) for p in parts]
    side = [lax.dot_general(at_strip, p, dims, preferred_element_type=jnp.float32) for p in parts]
    sums[...] = (main[0] + main[1] + main[2]).reshape(sums.shape)
    counts[...] = main[3].reshape(counts.shape)
    sums_strip[...] = side[0] + side[1] + side[2]
    counts_strip[...] = side[3]


def times_kernel(local, times):
    width_x, depth, quakes, _ = local.shape

    def step(x, carry):
        for z in range(depth):
            times[pl.ds(z * width_x + x, quakes, stride=depth * width_x), :] = local[x, z] * (1.0 / RATE)
        return carry

    by_steps(width_x, step, 0)


def linear_carry(me, backward, blocks, tile):
    count, block = blocks
    state = jnp.zeros(tile, jnp.float32)
    for lap in range(count):
        device = count - 1 - lap if backward else lap
        ahead = device > me if backward else device < me
        own, factor = block(device)
        state = jnp.where(ahead, own + factor * state, state)
    return state


def adjoint_kernel(
    place, received, slopes, slopes_strip, keeps, keeps_strip, misfits, misfits_strip,
    shares, shares_strip, anisotropy, slopes_one, entries, kernel, message, through,
):
    width_x, quakes, width_y = slopes.shape
    tile = (quakes, width_y)
    near = slopes_one.shape[1]
    count = received.shape[0]
    lane = iota(tile, 1)
    me = place[6]
    state = linear_carry(me, False, (count, lambda d: (received[d, 0], received[d, 1])), tile)
    strip = linear_carry(
        me, False, (count, lambda d: (received[d, 2], shifted_down(received[d, 2], 2))), tile
    )
    outgoing = jnp.zeros(tile, jnp.float32)
    for x in range(width_x):
        total = misfits[x] + state
        state = slopes[x] * total
        passed = keeps[x] * total
        through[x] = passed
        sideways = row(anisotropy, near, x, tile) * (shares[1, x] + shares[2, x])
        sideways = sideways + row(anisotropy, 2 * near, x, tile) * shares[3, x]
        terms = state * row(anisotropy, 0, x, tile) + passed * sideways
        kernel[x : x + 1, :] = jnp.sum(terms, axis=0, keepdims=True)
        total = misfits_strip[x] + strip
        strip = slopes_strip[x] * total
        sent = keeps_strip[x] * total * shares_strip[x]
        outgoing = jnp.where((lane >> 3) == x, pltpu.roll(sent, 8 * x, 1) if x else sent, outgoing)
    first, last = shifted_down(outgoing, 3), pltpu.roll(outgoing, 3, 0)
    halo = jnp.transpose(jnp.concatenate([first] * (width_y // 16) + [last] * (width_y // 16), 0))
    leaving = [jnp.zeros(tile, jnp.float32)] * near
    factor = [jnp.ones(tile, jnp.float32)] * near
    for x in reversed(range(width_x)):
        passed = through[x]
        edge = halo[8 * x : 8 * x + 8]
        above = jnp.where(lane == width_y - 1, edge, pltpu.roll(passed * shares[1, x], width_y - 1, 1))
        below = jnp.where(lane == 0, edge, pltpu.roll(passed * shares[2, x], 1, 1))
        entry = (passed * shares[0, x] + above + below, passed * shares[3, x])
        for z in range(near):
            entries[x, z] = entry[z]
            leaving[z] = slopes_one[x, z] * (entry[z] + leaving[z])
            factor[z] = slopes_one[x, z] * factor[z]
    for p in range(count):
        for z in range(near):
            message[p, z] = leaving[z]
            message[p, near + z] = factor[z]


def kernel_kernel(place, received, entries, slopes, gains, top, kernel):
    width_x, near, quakes, width_y = slopes.shape
    tile = (quakes, width_y)
    count = received.shape[0]
    state = [
        linear_carry(place[6], True, (count, lambda d, z=z: (received[d, z], received[d, near + z])), tile)
        for z in range(near)
    ]
    for x in reversed(range(width_x)):
        for z in range(near):
            total = entries[x, z] + state[z]
            state[z] = slopes[x, z] * total
            value = jnp.sum(total * gains[x, z], axis=0, keepdims=True)
            if z == 0:
                value = value + top[x : x + 1, :]
            kernel[z, x : x + 1, :] = value
    for z in range(near, kernel.shape[0]):
        kernel[z] = jnp.zeros(kernel.shape[1:], jnp.float32)


def call(kernel, shapes, operands, scratch=(), scalars=0, far=0, last=False):
    many = isinstance(shapes, list)
    shapes = shapes if many else [shapes]
    out = [jax.ShapeDtypeStruct(s, jnp.float32) if last else pltpu.VMEM(s, jnp.float32) for s in shapes]
    result = pl.pallas_call(
        kernel,
        out_shape=out,
        in_specs=[SMEM] * scalars + [FAR] * far + [VMEM] * (len(operands) - scalars - far),
        out_specs=[VMEM] * len(out),
        scratch_shapes=[pltpu.VMEM(s, jnp.float32) if isinstance(s, tuple) else s for s in scratch],
        compiler_params=PARAMS,
    )(*operands)
    return result if many else result[0]


def traded(message):
    return lax.all_to_all(message, "gx", 0, 0, tiled=True)


def rotated(value, axis, by):
    count = lax.axis_size(axis)
    return lax.ppermute(value, axis, [(i, (i + by) % count) for i in range(count)])


def body(warm_start, slowness, anisotropy, observed, station_cell, source_cell):
    quakes, depth, width_x, width_y = warm_start.shape
    count_x, count_y = lax.axis_size("gx"), lax.axis_size("gy")
    index_x, index_y = lax.axis_index("gx"), lax.axis_index("gy")
    span_x, span_y = width_x * count_x, width_y * count_y
    near = 2
    per = max(1, depth // count_x)
    tile = (quakes, width_y)
    top = (width_x,) + tile
    close = (width_x, near) + tile
    field = (width_x, depth) + tile
    place = jnp.stack(
        [
            index_x * width_x,
            index_y * width_y,
            jnp.int32(span_y),
            jnp.int32(span_x * span_y),
            (index_y == 0).astype(jnp.int32),
            (index_y == count_y - 1).astype(jnp.int32),
            index_x,
            jnp.int32(span_y.bit_length() - 1),
            index_y,
        ]
    ).astype(jnp.int32)
    anis = anisotropy.reshape(3 * depth, width_x, width_y)
    local_records = observed.shape[1]
    flat = (quakes * depth * width_x, width_y)

    base = width_x * 11
    sources = [warm_start.reshape(flat), observed, slowness, anis]
    sources = [pltpu.with_memory_space_constraint(a, pltpu.HBM) for a in sources]
    start, costs, anis, edge, records = call(
        pack_kernel,
        [field, anis.shape, (3 * near, width_x, width_y), (base + quakes, width_y), tile],
        [place, source_cell] + sources,
        [sources[i].shape for i in range(4)] + [pltpu.SemaphoreType.DMA((7,))],
        scalars=2,
        far=4,
    )
    from_left = rotated(edge, "gy", 1)
    from_right = rotated(edge, "gy", -1)
    others = [rotated(records, "gy", by) for by in range(2, count_y - 1)]

    message_shape = (count_x, 3 * per + (4 if per > 1 else 5)) + tile
    first, first_strip, edge_costs, levels_one, sides, message = call(
        functools.partial(first_sweep_kernel, local_records, count_y),
        [field, (width_x, 2) + tile, (6,) + top, close, close, message_shape],
        [place, start, edge, from_left, from_right, costs, anis] + others,
        [(depth,) + tile, (width_x, 2) + tile],
        scalars=1,
    )
    reach = traded(message)
    group = width_y // 8
    entering, entering_strips = call(
        functools.partial(blocks_kernel, per, depth),
        [(count_x, 2 * per) + tile, (2,) + tile],
        [place, reach],
        [(-(-count_x // group), depth) + tile],
        scalars=1,
    )
    entering = traded(entering)
    recorded = call(
        functools.partial(records_kernel, local_records * count_y, 3 * per + 3),
        [top, top, tile, tile],
        [place, station_cell.reshape(-1, width_y), reach],
        scalars=1,
    )
    second, shares, shares_strip, *rest = call(
        second_sweep_kernel,
        [field, (4,) + top] + [top] * 7 + [close, close, (count_x, 3) + tile],
        [place, first, first_strip, entering, entering_strips, costs, edge_costs, anis, levels_one, sides]
        + list(recorded),
        [field, (width_x, 2) + tile, (depth,) + tile],
        scalars=1,
    )
    slopes, slopes_strip, keeps, keeps_strip, misfits, misfits_strip, slopes_one, gains, message = rest
    received = traded(message)
    times = call(times_kernel, flat, [second], last=True)
    entries, kernel_two, message = call(
        adjoint_kernel,
        [close, (width_x, width_y), (count_x, 2 * near) + tile],
        [place, received, slopes, slopes_strip, keeps, keeps_strip, misfits, misfits_strip]
        + [shares, shares_strip, anis, slopes_one],
        [top],
        scalars=1,
    )
    kernel = call(
        kernel_kernel,
        (depth, width_x, width_y),
        [place, traded(message), entries, slopes_one, gains, kernel_two],
        scalars=1,
        last=True,
    )
    return (times.reshape(warm_start.shape), kernel)


def solution(mesh):
    return jax.shard_map(
        body,
        mesh=mesh,
        in_specs=(
            P(None, None, "gx", "gy"),
            P(None, "gx", "gy"),
            P(None, None, "gx", "gy"),
            P(None, ("gx", "gy")),
            P(),
            P(),
        ),
        out_specs=(P(None, None, "gx", "gy"), P(None, "gx", "gy")),
        check_vma=False,
    )
```

```python
import functools
import math

import jax
import jax.numpy as jnp
from jax import lax
from jax.experimental import pallas as pl
from jax.experimental.pallas import tpu as pltpu
from jax.sharding import PartitionSpec as P

TAU = 0.05
ADJ_SCALE = 0.1
LOG2E = math.log2(math.e)
RATE = LOG2E / TAU
BIG = 10000.0 * RATE
UNROLL = 4
VMEM = pl.BlockSpec(memory_space=pltpu.VMEM)
FAR = pl.BlockSpec(memory_space=pl.ANY)
SMEM = pl.BlockSpec(memory_space=pltpu.SMEM)
PARAMS = pltpu.CompilerParams(vmem_limit_bytes=8 * 1024 * 1024)


def softmin(values):
    least = functools.reduce(jnp.minimum, values)
    parts = [jnp.exp2(least - v) for v in values]
    total = functools.reduce(jnp.add, parts)
    return least - LOG2E * jnp.log(total), parts, total


def soft_pair(first, second):
    return jnp.minimum(first, second) - LOG2E * jnp.log(1.0 + jnp.exp2(-jnp.abs(first - second)))


def split_pair(first, second):
    gap = jnp.exp2(-jnp.abs(first - second))
    share = 1.0 / (1.0 + gap)
    less = gap * share
    nearer = first <= second
    return jnp.where(nearer, share, less), jnp.where(nearer, less, share)


def iota(shape, axis):
    return lax.broadcasted_iota(jnp.int32, shape, axis)


def row(ref, index, x, like):
    return jnp.broadcast_to(ref[index, pl.ds(x, 1), :], like)


def by_steps(count, step, carry):
    def group(i, carry):
        for j in range(UNROLL):
            carry = step(i * UNROLL + j, carry)
        return carry

    return lax.fori_loop(0, count // UNROLL, group, carry)


def packed(left, right):
    return jnp.where(iota(left.shape, 0) < 5, left, pltpu.roll(right, 2, 0))


def merged(left, right):
    return jnp.where(iota(left.shape, 0) < 4, left, right)


def shifted_down(tile, by):
    return pltpu.roll(tile, tile.shape[0] - by, 0)


def exact_parts(value):
    high = value.astype(jnp.bfloat16).astype(jnp.float32)
    middle = (value - high).astype(jnp.bfloat16).astype(jnp.float32)
    low = value - high - middle
    return [p.astype(jnp.bfloat16) for p in (high, middle, low)]


def pack_kernel(
    place, source, warm_far, observed_far, slowness_far, anisotropy_far, start, costs, near, edge, records,
    warm, observed, slowness, anisotropy, arrived,
):
    pairs = [(slowness_far, slowness), (anisotropy_far, anisotropy), (observed_far, observed)]
    share = warm.shape[0] // 4
    pairs += [(warm_far.at[pl.ds(i * share, share)], warm.at[pl.ds(i * share, share)]) for i in range(4)]
    copies = [pltpu.make_async_copy(a, b, arrived.at[i]) for i, (a, b) in enumerate(pairs)]
    for copy in copies:
        copy.start()
    width_x, depth, quakes, width_y = start.shape
    tile = (quakes, width_y)
    quake = iota(tile, 0)
    lane = iota(tile, 1)
    span_y = place[2]
    plane = place[3]
    cell = jnp.zeros(tile, jnp.int32)
    for e in range(quakes):
        cell = jnp.where(quake == e, source[e], cell)
    cell = cell - (lane + place[0] * span_y + place[1])

    def one(x, edges):
        here = (lane >> 3) == x
        out = []
        for z in range(depth):
            value = warm[pl.ds(z * width_x + x, quakes, stride=depth * width_x), :] * RATE
            value = jnp.where(cell == z * plane + x * span_y, 0.0, value)
            start[x, z] = value
            out.append(jnp.where(here, pltpu.roll(value, 8 * x + 4, 1), edges[z]))
        return out

    rows = width_x * 8
    wide = (width_x, width_y)
    group = iota(wide, 1) >> 3
    copies[0].wait()
    copies[1].wait()
    for k in range(3):
        columns = jnp.zeros(wide, jnp.float32)
        for z in range(depth):
            cost = slowness[z] * anisotropy[k * depth + z] * RATE
            costs[k * depth + z] = cost
            columns = jnp.where(group == z, pltpu.roll(cost, 8 * z + 4, 1), columns)
        edge[rows : rows + width_x, :] = columns
        rows += width_x
        for z in range(near.shape[0] // 3):
            near[k * (near.shape[0] // 3) + z] = anisotropy[k * depth + z]
    for copy in copies[3:]:
        copy.wait()
    edges = by_steps(width_x, one, [jnp.zeros(tile, jnp.float32)] * depth)
    edge[: width_x * 8, :] = jnp.transpose(jnp.concatenate(edges, 0))
    copies[2].wait()
    records[...] = jnp.zeros(tile, jnp.float32)
    records[:, : observed.shape[1]] = observed[...]
    edge[rows:, :] = records[...]


def halo_columns(left, right):
    rows = []
    for l, r in zip(left, right):
        rows.append(jnp.where(iota(l.shape, 0) == 4, r, pltpu.roll(l, 2, 0)))
    return jnp.transpose(jnp.concatenate(rows, 0))


def strip_costs(own, from_left, from_right, out, width_x, depth):
    tile = own.shape[1]
    base = width_x * 8
    lane = iota((8, tile), 1)
    low = (lane & 7) < 4
    mine = (lane & 7) == iota((8, tile), 0)
    spread = ((iota((tile, tile), 0) >> 3) == (iota((tile, tile), 1) >> 3)).astype(jnp.float32)
    spread = spread.astype(jnp.bfloat16)
    for side in range(2):
        for k in range(3):
            rows = []
            for x in range(width_x):
                at = slice(base + k * width_x + x, base + k * width_x + x + 1)
                here = jnp.broadcast_to(own[at, :], lane.shape)
                there = jnp.broadcast_to((from_right if side else from_left)[at, :], lane.shape)
                value = jnp.where(low, here, there) if side else jnp.where(low, there, here)
                rows.append(jnp.where(mine, value, 0.0))
            whole = jnp.concatenate(rows, 0)
            total = 0.0
            for part in reversed(exact_parts(whole)):
                total = total + lax.dot_general(
                    part, spread, (((1,), (0,)), ((), ())), preferred_element_type=jnp.float32
                )
            out[3 * side + k] = total.reshape(width_x, 8, tile)


def running_sum(value):
    rows = iota(value.shape, 0)
    by = 1
    while by < value.shape[0]:
        value = value + jnp.where(rows >= by, pltpu.roll(value, by, 0), 0.0)
        by *= 2
    return value


def log_sum(exponents):
    return -LOG2E * jnp.log(functools.reduce(jnp.add, [jnp.exp2(-e) for e in exponents]))


def passages(costs, own, from_left, from_right, depth):
    width_x, width_y = costs.shape[1:]
    base = 8 * width_x
    at = slice(base, base + width_x)
    lane = iota((width_x, width_y), 1)
    beside = jnp.where((lane & 7) == 4, running_sum(from_right[at, :]), pltpu.roll(running_sum(from_left[at, :]), 2, 1))
    sums = [running_sum(costs[z]) for z in range(depth)]
    sub = iota((8, width_y), 0)
    tiles = []
    for z in range(depth):
        back = sums[z] - costs[z]
        edge = pltpu.roll(beside, width_y - 5 - 8 * z, 1)
        below = jnp.where(lane == 0, edge, pltpu.roll(sums[z], 1, 1))
        above = jnp.where(lane == width_y - 1, edge, pltpu.roll(sums[z], width_y - 1, 1))
        step_y = back + costs[depth + z]
        step_z = back + costs[2 * depth + z]
        paths = [sums[z] + back, below + step_y, above + step_y]
        paths.append(sums[z - 1] + step_z if z > 0 else None)
        paths.append(sums[z + 1] + step_z if z < depth - 1 else None)
        tile = jnp.broadcast_to(sums[z][width_x - 1 :, :], sub.shape)
        for j, path in enumerate(paths):
            if path is None:
                tile = jnp.where(sub == j + 1, BIG, tile)
            else:
                total = jnp.sum(jnp.exp2(-path), axis=0, keepdims=True)
                tile = jnp.where(sub == j + 1, -LOG2E * jnp.log(total), tile)
        tiles.append(tile)
    return tiles


def strip_passages(edge_costs, width_x):
    shape = edge_costs.shape[2:]
    lane = iota(shape, 1)
    sums = jnp.zeros(shape, jnp.float32)
    totals = [jnp.zeros(shape, jnp.float32)] * 5
    for x in range(width_x):
        cost, step_y, step_z = [packed(edge_costs[k, x], edge_costs[3 + k, x]) for k in range(3)]
        back = sums
        sums = sums + cost
        step_y, step_z = step_y + back, step_z + back
        paths = [sums + back, pltpu.roll(sums, 1, 0) + step_y, shifted_down(sums, 1) + step_y]
        paths.append(jnp.where(lane < 8, BIG, pltpu.roll(sums, 8, 1) + step_z))
        paths.append(jnp.where(lane >= shape[1] - 8, BIG, pltpu.roll(sums, shape[1] - 8, 1) + step_z))
        totals = [t + jnp.exp2(-p) for t, p in zip(totals, paths)]
    return sums, [-LOG2E * jnp.log(jnp.maximum(t, 1e-37)) for t in totals]


def shared_rows(total, paths):
    place = iota(total.shape, 1) & 7
    first, second = total, total
    for q in range(6):
        value = pltpu.roll(total, (4 - q) % 8, 0)
        first = jnp.where(place == q, value, first)
    for q, (path, at) in enumerate([(p, r) for p in paths for r in (3, 6)]):
        if q < 2:
            first = jnp.where(place == 6 + q, pltpu.roll(path, (6 - at) % 8, 0), first)
        else:
            second = jnp.where(place == q - 2, pltpu.roll(path, (7 - at) % 8, 0), second)
    return jnp.where(iota(total.shape, 0) == 6, first, second)


def spread_rows(tiles):
    shape = tiles[0].shape
    wide = shape[1]
    sub = iota(shape, 0)
    mine = (iota(shape, 1) & 7) == sub
    spread = ((iota((wide, wide), 0) >> 3) == (iota((wide, wide), 1) >> 3)).astype(jnp.float32)
    spread = spread.astype(jnp.bfloat16)
    rows = [jnp.where(mine, jnp.broadcast_to(t[r : r + 1], shape), 0.0) for t in tiles for r in (6, 7)]
    whole = jnp.concatenate(rows, 0)
    value = 0.0
    for part in reversed(exact_parts(whole)):
        value = value + lax.dot_general(part, spread, (((1,), (0,)), ((), ())), preferred_element_type=jnp.float32)
    out = []
    for i in range(len(tiles)):
        first, second = value[16 * i : 16 * i + 8], value[16 * i + 8 : 16 * i + 16]
        paths = [jnp.where(sub == 3, pltpu.roll(first, 5, 0), pltpu.roll(first, 7, 0))]
        for q in range(4):
            at_three = pltpu.roll(second, (3 - 2 * q) % 8, 0)
            at_six = pltpu.roll(second, (6 - 2 * q - 1) % 8, 0)
            paths.append(jnp.where(sub == 3, at_three, at_six))
        out.append((pltpu.roll(first, 2, 0), paths))
    return out


def sweep_step(x, near, field, strip, costs, edge_costs, halo, state, strip_state, keep, keep_strip):
    depth = field.shape[1]
    tile = field.shape[2:]
    width_y = tile[1]
    lane = iota(tile, 1)
    out = []
    for z in range(depth):
        u = field[x, z]
        cost_y = row(costs, depth + z, x, tile)
        cost_z = row(costs, 2 * depth + z, x, tile)
        edge = pltpu.roll(halo[z], width_y - 5 - 8 * x, 1)
        values = [u]
        values.append(jnp.where(lane == 0, edge, pltpu.roll(u, 1, 1)) + cost_y)
        values.append(jnp.where(lane == width_y - 1, edge, pltpu.roll(u, width_y - 1, 1)) + cost_y)
        if z > 0:
            values.append(field[x, z - 1] + cost_z)
        if z < depth - 1:
            values.append(field[x, z + 1] + cost_z)
        level, parts, total = softmin(values)
        passed = state[z] + row(costs, z, x, tile)
        if z < near:
            scale = 1.0 / total
            keep(x, z, level, [p * scale for p in parts], passed)
        out.append(soft_pair(level, passed))
    strips, levels, weights, passes = [], [], [], []
    for side in range(2):
        u = strip[x, side]
        cost_y = edge_costs[3 * side + 1, x]
        cost_z = edge_costs[3 * side + 2, x]
        values = [u, pltpu.roll(u, 1, 0) + cost_y, pltpu.roll(u, 7, 0) + cost_y]
        values.append(jnp.where(lane < 8, BIG, pltpu.roll(u, 8, 1)) + cost_z)
        values.append(jnp.where(lane >= width_y - 8, BIG, pltpu.roll(u, width_y - 8, 1)) + cost_z)
        level, parts, total = softmin(values)
        passes.append(strip_state[side] + edge_costs[3 * side, x])
        strips.append(soft_pair(level, passes[side]))
        levels.append(level)
        weights.append(parts[2 - side] / total)
    if keep_strip is not None:
        keep_strip(x, merged(*levels), merged(*weights), merged(*passes), merged(*strips))
    return out, strips


def outside_strips(place, shape):
    sub = iota(shape, 0)
    return [(place[4] == 1) & (sub < 4), (place[5] == 1) & (sub >= 4)]


def first_sweep_kernel(
    rows_of, count_y, place, field, own, from_left, from_right, costs, anisotropy, *rest
):
    others = rest[: count_y - 3]
    local, local_strip, edge_costs, levels, sides, message, halo, strip = rest[count_y - 3 :]
    width_x, depth, quakes, width_y = field.shape
    tile = (quakes, width_y)
    sub = iota(tile, 0)
    low = sub < 4
    near = levels.shape[1]
    last = 11 * width_x
    far = [own[last:, :], from_left[last:, :]] + [o[...] for o in others] + [from_right[last:, :]]
    records = jnp.zeros(tile, jnp.float32)
    for by, piece in enumerate(far):
        owner = lax.rem(place[8] + count_y - by, count_y)
        records = records + pltpu.roll(piece, owner * rows_of, 1)
    left, right = [], []
    for x in range(width_x):
        at = slice(8 * x, 8 * x + 8)
        before = jnp.where(place[4] == 1, BIG, from_left[at, :])
        after = jnp.where(place[5] == 1, BIG, from_right[at, :])
        left.append(jnp.where(low, before, own[at, :]))
        right.append(jnp.where(low, own[at, :], after))
        strip[x, 0] = left[x]
        strip[x, 1] = right[x]
    halo[...] = halo_columns(left, right).reshape(halo.shape)
    strip_costs(own, from_left, from_right, edge_costs, width_x, depth)
    outside = outside_strips(place, tile)

    def keep(x, z, level, w, passed):
        levels[x, z] = level
        vertical = w[3] if z == 0 else w[3] + w[4]
        sideways = row(anisotropy, near + z, x, tile) * (w[1] + w[2])
        sides[x, z] = sideways + row(anisotropy, 2 * near + z, x, tile) * vertical

    def step(x, carry):
        state, strips = sweep_step(x, near, field, strip, costs, edge_costs, halo, *carry, keep, None)
        for z in range(depth):
            local[x, z] = state[z]
        for side in range(2):
            local_strip[x, side] = jnp.where(outside[side], BIG, strips[side])
        return state, strips

    blank = jnp.full(tile, BIG, jnp.float32)
    state, strips = by_steps(width_x, step, ([blank] * depth, [blank] * 2))
    reach_strip = packed(*[jnp.where(o, BIG, s) for o, s in zip(outside, strips)])

    edges = [[local_strip[x, side] for x in range(width_x)] for side in range(2)]
    halo[...] = halo_columns(*edges).reshape(halo.shape)

    def again(lap, carry):
        x = width_x - 1 - lap
        return sweep_step(x, 0, local, local_strip, costs, edge_costs, halo, *carry, None, None)

    back, back_strips = by_steps(width_x, again, ([blank] * depth, [blank] * 2))
    tiles = passages(costs, own, from_left, from_right, depth)
    strip_total, strip_paths = strip_passages(edge_costs, width_x)

    back_strip = packed(*back_strips)
    reach_strip = jnp.where(sub == 0, shifted_down(back_strip, 3), reach_strip)
    reach_strip = jnp.where(sub == 1, shifted_down(back_strip, 5), reach_strip)
    shared = shared_rows(strip_total, strip_paths)
    count = message.shape[0]
    per = message.shape[1] // 3 - 1
    for p in range(count):
        first = min(p * per, depth - per)
        for k in range(per + 2):
            z = first + k - 1
            message[p, k] = state[z] if 0 <= z < depth else blank
        for k in range(per):
            message[p, per + 2 + k] = back[first + k]
            value = tiles[first + k]
            if k == 0 and first > 0:
                value = jnp.where(sub == 6, jnp.broadcast_to(tiles[first - 1][:1], tile), value)
            if k == 0 and first + per < depth:
                value = jnp.where(sub == 7, jnp.broadcast_to(tiles[first + per][:1], tile), value)
            if per > 1 and k == 1:
                value = jnp.where(sub < 6, value, shared)
            message[p, 2 * per + 2 + k] = value
        message[p, 3 * per + 2] = reach_strip
        message[p, 3 * per + 3] = records
        if per == 1:
            message[p, 3 * per + 4] = shared


def blocks_kernel(per, depth, place, received, entering, entering_strips, halo):
    count = received.shape[0]
    tile = entering.shape[2:]
    lane = iota(tile, 1)
    width_y = tile[1]
    me = place[6]
    blank = jnp.full(tile, BIG, jnp.float32)
    side = 3 * per + 2

    def rows(device, k, j):
        return jnp.broadcast_to(received[device, 2 * per + 2 + k, j : j + 1, :], tile)

    def total(device, k):
        if k < 0:
            return rows(device, 0, 6)
        return rows(device, k, 0) if k < per else rows(device, 0, 7)

    shared = [received[d, 2 * per + 3] if per > 1 else received[d, 3 * per + 4] for d in range(count)]
    shared = spread_rows(shared)
    state = [blank] * (per + 2)
    strip = blank
    first, first_strip = [], []
    for device in range(count):
        first.append(state)
        first_strip.append(strip)
        state = [
            soft_pair(received[device, k], state[k] + total(device, k - 1)) for k in range(per + 2)
        ]
        strip = soft_pair(received[device, side], strip + shared[device][0])
    own = blank
    for device in range(count):
        own = jnp.where(device == me, first_strip[device], own)
        for k in range(per):
            entering[device, k] = first[device][k + 1]
    entering_strips[0] = own
    group = width_y // 8
    for at in range(0, count, group):
        some = first_strip[at : at + group]
        some = some + [blank] * (group - len(some))
        turned = halo_columns(some, [shifted_down(s, 2) for s in some])
        halo[at // group] = turned.reshape(halo.shape[1:])
    low = jnp.minimum(me * per, depth - per)
    edges = [[halo[i, low + k] for k in range(per)] for i in range(halo.shape[0])]
    state = [blank] * per
    strip = blank
    for device in reversed(range(count)):
        for k in range(per):
            entering[device, per + k] = state[k]
            u = first[device][k + 1]
            turn = (width_y - 5 - 8 * (device % group)) % width_y
            edge = pltpu.roll(edges[device // group][k], turn, 1)
            values = [received[device, per + 2 + k], u + rows(device, k, 1)]
            values.append(jnp.where(lane == 0, edge, pltpu.roll(u, 1, 1)) + rows(device, k, 2))
            values.append(jnp.where(lane == width_y - 1, edge, pltpu.roll(u, width_y - 1, 1)) + rows(device, k, 3))
            values.append(first[device][k] + rows(device, k, 4))
            values.append(first[device][k + 2] + rows(device, k, 5))
            state[k] = soft_pair(softmin(values)[0], state[k] + total(device, k))
        u = first_strip[device]
        back = received[device, side]
        back = jnp.where(iota(tile, 0) == 3, pltpu.roll(back, 3, 0), pltpu.roll(back, 5, 0))
        paths = shared[device][1]
        values = [back, u + paths[0], pltpu.roll(u, 1, 0) + paths[1], shifted_down(u, 1) + paths[2]]
        values.append(jnp.where(lane < 8, BIG, pltpu.roll(u, 8, 1)) + paths[3])
        values.append(jnp.where(lane >= width_y - 8, BIG, pltpu.roll(u, width_y - 8, 1)) + paths[4])
        passed = soft_pair(softmin(values)[0], strip + shared[device][0])
        strip = jnp.where(device > me, passed, strip)
    entering_strips[1] = strip


def second_sweep_kernel(
    place, first, first_strip, entering, entering_strips, costs, edge_costs, anisotropy, levels_one, sides,
    sums, counts, sums_strip, counts_strip,
    local, shares, slopes, keeps, misfits, edges_own, edges_factor, slopes_one, gains, message,
    field, strip, halo, shares_strip, slopes_strip, keeps_strip, misfits_strip,
):
    width_x, depth, quakes, width_y = first.shape
    tile = (quakes, width_y)
    near = levels_one.shape[1]
    per = entering.shape[1] // 2
    outside = outside_strips(place, tile)
    strips_in = [[s, shifted_down(s, 2)] for s in (entering_strips[0], entering_strips[1])]
    carried = [[entering[z // per, k * per + z % per] for z in range(depth)] for k in range(2)]

    def finish(x, carry):
        running, strip_running, prior = carry
        sums_now, values = [], []
        for z in range(depth):
            cost = row(costs, z, x, tile)
            sums_now.append(running[z] + cost)
            value = soft_pair(first[x, z], entering[z // per, z % per] + sums_now[z])
            field[x, z] = value
            if z < near:
                values.append(value)
                keep, slope = split_pair(levels_one[x, z], prior[z] + cost)
                slopes_one[x, z] = slope
                gains[x, z] = slope * row(anisotropy, z, x, tile) + keep * sides[x, z]
        strip_sums = []
        for side in range(2):
            strip_sums.append(strip_running[side] + edge_costs[3 * side, x])
            value = soft_pair(first_strip[x, side], strips_in[0][side] + strip_sums[side])
            strip[x, side] = jnp.where(outside[side], BIG, value)
        return sums_now, strip_sums, values

    blank = jnp.zeros(tile, jnp.float32)
    by_steps(width_x, finish, ([blank] * depth, [blank] * 2, carried[0][:near]))
    edges = [[strip[x, side] for x in range(width_x)] for side in range(2)]
    halo[...] = halo_columns(*edges).reshape(halo.shape)

    def keep(x, z, level, w, passed):
        for i in range(4):
            shares[i, x] = w[i]
        keeps[x], slopes[x] = split_pair(level, passed)

    def keep_strip(x, level, w, passed, value):
        shares_strip[x] = w
        keeps_strip[x], slopes_strip[x] = split_pair(level, passed)
        tally = pltpu.roll(counts_strip[...], lax.rem(width_y - 8 * x, width_y), 1)
        total = pltpu.roll(sums_strip[...], lax.rem(width_y - 8 * x, width_y), 1)
        misfits_strip[x] = ADJ_SCALE * (tally * (value * (1.0 / RATE)) - total)

    def step(lap, carry):
        x = width_x - 1 - lap
        state, strips = sweep_step(x, 1, field, strip, costs, edge_costs, halo, *carry, keep, keep_strip)
        for z in range(depth):
            local[x, z] = state[z]
        misfits[x] = ADJ_SCALE * (counts[x] * (state[0] * (1.0 / RATE)) - sums[x])
        return state, strips

    by_steps(width_x, step, (carried[1], strips_in[1]))
    zero, unit = jnp.zeros(tile, jnp.float32), jnp.ones(tile, jnp.float32)
    lane = iota(tile, 1)
    own, factor, strip_own, strip_factor = zero, unit, zero, unit
    owns, factors = [], []
    sent = [zero, zero]
    for x in range(width_x):
        own = misfits[x] + own
        owns.append(keeps[x] * own)
        factors.append(keeps[x] * factor)
        own, factor = slopes[x] * own, slopes[x] * factor
        strip_own = misfits_strip[x] + strip_own
        through = keeps_strip[x] * shares_strip[x]
        for i, value in enumerate((strip_own, strip_factor)):
            value = pltpu.roll(through * value, 8 * x, 1) if x else through * value
            sent[i] = jnp.where((lane >> 3) == x, value, sent[i])
        strip_own, strip_factor = slopes_strip[x] * strip_own, slopes_strip[x] * strip_factor
    edges_own[...] = end_columns(sent[0]).reshape(edges_own.shape)
    edges_factor[...] = end_columns(sent[1]).reshape(edges_factor.shape)
    chain = [unit] * near
    blocks = [zero] * near
    links = [zero] * 4
    for x in range(width_x):
        entry = entries_of(owns[x], shares, x, edges_own[x])
        for z in range(near):
            chain[z] = chain[z] * slopes_one[x, z]
            blocks[z] = blocks[z] + chain[z] * entry[z]
        for i, path in enumerate(ways_of(factors[x], shares, x, edges_factor[x])):
            links[i] = links[i] + chain[i // 3] * path
    both = jnp.where(iota(tile, 0) < 5, strip_own, pltpu.roll(strip_factor, 2, 0))
    tiles = [own, factor, both] + blocks + chain + links
    for p in range(message.shape[0]):
        for i, value in enumerate(tiles):
            message[p, i] = value


def end_columns(rows):
    wide = rows.shape[1]
    first, last = shifted_down(rows, 3), pltpu.roll(rows, 3, 0)
    return jnp.transpose(jnp.concatenate([first] * (wide // 16) + [last] * (wide // 16), 0))


def ways_of(passed, shares, x, edge):
    lane = iota(passed.shape, 1)
    last = passed.shape[1] - 1
    above = jnp.where(lane == last, edge, pltpu.roll(passed * shares[1, x], last, 1))
    below = jnp.where(lane == 0, edge, pltpu.roll(passed * shares[2, x], 1, 1))
    return passed * shares[0, x], above, below, passed * shares[3, x]


def entries_of(passed, shares, x, edge):
    own, above, below, deeper = ways_of(passed, shares, x, edge)
    return own + above + below, deeper


def records_kernel(rows_of, tile_of, place, cell, received, sums, counts, sums_strip, counts_strip):
    width_x, quakes, width_y = sums.shape
    last = tile_of
    span_y = place[2]
    lane = iota((quakes, width_y), 1)
    column = iota((width_y, width_y), 0)
    strip_column = iota((8, width_y), 0)
    strip_column = jnp.where(strip_column == 3, -1, jnp.where(strip_column == 4, width_y, -2))
    share = width_y // rows_of
    dims = (((1,), (1,)), ((), ()))
    one_x = iota((width_x, width_y), 0)
    parts = [[], [], [], []]
    at, at_strip = [], []
    for chunk in range(cell.shape[0]):
        records = jnp.zeros((quakes, width_y), jnp.float32)
        for part in range(share):
            piece = received[chunk * share + part, last]
            moved = pltpu.roll(piece, part * rows_of, 1) if part else piece
            records = jnp.where(lane // rows_of == part, moved, records)
        cells = cell[chunk : chunk + 1, :]
        station_x = lax.shift_right_logical(cells, place[7]) - place[0]
        station_y = (cells & (span_y - 1)) - place[1]
        at_x = (one_x == jnp.broadcast_to(station_x, one_x.shape)).astype(jnp.float32)
        pieces = [p.astype(jnp.float32) for p in exact_parts(records)] + [jnp.ones((quakes, width_y), jnp.float32)]
        for out, piece in zip(parts, pieces):
            spread = [piece * jnp.broadcast_to(at_x[x : x + 1], piece.shape) for x in range(width_x)]
            out.append(jnp.concatenate(spread, 0).astype(jnp.bfloat16))
        hit = column == jnp.broadcast_to(station_y, column.shape)
        at.append(hit.astype(jnp.float32).astype(jnp.bfloat16))
        hit = strip_column == jnp.broadcast_to(station_y, strip_column.shape)
        at_strip.append(hit.astype(jnp.float32).astype(jnp.bfloat16))
    at = jnp.concatenate(at, 1)
    at_strip = jnp.concatenate(at_strip, 1)
    parts = [jnp.concatenate(p, 1) for p in parts]
    main = [lax.dot_general(p, at, dims, preferred_element_type=jnp.float32) for p in parts]
    side = [lax.dot_general(at_strip, p, dims, preferred_element_type=jnp.float32) for p in parts]
    sums[...] = (main[0] + main[1] + main[2]).reshape(sums.shape)
    counts[...] = main[3].reshape(counts.shape)
    sums_strip[...] = side[0] + side[1] + side[2]
    counts_strip[...] = side[3]


def times_kernel(local, times):
    width_x, depth, quakes, _ = local.shape

    def step(x, carry):
        for z in range(depth):
            times[pl.ds(z * width_x + x, quakes, stride=depth * width_x), :] = local[x, z] * (1.0 / RATE)
        return carry

    by_steps(width_x, step, 0)


def kernel_kernel(
    place, received, shares, slopes, keeps, misfits, edges_own, edges_factor, slopes_one, gains, anisotropy, kernel,
    entries, top, sent,
):
    width_x, quakes, width_y = slopes.shape
    tile = (quakes, width_y)
    near = slopes_one.shape[1]
    count = received.shape[0]
    lane = iota(tile, 1)
    last = width_y - 1
    me = place[6]
    zero = jnp.zeros(tile, jnp.float32)
    group = width_y // 8
    state, strip, mine, mine_strip = zero, zero, zero, zero
    carries = []
    for device in range(count):
        carries.append(state)
        mine = jnp.where(device == me, state, mine)
        at = device % group
        moved = pltpu.roll(strip, 8 * at, 1) if at else strip
        sent[device // group] = moved if at == 0 else jnp.where((lane >> 3) == at, moved, sent[device // group])
        both = received[device, 2]
        state = received[device, 0] + received[device, 1] * state
        strip = both + shifted_down(both, 2) * strip
    ends = [end_columns(sent[i]) for i in range(sent.shape[0])]
    state = [zero] * near
    mine_edge = zero
    for device in reversed(range(count)):
        at = 8 * (device % group)
        edge = ends[device // group][at : at + 8]
        mine_edge = jnp.where(device == me, edge, mine_edge)
        carry = carries[device]
        block = [received[device, 3 + z] for z in range(near)]
        above = jnp.where(lane == last, edge, pltpu.roll(carry, last, 1))
        below = jnp.where(lane == 0, edge, pltpu.roll(carry, 1, 1))
        link = [received[device, 3 + 2 * near + i] for i in range(4)]
        block[0] = block[0] + link[0] * carry + link[1] * above + link[2] * below
        block[1] = block[1] + link[3] * carry
        for z in range(near):
            passed = block[z] + received[device, 3 + near + z] * state[z]
            state[z] = jnp.where(device > me, passed, state[z])
    carry = mine
    for x in range(width_x):
        total = misfits[x] + carry
        carry = slopes[x] * total
        passed = keeps[x] * total
        sideways = row(anisotropy, near, x, tile) * (shares[1, x] + shares[2, x])
        sideways = sideways + row(anisotropy, 2 * near, x, tile) * shares[3, x]
        terms = carry * row(anisotropy, 0, x, tile) + passed * sideways
        top[x : x + 1, :] = jnp.sum(terms, axis=0, keepdims=True)
        entry = entries_of(passed, shares, x, edges_own[x] + edges_factor[x] * mine_edge)
        for z in range(near):
            entries[x, z] = entry[z]
    for x in reversed(range(width_x)):
        for z in range(near):
            total = entries[x, z] + state[z]
            state[z] = slopes_one[x, z] * total
            value = jnp.sum(total * gains[x, z], axis=0, keepdims=True)
            if z == 0:
                value = value + top[x : x + 1, :]
            kernel[z, x : x + 1, :] = value
    for z in range(near, kernel.shape[0]):
        kernel[z] = jnp.zeros(kernel.shape[1:], jnp.float32)


def call(kernel, shapes, operands, scratch=(), scalars=0, far=0, last=False, aliases=()):
    many = isinstance(shapes, list)
    shapes = shapes if many else [shapes]
    out = [jax.ShapeDtypeStruct(s, jnp.float32) if last else pltpu.VMEM(s, jnp.float32) for s in shapes]
    result = pl.pallas_call(
        kernel,
        out_shape=out,
        in_specs=[SMEM] * scalars + [FAR] * far + [VMEM] * (len(operands) - scalars - far),
        out_specs=[VMEM] * len(out),
        scratch_shapes=[pltpu.VMEM(s, jnp.float32) if isinstance(s, tuple) else s for s in scratch],
        compiler_params=PARAMS,
        input_output_aliases=dict(aliases),
    )(*operands)
    return result if many else result[0]


def traded(message):
    return lax.all_to_all(message, "gx", 0, 0, tiled=True)


def rotated(value, axis, by):
    count = lax.axis_size(axis)
    return lax.ppermute(value, axis, [(i, (i + by) % count) for i in range(count)])


def body(warm_start, slowness, anisotropy, observed, station_cell, source_cell):
    quakes, depth, width_x, width_y = warm_start.shape
    count_x, count_y = lax.axis_size("gx"), lax.axis_size("gy")
    index_x, index_y = lax.axis_index("gx"), lax.axis_index("gy")
    span_x, span_y = width_x * count_x, width_y * count_y
    near = 2
    per = max(1, depth // count_x)
    tile = (quakes, width_y)
    top = (width_x,) + tile
    close = (width_x, near) + tile
    field = (width_x, depth) + tile
    place = jnp.stack(
        [
            index_x * width_x,
            index_y * width_y,
            jnp.int32(span_y),
            jnp.int32(span_x * span_y),
            (index_y == 0).astype(jnp.int32),
            (index_y == count_y - 1).astype(jnp.int32),
            index_x,
            jnp.int32(span_y.bit_length() - 1),
            index_y,
        ]
    ).astype(jnp.int32)
    anis = anisotropy.reshape(3 * depth, width_x, width_y)
    local_records = observed.shape[1]
    flat = (quakes * depth * width_x, width_y)

    base = width_x * 11
    sources = [warm_start.reshape(flat), observed, slowness, anis]
    sources = [pltpu.with_memory_space_constraint(a, pltpu.HBM) for a in sources]
    start, costs, anis, edge, records = call(
        pack_kernel,
        [field, anis.shape, (3 * near, width_x, width_y), (base + quakes, width_y), tile],
        [place, source_cell] + sources,
        [sources[i].shape for i in range(4)] + [pltpu.SemaphoreType.DMA((7,))],
        scalars=2,
        far=4,
    )
    from_left = rotated(edge, "gy", 1)
    from_right = rotated(edge, "gy", -1)
    others = [rotated(records, "gy", by) for by in range(2, count_y - 1)]

    message_shape = (count_x, 3 * per + (4 if per > 1 else 5)) + tile
    first, first_strip, edge_costs, levels_one, sides, message = call(
        functools.partial(first_sweep_kernel, local_records, count_y),
        [field, (width_x, 2) + tile, (6,) + top, close, close, message_shape],
        [place, start, edge, from_left, from_right, costs, anis] + others,
        [(depth,) + tile, (width_x, 2) + tile],
        scalars=1,
    )
    reach = traded(message)
    group = width_y // 8
    entering, entering_strips = call(
        functools.partial(blocks_kernel, per, depth),
        [(count_x, 2 * per) + tile, (2,) + tile],
        [place, reach],
        [(-(-count_x // group), depth) + tile],
        scalars=1,
    )
    entering = traded(entering)
    recorded = call(
        functools.partial(records_kernel, local_records * count_y, 3 * per + 3),
        [top, top, tile, tile],
        [place, station_cell.reshape(-1, width_y), reach],
        scalars=1,
    )
    second, *rest, message = call(
        second_sweep_kernel,
        [field, (4,) + top] + [top] * 5 + [close, close, (count_x, 7 + 2 * near) + tile],
        [place, first, first_strip, entering, entering_strips, costs, edge_costs, anis, levels_one, sides]
        + list(recorded),
        [field, (width_x, 2) + tile, (depth,) + tile] + [top] * 4,
        scalars=1,
        aliases={1: 0},
    )
    received = traded(message)
    times = call(times_kernel, flat, [second], last=True)
    kernel = call(
        kernel_kernel,
        (depth, width_x, width_y),
        [place, received] + rest + [anis],
        [close, (width_x, width_y), (-(-count_x // group),) + tile],
        scalars=1,
        last=True,
    )
    return (times.reshape(warm_start.shape), kernel)


def solution(mesh):
    return jax.shard_map(
        body,
        mesh=mesh,
        in_specs=(
            P(None, None, "gx", "gy"),
            P(None, "gx", "gy"),
            P(None, None, "gx", "gy"),
            P(None, ("gx", "gy")),
            P(),
            P(),
        ),
        out_specs=(P(None, None, "gx", "gy"), P(None, "gx", "gy")),
        check_vma=False,
    )
```

```python
import functools
import math

import jax
import jax.numpy as jnp
from jax import lax
from jax.experimental import pallas as pl
from jax.experimental.pallas import tpu as pltpu
from jax.sharding import PartitionSpec as P

TAU = 0.05
ADJ_SCALE = 0.1
LOG2E = math.log2(math.e)
RATE = LOG2E / TAU
BIG = 10000.0 * RATE
UNROLL = 4
CHUNKS = 4
VMEM = pl.BlockSpec(memory_space=pltpu.VMEM)
FAR = pl.BlockSpec(memory_space=pl.ANY)
SMEM = pl.BlockSpec(memory_space=pltpu.SMEM)
PARAMS = pltpu.CompilerParams(vmem_limit_bytes=8 * 1024 * 1024)


def softmin(values):
    least = functools.reduce(jnp.minimum, values)
    parts = [jnp.exp2(least - v) for v in values]
    return least, parts, functools.reduce(jnp.add, parts)


def soft_pair(first, second):
    return jnp.minimum(first, second) - LOG2E * jnp.log(1.0 + jnp.exp2(-jnp.abs(first - second)))


def add_pair(least, total, passed):
    low = jnp.minimum(least, passed)
    return low - LOG2E * jnp.log(total * jnp.exp2(low - least) + jnp.exp2(low - passed))


def join_pairs(first, second):
    low = jnp.minimum(first[0], second[0])
    return low, first[1] * jnp.exp2(low - first[0]) + second[1] * jnp.exp2(low - second[0])


def value_of(pair):
    return pair[0] - LOG2E * jnp.log(pair[1])


def split_pair(first, second):
    gap = jnp.exp2(-jnp.abs(first - second))
    share = 1.0 / (1.0 + gap)
    less = gap * share
    nearer = first <= second
    return jnp.where(nearer, share, less), jnp.where(nearer, less, share)


def iota(shape, axis):
    return lax.broadcasted_iota(jnp.int32, shape, axis)


def row(ref, index, x, like):
    return jnp.broadcast_to(ref[index, pl.ds(x, 1), :], like)


def row_of(ref, x, like):
    return jnp.broadcast_to(ref[pl.ds(x, 1), :], like)


def by_steps(count, step, carry):
    def group(i, carry):
        for j in range(UNROLL):
            carry = step(i * UNROLL + j, carry)
        return carry

    return lax.fori_loop(0, count // UNROLL, group, carry)


def packed(left, right):
    return jnp.where(iota(left.shape, 0) < 5, left, pltpu.roll(right, 2, 0))


def merged(left, right):
    return jnp.where(iota(left.shape, 0) < 4, left, right)


def shifted_down(tile, by):
    return pltpu.roll(tile, tile.shape[0] - by, 0)


def exact_parts(value):
    high = value.astype(jnp.bfloat16).astype(jnp.float32)
    middle = (value - high).astype(jnp.bfloat16).astype(jnp.float32)
    low = value - high - middle
    return [p.astype(jnp.bfloat16) for p in (high, middle, low)]


def pack_kernel(
    place, source_far, warm_far, observed_far, slowness_far, anisotropy_far, start, costs, near, edge, records,
    source, warm, observed, slowness, anisotropy, arrived,
):
    pairs = [(slowness_far, slowness), (anisotropy_far, anisotropy), (observed_far, observed)]
    share = start.shape[1] // CHUNKS
    span = share * start.shape[0]
    pairs += [(warm_far.at[:, pl.ds(i * span, span)], warm.at[i]) for i in range(CHUNKS)]
    pairs += [(source_far, source)]
    copies = [pltpu.make_async_copy(a, b, arrived.at[i]) for i, (a, b) in enumerate(pairs)]
    for copy in copies:
        copy.start()
    width_x, depth, quakes, width_y = start.shape
    tile = (quakes, width_y)
    quake = iota(tile, 0)
    lane = iota(tile, 1)
    span_y = place[2]
    plane = place[3]
    rows = width_x * 8
    wide = (width_x, width_y)
    group = iota(wide, 1) >> 3
    copies[0].wait()
    copies[1].wait()
    for k in range(3):
        columns = jnp.zeros(wide, jnp.float32)
        for z in range(depth):
            cost = slowness[z] * anisotropy[k * depth + z] * RATE
            costs[k * depth + z] = cost
            columns = jnp.where(group == z, pltpu.roll(cost, 8 * z + 4, 1), columns)
        edge[rows : rows + width_x, :] = columns
        rows += width_x
        for z in range(near.shape[0] // 3):
            near[k * (near.shape[0] // 3) + z] = anisotropy[k * depth + z]
    copies[-1].wait()
    cell = jnp.zeros(tile, jnp.int32)
    for e in range(quakes):
        cell = jnp.where(quake == e, source[e], cell)
    cell = cell - (lane + place[0] * span_y + place[1])
    edges = []
    for i in range(CHUNKS):
        copies[3 + i].wait()
        here = warm.at[i].reshape(quakes * share * width_x, width_y)

        def one(x, chunk, i=i, here=here):
            mine = (lane >> 3) == x
            out = []
            for k in range(share):
                value = here[pl.ds(k * width_x + x, quakes, stride=share * width_x), :] * RATE
                value = jnp.where(cell == (i * share + k) * plane + x * span_y, 0.0, value)
                start[x, i * share + k] = value
                out.append(jnp.where(mine, pltpu.roll(value, 8 * x + 4, 1), chunk[k]))
            return out

        edges += by_steps(width_x, one, [jnp.zeros(tile, jnp.float32)] * share)
    edge[: width_x * 8, :] = jnp.transpose(jnp.concatenate(edges, 0))
    copies[2].wait()
    records[...] = jnp.zeros(tile, jnp.float32)
    records[:, : observed.shape[1]] = observed[...]
    edge[rows:, :] = records[...]


def halo_columns(left, right):
    rows = []
    for l, r in zip(left, right):
        rows.append(jnp.where(iota(l.shape, 0) == 4, r, pltpu.roll(l, 2, 0)))
    return jnp.transpose(jnp.concatenate(rows, 0))


def strip_costs(own, from_left, from_right, out, width_x, depth):
    tile = own.shape[1]
    base = width_x * 8
    lane = iota((8, tile), 1)
    low = (lane & 7) < 4
    mine = (lane & 7) == iota((8, tile), 0)
    spread = ((iota((tile, tile), 0) >> 3) == (iota((tile, tile), 1) >> 3)).astype(jnp.float32)
    spread = spread.astype(jnp.bfloat16)
    for side in range(2):
        for k in range(3):
            rows = []
            for x in range(width_x):
                at = slice(base + k * width_x + x, base + k * width_x + x + 1)
                here = jnp.broadcast_to(own[at, :], lane.shape)
                there = jnp.broadcast_to((from_right if side else from_left)[at, :], lane.shape)
                value = jnp.where(low, here, there) if side else jnp.where(low, there, here)
                rows.append(jnp.where(mine, value, 0.0))
            whole = jnp.concatenate(rows, 0)
            total = 0.0
            for part in reversed(exact_parts(whole)):
                total = total + lax.dot_general(
                    part, spread, (((1,), (0,)), ((), ())), preferred_element_type=jnp.float32
                )
            out[3 * side + k] = total.reshape(width_x, 8, tile)


def running_sum(value):
    rows = iota(value.shape, 0)
    by = 1
    while by < value.shape[0]:
        value = value + jnp.where(rows >= by, pltpu.roll(value, by, 0), 0.0)
        by *= 2
    return value


def log_sum(exponents):
    return -LOG2E * jnp.log(functools.reduce(jnp.add, [jnp.exp2(-e) for e in exponents]))


def passages(costs, own, from_left, from_right, depth):
    width_x, width_y = costs.shape[1:]
    base = 8 * width_x
    at = slice(base, base + width_x)
    lane = iota((width_x, width_y), 1)
    beside = jnp.where((lane & 7) == 4, running_sum(from_right[at, :]), pltpu.roll(running_sum(from_left[at, :]), 2, 1))
    sums = [running_sum(costs[z]) for z in range(depth)]
    sub = iota((8, width_y), 0)
    tiles = []
    for z in range(depth):
        back = sums[z] - costs[z]
        edge = pltpu.roll(beside, width_y - 5 - 8 * z, 1)
        below = jnp.where(lane == 0, edge, pltpu.roll(sums[z], 1, 1))
        above = jnp.where(lane == width_y - 1, edge, pltpu.roll(sums[z], width_y - 1, 1))
        step_y = back + costs[depth + z]
        step_z = back + costs[2 * depth + z]
        paths = [sums[z] + back, below + step_y, above + step_y]
        paths.append(sums[z - 1] + step_z if z > 0 else None)
        paths.append(sums[z + 1] + step_z if z < depth - 1 else None)
        tile = jnp.broadcast_to(sums[z][width_x - 1 :, :], sub.shape)
        for j, path in enumerate(paths):
            if path is None:
                tile = jnp.where(sub == j + 1, BIG, tile)
            else:
                total = jnp.sum(jnp.exp2(-path), axis=0, keepdims=True)
                tile = jnp.where(sub == j + 1, -LOG2E * jnp.log(total), tile)
        tiles.append(tile)
    return tiles


def strip_passages(edge_costs, width_x):
    shape = edge_costs.shape[2:]
    lane = iota(shape, 1)
    sums = jnp.zeros(shape, jnp.float32)
    totals = [jnp.zeros(shape, jnp.float32)] * 5
    for x in range(width_x):
        cost, step_y, step_z = [packed(edge_costs[k, x], edge_costs[3 + k, x]) for k in range(3)]
        back = sums
        sums = sums + cost
        step_y, step_z = step_y + back, step_z + back
        paths = [sums + back, pltpu.roll(sums, 1, 0) + step_y, shifted_down(sums, 1) + step_y]
        paths.append(jnp.where(lane < 8, BIG, pltpu.roll(sums, 8, 1) + step_z))
        paths.append(jnp.where(lane >= shape[1] - 8, BIG, pltpu.roll(sums, shape[1] - 8, 1) + step_z))
        totals = [t + jnp.exp2(-p) for t, p in zip(totals, paths)]
    return sums, [-LOG2E * jnp.log(jnp.maximum(t, 1e-37)) for t in totals]


def shared_rows(total, paths):
    place = iota(total.shape, 1) & 7
    first, second = total, total
    for q in range(6):
        value = pltpu.roll(total, (4 - q) % 8, 0)
        first = jnp.where(place == q, value, first)
    for q, (path, at) in enumerate([(p, r) for p in paths for r in (3, 6)]):
        if q < 2:
            first = jnp.where(place == 6 + q, pltpu.roll(path, (6 - at) % 8, 0), first)
        else:
            second = jnp.where(place == q - 2, pltpu.roll(path, (7 - at) % 8, 0), second)
    return jnp.where(iota(total.shape, 0) == 6, first, second)


def spread_rows(tiles):
    shape = tiles[0].shape
    wide = shape[1]
    sub = iota(shape, 0)
    mine = (iota(shape, 1) & 7) == sub
    spread = ((iota((wide, wide), 0) >> 3) == (iota((wide, wide), 1) >> 3)).astype(jnp.float32)
    spread = spread.astype(jnp.bfloat16)
    rows = [jnp.where(mine, jnp.broadcast_to(t[r : r + 1], shape), 0.0) for t in tiles for r in (6, 7)]
    whole = jnp.concatenate(rows, 0)
    value = 0.0
    for part in reversed(exact_parts(whole)):
        value = value + lax.dot_general(part, spread, (((1,), (0,)), ((), ())), preferred_element_type=jnp.float32)
    out = []
    for i in range(len(tiles)):
        first, second = value[16 * i : 16 * i + 8], value[16 * i + 8 : 16 * i + 16]
        paths = [jnp.where(sub == 3, pltpu.roll(first, 5, 0), pltpu.roll(first, 7, 0))]
        for q in range(4):
            at_three = pltpu.roll(second, (3 - 2 * q) % 8, 0)
            at_six = pltpu.roll(second, (6 - 2 * q - 1) % 8, 0)
            paths.append(jnp.where(sub == 3, at_three, at_six))
        out.append((pltpu.roll(first, 2, 0), paths))
    return out


def sweep_step(x, near, field, strip, costs, edge_costs, halo, state, strip_state, keep, keep_strip):
    depth = field.shape[1]
    tile = field.shape[2:]
    width_y = tile[1]
    lane = iota(tile, 1)
    out = []
    for z in range(depth):
        u = field[x, z]
        cost_y = row(costs, depth + z, x, tile)
        cost_z = row(costs, 2 * depth + z, x, tile)
        edge = pltpu.roll(halo[z], width_y - 5 - 8 * x, 1)
        values = [u]
        values.append(jnp.where(lane == 0, edge, pltpu.roll(u, 1, 1)) + cost_y)
        values.append(jnp.where(lane == width_y - 1, edge, pltpu.roll(u, width_y - 1, 1)) + cost_y)
        if z > 0:
            values.append(field[x, z - 1] + cost_z)
        if z < depth - 1:
            values.append(field[x, z + 1] + cost_z)
        least, parts, total = softmin(values)
        passed = state[z] + row(costs, z, x, tile)
        if z < near:
            scale = 1.0 / total
            keep(x, z, value_of((least, total)), [p * scale for p in parts], passed)
        out.append(add_pair(least, total, passed))
    strips, levels, weights, passes = [], [], [], []
    for side in range(2):
        u = strip[x, side]
        cost_y = edge_costs[3 * side + 1, x]
        cost_z = edge_costs[3 * side + 2, x]
        values = [u, pltpu.roll(u, 1, 0) + cost_y, pltpu.roll(u, 7, 0) + cost_y]
        values.append(jnp.where(lane < 8, BIG, pltpu.roll(u, 8, 1)) + cost_z)
        values.append(jnp.where(lane >= width_y - 8, BIG, pltpu.roll(u, width_y - 8, 1)) + cost_z)
        least, parts, total = softmin(values)
        passes.append(strip_state[side] + edge_costs[3 * side, x])
        strips.append(add_pair(least, total, passes[side]))
        if keep_strip is not None:
            levels.append(value_of((least, total)))
            weights.append(parts[2 - side] / total)
    if keep_strip is not None:
        keep_strip(x, merged(*levels), merged(*weights), merged(*passes), merged(*strips))
    return out, strips


def outside_strips(place, shape):
    sub = iota(shape, 0)
    return [(place[4] == 1) & (sub < 4), (place[5] == 1) & (sub >= 4)]


def first_sweep_kernel(
    rows_of, count_y, place, field, own, from_left, from_right, costs, anisotropy, *rest
):
    others = rest[: count_y - 3]
    local, local_strip, edge_costs, levels, sides, message, halo, strip = rest[count_y - 3 :]
    width_x, depth, quakes, width_y = field.shape
    tile = (quakes, width_y)
    sub = iota(tile, 0)
    low = sub < 4
    near = levels.shape[1]
    last = 11 * width_x
    far = [own[last:, :], from_left[last:, :]] + [o[...] for o in others] + [from_right[last:, :]]
    records = jnp.zeros(tile, jnp.float32)
    for by, piece in enumerate(far):
        owner = lax.rem(place[8] + count_y - by, count_y)
        records = records + pltpu.roll(piece, owner * rows_of, 1)
    left, right = [], []
    for x in range(width_x):
        at = slice(8 * x, 8 * x + 8)
        before = jnp.where(place[4] == 1, BIG, from_left[at, :])
        after = jnp.where(place[5] == 1, BIG, from_right[at, :])
        left.append(jnp.where(low, before, own[at, :]))
        right.append(jnp.where(low, own[at, :], after))
        strip[x, 0] = left[x]
        strip[x, 1] = right[x]
    halo[...] = halo_columns(left, right).reshape(halo.shape)
    strip_costs(own, from_left, from_right, edge_costs, width_x, depth)
    outside = outside_strips(place, tile)

    def keep(x, z, level, w, passed):
        levels[x, z] = level
        vertical = w[3] if z == 0 else w[3] + w[4]
        sideways = row(anisotropy, near + z, x, tile) * (w[1] + w[2])
        sides[x, z] = sideways + row(anisotropy, 2 * near + z, x, tile) * vertical

    def step(x, carry):
        state, strips = sweep_step(x, near, field, strip, costs, edge_costs, halo, *carry, keep, None)
        for z in range(depth):
            local[x, z] = state[z]
        for side in range(2):
            local_strip[x, side] = jnp.where(outside[side], BIG, strips[side])
        return state, strips

    blank = jnp.full(tile, BIG, jnp.float32)
    state, strips = by_steps(width_x, step, ([blank] * depth, [blank] * 2))
    reach_strip = packed(*[jnp.where(o, BIG, s) for o, s in zip(outside, strips)])

    edges = [[local_strip[x, side] for x in range(width_x)] for side in range(2)]
    halo[...] = halo_columns(*edges).reshape(halo.shape)

    def again(lap, carry):
        x = width_x - 1 - lap
        return sweep_step(x, 0, local, local_strip, costs, edge_costs, halo, *carry, None, None)

    back, back_strips = by_steps(width_x, again, ([blank] * depth, [blank] * 2))
    tiles = passages(costs, own, from_left, from_right, depth)
    strip_total, strip_paths = strip_passages(edge_costs, width_x)

    back_strip = packed(*back_strips)
    reach_strip = jnp.where(sub == 0, shifted_down(back_strip, 3), reach_strip)
    reach_strip = jnp.where(sub == 1, shifted_down(back_strip, 5), reach_strip)
    shared = shared_rows(strip_total, strip_paths)
    count = message.shape[0]
    per = message.shape[1] // 3 - 1
    for p in range(count):
        first = min(p * per, depth - per)
        for k in range(per + 2):
            z = first + k - 1
            message[p, k] = state[z] if 0 <= z < depth else blank
        for k in range(per):
            message[p, per + 2 + k] = back[first + k]
            value = tiles[first + k]
            if k == 0 and first > 0:
                value = jnp.where(sub == 6, jnp.broadcast_to(tiles[first - 1][:1], tile), value)
            if k == 0 and first + per < depth:
                value = jnp.where(sub == 7, jnp.broadcast_to(tiles[first + per][:1], tile), value)
            if per > 1 and k == 1:
                value = jnp.where(sub < 6, value, shared)
            message[p, 2 * per + 2 + k] = value
        message[p, 3 * per + 2] = reach_strip
        message[p, 3 * per + 3] = records
        if per == 1:
            message[p, 3 * per + 4] = shared


def blocks_kernel(
    per, depth, rows_of, place, cell, received, entering, entering_strips, sums, counts, sums_strip, counts_strip, halo,
):
    count = received.shape[0]
    tile = entering.shape[2:]
    lane = iota(tile, 1)
    width_y = tile[1]
    me = place[6]
    blank = jnp.full(tile, BIG, jnp.float32)
    unit = jnp.ones(tile, jnp.float32)
    side = 3 * per + 2

    def rows(device, k, j):
        return jnp.broadcast_to(received[device, 2 * per + 2 + k, j : j + 1, :], tile)

    def total(device, k):
        if k < 0:
            return rows(device, 0, 6)
        return rows(device, k, 0) if k < per else rows(device, 0, 7)

    def further(pair, cost):
        return pair[0] + cost, pair[1]

    shared = [received[d, 2 * per + 3] if per > 1 else received[d, 3 * per + 4] for d in range(count)]
    shared = spread_rows(shared)
    state = [(blank, unit)] * (per + 2)
    strip = (blank, unit)
    first, first_strip = [], []
    for device in range(count):
        first.append([value_of(pair) for pair in state])
        first_strip.append(value_of(strip))
        state = [
            join_pairs((received[device, k], unit), further(state[k], total(device, k - 1))) for k in range(per + 2)
        ]
        strip = join_pairs((received[device, side], unit), further(strip, shared[device][0]))
    own = blank
    for device in range(count):
        own = jnp.where(device == me, first_strip[device], own)
        for k in range(per):
            entering[device, k] = first[device][k + 1]
    entering_strips[0] = own
    group = width_y // 8
    for at in range(0, count, group):
        some = first_strip[at : at + group]
        some = some + [blank] * (group - len(some))
        turned = halo_columns(some, [shifted_down(s, 2) for s in some])
        halo[at // group] = turned.reshape(halo.shape[1:])
    low = jnp.minimum(me * per, depth - per)
    edges = [[halo[i, low + k] for k in range(per)] for i in range(halo.shape[0])]
    state = [(blank, unit)] * per
    strip = (blank, unit)
    for device in reversed(range(count)):
        for k in range(per):
            entering[device, per + k] = value_of(state[k])
            u = first[device][k + 1]
            turn = (width_y - 5 - 8 * (device % group)) % width_y
            edge = pltpu.roll(edges[device // group][k], turn, 1)
            values = [received[device, per + 2 + k], u + rows(device, k, 1)]
            values.append(jnp.where(lane == 0, edge, pltpu.roll(u, 1, 1)) + rows(device, k, 2))
            values.append(jnp.where(lane == width_y - 1, edge, pltpu.roll(u, width_y - 1, 1)) + rows(device, k, 3))
            values.append(first[device][k] + rows(device, k, 4))
            values.append(first[device][k + 2] + rows(device, k, 5))
            least, _, amount = softmin(values)
            state[k] = join_pairs((least, amount), further(state[k], total(device, k)))
        u = first_strip[device]
        back = received[device, side]
        back = jnp.where(iota(tile, 0) == 3, pltpu.roll(back, 3, 0), pltpu.roll(back, 5, 0))
        paths = shared[device][1]
        values = [back, u + paths[0], pltpu.roll(u, 1, 0) + paths[1], shifted_down(u, 1) + paths[2]]
        values.append(jnp.where(lane < 8, BIG, pltpu.roll(u, 8, 1)) + paths[3])
        values.append(jnp.where(lane >= width_y - 8, BIG, pltpu.roll(u, width_y - 8, 1)) + paths[4])
        least, _, amount = softmin(values)
        passed = join_pairs((least, amount), further(strip, shared[device][0]))
        strip = [jnp.where(device > me, new, old) for new, old in zip(passed, strip)]
    entering_strips[1] = value_of(strip)
    add_records(rows_of, 3 * per + 3, place, cell, received, sums, counts, sums_strip, counts_strip)


def second_sweep_kernel(
    place, first, first_strip, entering, entering_strips, costs, edge_costs, anisotropy, levels_one, sides,
    sums, counts, sums_strip, counts_strip,
    local, shares, slopes, keeps, misfits, edges_own, edges_factor, slopes_one, gains, message,
    field, strip, halo, shares_strip, slopes_strip, keeps_strip, misfits_strip,
):
    width_x, depth, quakes, width_y = first.shape
    tile = (quakes, width_y)
    near = levels_one.shape[1]
    per = entering.shape[1] // 2
    outside = outside_strips(place, tile)
    strips_in = [[s, shifted_down(s, 2)] for s in (entering_strips[0], entering_strips[1])]
    carried = [[entering[z // per, k * per + z % per] for z in range(depth)] for k in range(2)]

    def finish(x, carry):
        running, strip_running, prior = carry
        sums_now, values = [], []
        for z in range(depth):
            cost = row(costs, z, x, tile)
            sums_now.append(running[z] + cost)
            value = soft_pair(first[x, z], entering[z // per, z % per] + sums_now[z])
            field[x, z] = value
            if z < near:
                values.append(value)
                keep, slope = split_pair(levels_one[x, z], prior[z] + cost)
                slopes_one[x, z] = slope
                gains[x, z] = slope * row(anisotropy, z, x, tile) + keep * sides[x, z]
        strip_sums = []
        for side in range(2):
            strip_sums.append(strip_running[side] + edge_costs[3 * side, x])
            value = soft_pair(first_strip[x, side], strips_in[0][side] + strip_sums[side])
            strip[x, side] = jnp.where(outside[side], BIG, value)
        return sums_now, strip_sums, values

    blank = jnp.zeros(tile, jnp.float32)
    by_steps(width_x, finish, ([blank] * depth, [blank] * 2, carried[0][:near]))
    edges = [[strip[x, side] for x in range(width_x)] for side in range(2)]
    halo[...] = halo_columns(*edges).reshape(halo.shape)

    def keep(x, z, level, w, passed):
        for i in range(4):
            shares[i, x] = w[i]
        keeps[x], slopes[x] = split_pair(level, passed)

    def keep_strip(x, level, w, passed, value):
        shares_strip[x] = w
        keeps_strip[x], slopes_strip[x] = split_pair(level, passed)
        tally = pltpu.roll(counts_strip[...], lax.rem(width_y - 8 * x, width_y), 1)
        total = pltpu.roll(sums_strip[...], lax.rem(width_y - 8 * x, width_y), 1)
        misfits_strip[x] = ADJ_SCALE * (tally * (value * (1.0 / RATE)) - total)

    def step(lap, carry):
        x = width_x - 1 - lap
        state, strips = sweep_step(x, 1, field, strip, costs, edge_costs, halo, *carry, keep, keep_strip)
        for z in range(depth):
            local[x, z] = state[z]
        misfits[x] = ADJ_SCALE * (row_of(counts, x, tile) * (state[0] * (1.0 / RATE)) - sums[x])
        return state, strips

    by_steps(width_x, step, (carried[1], strips_in[1]))
    zero, unit = jnp.zeros(tile, jnp.float32), jnp.ones(tile, jnp.float32)
    lane = iota(tile, 1)
    own, factor, strip_own, strip_factor = zero, unit, zero, unit
    owns, factors = [], []
    sent = [zero, zero]
    for x in range(width_x):
        own = misfits[x] + own
        owns.append(keeps[x] * own)
        factors.append(keeps[x] * factor)
        own, factor = slopes[x] * own, slopes[x] * factor
        strip_own = misfits_strip[x] + strip_own
        through = keeps_strip[x] * shares_strip[x]
        for i, value in enumerate((strip_own, strip_factor)):
            value = pltpu.roll(through * value, 8 * x, 1) if x else through * value
            sent[i] = jnp.where((lane >> 3) == x, value, sent[i])
        strip_own, strip_factor = slopes_strip[x] * strip_own, slopes_strip[x] * strip_factor
    edges_own[...] = end_columns(sent[0]).reshape(edges_own.shape)
    edges_factor[...] = end_columns(sent[1]).reshape(edges_factor.shape)
    chain = [unit] * near
    blocks = [zero] * near
    links = [zero] * 4
    for x in range(width_x):
        entry = entries_of(owns[x], shares, x, edges_own[x])
        for z in range(near):
            chain[z] = chain[z] * slopes_one[x, z]
            blocks[z] = blocks[z] + chain[z] * entry[z]
        for i, path in enumerate(ways_of(factors[x], shares, x, edges_factor[x])):
            links[i] = links[i] + chain[i // 3] * path
    both = jnp.where(iota(tile, 0) < 5, strip_own, pltpu.roll(strip_factor, 2, 0))
    tiles = [own, factor, both] + blocks + chain + links
    for p in range(message.shape[0]):
        for i, value in enumerate(tiles):
            message[p, i] = value


def end_columns(rows):
    wide = rows.shape[1]
    first, last = shifted_down(rows, 3), pltpu.roll(rows, 3, 0)
    return jnp.transpose(jnp.concatenate([first] * (wide // 16) + [last] * (wide // 16), 0))


def ways_of(passed, shares, x, edge):
    lane = iota(passed.shape, 1)
    last = passed.shape[1] - 1
    above = jnp.where(lane == last, edge, pltpu.roll(passed * shares[1, x], last, 1))
    below = jnp.where(lane == 0, edge, pltpu.roll(passed * shares[2, x], 1, 1))
    return passed * shares[0, x], above, below, passed * shares[3, x]


def entries_of(passed, shares, x, edge):
    own, above, below, deeper = ways_of(passed, shares, x, edge)
    return own + above + below, deeper


def add_records(rows_of, tile_of, place, cell, received, sums, counts, sums_strip, counts_strip):
    width_x, quakes, width_y = sums.shape
    last = tile_of
    span_y = place[2]
    lane = iota((quakes, width_y), 1)
    column = iota((width_y, width_y), 0)
    strip_column = iota((8, width_y), 0)
    strip_column = jnp.where(strip_column == 3, -1, jnp.where(strip_column == 4, width_y, -2))
    share = width_y // rows_of
    dims = (((1,), (1,)), ((), ()))
    one_x = iota((width_x, width_y), 0)
    parts = [[], [], []]
    at, at_rows, at_strip = [], [], []
    for chunk in range(cell.shape[0]):
        records = jnp.zeros((quakes, width_y), jnp.float32)
        for part in range(share):
            piece = received[chunk * share + part, last]
            moved = pltpu.roll(piece, part * rows_of, 1) if part else piece
            records = jnp.where(lane // rows_of == part, moved, records)
        cells = cell[chunk : chunk + 1, :]
        station_x = lax.shift_right_logical(cells, place[7]) - place[0]
        station_y = (cells & (span_y - 1)) - place[1]
        at_x = (one_x == jnp.broadcast_to(station_x, one_x.shape)).astype(jnp.float32)
        pieces = [p.astype(jnp.float32) for p in exact_parts(records)]
        for out, piece in zip(parts, pieces):
            spread = [piece * jnp.broadcast_to(at_x[x : x + 1], piece.shape) for x in range(width_x)]
            out.append(jnp.concatenate(spread, 0).astype(jnp.bfloat16))
        at_rows.append(at_x.astype(jnp.bfloat16))
        hit = column == jnp.broadcast_to(station_y, column.shape)
        at.append(hit.astype(jnp.float32).astype(jnp.bfloat16))
        hit = strip_column == jnp.broadcast_to(station_y, strip_column.shape)
        at_strip.append(hit.astype(jnp.float32).astype(jnp.bfloat16))
    at = jnp.concatenate(at, 1)
    at_rows = jnp.concatenate(at_rows, 1)
    at_strip = jnp.concatenate(at_strip, 1)
    parts = [jnp.concatenate(p, 1) for p in parts]

    def product(a, b):
        return lax.dot_general(a, b, dims, preferred_element_type=jnp.float32)

    main = [product(p, at) for p in parts]
    sums[...] = (main[0] + main[1] + main[2]).reshape(sums.shape)
    counts[...] = product(at_rows, at)
    sums_strip[...] = product(at_strip, parts[0]) + product(at_strip, parts[1]) + product(at_strip, parts[2])
    spread = ((iota((width_x, width_y), 1) >> 3) == one_x).astype(jnp.float32).astype(jnp.bfloat16)
    tally = 0.0
    for part in reversed(exact_parts(product(at_strip, at_rows))):
        tally += lax.dot_general(part, spread, (((1,), (0,)), ((), ())), preferred_element_type=jnp.float32)
    counts_strip[...] = tally


def times_kernel(local, times):
    width_x, depth, quakes, _ = local.shape

    def step(x, carry):
        for z in range(depth):
            times[pl.ds(z * width_x + x, quakes, stride=depth * width_x), :] = local[x, z] * (1.0 / RATE)
        return carry

    by_steps(width_x, step, 0)


def kernel_kernel(
    place, received, shares, slopes, keeps, misfits, edges_own, edges_factor, slopes_one, gains, anisotropy, kernel,
    entries, top, sent,
):
    width_x, quakes, width_y = slopes.shape
    tile = (quakes, width_y)
    near = slopes_one.shape[1]
    count = received.shape[0]
    lane = iota(tile, 1)
    last = width_y - 1
    me = place[6]
    zero = jnp.zeros(tile, jnp.float32)
    group = width_y // 8
    state, strip, mine, mine_strip = zero, zero, zero, zero
    carries = []
    for device in range(count):
        carries.append(state)
        mine = jnp.where(device == me, state, mine)
        at = device % group
        moved = pltpu.roll(strip, 8 * at, 1) if at else strip
        sent[device // group] = moved if at == 0 else jnp.where((lane >> 3) == at, moved, sent[device // group])
        both = received[device, 2]
        state = received[device, 0] + received[device, 1] * state
        strip = both + shifted_down(both, 2) * strip
    ends = [end_columns(sent[i]) for i in range(sent.shape[0])]
    state = [zero] * near
    mine_edge = zero
    for device in reversed(range(count)):
        at = 8 * (device % group)
        edge = ends[device // group][at : at + 8]
        mine_edge = jnp.where(device == me, edge, mine_edge)
        carry = carries[device]
        block = [received[device, 3 + z] for z in range(near)]
        above = jnp.where(lane == last, edge, pltpu.roll(carry, last, 1))
        below = jnp.where(lane == 0, edge, pltpu.roll(carry, 1, 1))
        link = [received[device, 3 + 2 * near + i] for i in range(4)]
        block[0] = block[0] + link[0] * carry + link[1] * above + link[2] * below
        block[1] = block[1] + link[3] * carry
        for z in range(near):
            passed = block[z] + received[device, 3 + near + z] * state[z]
            state[z] = jnp.where(device > me, passed, state[z])
    carry = mine
    for x in range(width_x):
        total = misfits[x] + carry
        carry = slopes[x] * total
        passed = keeps[x] * total
        sideways = row(anisotropy, near, x, tile) * (shares[1, x] + shares[2, x])
        sideways = sideways + row(anisotropy, 2 * near, x, tile) * shares[3, x]
        terms = carry * row(anisotropy, 0, x, tile) + passed * sideways
        top[x : x + 1, :] = jnp.sum(terms, axis=0, keepdims=True)
        entry = entries_of(passed, shares, x, edges_own[x] + edges_factor[x] * mine_edge)
        for z in range(near):
            entries[x, z] = entry[z]
    for x in reversed(range(width_x)):
        for z in range(near):
            total = entries[x, z] + state[z]
            state[z] = slopes_one[x, z] * total
            value = jnp.sum(total * gains[x, z], axis=0, keepdims=True)
            if z == 0:
                value = value + top[x : x + 1, :]
            kernel[z, x : x + 1, :] = value
    for z in range(near, kernel.shape[0]):
        kernel[z] = jnp.zeros(kernel.shape[1:], jnp.float32)


def call(kernel, shapes, operands, scratch=(), scalars=0, far=0, last=False, aliases=()):
    many = isinstance(shapes, list)
    shapes = shapes if many else [shapes]
    out = [jax.ShapeDtypeStruct(s, jnp.float32) if last else pltpu.VMEM(s, jnp.float32) for s in shapes]
    result = pl.pallas_call(
        kernel,
        out_shape=out,
        in_specs=[SMEM] * scalars + [FAR] * far + [VMEM] * (len(operands) - scalars - far),
        out_specs=[VMEM] * len(out),
        scratch_shapes=[pltpu.VMEM(s, jnp.float32) if isinstance(s, tuple) else s for s in scratch],
        compiler_params=PARAMS,
        input_output_aliases=dict(aliases),
    )(*operands)
    return result if many else result[0]


def traded(message):
    return lax.all_to_all(message, "gx", 0, 0, tiled=True)


def rotated(value, axis, by):
    count = lax.axis_size(axis)
    return lax.ppermute(value, axis, [(i, (i + by) % count) for i in range(count)])


def body(warm_start, slowness, anisotropy, observed, station_cell, source_cell):
    quakes, depth, width_x, width_y = warm_start.shape
    count_x, count_y = lax.axis_size("gx"), lax.axis_size("gy")
    index_x, index_y = lax.axis_index("gx"), lax.axis_index("gy")
    span_x, span_y = width_x * count_x, width_y * count_y
    near = 2
    per = max(1, depth // count_x)
    tile = (quakes, width_y)
    top = (width_x,) + tile
    close = (width_x, near) + tile
    field = (width_x, depth) + tile
    place = jnp.stack(
        [
            index_x * width_x,
            index_y * width_y,
            jnp.int32(span_y),
            jnp.int32(span_x * span_y),
            (index_y == 0).astype(jnp.int32),
            (index_y == count_y - 1).astype(jnp.int32),
            index_x,
            jnp.int32(span_y.bit_length() - 1),
            index_y,
        ]
    ).astype(jnp.int32)
    anis = anisotropy.reshape(3 * depth, width_x, width_y)
    local_records = observed.shape[1]
    flat = (quakes * depth * width_x, width_y)

    base = width_x * 11
    sources = [warm_start.reshape(quakes, depth * width_x, width_y), observed, slowness, anis]
    sources = [pltpu.with_memory_space_constraint(a, pltpu.HBM) for a in [source_cell] + sources]
    start, costs, anis, edge, records = call(
        pack_kernel,
        [field, anis.shape, (3 * near, width_x, width_y), (base + quakes, width_y), tile],
        [place] + sources,
        [pltpu.SMEM((quakes,), jnp.int32), (CHUNKS, quakes, depth // CHUNKS * width_x, width_y)]
        + [a.shape for a in sources[2:]]
        + [pltpu.SemaphoreType.DMA((4 + CHUNKS,))],
        scalars=1,
        far=5,
    )
    from_left = rotated(edge, "gy", 1)
    from_right = rotated(edge, "gy", -1)
    others = [rotated(records, "gy", by) for by in range(2, count_y - 1)]

    message_shape = (count_x, 3 * per + (4 if per > 1 else 5)) + tile
    first, first_strip, edge_costs, levels_one, sides, message = call(
        functools.partial(first_sweep_kernel, local_records, count_y),
        [field, (width_x, 2) + tile, (6,) + top, close, close, message_shape],
        [place, start, edge, from_left, from_right, costs, anis] + others,
        [(depth,) + tile, (width_x, 2) + tile],
        scalars=1,
    )
    reach = traded(message)
    group = width_y // 8
    entering, entering_strips, *recorded = call(
        functools.partial(blocks_kernel, per, depth, local_records * count_y),
        [(count_x, 2 * per) + tile, (2,) + tile, top, (width_x, width_y), tile, tile],
        [place, station_cell.reshape(-1, width_y), reach],
        [(-(-count_x // group), depth) + tile],
        scalars=1,
    )
    entering = traded(entering)
    second, *rest, message = call(
        second_sweep_kernel,
        [field, (4,) + top] + [top] * 5 + [close, close, (count_x, 7 + 2 * near) + tile],
        [place, first, first_strip, entering, entering_strips, costs, edge_costs, anis, levels_one, sides]
        + recorded,
        [field, (width_x, 2) + tile, (depth,) + tile] + [top] * 4,
        scalars=1,
        aliases={1: 0},
    )
    received = traded(message)
    times = call(times_kernel, flat, [second], last=True)
    kernel = call(
        kernel_kernel,
        (depth, width_x, width_y),
        [place, received] + rest + [anis],
        [close, (width_x, width_y), (-(-count_x // group),) + tile],
        scalars=1,
        last=True,
    )
    return (times.reshape(warm_start.shape), kernel)


def solution(mesh):
    return jax.shard_map(
        body,
        mesh=mesh,
        in_specs=(
            P(None, None, "gx", "gy"),
            P(None, "gx", "gy"),
            P(None, None, "gx", "gy"),
            P(None, ("gx", "gy")),
            P(),
            P(),
        ),
        out_specs=(P(None, None, "gx", "gy"), P(None, "gx", "gy")),
        check_vma=False,
    )
```

```python
import functools
import math

import jax
import jax.numpy as jnp
from jax import lax
from jax.experimental import pallas as pl
from jax.experimental.pallas import tpu as pltpu
from jax.sharding import PartitionSpec as P

TAU = 0.05
ADJ_SCALE = 0.1
LOG2E = math.log2(math.e)
RATE = LOG2E / TAU
BIG = 10000.0 * RATE
UNROLL = 8
CHUNKS = 4
VMEM = pl.BlockSpec(memory_space=pltpu.VMEM)
FAR = pl.BlockSpec(memory_space=pl.ANY)
SMEM = pl.BlockSpec(memory_space=pltpu.SMEM)
PARAMS = pltpu.CompilerParams(vmem_limit_bytes=8 * 1024 * 1024)


def softmin(values):
    least = functools.reduce(jnp.minimum, values)
    parts = [jnp.exp2(least - v) for v in values]
    return least, parts, functools.reduce(jnp.add, parts)


def soft_pair(first, second):
    return jnp.minimum(first, second) - LOG2E * jnp.log(1.0 + jnp.exp2(-jnp.abs(first - second)))


def add_pair(least, total, passed):
    low = jnp.minimum(least, passed)
    return low - LOG2E * jnp.log(total * jnp.exp2(low - least) + jnp.exp2(low - passed))


def join_pairs(first, second):
    low = jnp.minimum(first[0], second[0])
    return low, first[1] * jnp.exp2(low - first[0]) + second[1] * jnp.exp2(low - second[0])


def value_of(pair):
    return pair[0] - LOG2E * jnp.log(pair[1])


def split_pair(first, second):
    gap = jnp.exp2(-jnp.abs(first - second))
    share = 1.0 / (1.0 + gap)
    less = gap * share
    nearer = first <= second
    return jnp.where(nearer, share, less), jnp.where(nearer, less, share)


def iota(shape, axis):
    return lax.broadcasted_iota(jnp.int32, shape, axis)


def row(ref, index, x, like):
    return jnp.broadcast_to(ref[index, pl.ds(x, 1), :], like)


def row_of(ref, x, like):
    return jnp.broadcast_to(ref[pl.ds(x, 1), :], like)


def by_steps(count, step, carry):
    def group(i, carry):
        for j in range(UNROLL):
            carry = step(i * UNROLL + j, carry)
        return carry

    return lax.fori_loop(0, count // UNROLL, group, carry)


def packed(left, right):
    return jnp.where(iota(left.shape, 0) < 5, left, pltpu.roll(right, 2, 0))


def merged(left, right):
    return jnp.where(iota(left.shape, 0) < 4, left, right)


def shifted_down(tile, by):
    return pltpu.roll(tile, tile.shape[0] - by, 0)


def exact_parts(value):
    high = value.astype(jnp.bfloat16).astype(jnp.float32)
    middle = (value - high).astype(jnp.bfloat16).astype(jnp.float32)
    low = value - high - middle
    return [p.astype(jnp.bfloat16) for p in (high, middle, low)]


def pack_kernel(
    place, source_far, warm_far, observed_far, slowness_far, anisotropy_far, start, costs, near, edge, records,
    source, warm, observed, slowness, anisotropy, arrived,
):
    pairs = [(slowness_far, slowness), (anisotropy_far, anisotropy), (observed_far, observed)]
    share = start.shape[1] // CHUNKS
    span = share * start.shape[0]
    pairs += [(warm_far.at[:, pl.ds(i * span, span)], warm.at[i]) for i in range(CHUNKS)]
    pairs += [(source_far, source)]
    copies = [pltpu.make_async_copy(a, b, arrived.at[i]) for i, (a, b) in enumerate(pairs)]
    for copy in copies:
        copy.start()
    width_x, depth, quakes, width_y = start.shape
    tile = (quakes, width_y)
    quake = iota(tile, 0)
    lane = iota(tile, 1)
    span_y = place[2]
    plane = place[3]
    rows = width_x * 8
    wide = (width_x, width_y)
    group = iota(wide, 1) >> 3
    copies[0].wait()
    copies[1].wait()
    for k in range(3):
        columns = jnp.zeros(wide, jnp.float32)
        for z in range(depth):
            cost = slowness[z] * anisotropy[k * depth + z] * RATE
            costs[k * depth + z] = cost
            columns = jnp.where(group == z, pltpu.roll(cost, 8 * z + 4, 1), columns)
        edge[rows : rows + width_x, :] = columns
        rows += width_x
        for z in range(near.shape[0] // 3):
            near[k * (near.shape[0] // 3) + z] = anisotropy[k * depth + z]
    copies[-1].wait()
    cell = jnp.zeros(tile, jnp.int32)
    for e in range(quakes):
        cell = jnp.where(quake == e, source[e], cell)
    cell = cell - (lane + place[0] * span_y + place[1])
    edges = []
    for i in range(CHUNKS):
        copies[3 + i].wait()
        here = warm.at[i].reshape(quakes * share * width_x, width_y)

        chunk = [jnp.zeros(tile, jnp.float32)] * share
        for x in range(width_x):
            mine = (lane >> 3) == x
            for k in range(share):
                value = here[pl.ds(k * width_x + x, quakes, stride=share * width_x), :] * RATE
                value = jnp.where(cell == (i * share + k) * plane + x * span_y, 0.0, value)
                start[x, i * share + k] = value
                chunk[k] = jnp.where(mine, pltpu.roll(value, (8 * x + 4) % width_y, 1), chunk[k])
        edges += chunk
    edge[: width_x * 8, :] = jnp.transpose(jnp.concatenate(edges, 0))
    copies[2].wait()
    records[...] = jnp.zeros(tile, jnp.float32)
    records[:, : observed.shape[1]] = observed[...]
    edge[rows:, :] = records[...]


def halo_columns(left, right):
    rows = []
    for l, r in zip(left, right):
        rows.append(jnp.where(iota(l.shape, 0) == 4, r, pltpu.roll(l, 2, 0)))
    return jnp.transpose(jnp.concatenate(rows, 0))


def strip_costs(own, from_left, from_right, out, width_x, depth):
    tile = own.shape[1]
    base = width_x * 8
    lane = iota((8, tile), 1)
    low = (lane & 7) < 4
    mine = (lane & 7) == iota((8, tile), 0)
    spread = ((iota((tile, tile), 0) >> 3) == (iota((tile, tile), 1) >> 3)).astype(jnp.float32)
    spread = spread.astype(jnp.bfloat16)
    for side in range(2):
        for k in range(3):
            rows = []
            for x in range(width_x):
                at = slice(base + k * width_x + x, base + k * width_x + x + 1)
                here = jnp.broadcast_to(own[at, :], lane.shape)
                there = jnp.broadcast_to((from_right if side else from_left)[at, :], lane.shape)
                value = jnp.where(low, here, there) if side else jnp.where(low, there, here)
                rows.append(jnp.where(mine, value, 0.0))
            whole = jnp.concatenate(rows, 0)
            total = 0.0
            for part in reversed(exact_parts(whole)):
                total = total + lax.dot_general(
                    part, spread, (((1,), (0,)), ((), ())), preferred_element_type=jnp.float32
                )
            out[3 * side + k] = total.reshape(width_x, 8, tile)


def running_sum(value):
    rows = iota(value.shape, 0)
    by = 1
    while by < value.shape[0]:
        value = value + jnp.where(rows >= by, pltpu.roll(value, by, 0), 0.0)
        by *= 2
    return value


def log_sum(exponents):
    return -LOG2E * jnp.log(functools.reduce(jnp.add, [jnp.exp2(-e) for e in exponents]))


def passages(costs, own, from_left, from_right, depth, sums_out):
    width_x, width_y = costs.shape[1:]
    base = 8 * width_x
    at = slice(base, base + width_x)
    lane = iota((width_x, width_y), 1)
    beside = jnp.where((lane & 7) == 4, running_sum(from_right[at, :]), pltpu.roll(running_sum(from_left[at, :]), 2, 1))
    sums = [running_sum(costs[z]) for z in range(depth)]
    for z in range(depth):
        sums_out[z] = sums[z]
    sub = iota((8, width_y), 0)
    tiles = []
    for z in range(depth):
        back = sums[z] - costs[z]
        edge = pltpu.roll(beside, width_y - 5 - 8 * z, 1)
        below = jnp.where(lane == 0, edge, pltpu.roll(sums[z], 1, 1))
        above = jnp.where(lane == width_y - 1, edge, pltpu.roll(sums[z], width_y - 1, 1))
        step_y = back + costs[depth + z]
        step_z = back + costs[2 * depth + z]
        paths = [sums[z] + back, below + step_y, above + step_y]
        paths.append(sums[z - 1] + step_z if z > 0 else None)
        paths.append(sums[z + 1] + step_z if z < depth - 1 else None)
        tile = jnp.broadcast_to(sums[z][width_x - 1 :, :], sub.shape)
        for j, path in enumerate(paths):
            if path is None:
                tile = jnp.where(sub == j + 1, BIG, tile)
            else:
                total = jnp.sum(jnp.exp2(-path), axis=0, keepdims=True)
                tile = jnp.where(sub == j + 1, -LOG2E * jnp.log(total), tile)
        tiles.append(tile)
    return tiles


def strip_passages(edge_costs, width_x):
    shape = edge_costs.shape[2:]
    lane = iota(shape, 1)
    sums = jnp.zeros(shape, jnp.float32)
    totals = [jnp.zeros(shape, jnp.float32)] * 5
    for x in range(width_x):
        cost, step_y, step_z = [packed(edge_costs[k, x], edge_costs[3 + k, x]) for k in range(3)]
        back = sums
        sums = sums + cost
        step_y, step_z = step_y + back, step_z + back
        paths = [sums + back, pltpu.roll(sums, 1, 0) + step_y, shifted_down(sums, 1) + step_y]
        paths.append(jnp.where(lane < 8, BIG, pltpu.roll(sums, 8, 1) + step_z))
        paths.append(jnp.where(lane >= shape[1] - 8, BIG, pltpu.roll(sums, shape[1] - 8, 1) + step_z))
        totals = [t + jnp.exp2(-p) for t, p in zip(totals, paths)]
    return sums, [-LOG2E * jnp.log(jnp.maximum(t, 1e-37)) for t in totals]


def shared_rows(total, paths):
    place = iota(total.shape, 1) & 7
    first, second = total, total
    for q in range(6):
        value = pltpu.roll(total, (4 - q) % 8, 0)
        first = jnp.where(place == q, value, first)
    for q, (path, at) in enumerate([(p, r) for p in paths for r in (3, 6)]):
        if q < 2:
            first = jnp.where(place == 6 + q, pltpu.roll(path, (6 - at) % 8, 0), first)
        else:
            second = jnp.where(place == q - 2, pltpu.roll(path, (7 - at) % 8, 0), second)
    return jnp.where(iota(total.shape, 0) == 6, first, second)


def spread_rows(tiles):
    shape = tiles[0].shape
    wide = shape[1]
    sub = iota(shape, 0)
    mine = (iota(shape, 1) & 7) == sub
    spread = ((iota((wide, wide), 0) >> 3) == (iota((wide, wide), 1) >> 3)).astype(jnp.float32)
    spread = spread.astype(jnp.bfloat16)
    rows = [jnp.where(mine, jnp.broadcast_to(t[r : r + 1], shape), 0.0) for t in tiles for r in (6, 7)]
    whole = jnp.concatenate(rows, 0)
    value = 0.0
    for part in reversed(exact_parts(whole)):
        value = value + lax.dot_general(part, spread, (((1,), (0,)), ((), ())), preferred_element_type=jnp.float32)
    out = []
    for i in range(len(tiles)):
        first, second = value[16 * i : 16 * i + 8], value[16 * i + 8 : 16 * i + 16]
        paths = [jnp.where(sub == 3, pltpu.roll(first, 5, 0), pltpu.roll(first, 7, 0))]
        for q in range(4):
            at_three = pltpu.roll(second, (3 - 2 * q) % 8, 0)
            at_six = pltpu.roll(second, (6 - 2 * q - 1) % 8, 0)
            paths.append(jnp.where(sub == 3, at_three, at_six))
        out.append((pltpu.roll(first, 2, 0), paths))
    return out


def sweep_step(x, near, levels, strip, costs, edge_costs, halo, state, strip_state, keep, keep_strip):
    depth = len(levels)
    tile = levels[0].shape
    width_y = tile[1]
    lane = iota(tile, 1)
    out = []
    for z in range(depth):
        u = levels[z]
        cost_y = row(costs, depth + z, x, tile)
        cost_z = row(costs, 2 * depth + z, x, tile)
        edge = pltpu.roll(halo[z], width_y - 5 - 8 * x, 1)
        values = [u]
        values.append(jnp.where(lane == 0, edge, pltpu.roll(u, 1, 1)) + cost_y)
        values.append(jnp.where(lane == width_y - 1, edge, pltpu.roll(u, width_y - 1, 1)) + cost_y)
        if z > 0:
            values.append(levels[z - 1] + cost_z)
        if z < depth - 1:
            values.append(levels[z + 1] + cost_z)
        least, parts, total = softmin(values)
        passed = state[z] + row(costs, z, x, tile)
        if z < near:
            scale = 1.0 / total
            keep(x, z, value_of((least, total)), [p * scale for p in parts], passed)
        out.append(add_pair(least, total, passed))
    strips, relaxed, weights, passes = [], [], [], []
    for side in range(2):
        u = strip[x, side]
        cost_y = edge_costs[3 * side + 1, x]
        cost_z = edge_costs[3 * side + 2, x]
        values = [u, pltpu.roll(u, 1, 0) + cost_y, pltpu.roll(u, 7, 0) + cost_y]
        values.append(jnp.where(lane < 8, BIG, pltpu.roll(u, 8, 1)) + cost_z)
        values.append(jnp.where(lane >= width_y - 8, BIG, pltpu.roll(u, width_y - 8, 1)) + cost_z)
        least, parts, total = softmin(values)
        passes.append(strip_state[side] + edge_costs[3 * side, x])
        strips.append(add_pair(least, total, passes[side]))
        if keep_strip is not None:
            relaxed.append(value_of((least, total)))
            weights.append(parts[2 - side] / total)
    if keep_strip is not None:
        keep_strip(x, merged(*relaxed), merged(*weights), merged(*passes), merged(*strips))
    return out, strips


def outside_strips(place, shape):
    sub = iota(shape, 0)
    return [(place[4] == 1) & (sub < 4), (place[5] == 1) & (sub >= 4)]


def first_sweep_kernel(
    rows_of, count_y, place, field, own, from_left, from_right, costs, anisotropy, *rest
):
    others = rest[: count_y - 3]
    local, local_strip, edge_costs, levels, sides, sums, message, halo, strip = rest[count_y - 3 :]
    width_x, depth, quakes, width_y = field.shape
    tile = (quakes, width_y)
    sub = iota(tile, 0)
    low = sub < 4
    near = levels.shape[1]
    last = 11 * width_x
    far = [own[last:, :], from_left[last:, :]] + [o[...] for o in others] + [from_right[last:, :]]
    records = jnp.zeros(tile, jnp.float32)
    for by, piece in enumerate(far):
        owner = lax.rem(place[8] + count_y - by, count_y)
        records = records + pltpu.roll(piece, owner * rows_of, 1)
    left, right = [], []
    for x in range(width_x):
        at = slice(8 * x, 8 * x + 8)
        before = jnp.where(place[4] == 1, BIG, from_left[at, :])
        after = jnp.where(place[5] == 1, BIG, from_right[at, :])
        left.append(jnp.where(low, before, own[at, :]))
        right.append(jnp.where(low, own[at, :], after))
        strip[x, 0] = left[x]
        strip[x, 1] = right[x]
    halo[...] = halo_columns(left, right).reshape(halo.shape)
    strip_costs(own, from_left, from_right, edge_costs, width_x, depth)
    outside = outside_strips(place, tile)

    def keep(x, z, level, w, passed):
        levels[x, z] = level
        vertical = w[3] if z == 0 else w[3] + w[4]
        sideways = row(anisotropy, near + z, x, tile) * (w[1] + w[2])
        sides[x, z] = sideways + row(anisotropy, 2 * near + z, x, tile) * vertical

    def step(x, carry):
        state, strips = sweep_step(x, near, [field[x, z] for z in range(depth)], strip, costs, edge_costs, halo, *carry, keep, None)
        for z in range(depth):
            local[x, z] = state[z]
        for side in range(2):
            local_strip[x, side] = jnp.where(outside[side], BIG, strips[side])
        return state, strips

    blank = jnp.full(tile, BIG, jnp.float32)
    state, strips = by_steps(width_x, step, ([blank] * depth, [blank] * 2))
    reach_strip = packed(*[jnp.where(o, BIG, s) for o, s in zip(outside, strips)])

    edges = [[local_strip[x, side] for x in range(width_x)] for side in range(2)]
    halo[...] = halo_columns(*edges).reshape(halo.shape)

    def again(lap, carry):
        x = width_x - 1 - lap
        values = [local[x, z] for z in range(depth)]
        return sweep_step(x, 0, values, local_strip, costs, edge_costs, halo, *carry, None, None)

    back, back_strips = by_steps(width_x, again, ([blank] * depth, [blank] * 2))
    tiles = passages(costs, own, from_left, from_right, depth, sums)
    strip_total, strip_paths = strip_passages(edge_costs, width_x)

    back_strip = packed(*back_strips)
    reach_strip = jnp.where(sub == 0, shifted_down(back_strip, 3), reach_strip)
    reach_strip = jnp.where(sub == 1, shifted_down(back_strip, 5), reach_strip)
    shared = shared_rows(strip_total, strip_paths)
    count = message.shape[0]
    per = message.shape[1] // 3 - 1
    for p in range(count):
        first = min(p * per, depth - per)
        for k in range(per + 2):
            z = first + k - 1
            message[p, k] = state[z] if 0 <= z < depth else blank
        for k in range(per):
            message[p, per + 2 + k] = back[first + k]
            value = tiles[first + k]
            if k == 0 and first > 0:
                value = jnp.where(sub == 6, jnp.broadcast_to(tiles[first - 1][:1], tile), value)
            if k == 0 and first + per < depth:
                value = jnp.where(sub == 7, jnp.broadcast_to(tiles[first + per][:1], tile), value)
            if per > 1 and k == 1:
                value = jnp.where(sub < 6, value, shared)
            message[p, 2 * per + 2 + k] = value
        message[p, 3 * per + 2] = reach_strip
        message[p, 3 * per + 3] = records
        if per == 1:
            message[p, 3 * per + 4] = shared


def blocks_kernel(
    per, depth, rows_of, place, cell, received, entering, entering_strips, sums, counts, sums_strip, counts_strip, halo,
):
    count = received.shape[0]
    tile = entering.shape[2:]
    lane = iota(tile, 1)
    width_y = tile[1]
    me = place[6]
    blank = jnp.full(tile, BIG, jnp.float32)
    unit = jnp.ones(tile, jnp.float32)
    side = 3 * per + 2

    def rows(device, k, j):
        return jnp.broadcast_to(received[device, 2 * per + 2 + k, j : j + 1, :], tile)

    def total(device, k):
        if k < 0:
            return rows(device, 0, 6)
        return rows(device, k, 0) if k < per else rows(device, 0, 7)

    def further(pair, cost):
        return pair[0] + cost, pair[1]

    shared = [received[d, 2 * per + 3] if per > 1 else received[d, 3 * per + 4] for d in range(count)]
    shared = spread_rows(shared)
    state = [(blank, unit)] * (per + 2)
    strip = (blank, unit)
    first, first_strip = [], []
    for device in range(count):
        first.append([value_of(pair) for pair in state])
        first_strip.append(value_of(strip))
        state = [
            join_pairs((received[device, k], unit), further(state[k], total(device, k - 1))) for k in range(per + 2)
        ]
        strip = join_pairs((received[device, side], unit), further(strip, shared[device][0]))
    own = blank
    for device in range(count):
        own = jnp.where(device == me, first_strip[device], own)
        for k in range(per):
            entering[device, k] = first[device][k + 1]
    entering_strips[0] = own
    group = width_y // 8
    for at in range(0, count, group):
        some = first_strip[at : at + group]
        some = some + [blank] * (group - len(some))
        turned = halo_columns(some, [shifted_down(s, 2) for s in some])
        halo[at // group] = turned.reshape(halo.shape[1:])
    low = jnp.minimum(me * per, depth - per)
    edges = [[halo[i, low + k] for k in range(per)] for i in range(halo.shape[0])]
    state = [(blank, unit)] * per
    strip = (blank, unit)
    for device in reversed(range(count)):
        for k in range(per):
            entering[device, per + k] = value_of(state[k])
            u = first[device][k + 1]
            turn = (width_y - 5 - 8 * (device % group)) % width_y
            edge = pltpu.roll(edges[device // group][k], turn, 1)
            values = [received[device, per + 2 + k], u + rows(device, k, 1)]
            values.append(jnp.where(lane == 0, edge, pltpu.roll(u, 1, 1)) + rows(device, k, 2))
            values.append(jnp.where(lane == width_y - 1, edge, pltpu.roll(u, width_y - 1, 1)) + rows(device, k, 3))
            values.append(first[device][k] + rows(device, k, 4))
            values.append(first[device][k + 2] + rows(device, k, 5))
            least, _, amount = softmin(values)
            state[k] = join_pairs((least, amount), further(state[k], total(device, k)))
        u = first_strip[device]
        back = received[device, side]
        back = jnp.where(iota(tile, 0) == 3, pltpu.roll(back, 3, 0), pltpu.roll(back, 5, 0))
        paths = shared[device][1]
        values = [back, u + paths[0], pltpu.roll(u, 1, 0) + paths[1], shifted_down(u, 1) + paths[2]]
        values.append(jnp.where(lane < 8, BIG, pltpu.roll(u, 8, 1)) + paths[3])
        values.append(jnp.where(lane >= width_y - 8, BIG, pltpu.roll(u, width_y - 8, 1)) + paths[4])
        least, _, amount = softmin(values)
        passed = join_pairs((least, amount), further(strip, shared[device][0]))
        strip = [jnp.where(device > me, new, old) for new, old in zip(passed, strip)]
    entering_strips[1] = value_of(strip)
    add_records(rows_of, 3 * per + 3, place, cell, received, sums, counts, sums_strip, counts_strip)


def second_sweep_kernel(
    place, first, first_strip, entering, entering_strips, costs, cost_sums, edge_costs, anisotropy, levels_one, sides,
    sums, counts, sums_strip, counts_strip,
    local, shares, slopes, keeps, misfits, edges_own, edges_factor, slopes_one, gains, message,
    strip, halo, shares_strip, slopes_strip, keeps_strip, misfits_strip,
):
    width_x, depth, quakes, width_y = first.shape
    tile = (quakes, width_y)
    near = levels_one.shape[1]
    per = entering.shape[1] // 2
    outside = outside_strips(place, tile)
    strips_in = [[s, shifted_down(s, 2)] for s in (entering_strips[0], entering_strips[1])]
    carried = [[entering[z // per, k * per + z % per] for z in range(depth)] for k in range(2)]

    running = [jnp.zeros(tile, jnp.float32)] * 2
    for x in range(width_x):
        for side in range(2):
            running[side] = running[side] + edge_costs[3 * side, x]
            value = soft_pair(first_strip[x, side], strips_in[0][side] + running[side])
            strip[x, side] = jnp.where(outside[side], BIG, value)
    edges = [[strip[x, side] for x in range(width_x)] for side in range(2)]
    halo[...] = halo_columns(*edges).reshape(halo.shape)

    def keep(x, z, level, w, passed):
        for i in range(4):
            shares[i, x] = w[i]
        keeps[x], slopes[x] = split_pair(level, passed)

    def keep_strip(x, level, w, passed, value):
        shares_strip[x] = w
        keeps_strip[x], slopes_strip[x] = split_pair(level, passed)
        tally = pltpu.roll(counts_strip[...], lax.rem(width_y - 8 * x, width_y), 1)
        total = pltpu.roll(sums_strip[...], lax.rem(width_y - 8 * x, width_y), 1)
        misfits_strip[x] = ADJ_SCALE * (tally * (value * (1.0 / RATE)) - total)

    def finished(x, z):
        return soft_pair(first[x, z], carried[0][z] + row(cost_sums, z, x, tile))

    def step(lap, carry):
        x = width_x - 1 - lap
        *carry, values = carry
        values = values + [finished(x, z) for z in range(near, depth)]
        priors = [jnp.where(x == 0, carried[0][z], finished(jnp.maximum(x - 1, 0), z)) for z in range(near)]
        for z in range(near):
            prior = priors[z]
            keep_one, slope = split_pair(levels_one[x, z], prior + row(costs, z, x, tile))
            slopes_one[x, z] = slope
            gains[x, z] = slope * row(anisotropy, z, x, tile) + keep_one * sides[x, z]
        state, strips = sweep_step(x, 1, values, strip, costs, edge_costs, halo, *carry, keep, keep_strip)
        for z in range(depth):
            local[x, z] = state[z]
        misfits[x] = ADJ_SCALE * (row_of(counts, x, tile) * (state[0] * (1.0 / RATE)) - sums[x])
        return state, strips, priors

    by_steps(width_x, step, (carried[1], strips_in[1], [finished(width_x - 1, z) for z in range(near)]))
    zero, unit = jnp.zeros(tile, jnp.float32), jnp.ones(tile, jnp.float32)
    lane = iota(tile, 1)
    own, factor, strip_own, strip_factor = zero, unit, zero, unit
    owns, factors = [], []
    sent = [zero, zero]
    for x in range(width_x):
        own = misfits[x] + own
        owns.append(keeps[x] * own)
        factors.append(keeps[x] * factor)
        own, factor = slopes[x] * own, slopes[x] * factor
        strip_own = misfits_strip[x] + strip_own
        through = keeps_strip[x] * shares_strip[x]
        for i, value in enumerate((strip_own, strip_factor)):
            value = pltpu.roll(through * value, 8 * x, 1) if x else through * value
            sent[i] = jnp.where((lane >> 3) == x, value, sent[i])
        strip_own, strip_factor = slopes_strip[x] * strip_own, slopes_strip[x] * strip_factor
    edges_own[...] = end_columns(sent[0]).reshape(edges_own.shape)
    edges_factor[...] = end_columns(sent[1]).reshape(edges_factor.shape)
    chain = [unit] * near
    blocks = [zero] * near
    links = [zero] * 4
    for x in range(width_x):
        entry = entries_of(owns[x], shares, x, edges_own[x])
        for z in range(near):
            chain[z] = chain[z] * slopes_one[x, z]
            blocks[z] = blocks[z] + chain[z] * entry[z]
        for i, path in enumerate(ways_of(factors[x], shares, x, edges_factor[x])):
            links[i] = links[i] + chain[i // 3] * path
    both = jnp.where(iota(tile, 0) < 5, strip_own, pltpu.roll(strip_factor, 2, 0))
    tiles = [own, factor, both] + blocks + chain + links
    for p in range(message.shape[0]):
        for i, value in enumerate(tiles):
            message[p, i] = value


def end_columns(rows):
    wide = rows.shape[1]
    first, last = shifted_down(rows, 3), pltpu.roll(rows, 3, 0)
    return jnp.transpose(jnp.concatenate([first] * (wide // 16) + [last] * (wide // 16), 0))


def ways_of(passed, shares, x, edge):
    lane = iota(passed.shape, 1)
    last = passed.shape[1] - 1
    above = jnp.where(lane == last, edge, pltpu.roll(passed * shares[1, x], last, 1))
    below = jnp.where(lane == 0, edge, pltpu.roll(passed * shares[2, x], 1, 1))
    return passed * shares[0, x], above, below, passed * shares[3, x]


def entries_of(passed, shares, x, edge):
    own, above, below, deeper = ways_of(passed, shares, x, edge)
    return own + above + below, deeper


def add_records(rows_of, tile_of, place, cell, received, sums, counts, sums_strip, counts_strip):
    width_x, quakes, width_y = sums.shape
    last = tile_of
    span_y = place[2]
    lane = iota((quakes, width_y), 1)
    column = iota((width_y, width_y), 0)
    strip_column = iota((8, width_y), 0)
    strip_column = jnp.where(strip_column == 3, -1, jnp.where(strip_column == 4, width_y, -2))
    share = width_y // rows_of
    dims = (((1,), (1,)), ((), ()))
    one_x = iota((width_x, width_y), 0)
    parts = [[], [], []]
    at, at_rows, at_strip = [], [], []
    for chunk in range(cell.shape[0]):
        records = jnp.zeros((quakes, width_y), jnp.float32)
        for part in range(share):
            piece = received[chunk * share + part, last]
            moved = pltpu.roll(piece, part * rows_of, 1) if part else piece
            records = jnp.where(lane // rows_of == part, moved, records)
        cells = cell[chunk : chunk + 1, :]
        station_x = lax.shift_right_logical(cells, place[7]) - place[0]
        station_y = (cells & (span_y - 1)) - place[1]
        at_x = (one_x == jnp.broadcast_to(station_x, one_x.shape)).astype(jnp.float32)
        pieces = [p.astype(jnp.float32) for p in exact_parts(records)]
        for out, piece in zip(parts, pieces):
            spread = [piece * jnp.broadcast_to(at_x[x : x + 1], piece.shape) for x in range(width_x)]
            out.append(jnp.concatenate(spread, 0).astype(jnp.bfloat16))
        at_rows.append(at_x.astype(jnp.bfloat16))
        hit = column == jnp.broadcast_to(station_y, column.shape)
        at.append(hit.astype(jnp.float32).astype(jnp.bfloat16))
        hit = strip_column == jnp.broadcast_to(station_y, strip_column.shape)
        at_strip.append(hit.astype(jnp.float32).astype(jnp.bfloat16))
    at = jnp.concatenate(at, 1)
    at_rows = jnp.concatenate(at_rows, 1)
    at_strip = jnp.concatenate(at_strip, 1)
    parts = [jnp.concatenate(p, 1) for p in parts]

    def product(a, b):
        return lax.dot_general(a, b, dims, preferred_element_type=jnp.float32)

    main = [product(p, at) for p in parts]
    sums[...] = (main[0] + main[1] + main[2]).reshape(sums.shape)
    counts[...] = product(at_rows, at)
    sums_strip[...] = product(at_strip, parts[0]) + product(at_strip, parts[1]) + product(at_strip, parts[2])
    spread = ((iota((width_x, width_y), 1) >> 3) == one_x).astype(jnp.float32).astype(jnp.bfloat16)
    tally = 0.0
    for part in reversed(exact_parts(product(at_strip, at_rows))):
        tally += lax.dot_general(part, spread, (((1,), (0,)), ((), ())), preferred_element_type=jnp.float32)
    counts_strip[...] = tally


def times_kernel(local, times):
    width_x, depth, quakes, _ = local.shape

    def step(x, carry):
        for z in range(depth):
            times[pl.ds(z * width_x + x, quakes, stride=depth * width_x), :] = local[x, z] * (1.0 / RATE)
        return carry

    by_steps(width_x, step, 0)


def kernel_kernel(
    place, received, shares, slopes, keeps, misfits, edges_own, edges_factor, slopes_one, gains, anisotropy, kernel,
    entries, top, sent,
):
    width_x, quakes, width_y = slopes.shape
    tile = (quakes, width_y)
    near = slopes_one.shape[1]
    count = received.shape[0]
    lane = iota(tile, 1)
    last = width_y - 1
    me = place[6]
    zero = jnp.zeros(tile, jnp.float32)
    group = width_y // 8
    state, strip, mine, mine_strip = zero, zero, zero, zero
    carries = []
    for device in range(count):
        carries.append(state)
        mine = jnp.where(device == me, state, mine)
        at = device % group
        moved = pltpu.roll(strip, 8 * at, 1) if at else strip
        sent[device // group] = moved if at == 0 else jnp.where((lane >> 3) == at, moved, sent[device // group])
        both = received[device, 2]
        state = received[device, 0] + received[device, 1] * state
        strip = both + shifted_down(both, 2) * strip
    ends = [end_columns(sent[i]) for i in range(sent.shape[0])]
    state = [zero] * near
    mine_edge = zero
    for device in reversed(range(count)):
        at = 8 * (device % group)
        edge = ends[device // group][at : at + 8]
        mine_edge = jnp.where(device == me, edge, mine_edge)
        carry = carries[device]
        block = [received[device, 3 + z] for z in range(near)]
        above = jnp.where(lane == last, edge, pltpu.roll(carry, last, 1))
        below = jnp.where(lane == 0, edge, pltpu.roll(carry, 1, 1))
        link = [received[device, 3 + 2 * near + i] for i in range(4)]
        block[0] = block[0] + link[0] * carry + link[1] * above + link[2] * below
        block[1] = block[1] + link[3] * carry
        for z in range(near):
            passed = block[z] + received[device, 3 + near + z] * state[z]
            state[z] = jnp.where(device > me, passed, state[z])
    carry = mine
    for x in range(width_x):
        total = misfits[x] + carry
        carry = slopes[x] * total
        passed = keeps[x] * total
        sideways = row(anisotropy, near, x, tile) * (shares[1, x] + shares[2, x])
        sideways = sideways + row(anisotropy, 2 * near, x, tile) * shares[3, x]
        terms = carry * row(anisotropy, 0, x, tile) + passed * sideways
        top[x : x + 1, :] = jnp.sum(terms, axis=0, keepdims=True)
        entry = entries_of(passed, shares, x, edges_own[x] + edges_factor[x] * mine_edge)
        for z in range(near):
            entries[x, z] = entry[z]
    for x in reversed(range(width_x)):
        for z in range(near):
            total = entries[x, z] + state[z]
            state[z] = slopes_one[x, z] * total
            value = jnp.sum(total * gains[x, z], axis=0, keepdims=True)
            if z == 0:
                value = value + top[x : x + 1, :]
            kernel[z, x : x + 1, :] = value
    for z in range(near, kernel.shape[0]):
        kernel[z] = jnp.zeros(kernel.shape[1:], jnp.float32)


def call(kernel, shapes, operands, scratch=(), scalars=0, far=0, last=False, aliases=()):
    many = isinstance(shapes, list)
    shapes = shapes if many else [shapes]
    out = [jax.ShapeDtypeStruct(s, jnp.float32) if last else pltpu.VMEM(s, jnp.float32) for s in shapes]
    result = pl.pallas_call(
        kernel,
        out_shape=out,
        in_specs=[SMEM] * scalars + [FAR] * far + [VMEM] * (len(operands) - scalars - far),
        out_specs=[VMEM] * len(out),
        scratch_shapes=[pltpu.VMEM(s, jnp.float32) if isinstance(s, tuple) else s for s in scratch],
        compiler_params=PARAMS,
        input_output_aliases=dict(aliases),
    )(*operands)
    return result if many else result[0]


def traded(message):
    return lax.all_to_all(message, "gx", 0, 0, tiled=True)


def rotated(value, axis, by):
    count = lax.axis_size(axis)
    return lax.ppermute(value, axis, [(i, (i + by) % count) for i in range(count)])


def body(warm_start, slowness, anisotropy, observed, station_cell, source_cell):
    quakes, depth, width_x, width_y = warm_start.shape
    count_x, count_y = lax.axis_size("gx"), lax.axis_size("gy")
    index_x, index_y = lax.axis_index("gx"), lax.axis_index("gy")
    span_x, span_y = width_x * count_x, width_y * count_y
    near = 2
    per = max(1, depth // count_x)
    tile = (quakes, width_y)
    top = (width_x,) + tile
    close = (width_x, near) + tile
    field = (width_x, depth) + tile
    place = jnp.stack(
        [
            index_x * width_x,
            index_y * width_y,
            jnp.int32(span_y),
            jnp.int32(span_x * span_y),
            (index_y == 0).astype(jnp.int32),
            (index_y == count_y - 1).astype(jnp.int32),
            index_x,
            jnp.int32(span_y.bit_length() - 1),
            index_y,
        ]
    ).astype(jnp.int32)
    anis = anisotropy.reshape(3 * depth, width_x, width_y)
    local_records = observed.shape[1]
    flat = (quakes * depth * width_x, width_y)

    base = width_x * 11
    sources = [warm_start.reshape(quakes, depth * width_x, width_y), observed, slowness, anis]
    sources = [pltpu.with_memory_space_constraint(a, pltpu.HBM) for a in [source_cell] + sources]
    start, costs, anis, edge, records = call(
        pack_kernel,
        [field, anis.shape, (3 * near, width_x, width_y), (base + quakes, width_y), tile],
        [place] + sources,
        [pltpu.SMEM((quakes,), jnp.int32), (CHUNKS, quakes, depth // CHUNKS * width_x, width_y)]
        + [a.shape for a in sources[2:]]
        + [pltpu.SemaphoreType.DMA((4 + CHUNKS,))],
        scalars=1,
        far=5,
    )
    from_left = rotated(edge, "gy", 1)
    from_right = rotated(edge, "gy", -1)
    others = [rotated(records, "gy", by) for by in range(2, count_y - 1)]

    message_shape = (count_x, 3 * per + (4 if per > 1 else 5)) + tile
    first, first_strip, edge_costs, levels_one, sides, sums, message = call(
        functools.partial(first_sweep_kernel, local_records, count_y),
        [field, (width_x, 2) + tile, (6,) + top, close, close, (depth, width_x, width_y), message_shape],
        [place, start, edge, from_left, from_right, costs, anis] + others,
        [(depth,) + tile, (width_x, 2) + tile],
        scalars=1,
    )
    reach = traded(message)
    group = width_y // 8
    entering, entering_strips, *recorded = call(
        functools.partial(blocks_kernel, per, depth, local_records * count_y),
        [(count_x, 2 * per) + tile, (2,) + tile, top, (width_x, width_y), tile, tile],
        [place, station_cell.reshape(-1, width_y), reach],
        [(-(-count_x // group), depth) + tile],
        scalars=1,
    )
    entering = traded(entering)
    second, *rest, message = call(
        second_sweep_kernel,
        [field, (4,) + top] + [top] * 5 + [close, close, (count_x, 7 + 2 * near) + tile],
        [place, first, first_strip, entering, entering_strips, costs, sums, edge_costs, anis, levels_one, sides]
        + recorded,
        [(width_x, 2) + tile, (depth,) + tile] + [top] * 4,
        scalars=1,
        aliases={1: 0},
    )
    received = traded(message)
    times = call(times_kernel, flat, [second], last=True)
    kernel = call(
        kernel_kernel,
        (depth, width_x, width_y),
        [place, received] + rest + [anis],
        [close, (width_x, width_y), (-(-count_x // group),) + tile],
        scalars=1,
        last=True,
    )
    return (times.reshape(warm_start.shape), kernel)


def solution(mesh):
    return jax.shard_map(
        body,
        mesh=mesh,
        in_specs=(
            P(None, None, "gx", "gy"),
            P(None, "gx", "gy"),
            P(None, None, "gx", "gy"),
            P(None, ("gx", "gy")),
            P(),
            P(),
        ),
        out_specs=(P(None, None, "gx", "gy"), P(None, "gx", "gy")),
        check_vma=False,
    )
```

```python
import functools
import math

import jax
import jax.numpy as jnp
from jax import lax
from jax.experimental import pallas as pl
from jax.experimental.pallas import tpu as pltpu
from jax.sharding import PartitionSpec as P

TAU = 0.05
ADJ_SCALE = 0.1
LOG2E = math.log2(math.e)
RATE = LOG2E / TAU
BIG = 10000.0 * RATE
UNROLL = 8
CHUNKS = 4
VMEM = pl.BlockSpec(memory_space=pltpu.VMEM)
FAR = pl.BlockSpec(memory_space=pl.ANY)
SMEM = pl.BlockSpec(memory_space=pltpu.SMEM)
PARAMS = pltpu.CompilerParams(vmem_limit_bytes=8 * 1024 * 1024)


def softmin(values):
    least = functools.reduce(jnp.minimum, values)
    parts = [jnp.exp2(least - v) for v in values]
    return least, parts, functools.reduce(jnp.add, parts)


def soft_pair(first, second):
    return jnp.minimum(first, second) - LOG2E * jnp.log(1.0 + jnp.exp2(-jnp.abs(first - second)))


def add_pair(least, total, passed):
    low = jnp.minimum(least, passed)
    return low - LOG2E * jnp.log(total * jnp.exp2(low - least) + jnp.exp2(low - passed))


def join_pairs(first, second):
    low = jnp.minimum(first[0], second[0])
    return low, first[1] * jnp.exp2(low - first[0]) + second[1] * jnp.exp2(low - second[0])


def value_of(pair):
    return pair[0] - LOG2E * jnp.log(pair[1])


def split_pair(first, second):
    gap = jnp.exp2(-jnp.abs(first - second))
    share = 1.0 / (1.0 + gap)
    less = gap * share
    nearer = first <= second
    return jnp.where(nearer, share, less), jnp.where(nearer, less, share)


def iota(shape, axis):
    return lax.broadcasted_iota(jnp.int32, shape, axis)


def row(ref, index, x, like):
    return jnp.broadcast_to(ref[index, pl.ds(x, 1), :], like)


def row_of(ref, x, like):
    return jnp.broadcast_to(ref[pl.ds(x, 1), :], like)


def all_steps(count, step, carry):
    for i in range(count):
        carry = step(i, carry)
    return carry


def by_steps(count, step, carry):
    def group(i, carry):
        for j in range(UNROLL):
            carry = step(i * UNROLL + j, carry)
        return carry

    return lax.fori_loop(0, count // UNROLL, group, carry)


def packed(left, right):
    return jnp.where(iota(left.shape, 0) < 5, left, pltpu.roll(right, 2, 0))


def merged(left, right):
    return jnp.where(iota(left.shape, 0) < 4, left, right)


def shifted_down(tile, by):
    return pltpu.roll(tile, tile.shape[0] - by, 0)


def exact_parts(value):
    high = value.astype(jnp.bfloat16).astype(jnp.float32)
    middle = (value - high).astype(jnp.bfloat16).astype(jnp.float32)
    low = value - high - middle
    return [p.astype(jnp.bfloat16) for p in (high, middle, low)]


def pack_kernel(
    place, source_far, warm_far, observed_far, slowness_far, anisotropy_far, start, costs, near, edge, to_right, to_left, records,
    source, warm, observed, slowness, anisotropy, arrived,
):
    pairs = [(slowness_far, slowness), (anisotropy_far, anisotropy), (observed_far, observed)]
    share = start.shape[1] // CHUNKS
    span = share * start.shape[0]
    pairs += [(warm_far.at[:, pl.ds(i * span, span)], warm.at[i]) for i in range(CHUNKS)]
    pairs += [(source_far, source)]
    copies = [pltpu.make_async_copy(a, b, arrived.at[i]) for i, (a, b) in enumerate(pairs)]
    for copy in copies:
        copy.start()
    width_x, depth, quakes, width_y = start.shape
    tile = (quakes, width_y)
    quake = iota(tile, 0)
    lane = iota(tile, 1)
    span_y = place[2]
    plane = place[3]
    rows = width_x * 8
    wide = (width_x, width_y)
    group = iota(wide, 1) >> 3
    copies[0].wait()
    copies[1].wait()
    native = []
    for k in range(3):
        columns = jnp.zeros(wide, jnp.float32)
        for z in range(depth):
            cost = slowness[z] * anisotropy[k * depth + z] * RATE
            costs[k * depth + z] = cost
            columns = jnp.where(group == z, pltpu.roll(cost, 8 * z + 4, 1), columns)
        edge[rows : rows + width_x, :] = columns
        rows += width_x
        native.append(columns)
        for z in range(near.shape[0] // 3):
            near[k * (near.shape[0] // 3) + z] = anisotropy[k * depth + z]
    early = (iota(wide, 1) & 7) < 4
    at = slice(4 * width_x, 5 * width_x)
    to_right[at, :] = jnp.where(early, native[0], pltpu.roll(native[1], 4, 1))
    to_left[at, :] = jnp.where(early, pltpu.roll(native[1], width_y - 4, 1), native[0])
    at = slice(5 * width_x, 6 * width_x)
    to_right[at, :] = native[2]
    to_left[at, :] = native[2]
    copies[-1].wait()
    cell = jnp.zeros(tile, jnp.int32)
    for e in range(quakes):
        cell = jnp.where(quake == e, source[e], cell)
    cell = cell - (lane + place[0] * span_y + place[1])
    edges = []
    for i in range(CHUNKS):
        copies[3 + i].wait()
        here = warm.at[i].reshape(quakes * share * width_x, width_y)

        chunk = [jnp.zeros(tile, jnp.float32)] * share
        for x in range(width_x):
            mine = (lane >> 3) == x
            for k in range(share):
                value = here[pl.ds(k * width_x + x, quakes, stride=share * width_x), :] * RATE
                value = jnp.where(cell == (i * share + k) * plane + x * span_y, 0.0, value)
                start[x, i * share + k] = value
                chunk[k] = jnp.where(mine, pltpu.roll(value, (8 * x + 4) % width_y, 1), chunk[k])
        edges += chunk
    columns = jnp.transpose(jnp.concatenate(edges, 0))
    edge[: width_x * 8, :] = columns
    low = quake < 4
    for x in range(0, width_x, 2):
        one, two = columns[8 * x : 8 * x + 8], columns[8 * x + 8 : 8 * x + 16]
        to_right[4 * x : 4 * x + 8, :] = jnp.where(low, one, pltpu.roll(two, 4, 0))
        to_left[4 * x : 4 * x + 8, :] = jnp.where(low, pltpu.roll(one, 4, 0), two)
    copies[2].wait()
    records[...] = jnp.zeros(tile, jnp.float32)
    records[:, : observed.shape[1]] = observed[...]
    for message in (to_right, to_left):
        message[6 * width_x :, :] = records[...]


def halo_columns(left, right):
    rows = []
    for l, r in zip(left, right):
        rows.append(jnp.where(iota(l.shape, 0) == 4, r, pltpu.roll(l, 2, 0)))
    return jnp.transpose(jnp.concatenate(rows, 0))


def cost_columns(message, width_x, turn):
    pair = message[4 * width_x : 5 * width_x, :]
    return [pair, pltpu.roll(pair, turn, 1), message[5 * width_x : 6 * width_x, :]]


def strip_costs(own, from_left, from_right, out, width_x, depth):
    tile = own.shape[1]
    base = width_x * 8
    lane = iota((8, tile), 1)
    low = (lane & 7) < 4
    mine = (lane & 7) == iota((8, tile), 0)
    spread = ((iota((tile, tile), 0) >> 3) == (iota((tile, tile), 1) >> 3)).astype(jnp.float32)
    spread = spread.astype(jnp.bfloat16)
    for side in range(2):
        for k in range(3):
            rows = []
            for x in range(width_x):
                at = slice(base + k * width_x + x, base + k * width_x + x + 1)
                here = jnp.broadcast_to(own[at, :], lane.shape)
                there = jnp.broadcast_to((from_right if side else from_left)[k][x : x + 1], lane.shape)
                value = jnp.where(low, here, there) if side else jnp.where(low, there, here)
                rows.append(jnp.where(mine, value, 0.0))
            whole = jnp.concatenate(rows, 0)
            total = 0.0
            for part in reversed(exact_parts(whole)):
                total = total + lax.dot_general(
                    part, spread, (((1,), (0,)), ((), ())), preferred_element_type=jnp.float32
                )
            out[3 * side + k] = total.reshape(width_x, 8, tile)


def running_sum(value):
    rows = iota(value.shape, 0)
    by = 1
    while by < value.shape[0]:
        value = value + jnp.where(rows >= by, pltpu.roll(value, by, 0), 0.0)
        by *= 2
    return value


def log_sum(exponents):
    return -LOG2E * jnp.log(functools.reduce(jnp.add, [jnp.exp2(-e) for e in exponents]))


def passages(costs, from_left, from_right, depth):
    width_x, width_y = costs.shape[1:]
    lane = iota((width_x, width_y), 1)
    beside = jnp.where((lane & 7) == 4, running_sum(from_right), pltpu.roll(running_sum(from_left), 2, 1))
    sums = [running_sum(costs[z]) for z in range(depth)]
    sub = iota((8, width_y), 0)
    tiles = []
    for z in range(depth):
        back = sums[z] - costs[z]
        edge = pltpu.roll(beside, width_y - 5 - 8 * z, 1)
        below = jnp.where(lane == 0, edge, pltpu.roll(sums[z], 1, 1))
        above = jnp.where(lane == width_y - 1, edge, pltpu.roll(sums[z], width_y - 1, 1))
        step_y = back + costs[depth + z]
        step_z = back + costs[2 * depth + z]
        paths = [sums[z] + back, below + step_y, above + step_y]
        paths.append(sums[z - 1] + step_z if z > 0 else None)
        paths.append(sums[z + 1] + step_z if z < depth - 1 else None)
        tile = jnp.broadcast_to(sums[z][width_x - 1 :, :], sub.shape)
        for j, path in enumerate(paths):
            if path is None:
                tile = jnp.where(sub == j + 1, BIG, tile)
            else:
                total = jnp.sum(jnp.exp2(-path), axis=0, keepdims=True)
                tile = jnp.where(sub == j + 1, -LOG2E * jnp.log(total), tile)
        tiles.append(tile)
    return tiles


def strip_passages(edge_costs, width_x):
    shape = edge_costs.shape[2:]
    lane = iota(shape, 1)
    sums = jnp.zeros(shape, jnp.float32)
    totals = [jnp.zeros(shape, jnp.float32)] * 5
    for x in range(width_x):
        cost, step_y, step_z = [packed(edge_costs[k, x], edge_costs[3 + k, x]) for k in range(3)]
        back = sums
        sums = sums + cost
        step_y, step_z = step_y + back, step_z + back
        paths = [sums + back, pltpu.roll(sums, 1, 0) + step_y, shifted_down(sums, 1) + step_y]
        paths.append(jnp.where(lane < 8, BIG, pltpu.roll(sums, 8, 1) + step_z))
        paths.append(jnp.where(lane >= shape[1] - 8, BIG, pltpu.roll(sums, shape[1] - 8, 1) + step_z))
        totals = [t + jnp.exp2(-p) for t, p in zip(totals, paths)]
    return sums, [-LOG2E * jnp.log(jnp.maximum(t, 1e-37)) for t in totals]


def shared_rows(total, paths):
    place = iota(total.shape, 1) & 7
    first, second = total, total
    for q in range(6):
        value = pltpu.roll(total, (4 - q) % 8, 0)
        first = jnp.where(place == q, value, first)
    for q, (path, at) in enumerate([(p, r) for p in paths for r in (3, 6)]):
        if q < 2:
            first = jnp.where(place == 6 + q, pltpu.roll(path, (6 - at) % 8, 0), first)
        else:
            second = jnp.where(place == q - 2, pltpu.roll(path, (7 - at) % 8, 0), second)
    return jnp.where(iota(total.shape, 0) == 6, first, second)


def spread_rows(tiles):
    shape = tiles[0].shape
    wide = shape[1]
    sub = iota(shape, 0)
    mine = (iota(shape, 1) & 7) == sub
    spread = ((iota((wide, wide), 0) >> 3) == (iota((wide, wide), 1) >> 3)).astype(jnp.float32)
    spread = spread.astype(jnp.bfloat16)
    rows = [jnp.where(mine, jnp.broadcast_to(t[r : r + 1], shape), 0.0) for t in tiles for r in (6, 7)]
    whole = jnp.concatenate(rows, 0)
    value = 0.0
    for part in reversed(exact_parts(whole)):
        value = value + lax.dot_general(part, spread, (((1,), (0,)), ((), ())), preferred_element_type=jnp.float32)
    out = []
    for i in range(len(tiles)):
        first, second = value[16 * i : 16 * i + 8], value[16 * i + 8 : 16 * i + 16]
        paths = [jnp.where(sub == 3, pltpu.roll(first, 5, 0), pltpu.roll(first, 7, 0))]
        for q in range(4):
            at_three = pltpu.roll(second, (3 - 2 * q) % 8, 0)
            at_six = pltpu.roll(second, (6 - 2 * q - 1) % 8, 0)
            paths.append(jnp.where(sub == 3, at_three, at_six))
        out.append((pltpu.roll(first, 2, 0), paths))
    return out


def sweep_step(x, near, field, strip, costs, edge_costs, halo, state, strip_state, keep, keep_strip):
    depth = field.shape[1]
    tile = field.shape[2:]
    width_y = tile[1]
    lane = iota(tile, 1)
    out = []
    for z in range(depth):
        u = field[x, z]
        cost_y = row(costs, depth + z, x, tile)
        cost_z = row(costs, 2 * depth + z, x, tile)
        edge = pltpu.roll(halo[z], width_y - 5 - 8 * x, 1)
        values = [u]
        values.append(jnp.where(lane == 0, edge, pltpu.roll(u, 1, 1)) + cost_y)
        values.append(jnp.where(lane == width_y - 1, edge, pltpu.roll(u, width_y - 1, 1)) + cost_y)
        if z > 0:
            values.append(field[x, z - 1] + cost_z)
        if z < depth - 1:
            values.append(field[x, z + 1] + cost_z)
        least, parts, total = softmin(values)
        passed = state[z] + row(costs, z, x, tile)
        if z < near:
            scale = 1.0 / total
            keep(x, z, value_of((least, total)), [p * scale for p in parts], passed)
        out.append(add_pair(least, total, passed))
    strips, levels, weights, passes = [], [], [], []
    for side in range(2):
        u = strip[x, side]
        cost_y = edge_costs[3 * side + 1, x]
        cost_z = edge_costs[3 * side + 2, x]
        values = [u, pltpu.roll(u, 1, 0) + cost_y, pltpu.roll(u, 7, 0) + cost_y]
        values.append(jnp.where(lane < 8, BIG, pltpu.roll(u, 8, 1)) + cost_z)
        values.append(jnp.where(lane >= width_y - 8, BIG, pltpu.roll(u, width_y - 8, 1)) + cost_z)
        least, parts, total = softmin(values)
        passes.append(strip_state[side] + edge_costs[3 * side, x])
        strips.append(add_pair(least, total, passes[side]))
        if keep_strip is not None:
            levels.append(value_of((least, total)))
            weights.append(parts[2 - side] / total)
    if keep_strip is not None:
        keep_strip(x, merged(*levels), merged(*weights), merged(*passes), merged(*strips))
    return out, strips


def outside_strips(place, shape):
    sub = iota(shape, 0)
    return [(place[4] == 1) & (sub < 4), (place[5] == 1) & (sub >= 4)]


def first_sweep_kernel(
    rows_of, count_y, place, field, own, mine, from_left, from_right, costs, anisotropy, *rest
):
    others = rest[: count_y - 3]
    local, local_strip, edge_costs, levels, sides, message, halo, strip = rest[count_y - 3 :]
    width_x, depth, quakes, width_y = field.shape
    tile = (quakes, width_y)
    sub = iota(tile, 0)
    low = sub < 4
    near = levels.shape[1]
    last = 6 * width_x
    far = [mine[...], from_left[last:, :]] + [o[...] for o in others] + [from_right[last:, :]]
    records = jnp.zeros(tile, jnp.float32)
    for by, piece in enumerate(far):
        owner = lax.rem(place[8] + count_y - by, count_y)
        records = records + pltpu.roll(piece, owner * rows_of, 1)
    left, right = [], []
    for x in range(width_x):
        at = slice(8 * x, 8 * x + 8)
        two = slice(8 * (x // 2), 8 * (x // 2) + 8)
        before, after = from_left[two, :], from_right[two, :]
        if x % 2:
            before = pltpu.roll(before, 4, 0)
        else:
            after = pltpu.roll(after, 4, 0)
        before = jnp.where(place[4] == 1, BIG, before)
        after = jnp.where(place[5] == 1, BIG, after)
        left.append(jnp.where(low, before, own[at, :]))
        right.append(jnp.where(low, own[at, :], after))
        strip[x, 0] = left[x]
        strip[x, 1] = right[x]
    halo[...] = halo_columns(left, right).reshape(halo.shape)
    left_costs = cost_columns(from_left, width_x, width_y - 4)
    right_costs = cost_columns(from_right, width_x, 4)
    strip_costs(own, left_costs, right_costs, edge_costs, width_x, depth)
    outside = outside_strips(place, tile)

    def keep(x, z, level, w, passed):
        levels[x, z] = level
        vertical = w[3] if z == 0 else w[3] + w[4]
        sideways = row(anisotropy, near + z, x, tile) * (w[1] + w[2])
        sides[x, z] = sideways + row(anisotropy, 2 * near + z, x, tile) * vertical

    def step(x, carry):
        state, strips = sweep_step(x, near, field, strip, costs, edge_costs, halo, *carry, keep, None)
        for z in range(depth):
            local[x, z] = state[z]
        for side in range(2):
            local_strip[x, side] = jnp.where(outside[side], BIG, strips[side])
        return state, strips

    blank = jnp.full(tile, BIG, jnp.float32)
    state, strips = all_steps(width_x, step, ([blank] * depth, [blank] * 2))
    reach_strip = packed(*[jnp.where(o, BIG, s) for o, s in zip(outside, strips)])

    edges = [[local_strip[x, side] for x in range(width_x)] for side in range(2)]
    halo[...] = halo_columns(*edges).reshape(halo.shape)

    def again(lap, carry):
        x = width_x - 1 - lap
        return sweep_step(x, 0, local, local_strip, costs, edge_costs, halo, *carry, None, None)

    back, back_strips = all_steps(width_x, again, ([blank] * depth, [blank] * 2))
    tiles = passages(costs, left_costs[0], right_costs[0], depth)
    strip_total, strip_paths = strip_passages(edge_costs, width_x)

    back_strip = packed(*back_strips)
    reach_strip = jnp.where(sub == 0, shifted_down(back_strip, 3), reach_strip)
    reach_strip = jnp.where(sub == 1, shifted_down(back_strip, 5), reach_strip)
    shared = shared_rows(strip_total, strip_paths)
    count = message.shape[0]
    per = message.shape[1] // 3 - 1
    for p in range(count):
        first = min(p * per, depth - per)
        for k in range(per + 2):
            z = first + k - 1
            message[p, k] = state[z] if 0 <= z < depth else blank
        for k in range(per):
            message[p, per + 2 + k] = back[first + k]
            value = tiles[first + k]
            if k == 0 and first > 0:
                value = jnp.where(sub == 6, jnp.broadcast_to(tiles[first - 1][:1], tile), value)
            if k == 0 and first + per < depth:
                value = jnp.where(sub == 7, jnp.broadcast_to(tiles[first + per][:1], tile), value)
            if per > 1 and k == 1:
                value = jnp.where(sub < 6, value, shared)
            message[p, 2 * per + 2 + k] = value
        message[p, 3 * per + 2] = reach_strip
        message[p, 3 * per + 3] = records
        if per == 1:
            message[p, 3 * per + 4] = shared


def blocks_kernel(
    per, depth, rows_of, place, cell, received, entering, entering_strips, sums, counts, sums_strip, counts_strip, halo,
):
    count = received.shape[0]
    tile = entering.shape[2:]
    lane = iota(tile, 1)
    width_y = tile[1]
    me = place[6]
    blank = jnp.full(tile, BIG, jnp.float32)
    unit = jnp.ones(tile, jnp.float32)
    side = 3 * per + 2

    def rows(device, k, j):
        return jnp.broadcast_to(received[device, 2 * per + 2 + k, j : j + 1, :], tile)

    def total(device, k):
        if k < 0:
            return rows(device, 0, 6)
        return rows(device, k, 0) if k < per else rows(device, 0, 7)

    def further(pair, cost):
        return pair[0] + cost, pair[1]

    shared = [received[d, 2 * per + 3] if per > 1 else received[d, 3 * per + 4] for d in range(count)]
    shared = spread_rows(shared)
    state = [(blank, unit)] * (per + 2)
    strip = (blank, unit)
    first, first_strip = [], []
    for device in range(count):
        first.append([value_of(pair) for pair in state])
        first_strip.append(value_of(strip))
        state = [
            join_pairs((received[device, k], unit), further(state[k], total(device, k - 1))) for k in range(per + 2)
        ]
        strip = join_pairs((received[device, side], unit), further(strip, shared[device][0]))
    own = blank
    for device in range(count):
        own = jnp.where(device == me, first_strip[device], own)
        for k in range(per):
            entering[device, k] = first[device][k + 1]
    entering_strips[0] = own
    group = width_y // 8
    for at in range(0, count, group):
        some = first_strip[at : at + group]
        some = some + [blank] * (group - len(some))
        turned = halo_columns(some, [shifted_down(s, 2) for s in some])
        halo[at // group] = turned.reshape(halo.shape[1:])
    low = jnp.minimum(me * per, depth - per)
    edges = [[halo[i, low + k] for k in range(per)] for i in range(halo.shape[0])]
    state = [(blank, unit)] * per
    strip = (blank, unit)
    for device in reversed(range(count)):
        for k in range(per):
            entering[device, per + k] = value_of(state[k])
            u = first[device][k + 1]
            turn = (width_y - 5 - 8 * (device % group)) % width_y
            edge = pltpu.roll(edges[device // group][k], turn, 1)
            values = [received[device, per + 2 + k], u + rows(device, k, 1)]
            values.append(jnp.where(lane == 0, edge, pltpu.roll(u, 1, 1)) + rows(device, k, 2))
            values.append(jnp.where(lane == width_y - 1, edge, pltpu.roll(u, width_y - 1, 1)) + rows(device, k, 3))
            values.append(first[device][k] + rows(device, k, 4))
            values.append(first[device][k + 2] + rows(device, k, 5))
            least, _, amount = softmin(values)
            state[k] = join_pairs((least, amount), further(state[k], total(device, k)))
        u = first_strip[device]
        back = received[device, side]
        back = jnp.where(iota(tile, 0) == 3, pltpu.roll(back, 3, 0), pltpu.roll(back, 5, 0))
        paths = shared[device][1]
        values = [back, u + paths[0], pltpu.roll(u, 1, 0) + paths[1], shifted_down(u, 1) + paths[2]]
        values.append(jnp.where(lane < 8, BIG, pltpu.roll(u, 8, 1)) + paths[3])
        values.append(jnp.where(lane >= width_y - 8, BIG, pltpu.roll(u, width_y - 8, 1)) + paths[4])
        least, _, amount = softmin(values)
        passed = join_pairs((least, amount), further(strip, shared[device][0]))
        strip = [jnp.where(device > me, new, old) for new, old in zip(passed, strip)]
    entering_strips[1] = value_of(strip)
    add_records(rows_of, 3 * per + 3, place, cell, received, sums, counts, sums_strip, counts_strip)


def second_sweep_kernel(
    place, first, first_strip, entering, entering_strips, costs, edge_costs, anisotropy, levels_one, sides,
    sums, counts, sums_strip, counts_strip,
    local, shares, slopes, keeps, misfits, edges_own, edges_factor, slopes_one, gains, message,
    field, strip, halo, shares_strip, slopes_strip, keeps_strip, misfits_strip,
):
    width_x, depth, quakes, width_y = first.shape
    tile = (quakes, width_y)
    near = levels_one.shape[1]
    per = entering.shape[1] // 2
    outside = outside_strips(place, tile)
    strips_in = [[s, shifted_down(s, 2)] for s in (entering_strips[0], entering_strips[1])]
    carried = [[entering[z // per, k * per + z % per] for z in range(depth)] for k in range(2)]

    def finish(x, carry):
        running, strip_running, prior = carry
        sums_now, values = [], []
        for z in range(depth):
            cost = row(costs, z, x, tile)
            sums_now.append(running[z] + cost)
            value = soft_pair(first[x, z], entering[z // per, z % per] + sums_now[z])
            field[x, z] = value
            if z < near:
                values.append(value)
                keep, slope = split_pair(levels_one[x, z], prior[z] + cost)
                slopes_one[x, z] = slope
                gains[x, z] = slope * row(anisotropy, z, x, tile) + keep * sides[x, z]
        strip_sums = []
        for side in range(2):
            strip_sums.append(strip_running[side] + edge_costs[3 * side, x])
            value = soft_pair(first_strip[x, side], strips_in[0][side] + strip_sums[side])
            strip[x, side] = jnp.where(outside[side], BIG, value)
        return sums_now, strip_sums, values

    blank = jnp.zeros(tile, jnp.float32)
    all_steps(width_x, finish, ([blank] * depth, [blank] * 2, carried[0][:near]))
    edges = [[strip[x, side] for x in range(width_x)] for side in range(2)]
    halo[...] = halo_columns(*edges).reshape(halo.shape)

    def keep(x, z, level, w, passed):
        for i in range(4):
            shares[i, x] = w[i]
        keeps[x], slopes[x] = split_pair(level, passed)

    def keep_strip(x, level, w, passed, value):
        shares_strip[x] = w
        keeps_strip[x], slopes_strip[x] = split_pair(level, passed)
        tally = pltpu.roll(counts_strip[...], (width_y - 8 * x) % width_y, 1)
        total = pltpu.roll(sums_strip[...], (width_y - 8 * x) % width_y, 1)
        misfits_strip[x] = ADJ_SCALE * (tally * (value * (1.0 / RATE)) - total)

    def step(lap, carry):
        x = width_x - 1 - lap
        state, strips = sweep_step(x, 1, field, strip, costs, edge_costs, halo, *carry, keep, keep_strip)
        for z in range(depth):
            local[x, z] = state[z]
        misfits[x] = ADJ_SCALE * (row_of(counts, x, tile) * (state[0] * (1.0 / RATE)) - sums[x])
        return state, strips

    all_steps(width_x, step, (carried[1], strips_in[1]))
    zero, unit = jnp.zeros(tile, jnp.float32), jnp.ones(tile, jnp.float32)
    lane = iota(tile, 1)
    own, factor, strip_own, strip_factor = zero, unit, zero, unit
    owns, factors = [], []
    sent = [zero, zero]
    for x in range(width_x):
        own = misfits[x] + own
        owns.append(keeps[x] * own)
        factors.append(keeps[x] * factor)
        own, factor = slopes[x] * own, slopes[x] * factor
        strip_own = misfits_strip[x] + strip_own
        through = keeps_strip[x] * shares_strip[x]
        for i, value in enumerate((strip_own, strip_factor)):
            value = pltpu.roll(through * value, 8 * x, 1) if x else through * value
            sent[i] = jnp.where((lane >> 3) == x, value, sent[i])
        strip_own, strip_factor = slopes_strip[x] * strip_own, slopes_strip[x] * strip_factor
    edges_own[...] = end_columns(sent[0]).reshape(edges_own.shape)
    edges_factor[...] = end_columns(sent[1]).reshape(edges_factor.shape)
    chain = [unit] * near
    blocks = [zero] * near
    links = [zero] * 4
    for x in range(width_x):
        entry = entries_of(owns[x], shares, x, edges_own[x])
        for z in range(near):
            chain[z] = chain[z] * slopes_one[x, z]
            blocks[z] = blocks[z] + chain[z] * entry[z]
        for i, path in enumerate(ways_of(factors[x], shares, x, edges_factor[x])):
            links[i] = links[i] + chain[i // 3] * path
    both = jnp.where(iota(tile, 0) < 5, strip_own, pltpu.roll(strip_factor, 2, 0))
    tiles = [own, factor, both] + blocks + chain + links
    for p in range(message.shape[0]):
        for i, value in enumerate(tiles):
            message[p, i] = value


def end_columns(rows):
    wide = rows.shape[1]
    first, last = shifted_down(rows, 3), pltpu.roll(rows, 3, 0)
    return jnp.transpose(jnp.concatenate([first] * (wide // 16) + [last] * (wide // 16), 0))


def ways_of(passed, shares, x, edge):
    lane = iota(passed.shape, 1)
    last = passed.shape[1] - 1
    above = jnp.where(lane == last, edge, pltpu.roll(passed * shares[1, x], last, 1))
    below = jnp.where(lane == 0, edge, pltpu.roll(passed * shares[2, x], 1, 1))
    return passed * shares[0, x], above, below, passed * shares[3, x]


def entries_of(passed, shares, x, edge):
    own, above, below, deeper = ways_of(passed, shares, x, edge)
    return own + above + below, deeper


def add_records(rows_of, tile_of, place, cell, received, sums, counts, sums_strip, counts_strip):
    width_x, quakes, width_y = sums.shape
    last = tile_of
    span_y = place[2]
    lane = iota((quakes, width_y), 1)
    column = iota((width_y, width_y), 0)
    strip_column = iota((8, width_y), 0)
    strip_column = jnp.where(strip_column == 3, -1, jnp.where(strip_column == 4, width_y, -2))
    share = width_y // rows_of
    dims = (((1,), (1,)), ((), ()))
    one_x = iota((width_x, width_y), 0)
    parts = [[], [], []]
    at, at_rows, at_strip = [], [], []
    for chunk in range(cell.shape[0]):
        records = jnp.zeros((quakes, width_y), jnp.float32)
        for part in range(share):
            piece = received[chunk * share + part, last]
            moved = pltpu.roll(piece, part * rows_of, 1) if part else piece
            records = jnp.where(lane // rows_of == part, moved, records)
        cells = cell[chunk : chunk + 1, :]
        station_x = lax.shift_right_logical(cells, place[7]) - place[0]
        station_y = (cells & (span_y - 1)) - place[1]
        at_x = (one_x == jnp.broadcast_to(station_x, one_x.shape)).astype(jnp.float32)
        pieces = [p.astype(jnp.float32) for p in exact_parts(records)]
        for out, piece in zip(parts, pieces):
            spread = [piece * jnp.broadcast_to(at_x[x : x + 1], piece.shape) for x in range(width_x)]
            out.append(jnp.concatenate(spread, 0).astype(jnp.bfloat16))
        at_rows.append(at_x.astype(jnp.bfloat16))
        hit = column == jnp.broadcast_to(station_y, column.shape)
        at.append(hit.astype(jnp.float32).astype(jnp.bfloat16))
        hit = strip_column == jnp.broadcast_to(station_y, strip_column.shape)
        at_strip.append(hit.astype(jnp.float32).astype(jnp.bfloat16))
    at = jnp.concatenate(at, 1)
    at_rows = jnp.concatenate(at_rows, 1)
    at_strip = jnp.concatenate(at_strip, 1)
    parts = [jnp.concatenate(p, 1) for p in parts]

    def product(a, b):
        return lax.dot_general(a, b, dims, preferred_element_type=jnp.float32)

    main = [product(p, at) for p in parts]
    sums[...] = (main[0] + main[1] + main[2]).reshape(sums.shape)
    counts[...] = product(at_rows, at)
    sums_strip[...] = product(at_strip, parts[0]) + product(at_strip, parts[1]) + product(at_strip, parts[2])
    spread = ((iota((width_x, width_y), 1) >> 3) == one_x).astype(jnp.float32).astype(jnp.bfloat16)
    tally = 0.0
    for part in reversed(exact_parts(product(at_strip, at_rows))):
        tally += lax.dot_general(part, spread, (((1,), (0,)), ((), ())), preferred_element_type=jnp.float32)
    counts_strip[...] = tally


def times_kernel(local, times):
    width_x, depth, quakes, _ = local.shape

    def step(x, carry):
        for z in range(depth):
            times[pl.ds(z * width_x + x, quakes, stride=depth * width_x), :] = local[x, z] * (1.0 / RATE)
        return carry

    by_steps(width_x, step, 0)


def kernel_kernel(
    place, received, shares, slopes, keeps, misfits, edges_own, edges_factor, slopes_one, gains, anisotropy, kernel,
    entries, top, sent,
):
    width_x, quakes, width_y = slopes.shape
    tile = (quakes, width_y)
    near = slopes_one.shape[1]
    count = received.shape[0]
    lane = iota(tile, 1)
    last = width_y - 1
    me = place[6]
    zero = jnp.zeros(tile, jnp.float32)
    group = width_y // 8
    state, strip, mine, mine_strip = zero, zero, zero, zero
    carries = []
    for device in range(count):
        carries.append(state)
        mine = jnp.where(device == me, state, mine)
        at = device % group
        moved = pltpu.roll(strip, 8 * at, 1) if at else strip
        sent[device // group] = moved if at == 0 else jnp.where((lane >> 3) == at, moved, sent[device // group])
        both = received[device, 2]
        state = received[device, 0] + received[device, 1] * state
        strip = both + shifted_down(both, 2) * strip
    ends = [end_columns(sent[i]) for i in range(sent.shape[0])]
    state = [zero] * near
    mine_edge = zero
    for device in reversed(range(count)):
        at = 8 * (device % group)
        edge = ends[device // group][at : at + 8]
        mine_edge = jnp.where(device == me, edge, mine_edge)
        carry = carries[device]
        block = [received[device, 3 + z] for z in range(near)]
        above = jnp.where(lane == last, edge, pltpu.roll(carry, last, 1))
        below = jnp.where(lane == 0, edge, pltpu.roll(carry, 1, 1))
        link = [received[device, 3 + 2 * near + i] for i in range(4)]
        block[0] = block[0] + link[0] * carry + link[1] * above + link[2] * below
        block[1] = block[1] + link[3] * carry
        for z in range(near):
            passed = block[z] + received[device, 3 + near + z] * state[z]
            state[z] = jnp.where(device > me, passed, state[z])
    carry = mine
    for x in range(width_x):
        total = misfits[x] + carry
        carry = slopes[x] * total
        passed = keeps[x] * total
        sideways = row(anisotropy, near, x, tile) * (shares[1, x] + shares[2, x])
        sideways = sideways + row(anisotropy, 2 * near, x, tile) * shares[3, x]
        terms = carry * row(anisotropy, 0, x, tile) + passed * sideways
        top[x : x + 1, :] = jnp.sum(terms, axis=0, keepdims=True)
        entry = entries_of(passed, shares, x, edges_own[x] + edges_factor[x] * mine_edge)
        for z in range(near):
            entries[x, z] = entry[z]
    for x in reversed(range(width_x)):
        for z in range(near):
            total = entries[x, z] + state[z]
            state[z] = slopes_one[x, z] * total
            value = jnp.sum(total * gains[x, z], axis=0, keepdims=True)
            if z == 0:
                value = value + top[x : x + 1, :]
            kernel[z, x : x + 1, :] = value
    for z in range(near, kernel.shape[0]):
        kernel[z] = jnp.zeros(kernel.shape[1:], jnp.float32)


def call(kernel, shapes, operands, scratch=(), scalars=0, far=0, last=False, aliases=()):
    many = isinstance(shapes, list)
    shapes = shapes if many else [shapes]
    out = [jax.ShapeDtypeStruct(s, jnp.float32) if last else pltpu.VMEM(s, jnp.float32) for s in shapes]
    result = pl.pallas_call(
        kernel,
        out_shape=out,
        in_specs=[SMEM] * scalars + [FAR] * far + [VMEM] * (len(operands) - scalars - far),
        out_specs=[VMEM] * len(out),
        scratch_shapes=[pltpu.VMEM(s, jnp.float32) if isinstance(s, tuple) else s for s in scratch],
        compiler_params=PARAMS,
        input_output_aliases=dict(aliases),
    )(*operands)
    return result if many else result[0]


def traded(message):
    return lax.all_to_all(message, "gx", 0, 0, tiled=True)


def rotated(value, axis, by):
    count = lax.axis_size(axis)
    return lax.ppermute(value, axis, [(i, (i + by) % count) for i in range(count)])


def body(warm_start, slowness, anisotropy, observed, station_cell, source_cell):
    quakes, depth, width_x, width_y = warm_start.shape
    count_x, count_y = lax.axis_size("gx"), lax.axis_size("gy")
    index_x, index_y = lax.axis_index("gx"), lax.axis_index("gy")
    span_x, span_y = width_x * count_x, width_y * count_y
    near = 2
    per = max(1, depth // count_x)
    tile = (quakes, width_y)
    top = (width_x,) + tile
    close = (width_x, near) + tile
    field = (width_x, depth) + tile
    place = jnp.stack(
        [
            index_x * width_x,
            index_y * width_y,
            jnp.int32(span_y),
            jnp.int32(span_x * span_y),
            (index_y == 0).astype(jnp.int32),
            (index_y == count_y - 1).astype(jnp.int32),
            index_x,
            jnp.int32(span_y.bit_length() - 1),
            index_y,
        ]
    ).astype(jnp.int32)
    anis = anisotropy.reshape(3 * depth, width_x, width_y)
    local_records = observed.shape[1]
    flat = (quakes * depth * width_x, width_y)

    sources = [warm_start.reshape(quakes, depth * width_x, width_y), observed, slowness, anis]
    sources = [pltpu.with_memory_space_constraint(a, pltpu.HBM) for a in [source_cell] + sources]
    start, costs, anis, edge, to_right, to_left, records = call(
        pack_kernel,
        [field, anis.shape, (3 * near, width_x, width_y), (11 * width_x, width_y)]
        + [(6 * width_x + quakes, width_y)] * 2
        + [tile],
        [place] + sources,
        [pltpu.SMEM((quakes,), jnp.int32), (CHUNKS, quakes, depth // CHUNKS * width_x, width_y)]
        + [a.shape for a in sources[2:]]
        + [pltpu.SemaphoreType.DMA((4 + CHUNKS,))],
        scalars=1,
        far=5,
    )
    from_left = rotated(to_right, "gy", 1)
    from_right = rotated(to_left, "gy", -1)
    others = [rotated(records, "gy", by) for by in range(2, count_y - 1)]

    message_shape = (count_x, 3 * per + (4 if per > 1 else 5)) + tile
    first, first_strip, edge_costs, levels_one, sides, message = call(
        functools.partial(first_sweep_kernel, local_records, count_y),
        [field, (width_x, 2) + tile, (6,) + top, close, close, message_shape],
        [place, start, edge, records, from_left, from_right, costs, anis] + others,
        [(depth,) + tile, (width_x, 2) + tile],
        scalars=1,
    )
    reach = traded(message)
    group = width_y // 8
    entering, entering_strips, *recorded = call(
        functools.partial(blocks_kernel, per, depth, local_records * count_y),
        [(count_x, 2 * per) + tile, (2,) + tile, top, (width_x, width_y), tile, tile],
        [place, station_cell.reshape(-1, width_y), reach],
        [(-(-count_x // group), depth) + tile],
        scalars=1,
    )
    entering = traded(entering)
    second, *rest, message = call(
        second_sweep_kernel,
        [field, (4,) + top] + [top] * 5 + [close, close, (count_x, 7 + 2 * near) + tile],
        [place, first, first_strip, entering, entering_strips, costs, edge_costs, anis, levels_one, sides]
        + recorded,
        [field, (width_x, 2) + tile, (depth,) + tile] + [top] * 4,
        scalars=1,
        aliases={1: 0},
    )
    received = traded(message)
    times = call(times_kernel, flat, [second], last=True)
    kernel = call(
        kernel_kernel,
        (depth, width_x, width_y),
        [place, received] + rest + [anis],
        [close, (width_x, width_y), (-(-count_x // group),) + tile],
        scalars=1,
        last=True,
    )
    return (times.reshape(warm_start.shape), kernel)


def solution(mesh):
    return jax.shard_map(
        body,
        mesh=mesh,
        in_specs=(
            P(None, None, "gx", "gy"),
            P(None, "gx", "gy"),
            P(None, None, "gx", "gy"),
            P(None, ("gx", "gy")),
            P(),
            P(),
        ),
        out_specs=(P(None, None, "gx", "gy"), P(None, "gx", "gy")),
        check_vma=False,
    )
```

```python
import functools
import math

import jax
import jax.numpy as jnp
from jax import lax
from jax.experimental import pallas as pl
from jax.experimental.pallas import tpu as pltpu
from jax.sharding import PartitionSpec as P

TAU = 0.05
ADJ_SCALE = 0.1
LOG2E = math.log2(math.e)
RATE = LOG2E / TAU
BIG = 10000.0 * RATE
UNROLL = 8
CHUNKS = 4
VMEM = pl.BlockSpec(memory_space=pltpu.VMEM)
FAR = pl.BlockSpec(memory_space=pl.ANY)
SMEM = pl.BlockSpec(memory_space=pltpu.SMEM)
PARAMS = pltpu.CompilerParams(vmem_limit_bytes=8 * 1024 * 1024)


def softmin(values):
    least = functools.reduce(jnp.minimum, values)
    parts = [jnp.exp2(least - v) for v in values]
    return least, parts, functools.reduce(jnp.add, parts)


def soft_pair(first, second):
    return jnp.minimum(first, second) - LOG2E * jnp.log(1.0 + jnp.exp2(-jnp.abs(first - second)))


def add_pair(least, total, passed):
    low = jnp.minimum(least, passed)
    return low - LOG2E * jnp.log(total * jnp.exp2(low - least) + jnp.exp2(low - passed))


def join_pairs(first, second):
    low = jnp.minimum(first[0], second[0])
    return low, first[1] * jnp.exp2(low - first[0]) + second[1] * jnp.exp2(low - second[0])


def value_of(pair):
    return pair[0] - LOG2E * jnp.log(pair[1])


def split_pair(first, second):
    gap = jnp.exp2(-jnp.abs(first - second))
    share = 1.0 / (1.0 + gap)
    less = gap * share
    nearer = first <= second
    return jnp.where(nearer, share, less), jnp.where(nearer, less, share)


def iota(shape, axis):
    return lax.broadcasted_iota(jnp.int32, shape, axis)


def row(ref, index, x, like):
    return jnp.broadcast_to(ref[index, pl.ds(x, 1), :], like)


def row_of(ref, x, like):
    return jnp.broadcast_to(ref[pl.ds(x, 1), :], like)


def all_steps(count, step, carry):
    for i in range(count):
        carry = step(i, carry)
    return carry


def by_steps(count, step, carry):
    def group(i, carry):
        for j in range(UNROLL):
            carry = step(i * UNROLL + j, carry)
        return carry

    return lax.fori_loop(0, count // UNROLL, group, carry)


def packed(left, right):
    return jnp.where(iota(left.shape, 0) < 5, left, pltpu.roll(right, 2, 0))


def merged(left, right):
    return jnp.where(iota(left.shape, 0) < 4, left, right)


def shifted_down(tile, by):
    return pltpu.roll(tile, tile.shape[0] - by, 0)


def exact_parts(value):
    high = value.astype(jnp.bfloat16).astype(jnp.float32)
    middle = (value - high).astype(jnp.bfloat16).astype(jnp.float32)
    low = value - high - middle
    return [p.astype(jnp.bfloat16) for p in (high, middle, low)]


def pack_kernel(
    place, source_far, warm_far, observed_far, slowness_far, anisotropy_far, start, costs, near, edge, to_right, to_left, records,
    source, warm, observed, slowness, anisotropy, arrived,
):
    pairs = [(slowness_far, slowness), (anisotropy_far, anisotropy), (observed_far, observed)]
    share = start.shape[1] // CHUNKS
    span = share * start.shape[0]
    pairs += [(warm_far.at[:, pl.ds(i * span, span)], warm.at[i]) for i in range(CHUNKS)]
    pairs += [(source_far, source)]
    copies = [pltpu.make_async_copy(a, b, arrived.at[i]) for i, (a, b) in enumerate(pairs)]
    for copy in copies:
        copy.start()
    width_x, depth, quakes, width_y = start.shape
    tile = (quakes, width_y)
    quake = iota(tile, 0)
    lane = iota(tile, 1)
    span_y = place[2]
    plane = place[3]
    rows = width_x * 8
    wide = (width_x, width_y)
    group = iota(wide, 1) >> 3
    copies[0].wait()
    copies[1].wait()
    native = []
    for k in range(3):
        columns = jnp.zeros(wide, jnp.float32)
        for z in range(depth):
            cost = slowness[z] * anisotropy[k * depth + z] * RATE
            costs[k * depth + z] = cost
            columns = jnp.where(group == z, pltpu.roll(cost, 8 * z + 4, 1), columns)
        edge[rows : rows + width_x, :] = columns
        rows += width_x
        native.append(columns)
        for z in range(near.shape[0] // 3):
            near[k * (near.shape[0] // 3) + z] = anisotropy[k * depth + z]
    early = (iota(wide, 1) & 7) < 4
    at = slice(4 * width_x, 5 * width_x)
    to_right[at, :] = jnp.where(early, native[0], pltpu.roll(native[1], 4, 1))
    to_left[at, :] = jnp.where(early, pltpu.roll(native[1], width_y - 4, 1), native[0])
    at = slice(5 * width_x, 6 * width_x)
    to_right[at, :] = native[2]
    to_left[at, :] = native[2]
    copies[-1].wait()
    cell = jnp.zeros(tile, jnp.int32)
    for e in range(quakes):
        cell = jnp.where(quake == e, source[e], cell)
    cell = cell - (lane + place[0] * span_y + place[1])
    edges = []
    for i in range(CHUNKS):
        copies[3 + i].wait()
        here = warm.at[i].reshape(quakes * share * width_x, width_y)

        chunk = [jnp.zeros(tile, jnp.float32)] * share
        for x in range(width_x):
            mine = (lane >> 3) == x
            for k in range(share):
                value = here[pl.ds(k * width_x + x, quakes, stride=share * width_x), :] * RATE
                value = jnp.where(cell == (i * share + k) * plane + x * span_y, 0.0, value)
                start[x, i * share + k] = value
                chunk[k] = jnp.where(mine, pltpu.roll(value, (8 * x + 4) % width_y, 1), chunk[k])
        edges += chunk
    columns = jnp.transpose(jnp.concatenate(edges, 0))
    edge[: width_x * 8, :] = columns
    low = quake < 4
    for x in range(0, width_x, 2):
        one, two = columns[8 * x : 8 * x + 8], columns[8 * x + 8 : 8 * x + 16]
        to_right[4 * x : 4 * x + 8, :] = jnp.where(low, one, pltpu.roll(two, 4, 0))
        to_left[4 * x : 4 * x + 8, :] = jnp.where(low, pltpu.roll(one, 4, 0), two)
    copies[2].wait()
    records[...] = jnp.zeros(tile, jnp.float32)
    records[:, : observed.shape[1]] = observed[...]
    for message in (to_right, to_left):
        message[6 * width_x :, :] = records[...]


def halo_columns(left, right):
    rows = []
    for l, r in zip(left, right):
        rows.append(jnp.where(iota(l.shape, 0) == 4, r, pltpu.roll(l, 2, 0)))
    return jnp.transpose(jnp.concatenate(rows, 0))


def cost_columns(message, width_x, turn):
    pair = message[4 * width_x : 5 * width_x, :]
    return [pair, pltpu.roll(pair, turn, 1), message[5 * width_x : 6 * width_x, :]]


def strip_costs(own, from_left, from_right, out, width_x, depth):
    tile = own.shape[1]
    base = width_x * 8
    lane = iota((8, tile), 1)
    low = (lane & 7) < 4
    mine = (lane & 7) == iota((8, tile), 0)
    spread = ((iota((tile, tile), 0) >> 3) == (iota((tile, tile), 1) >> 3)).astype(jnp.float32)
    spread = spread.astype(jnp.bfloat16)
    for side in range(2):
        for k in range(3):
            rows = []
            for x in range(width_x):
                at = slice(base + k * width_x + x, base + k * width_x + x + 1)
                here = jnp.broadcast_to(own[at, :], lane.shape)
                there = jnp.broadcast_to((from_right if side else from_left)[k][x : x + 1], lane.shape)
                value = jnp.where(low, here, there) if side else jnp.where(low, there, here)
                rows.append(jnp.where(mine, value, 0.0))
            whole = jnp.concatenate(rows, 0)
            total = 0.0
            for part in reversed(exact_parts(whole)):
                total = total + lax.dot_general(
                    part, spread, (((1,), (0,)), ((), ())), preferred_element_type=jnp.float32
                )
            out[3 * side + k] = total.reshape(width_x, 8, tile)


def running_sum(value):
    rows = iota(value.shape, 0)
    by = 1
    while by < value.shape[0]:
        value = value + jnp.where(rows >= by, pltpu.roll(value, by, 0), 0.0)
        by *= 2
    return value


def log_sum(exponents):
    return -LOG2E * jnp.log(functools.reduce(jnp.add, [jnp.exp2(-e) for e in exponents]))


def passages(costs, from_left, from_right, depth):
    width_x, width_y = costs.shape[1:]
    lane = iota((width_x, width_y), 1)
    beside = jnp.where((lane & 7) == 4, running_sum(from_right), pltpu.roll(running_sum(from_left), 2, 1))
    sums = [running_sum(costs[z]) for z in range(depth)]
    sub = iota((8, width_y), 0)
    tiles = []
    for z in range(depth):
        back = sums[z] - costs[z]
        edge = pltpu.roll(beside, width_y - 5 - 8 * z, 1)
        below = jnp.where(lane == 0, edge, pltpu.roll(sums[z], 1, 1))
        above = jnp.where(lane == width_y - 1, edge, pltpu.roll(sums[z], width_y - 1, 1))
        step_y = back + costs[depth + z]
        step_z = back + costs[2 * depth + z]
        paths = [sums[z] + back, below + step_y, above + step_y]
        paths.append(sums[z - 1] + step_z if z > 0 else None)
        paths.append(sums[z + 1] + step_z if z < depth - 1 else None)
        tile = jnp.broadcast_to(sums[z][width_x - 1 :, :], sub.shape)
        for j, path in enumerate(paths):
            if path is None:
                tile = jnp.where(sub == j + 1, BIG, tile)
            else:
                total = jnp.sum(jnp.exp2(-path), axis=0, keepdims=True)
                tile = jnp.where(sub == j + 1, -LOG2E * jnp.log(total), tile)
        tiles.append(tile)
    return tiles


def strip_passages(edge_costs, width_x):
    shape = edge_costs.shape[2:]
    lane = iota(shape, 1)
    sums = jnp.zeros(shape, jnp.float32)
    totals = [jnp.zeros(shape, jnp.float32)] * 5
    for x in range(width_x):
        cost, step_y, step_z = [packed(edge_costs[k, x], edge_costs[3 + k, x]) for k in range(3)]
        back = sums
        sums = sums + cost
        step_y, step_z = step_y + back, step_z + back
        paths = [sums + back, pltpu.roll(sums, 1, 0) + step_y, shifted_down(sums, 1) + step_y]
        paths.append(jnp.where(lane < 8, BIG, pltpu.roll(sums, 8, 1) + step_z))
        paths.append(jnp.where(lane >= shape[1] - 8, BIG, pltpu.roll(sums, shape[1] - 8, 1) + step_z))
        totals = [t + jnp.exp2(-p) for t, p in zip(totals, paths)]
    return sums, [-LOG2E * jnp.log(jnp.maximum(t, 1e-37)) for t in totals]


def shared_rows(total, paths):
    place = iota(total.shape, 1) & 7
    first, second = total, total
    for q in range(6):
        value = pltpu.roll(total, (4 - q) % 8, 0)
        first = jnp.where(place == q, value, first)
    for q, (path, at) in enumerate([(p, r) for p in paths for r in (3, 6)]):
        if q < 2:
            first = jnp.where(place == 6 + q, pltpu.roll(path, (6 - at) % 8, 0), first)
        else:
            second = jnp.where(place == q - 2, pltpu.roll(path, (7 - at) % 8, 0), second)
    return jnp.where(iota(total.shape, 0) == 6, first, second)


def spread_rows(tiles):
    shape = tiles[0].shape
    wide = shape[1]
    sub = iota(shape, 0)
    mine = (iota(shape, 1) & 7) == sub
    spread = ((iota((wide, wide), 0) >> 3) == (iota((wide, wide), 1) >> 3)).astype(jnp.float32)
    spread = spread.astype(jnp.bfloat16)
    rows = [jnp.where(mine, jnp.broadcast_to(t[r : r + 1], shape), 0.0) for t in tiles for r in (6, 7)]
    whole = jnp.concatenate(rows, 0)
    value = 0.0
    for part in reversed(exact_parts(whole)):
        value = value + lax.dot_general(part, spread, (((1,), (0,)), ((), ())), preferred_element_type=jnp.float32)
    out = []
    for i in range(len(tiles)):
        first, second = value[16 * i : 16 * i + 8], value[16 * i + 8 : 16 * i + 16]
        paths = [jnp.where(sub == 3, pltpu.roll(first, 5, 0), pltpu.roll(first, 7, 0))]
        for q in range(4):
            at_three = pltpu.roll(second, (3 - 2 * q) % 8, 0)
            at_six = pltpu.roll(second, (6 - 2 * q - 1) % 8, 0)
            paths.append(jnp.where(sub == 3, at_three, at_six))
        out.append((pltpu.roll(first, 2, 0), paths))
    return out


def sweep_step(x, near, levels, strip, costs, edge_costs, halo, state, strip_state, keep, keep_strip):
    depth = costs.shape[0] // 3
    tile = levels[0].shape
    width_y = tile[1]
    lane = iota(tile, 1)
    out = []
    for z in range(len(state)):
        u = levels[z]
        cost_y = row(costs, depth + z, x, tile)
        cost_z = row(costs, 2 * depth + z, x, tile)
        edge = pltpu.roll(halo[z], width_y - 5 - 8 * x, 1)
        values = [u]
        values.append(jnp.where(lane == 0, edge, pltpu.roll(u, 1, 1)) + cost_y)
        values.append(jnp.where(lane == width_y - 1, edge, pltpu.roll(u, width_y - 1, 1)) + cost_y)
        if z > 0:
            values.append(levels[z - 1] + cost_z)
        if z < depth - 1:
            values.append(levels[z + 1] + cost_z)
        least, parts, total = softmin(values)
        passed = state[z] + row(costs, z, x, tile)
        if z < near:
            scale = 1.0 / total
            keep(x, z, value_of((least, total)), [p * scale for p in parts], passed)
        out.append(add_pair(least, total, passed))
    strips, relaxed, weights, passes = [], [], [], []
    for side in range(2 if strip is not None else 0):
        u = strip[x, side]
        cost_y = edge_costs[3 * side + 1, x]
        cost_z = edge_costs[3 * side + 2, x]
        values = [u, pltpu.roll(u, 1, 0) + cost_y, pltpu.roll(u, 7, 0) + cost_y]
        values.append(jnp.where(lane < 8, BIG, pltpu.roll(u, 8, 1)) + cost_z)
        values.append(jnp.where(lane >= width_y - 8, BIG, pltpu.roll(u, width_y - 8, 1)) + cost_z)
        least, parts, total = softmin(values)
        passes.append(strip_state[side] + edge_costs[3 * side, x])
        strips.append(add_pair(least, total, passes[side]))
        if keep_strip is not None:
            relaxed.append(value_of((least, total)))
            weights.append(parts[2 - side] / total)
    if keep_strip is not None:
        keep_strip(x, merged(*relaxed), merged(*weights), merged(*passes), merged(*strips))
    return out, strips


def outside_strips(place, shape):
    sub = iota(shape, 0)
    return [(place[4] == 1) & (sub < 4), (place[5] == 1) & (sub >= 4)]


def first_sweep_kernel(
    rows_of, count_y, per, place, field, own, mine, from_left, from_right, costs, anisotropy, *rest
):
    others = rest[: count_y - 3]
    local, local_strip, edge_costs, levels, sides, message, halo, strip = rest[count_y - 3 :]
    width_x, depth, quakes, width_y = field.shape
    tile = (quakes, width_y)
    sub = iota(tile, 0)
    low = sub < 4
    near = levels.shape[1]
    last = 6 * width_x
    far = [mine[...], from_left[last:, :]] + [o[...] for o in others] + [from_right[last:, :]]
    records = jnp.zeros(tile, jnp.float32)
    for by, piece in enumerate(far):
        owner = lax.rem(place[8] + count_y - by, count_y)
        records = records + pltpu.roll(piece, owner * rows_of, 1)
    left, right = [], []
    for x in range(width_x):
        at = slice(8 * x, 8 * x + 8)
        two = slice(8 * (x // 2), 8 * (x // 2) + 8)
        before, after = from_left[two, :], from_right[two, :]
        if x % 2:
            before = pltpu.roll(before, 4, 0)
        else:
            after = pltpu.roll(after, 4, 0)
        before = jnp.where(place[4] == 1, BIG, before)
        after = jnp.where(place[5] == 1, BIG, after)
        left.append(jnp.where(low, before, own[at, :]))
        right.append(jnp.where(low, own[at, :], after))
        strip[x, 0] = left[x]
        strip[x, 1] = right[x]
    halo[...] = halo_columns(left, right).reshape(halo.shape)
    left_costs = cost_columns(from_left, width_x, width_y - 4)
    right_costs = cost_columns(from_right, width_x, 4)
    strip_costs(own, left_costs, right_costs, edge_costs, width_x, depth)
    outside = outside_strips(place, tile)

    def keep(x, z, level, w, passed):
        levels[x, z] = level
        vertical = w[3] if z == 0 else w[3] + w[4]
        sideways = row(anisotropy, near + z, x, tile) * (w[1] + w[2])
        sides[x, z] = sideways + row(anisotropy, 2 * near + z, x, tile) * vertical

    def step(x, carry):
        state, strips = sweep_step(x, near, [field[x, z] for z in range(depth)], strip, costs, edge_costs, halo, *carry, keep, None)
        for z in range(depth):
            local[x, z] = state[z]
        for side in range(2):
            local_strip[x, side] = jnp.where(outside[side], BIG, strips[side])
        return state, strips

    blank = jnp.full(tile, BIG, jnp.float32)
    state, strips = all_steps(width_x, step, ([blank] * depth, [blank] * 2))
    reach_strip = packed(*[jnp.where(o, BIG, s) for o, s in zip(outside, strips)])

    edges = [[local_strip[x, side] for x in range(width_x)] for side in range(2)]
    halo[...] = halo_columns(*edges).reshape(halo.shape)

    def again(lap, carry):
        x = width_x - 1 - lap
        values = [local[x, z] for z in range(depth)]
        return sweep_step(x, 0, values, local_strip, costs, edge_costs, halo, *carry, None, None)

    back, back_strips = all_steps(width_x, again, ([blank] * depth, [blank] * 2))
    tiles = passages(costs, left_costs[0], right_costs[0], depth)
    strip_total, strip_paths = strip_passages(edge_costs, width_x)

    back_strip = packed(*back_strips)
    reach_strip = jnp.where(sub == 0, shifted_down(back_strip, 3), reach_strip)
    reach_strip = jnp.where(sub == 1, shifted_down(back_strip, 5), reach_strip)
    shared = shared_rows(strip_total, strip_paths)
    count = message.shape[0]
    for p in range(count):
        first = min(p * per, depth - per)
        for k in range(per + 2):
            z = first + k - 1
            message[p, k] = state[z] if 0 <= z < depth else blank
        for k in range(per):
            message[p, per + 2 + k] = back[first + k]
            value = tiles[first + k]
            if k == 0 and first > 0:
                value = jnp.where(sub == 6, jnp.broadcast_to(tiles[first - 1][:1], tile), value)
            if k == 0 and first + per < depth:
                value = jnp.where(sub == 7, jnp.broadcast_to(tiles[first + per][:1], tile), value)
            if per > 1 and k == 1:
                value = jnp.where(sub < 6, value, shared)
            message[p, 2 * per + 2 + k] = value
        message[p, 3 * per + 2] = reach_strip
        message[p, 3 * per + 3] = records
        if per == 1:
            message[p, 3 * per + 4] = shared
        surface = [state[0], state[1], back[0], jnp.where(sub < 6, tiles[0], jnp.broadcast_to(tiles[1][:1], tile))]
        for i, value in enumerate(surface):
            message[p, message.shape[1] - 4 + i] = value


def blocks_kernel(
    per, depth, place, received, entering, entering_strips, surface_edges, halo,
):
    count = received.shape[0]
    tile = entering.shape[2:]
    lane = iota(tile, 1)
    width_y = tile[1]
    me = place[6]
    blank = jnp.full(tile, BIG, jnp.float32)
    unit = jnp.ones(tile, jnp.float32)
    side = 3 * per + 2

    def rows(device, k, j):
        return jnp.broadcast_to(received[device, 2 * per + 2 + k, j : j + 1, :], tile)

    def total(device, k):
        if k < 0:
            return rows(device, 0, 6)
        return rows(device, k, 0) if k < per else rows(device, 0, 7)

    def further(pair, cost):
        return pair[0] + cost, pair[1]

    shared = [received[d, 2 * per + 3] if per > 1 else received[d, 3 * per + 4] for d in range(count)]
    shared = spread_rows(shared)
    state = [(blank, unit)] * (per + 2)
    strip = (blank, unit)
    first, first_strip = [], []
    for device in range(count):
        first.append([value_of(pair) for pair in state])
        first_strip.append(value_of(strip))
        state = [
            join_pairs((received[device, k], unit), further(state[k], total(device, k - 1))) for k in range(per + 2)
        ]
        strip = join_pairs((received[device, side], unit), further(strip, shared[device][0]))
    own = blank
    for device in range(count):
        own = jnp.where(device == me, first_strip[device], own)
        for k in range(per):
            entering[device, k] = first[device][k + 1]
    entering_strips[0] = own
    group = width_y // 8
    for at in range(0, count, group):
        some = first_strip[at : at + group]
        some = some + [blank] * (group - len(some))
        turned = halo_columns(some, [shifted_down(s, 2) for s in some])
        halo[at // group] = turned.reshape(halo.shape[1:])
        surface_edges[at // group] = turned[: tile[0]]
    low = jnp.minimum(me * per, depth - per)
    edges = [[halo[i, low + k] for k in range(per)] for i in range(halo.shape[0])]
    state = [(blank, unit)] * per
    strip = (blank, unit)
    for device in reversed(range(count)):
        for k in range(per):
            entering[device, per + k] = value_of(state[k])
            u = first[device][k + 1]
            turn = (width_y - 5 - 8 * (device % group)) % width_y
            edge = pltpu.roll(edges[device // group][k], turn, 1)
            values = [received[device, per + 2 + k], u + rows(device, k, 1)]
            values.append(jnp.where(lane == 0, edge, pltpu.roll(u, 1, 1)) + rows(device, k, 2))
            values.append(jnp.where(lane == width_y - 1, edge, pltpu.roll(u, width_y - 1, 1)) + rows(device, k, 3))
            values.append(first[device][k] + rows(device, k, 4))
            values.append(first[device][k + 2] + rows(device, k, 5))
            least, _, amount = softmin(values)
            state[k] = join_pairs((least, amount), further(state[k], total(device, k)))
        u = first_strip[device]
        back = received[device, side]
        back = jnp.where(iota(tile, 0) == 3, pltpu.roll(back, 3, 0), pltpu.roll(back, 5, 0))
        paths = shared[device][1]
        values = [back, u + paths[0], pltpu.roll(u, 1, 0) + paths[1], shifted_down(u, 1) + paths[2]]
        values.append(jnp.where(lane < 8, BIG, pltpu.roll(u, 8, 1)) + paths[3])
        values.append(jnp.where(lane >= width_y - 8, BIG, pltpu.roll(u, width_y - 8, 1)) + paths[4])
        least, _, amount = softmin(values)
        passed = join_pairs((least, amount), further(strip, shared[device][0]))
        strip = [jnp.where(device > me, new, old) for new, old in zip(passed, strip)]
    entering_strips[1] = value_of(strip)


def surface_kernel(
    per, rows_of, place, cell, received, first, first_strip, entering_strips, surface_edges,
    costs, edge_costs, anisotropy, levels_one, sides,
    halo, shares, slopes, keeps, misfits, edges_own, edges_factor, slopes_one, gains, message,
    strip, shares_strip, slopes_strip, keeps_strip, misfits_strip, sums, counts, sums_strip, counts_strip,
):
    width_x, near, quakes, width_y = levels_one.shape
    tile = (quakes, width_y)
    lane = iota(tile, 1)
    count = received.shape[0]
    base = received.shape[1] - 4
    me = place[6]
    add_records(rows_of, 3 * per + 3, place, cell, received, sums, counts, sums_strip, counts_strip)
    blank = jnp.full(tile, BIG, jnp.float32)
    unit = jnp.ones(tile, jnp.float32)

    def rows(device, j):
        return jnp.broadcast_to(received[device, base + 3, j : j + 1, :], tile)

    state = [(blank, unit)] * near
    into = []
    for device in range(count):
        into.append([value_of(pair) for pair in state])
        state = [
            join_pairs((received[device, base + z], unit), (state[z][0] + rows(device, 6 * z), state[z][1]))
            for z in range(near)
        ]
    carried = [blank] * near
    for device in range(count):
        carried = [jnp.where(device == me, new, old) for new, old in zip(into[device], carried)]
    back = (blank, unit)
    group = width_y // 8
    for device in reversed(range(count)):
        u, deeper = into[device]
        edge = pltpu.roll(surface_edges[device // group], (width_y - 5 - 8 * (device % group)) % width_y, 1)
        values = [received[device, base + 2], u + rows(device, 1), deeper + rows(device, 5)]
        values.append(jnp.where(lane == 0, edge, pltpu.roll(u, 1, 1)) + rows(device, 2))
        values.append(jnp.where(lane == width_y - 1, edge, pltpu.roll(u, width_y - 1, 1)) + rows(device, 3))
        least, _, amount = softmin(values)
        passed = join_pairs((least, amount), (back[0] + rows(device, 0), back[1]))
        back = [jnp.where(device > me, new, old) for new, old in zip(passed, back)]
    back = value_of(back)

    outside = outside_strips(place, tile)
    strips_in = [[s, shifted_down(s, 2)] for s in (entering_strips[0], entering_strips[1])]
    running = [jnp.zeros(tile, jnp.float32)] * (near + 2)
    prior = carried
    close = []
    for x in range(width_x):
        values = []
        for z in range(near):
            cost = row(costs, z, x, tile)
            running[z] = running[z] + cost
            values.append(soft_pair(first[x, z], carried[z] + running[z]))
            keep, slope = split_pair(levels_one[x, z], prior[z] + cost)
            slopes_one[x, z] = slope
            gains[x, z] = slope * row(anisotropy, z, x, tile) + keep * sides[x, z]
        prior = values
        close.append(values)
        for side in range(2):
            running[near + side] = running[near + side] + edge_costs[3 * side, x]
            value = soft_pair(first_strip[x, side], strips_in[0][side] + running[near + side])
            strip[x, side] = jnp.where(outside[side], BIG, value)
    edges = [[strip[x, side] for x in range(width_x)] for side in range(2)]
    halo[...] = halo_columns(*edges).reshape(halo.shape)

    def keep(x, z, level, w, passed):
        for i in range(4):
            shares[i, x] = w[i]
        keeps[x], slopes[x] = split_pair(level, passed)

    def keep_strip(x, level, w, passed, value):
        shares_strip[x] = w
        keeps_strip[x], slopes_strip[x] = split_pair(level, passed)
        tally = pltpu.roll(counts_strip[...], (width_y - 8 * x) % width_y, 1)
        total = pltpu.roll(sums_strip[...], (width_y - 8 * x) % width_y, 1)
        misfits_strip[x] = ADJ_SCALE * (tally * (value * (1.0 / RATE)) - total)

    def step(lap, carry):
        x = width_x - 1 - lap
        state, strips = sweep_step(x, 1, close[x], strip, costs, edge_costs, halo, *carry, keep, keep_strip)
        misfits[x] = ADJ_SCALE * (row_of(counts, x, tile) * (state[0] * (1.0 / RATE)) - sums[x])
        return state, strips

    all_steps(width_x, step, ([back], strips_in[1]))
    zero = jnp.zeros(tile, jnp.float32)
    own, factor, strip_own, strip_factor = zero, unit, zero, unit
    owns, factors = [], []
    sent = [zero, zero]
    for x in range(width_x):
        own = misfits[x] + own
        owns.append(keeps[x] * own)
        factors.append(keeps[x] * factor)
        own, factor = slopes[x] * own, slopes[x] * factor
        strip_own = misfits_strip[x] + strip_own
        through = keeps_strip[x] * shares_strip[x]
        for i, value in enumerate((strip_own, strip_factor)):
            value = pltpu.roll(through * value, 8 * x, 1) if x else through * value
            sent[i] = jnp.where((lane >> 3) == x, value, sent[i])
        strip_own, strip_factor = slopes_strip[x] * strip_own, slopes_strip[x] * strip_factor
    edges_own[...] = end_columns(sent[0]).reshape(edges_own.shape)
    edges_factor[...] = end_columns(sent[1]).reshape(edges_factor.shape)
    chain = [unit] * near
    blocks = [zero] * near
    links = [zero] * 4
    for x in range(width_x):
        entry = entries_of(owns[x], shares, x, edges_own[x])
        for z in range(near):
            chain[z] = chain[z] * slopes_one[x, z]
            blocks[z] = blocks[z] + chain[z] * entry[z]
        for i, path in enumerate(ways_of(factors[x], shares, x, edges_factor[x])):
            links[i] = links[i] + chain[i // 3] * path
    both = jnp.where(iota(tile, 0) < 5, strip_own, pltpu.roll(strip_factor, 2, 0))
    tiles = [own, factor, both] + blocks + chain + links
    for p in range(message.shape[0]):
        for i, value in enumerate(tiles):
            message[p, i] = value


def end_columns(rows):
    wide = rows.shape[1]
    first, last = shifted_down(rows, 3), pltpu.roll(rows, 3, 0)
    return jnp.transpose(jnp.concatenate([first] * (wide // 16) + [last] * (wide // 16), 0))


def ways_of(passed, shares, x, edge):
    lane = iota(passed.shape, 1)
    last = passed.shape[1] - 1
    above = jnp.where(lane == last, edge, pltpu.roll(passed * shares[1, x], last, 1))
    below = jnp.where(lane == 0, edge, pltpu.roll(passed * shares[2, x], 1, 1))
    return passed * shares[0, x], above, below, passed * shares[3, x]


def entries_of(passed, shares, x, edge):
    own, above, below, deeper = ways_of(passed, shares, x, edge)
    return own + above + below, deeper


def add_records(rows_of, tile_of, place, cell, received, sums, counts, sums_strip, counts_strip):
    width_x, quakes, width_y = sums.shape
    last = tile_of
    span_y = place[2]
    lane = iota((quakes, width_y), 1)
    column = iota((width_y, width_y), 0)
    strip_column = iota((8, width_y), 0)
    strip_column = jnp.where(strip_column == 3, -1, jnp.where(strip_column == 4, width_y, -2))
    share = width_y // rows_of
    dims = (((1,), (1,)), ((), ()))
    one_x = iota((width_x, width_y), 0)
    parts = [[], [], []]
    at, at_rows, at_strip = [], [], []
    for chunk in range(cell.shape[0]):
        records = jnp.zeros((quakes, width_y), jnp.float32)
        for part in range(share):
            piece = received[chunk * share + part, last]
            moved = pltpu.roll(piece, part * rows_of, 1) if part else piece
            records = jnp.where(lane // rows_of == part, moved, records)
        cells = cell[chunk : chunk + 1, :]
        station_x = lax.shift_right_logical(cells, place[7]) - place[0]
        station_y = (cells & (span_y - 1)) - place[1]
        at_x = (one_x == jnp.broadcast_to(station_x, one_x.shape)).astype(jnp.float32)
        pieces = [p.astype(jnp.float32) for p in exact_parts(records)]
        for out, piece in zip(parts, pieces):
            spread = [piece * jnp.broadcast_to(at_x[x : x + 1], piece.shape) for x in range(width_x)]
            out.append(jnp.concatenate(spread, 0).astype(jnp.bfloat16))
        at_rows.append(at_x.astype(jnp.bfloat16))
        hit = column == jnp.broadcast_to(station_y, column.shape)
        at.append(hit.astype(jnp.float32).astype(jnp.bfloat16))
        hit = strip_column == jnp.broadcast_to(station_y, strip_column.shape)
        at_strip.append(hit.astype(jnp.float32).astype(jnp.bfloat16))
    at = jnp.concatenate(at, 1)
    at_rows = jnp.concatenate(at_rows, 1)
    at_strip = jnp.concatenate(at_strip, 1)
    parts = [jnp.concatenate(p, 1) for p in parts]

    def product(a, b):
        return lax.dot_general(a, b, dims, preferred_element_type=jnp.float32)

    main = [product(p, at) for p in parts]
    sums[...] = (main[0] + main[1] + main[2]).reshape(sums.shape)
    counts[...] = product(at_rows, at)
    sums_strip[...] = product(at_strip, parts[0]) + product(at_strip, parts[1]) + product(at_strip, parts[2])
    spread = ((iota((width_x, width_y), 1) >> 3) == one_x).astype(jnp.float32).astype(jnp.bfloat16)
    tally = 0.0
    for part in reversed(exact_parts(product(at_strip, at_rows))):
        tally += lax.dot_general(part, spread, (((1,), (0,)), ((), ())), preferred_element_type=jnp.float32)
    counts_strip[...] = tally


def times_kernel(per, first, entering, costs, halo, times, field):
    width_x, depth, quakes, width_y = first.shape
    tile = (quakes, width_y)
    carried = [[entering[z // per, k * per + z % per] for z in range(depth)] for k in range(2)]

    def finish(x, running):
        sums = [running[z] + row(costs, z, x, tile) for z in range(depth)]
        for z in range(depth):
            field[x, z] = soft_pair(first[x, z], carried[0][z] + sums[z])
        return sums

    all_steps(width_x, finish, [jnp.zeros(tile, jnp.float32)] * depth)

    def step(lap, state):
        x = width_x - 1 - lap
        values = [field[x, z] for z in range(depth)]
        state, _ = sweep_step(x, 0, values, None, costs, None, halo, state, None, None, None)
        for z in range(depth):
            times[pl.ds(z * width_x + x, quakes, stride=depth * width_x), :] = state[z] * (1.0 / RATE)
        return state

    all_steps(width_x, step, carried[1])


def kernel_kernel(
    place, received, shares, slopes, keeps, misfits, edges_own, edges_factor, slopes_one, gains, anisotropy, kernel,
    entries, top, sent,
):
    width_x, quakes, width_y = slopes.shape
    tile = (quakes, width_y)
    near = slopes_one.shape[1]
    count = received.shape[0]
    lane = iota(tile, 1)
    last = width_y - 1
    me = place[6]
    zero = jnp.zeros(tile, jnp.float32)
    group = width_y // 8
    state, strip, mine, mine_strip = zero, zero, zero, zero
    carries = []
    for device in range(count):
        carries.append(state)
        mine = jnp.where(device == me, state, mine)
        at = device % group
        moved = pltpu.roll(strip, 8 * at, 1) if at else strip
        sent[device // group] = moved if at == 0 else jnp.where((lane >> 3) == at, moved, sent[device // group])
        both = received[device, 2]
        state = received[device, 0] + received[device, 1] * state
        strip = both + shifted_down(both, 2) * strip
    ends = [end_columns(sent[i]) for i in range(sent.shape[0])]
    state = [zero] * near
    mine_edge = zero
    for device in reversed(range(count)):
        at = 8 * (device % group)
        edge = ends[device // group][at : at + 8]
        mine_edge = jnp.where(device == me, edge, mine_edge)
        carry = carries[device]
        block = [received[device, 3 + z] for z in range(near)]
        above = jnp.where(lane == last, edge, pltpu.roll(carry, last, 1))
        below = jnp.where(lane == 0, edge, pltpu.roll(carry, 1, 1))
        link = [received[device, 3 + 2 * near + i] for i in range(4)]
        block[0] = block[0] + link[0] * carry + link[1] * above + link[2] * below
        block[1] = block[1] + link[3] * carry
        for z in range(near):
            passed = block[z] + received[device, 3 + near + z] * state[z]
            state[z] = jnp.where(device > me, passed, state[z])
    carry = mine
    for x in range(width_x):
        total = misfits[x] + carry
        carry = slopes[x] * total
        passed = keeps[x] * total
        sideways = row(anisotropy, near, x, tile) * (shares[1, x] + shares[2, x])
        sideways = sideways + row(anisotropy, 2 * near, x, tile) * shares[3, x]
        terms = carry * row(anisotropy, 0, x, tile) + passed * sideways
        top[x : x + 1, :] = jnp.sum(terms, axis=0, keepdims=True)
        entry = entries_of(passed, shares, x, edges_own[x] + edges_factor[x] * mine_edge)
        for z in range(near):
            entries[x, z] = entry[z]
    for x in reversed(range(width_x)):
        for z in range(near):
            total = entries[x, z] + state[z]
            state[z] = slopes_one[x, z] * total
            value = jnp.sum(total * gains[x, z], axis=0, keepdims=True)
            if z == 0:
                value = value + top[x : x + 1, :]
            kernel[z, x : x + 1, :] = value
    for z in range(near, kernel.shape[0]):
        kernel[z] = jnp.zeros(kernel.shape[1:], jnp.float32)


def call(kernel, shapes, operands, scratch=(), scalars=0, far=0, last=False, aliases=()):
    many = isinstance(shapes, list)
    shapes = shapes if many else [shapes]
    out = [jax.ShapeDtypeStruct(s, jnp.float32) if last else pltpu.VMEM(s, jnp.float32) for s in shapes]
    result = pl.pallas_call(
        kernel,
        out_shape=out,
        in_specs=[SMEM] * scalars + [FAR] * far + [VMEM] * (len(operands) - scalars - far),
        out_specs=[VMEM] * len(out),
        scratch_shapes=[pltpu.VMEM(s, jnp.float32) if isinstance(s, tuple) else s for s in scratch],
        compiler_params=PARAMS,
        input_output_aliases=dict(aliases),
    )(*operands)
    return result if many else result[0]


def traded(message):
    return lax.all_to_all(message, "gx", 0, 0, tiled=True)


def rotated(value, axis, by):
    count = lax.axis_size(axis)
    return lax.ppermute(value, axis, [(i, (i + by) % count) for i in range(count)])


def body(warm_start, slowness, anisotropy, observed, station_cell, source_cell):
    quakes, depth, width_x, width_y = warm_start.shape
    count_x, count_y = lax.axis_size("gx"), lax.axis_size("gy")
    index_x, index_y = lax.axis_index("gx"), lax.axis_index("gy")
    span_x, span_y = width_x * count_x, width_y * count_y
    near = 2
    per = max(1, depth // count_x)
    tile = (quakes, width_y)
    top = (width_x,) + tile
    close = (width_x, near) + tile
    field = (width_x, depth) + tile
    place = jnp.stack(
        [
            index_x * width_x,
            index_y * width_y,
            jnp.int32(span_y),
            jnp.int32(span_x * span_y),
            (index_y == 0).astype(jnp.int32),
            (index_y == count_y - 1).astype(jnp.int32),
            index_x,
            jnp.int32(span_y.bit_length() - 1),
            index_y,
        ]
    ).astype(jnp.int32)
    anis = anisotropy.reshape(3 * depth, width_x, width_y)
    local_records = observed.shape[1]
    flat = (quakes * depth * width_x, width_y)

    sources = [warm_start.reshape(quakes, depth * width_x, width_y), observed, slowness, anis]
    sources = [pltpu.with_memory_space_constraint(a, pltpu.HBM) for a in [source_cell] + sources]
    start, costs, anis, edge, to_right, to_left, records = call(
        pack_kernel,
        [field, anis.shape, (3 * near, width_x, width_y), (11 * width_x, width_y)]
        + [(6 * width_x + quakes, width_y)] * 2
        + [tile],
        [place] + sources,
        [pltpu.SMEM((quakes,), jnp.int32), (CHUNKS, quakes, depth // CHUNKS * width_x, width_y)]
        + [a.shape for a in sources[2:]]
        + [pltpu.SemaphoreType.DMA((4 + CHUNKS,))],
        scalars=1,
        far=5,
    )
    from_left = rotated(to_right, "gy", 1)
    from_right = rotated(to_left, "gy", -1)
    others = [rotated(records, "gy", by) for by in range(2, count_y - 1)]

    message_shape = (count_x, 3 * per + (8 if per > 1 else 9)) + tile
    first, first_strip, edge_costs, levels_one, sides, message = call(
        functools.partial(first_sweep_kernel, local_records, count_y, per),
        [field, (width_x, 2) + tile, (6,) + top, close, close, message_shape],
        [place, start, edge, records, from_left, from_right, costs, anis] + others,
        [(depth,) + tile, (width_x, 2) + tile],
        scalars=1,
    )
    reach = traded(message)
    group = width_y // 8
    chunks = -(-count_x // group)
    entering, entering_strips, surface_edges = call(
        functools.partial(blocks_kernel, per, depth),
        [(count_x, 2 * per) + tile, (2,) + tile, (chunks,) + tile],
        [place, reach],
        [(chunks, depth) + tile],
        scalars=1,
    )
    entering = traded(entering)
    halo, *rest, message = call(
        functools.partial(surface_kernel, per, local_records * count_y),
        [(depth,) + tile, (4,) + top] + [top] * 5 + [close, close, (count_x, 7 + 2 * near) + tile],
        [place, station_cell.reshape(-1, width_y), reach, first, first_strip, entering_strips, surface_edges]
        + [costs, edge_costs, anis, levels_one, sides],
        [(width_x, 2) + tile] + [top] * 5 + [(width_x, width_y), tile, tile],
        scalars=1,
    )
    received = traded(message)
    times = call(functools.partial(times_kernel, per), flat, [first, entering, costs, halo], [field], last=True)
    kernel = call(
        kernel_kernel,
        (depth, width_x, width_y),
        [place, received] + rest + [anis],
        [close, (width_x, width_y), (-(-count_x // group),) + tile],
        scalars=1,
        last=True,
    )
    return (times.reshape(warm_start.shape), kernel)


def solution(mesh):
    return jax.shard_map(
        body,
        mesh=mesh,
        in_specs=(
            P(None, None, "gx", "gy"),
            P(None, "gx", "gy"),
            P(None, None, "gx", "gy"),
            P(None, ("gx", "gy")),
            P(),
            P(),
        ),
        out_specs=(P(None, None, "gx", "gy"), P(None, "gx", "gy")),
        check_vma=False,
    )
```

```python
import functools
import math

import jax
import jax.numpy as jnp
from jax import lax
from jax.experimental import pallas as pl
from jax.experimental.pallas import tpu as pltpu
from jax.sharding import PartitionSpec as P

TAU = 0.05
ADJ_SCALE = 0.1
LOG2E = math.log2(math.e)
RATE = LOG2E / TAU
BIG = 10000.0 * RATE
UNROLL = 8
CHUNKS = 4
VMEM = pl.BlockSpec(memory_space=pltpu.VMEM)
FAR = pl.BlockSpec(memory_space=pl.ANY)
SMEM = pl.BlockSpec(memory_space=pltpu.SMEM)
PARAMS = pltpu.CompilerParams(vmem_limit_bytes=8 * 1024 * 1024)


def softmin(values):
    least = functools.reduce(jnp.minimum, values)
    parts = [jnp.exp2(least - v) for v in values]
    return least, parts, functools.reduce(jnp.add, parts)


def soft_pair(first, second):
    return jnp.minimum(first, second) - LOG2E * jnp.log(1.0 + jnp.exp2(-jnp.abs(first - second)))


def add_pair(least, total, passed):
    low = jnp.minimum(least, passed)
    return low - LOG2E * jnp.log(total * jnp.exp2(low - least) + jnp.exp2(low - passed))


def join_pairs(first, second):
    low = jnp.minimum(first[0], second[0])
    return low, first[1] * jnp.exp2(low - first[0]) + second[1] * jnp.exp2(low - second[0])


def value_of(pair):
    return pair[0] - LOG2E * jnp.log(pair[1])


def split_pair(first, second):
    gap = jnp.exp2(-jnp.abs(first - second))
    share = 1.0 / (1.0 + gap)
    less = gap * share
    nearer = first <= second
    return jnp.where(nearer, share, less), jnp.where(nearer, less, share)


def iota(shape, axis):
    return lax.broadcasted_iota(jnp.int32, shape, axis)


def row(ref, index, x, like):
    return jnp.broadcast_to(ref[index, pl.ds(x, 1), :], like)


def row_of(ref, x, like):
    return jnp.broadcast_to(ref[pl.ds(x, 1), :], like)


def all_steps(count, step, carry):
    for i in range(count):
        carry = step(i, carry)
    return carry


def by_steps(count, step, carry):
    def group(i, carry):
        for j in range(UNROLL):
            carry = step(i * UNROLL + j, carry)
        return carry

    return lax.fori_loop(0, count // UNROLL, group, carry)


def packed(left, right):
    return jnp.where(iota(left.shape, 0) < 5, left, pltpu.roll(right, 2, 0))


def merged(left, right):
    return jnp.where(iota(left.shape, 0) < 4, left, right)


def shifted_down(tile, by):
    return pltpu.roll(tile, tile.shape[0] - by, 0)


def exact_parts(value):
    high = value.astype(jnp.bfloat16).astype(jnp.float32)
    middle = (value - high).astype(jnp.bfloat16).astype(jnp.float32)
    low = value - high - middle
    return [p.astype(jnp.bfloat16) for p in (high, middle, low)]


def pack_kernel(
    place, source_far, warm_far, observed_far, slowness_far, anisotropy_far, start, costs, near, edge, to_right, to_left, records,
    source, warm, observed, slowness, anisotropy, arrived,
):
    pairs = [(slowness_far, slowness), (anisotropy_far, anisotropy), (observed_far, observed)]
    share = start.shape[1] // CHUNKS
    span = share * start.shape[0]
    pairs += [(warm_far.at[:, pl.ds(i * span, span)], warm.at[i]) for i in range(CHUNKS)]
    pairs += [(source_far, source)]
    copies = [pltpu.make_async_copy(a, b, arrived.at[i]) for i, (a, b) in enumerate(pairs)]
    for copy in copies:
        copy.start()
    width_x, depth, quakes, width_y = start.shape
    tile = (quakes, width_y)
    quake = iota(tile, 0)
    lane = iota(tile, 1)
    span_y = place[2]
    plane = place[3]
    rows = width_x * 8
    wide = (width_x, width_y)
    group = iota(wide, 1) >> 3
    copies[0].wait()
    copies[1].wait()
    native = []
    for k in range(3):
        columns = jnp.zeros(wide, jnp.float32)
        for z in range(depth):
            cost = slowness[z] * anisotropy[k * depth + z] * RATE
            costs[k * depth + z] = cost
            columns = jnp.where(group == z, pltpu.roll(cost, 8 * z + 4, 1), columns)
        edge[rows : rows + width_x, :] = columns
        rows += width_x
        native.append(columns)
        for z in range(near.shape[0] // 3):
            near[k * (near.shape[0] // 3) + z] = anisotropy[k * depth + z]
    early = (iota(wide, 1) & 7) < 4
    at = slice(4 * width_x, 5 * width_x)
    to_right[at, :] = jnp.where(early, native[0], pltpu.roll(native[1], 4, 1))
    to_left[at, :] = jnp.where(early, pltpu.roll(native[1], width_y - 4, 1), native[0])
    at = slice(5 * width_x, 6 * width_x)
    to_right[at, :] = native[2]
    to_left[at, :] = native[2]
    copies[-1].wait()
    cell = jnp.zeros(tile, jnp.int32)
    for e in range(quakes):
        cell = jnp.where(quake == e, source[e], cell)
    cell = cell - (lane + place[0] * span_y + place[1])
    edges = []
    for i in range(CHUNKS):
        copies[3 + i].wait()
        here = warm.at[i].reshape(quakes * share * width_x, width_y)

        chunk = [jnp.zeros(tile, jnp.float32)] * share
        for x in range(width_x):
            mine = (lane >> 3) == x
            for k in range(share):
                value = here[pl.ds(k * width_x + x, quakes, stride=share * width_x), :] * RATE
                value = jnp.where(cell == (i * share + k) * plane + x * span_y, 0.0, value)
                start[x, i * share + k] = value
                chunk[k] = jnp.where(mine, pltpu.roll(value, (8 * x + 4) % width_y, 1), chunk[k])
        edges += chunk
    columns = jnp.transpose(jnp.concatenate(edges, 0))
    edge[: width_x * 8, :] = columns
    low = quake < 4
    for x in range(0, width_x, 2):
        one, two = columns[8 * x : 8 * x + 8], columns[8 * x + 8 : 8 * x + 16]
        to_right[4 * x : 4 * x + 8, :] = jnp.where(low, one, pltpu.roll(two, 4, 0))
        to_left[4 * x : 4 * x + 8, :] = jnp.where(low, pltpu.roll(one, 4, 0), two)
    copies[2].wait()
    records[...] = jnp.zeros(tile, jnp.float32)
    records[:, : observed.shape[1]] = observed[...]
    for message in (to_right, to_left):
        message[6 * width_x :, :] = records[...]


def halo_columns(left, right):
    rows = []
    for l, r in zip(left, right):
        rows.append(jnp.where(iota(l.shape, 0) == 4, r, pltpu.roll(l, 2, 0)))
    return jnp.transpose(jnp.concatenate(rows, 0))


def cost_columns(message, width_x, turn):
    pair = message[4 * width_x : 5 * width_x, :]
    return [pair, pltpu.roll(pair, turn, 1), message[5 * width_x : 6 * width_x, :]]


def strip_costs(own, from_left, from_right, out, width_x, depth):
    tile = own.shape[1]
    base = width_x * 8
    lane = iota((8, tile), 1)
    low = (lane & 7) < 4
    mine = (lane & 7) == iota((8, tile), 0)
    spread = ((iota((tile, tile), 0) >> 3) == (iota((tile, tile), 1) >> 3)).astype(jnp.float32)
    spread = spread.astype(jnp.bfloat16)
    for side in range(2):
        for k in range(3):
            rows = []
            for x in range(width_x):
                at = slice(base + k * width_x + x, base + k * width_x + x + 1)
                here = jnp.broadcast_to(own[at, :], lane.shape)
                there = jnp.broadcast_to((from_right if side else from_left)[k][x : x + 1], lane.shape)
                value = jnp.where(low, here, there) if side else jnp.where(low, there, here)
                rows.append(jnp.where(mine, value, 0.0))
            whole = jnp.concatenate(rows, 0)
            total = 0.0
            for part in reversed(exact_parts(whole)):
                total = total + lax.dot_general(
                    part, spread, (((1,), (0,)), ((), ())), preferred_element_type=jnp.float32
                )
            out[3 * side + k] = total.reshape(width_x, 8, tile)


def running_sum(value):
    rows = iota(value.shape, 0)
    by = 1
    while by < value.shape[0]:
        value = value + jnp.where(rows >= by, pltpu.roll(value, by, 0), 0.0)
        by *= 2
    return value


def log_sum(exponents):
    return -LOG2E * jnp.log(functools.reduce(jnp.add, [jnp.exp2(-e) for e in exponents]))


def passages(costs, from_left, from_right, depth):
    width_x, width_y = costs.shape[1:]
    lane = iota((width_x, width_y), 1)
    beside = jnp.where((lane & 7) == 4, running_sum(from_right), pltpu.roll(running_sum(from_left), 2, 1))
    sums = [running_sum(costs[z]) for z in range(depth)]
    sub = iota((8, width_y), 0)
    tiles = []
    for z in range(depth):
        back = sums[z] - costs[z]
        edge = pltpu.roll(beside, width_y - 5 - 8 * z, 1)
        below = jnp.where(lane == 0, edge, pltpu.roll(sums[z], 1, 1))
        above = jnp.where(lane == width_y - 1, edge, pltpu.roll(sums[z], width_y - 1, 1))
        step_y = back + costs[depth + z]
        step_z = back + costs[2 * depth + z]
        paths = [sums[z] + back, below + step_y, above + step_y]
        paths.append(sums[z - 1] + step_z if z > 0 else None)
        paths.append(sums[z + 1] + step_z if z < depth - 1 else None)
        tile = jnp.broadcast_to(sums[z][width_x - 1 :, :], sub.shape)
        for j, path in enumerate(paths):
            if path is None:
                tile = jnp.where(sub == j + 1, BIG, tile)
            else:
                total = jnp.sum(jnp.exp2(-path), axis=0, keepdims=True)
                tile = jnp.where(sub == j + 1, -LOG2E * jnp.log(total), tile)
        tiles.append(tile)
    return tiles


def strip_passages(edge_costs, width_x):
    shape = edge_costs.shape[2:]
    lane = iota(shape, 1)
    sums = jnp.zeros(shape, jnp.float32)
    totals = [jnp.zeros(shape, jnp.float32)] * 5
    for x in range(width_x):
        cost, step_y, step_z = [packed(edge_costs[k, x], edge_costs[3 + k, x]) for k in range(3)]
        back = sums
        sums = sums + cost
        step_y, step_z = step_y + back, step_z + back
        paths = [sums + back, pltpu.roll(sums, 1, 0) + step_y, shifted_down(sums, 1) + step_y]
        paths.append(jnp.where(lane < 8, BIG, pltpu.roll(sums, 8, 1) + step_z))
        paths.append(jnp.where(lane >= shape[1] - 8, BIG, pltpu.roll(sums, shape[1] - 8, 1) + step_z))
        totals = [t + jnp.exp2(-p) for t, p in zip(totals, paths)]
    return sums, [-LOG2E * jnp.log(jnp.maximum(t, 1e-37)) for t in totals]


def shared_rows(total, paths):
    place = iota(total.shape, 1) & 7
    first, second = total, total
    for q in range(6):
        value = pltpu.roll(total, (4 - q) % 8, 0)
        first = jnp.where(place == q, value, first)
    for q, (path, at) in enumerate([(p, r) for p in paths for r in (3, 6)]):
        if q < 2:
            first = jnp.where(place == 6 + q, pltpu.roll(path, (6 - at) % 8, 0), first)
        else:
            second = jnp.where(place == q - 2, pltpu.roll(path, (7 - at) % 8, 0), second)
    return jnp.where(iota(total.shape, 0) == 6, first, second)


def spread_rows(tiles):
    shape = tiles[0].shape
    wide = shape[1]
    sub = iota(shape, 0)
    mine = (iota(shape, 1) & 7) == sub
    spread = ((iota((wide, wide), 0) >> 3) == (iota((wide, wide), 1) >> 3)).astype(jnp.float32)
    spread = spread.astype(jnp.bfloat16)
    rows = [jnp.where(mine, jnp.broadcast_to(t[r : r + 1], shape), 0.0) for t in tiles for r in (6, 7)]
    whole = jnp.concatenate(rows, 0)
    value = 0.0
    for part in reversed(exact_parts(whole)):
        value = value + lax.dot_general(part, spread, (((1,), (0,)), ((), ())), preferred_element_type=jnp.float32)
    out = []
    for i in range(len(tiles)):
        first, second = value[16 * i : 16 * i + 8], value[16 * i + 8 : 16 * i + 16]
        paths = [jnp.where(sub == 3, pltpu.roll(first, 5, 0), pltpu.roll(first, 7, 0))]
        for q in range(4):
            at_three = pltpu.roll(second, (3 - 2 * q) % 8, 0)
            at_six = pltpu.roll(second, (6 - 2 * q - 1) % 8, 0)
            paths.append(jnp.where(sub == 3, at_three, at_six))
        out.append((pltpu.roll(first, 2, 0), paths))
    return out


def sweep_step(x, near, levels, strip, costs, edge_costs, halo, state, strip_state, keep, keep_strip):
    depth = costs.shape[0] // 3
    tile = levels[0].shape
    width_y = tile[1]
    lane = iota(tile, 1)
    out = []
    for z in range(len(state)):
        u = levels[z]
        cost_y = row(costs, depth + z, x, tile)
        cost_z = row(costs, 2 * depth + z, x, tile)
        edge = pltpu.roll(halo[z], width_y - 5 - 8 * x, 1)
        values = [u]
        values.append(jnp.where(lane == 0, edge, pltpu.roll(u, 1, 1)) + cost_y)
        values.append(jnp.where(lane == width_y - 1, edge, pltpu.roll(u, width_y - 1, 1)) + cost_y)
        if z > 0:
            values.append(levels[z - 1] + cost_z)
        if z < depth - 1:
            values.append(levels[z + 1] + cost_z)
        least, parts, total = softmin(values)
        passed = state[z] + row(costs, z, x, tile)
        if z < near:
            scale = 1.0 / total
            keep(x, z, value_of((least, total)), [p * scale for p in parts], passed)
        out.append(add_pair(least, total, passed))
    strips, relaxed, weights, passes = [], [], [], []
    for side in range(2 if strip is not None else 0):
        u = strip[x, side]
        cost_y = edge_costs[3 * side + 1, x]
        cost_z = edge_costs[3 * side + 2, x]
        values = [u, pltpu.roll(u, 1, 0) + cost_y, pltpu.roll(u, 7, 0) + cost_y]
        values.append(jnp.where(lane < 8, BIG, pltpu.roll(u, 8, 1)) + cost_z)
        values.append(jnp.where(lane >= width_y - 8, BIG, pltpu.roll(u, width_y - 8, 1)) + cost_z)
        least, parts, total = softmin(values)
        passes.append(strip_state[side] + edge_costs[3 * side, x])
        strips.append(add_pair(least, total, passes[side]))
        if keep_strip is not None:
            relaxed.append(value_of((least, total)))
            weights.append(parts[2 - side] / total)
    if keep_strip is not None:
        keep_strip(x, merged(*relaxed), merged(*weights), merged(*passes), merged(*strips))
    return out, strips


def outside_strips(place, shape):
    sub = iota(shape, 0)
    return [(place[4] == 1) & (sub < 4), (place[5] == 1) & (sub >= 4)]


def first_sweep_kernel(
    rows_of, count_y, per, place, field, own, mine, from_left, from_right, costs, anisotropy, *rest
):
    others = rest[: count_y - 3]
    local, local_strip, edge_costs, levels, sides, message, halo, strip = rest[count_y - 3 :]
    width_x, depth, quakes, width_y = field.shape
    tile = (quakes, width_y)
    sub = iota(tile, 0)
    low = sub < 4
    near = levels.shape[1]
    last = 6 * width_x
    far = [mine[...], from_left[last:, :]] + [o[...] for o in others] + [from_right[last:, :]]
    records = jnp.zeros(tile, jnp.float32)
    for by, piece in enumerate(far):
        owner = lax.rem(place[8] + count_y - by, count_y)
        records = records + pltpu.roll(piece, owner * rows_of, 1)
    left, right = [], []
    for x in range(width_x):
        at = slice(8 * x, 8 * x + 8)
        two = slice(8 * (x // 2), 8 * (x // 2) + 8)
        before, after = from_left[two, :], from_right[two, :]
        if x % 2:
            before = pltpu.roll(before, 4, 0)
        else:
            after = pltpu.roll(after, 4, 0)
        before = jnp.where(place[4] == 1, BIG, before)
        after = jnp.where(place[5] == 1, BIG, after)
        left.append(jnp.where(low, before, own[at, :]))
        right.append(jnp.where(low, own[at, :], after))
        strip[x, 0] = left[x]
        strip[x, 1] = right[x]
    halo[...] = halo_columns(left, right).reshape(halo.shape)
    left_costs = cost_columns(from_left, width_x, width_y - 4)
    right_costs = cost_columns(from_right, width_x, 4)
    strip_costs(own, left_costs, right_costs, edge_costs, width_x, depth)
    outside = outside_strips(place, tile)

    def keep(x, z, level, w, passed):
        levels[x, z] = level
        vertical = w[3] if z == 0 else w[3] + w[4]
        sideways = row(anisotropy, near + z, x, tile) * (w[1] + w[2])
        sides[x, z] = sideways + row(anisotropy, 2 * near + z, x, tile) * vertical

    def step(x, carry):
        state, strips = sweep_step(x, near, [field[x, z] for z in range(depth)], strip, costs, edge_costs, halo, *carry, keep, None)
        for z in range(depth):
            local[x, z] = state[z]
        for side in range(2):
            local_strip[x, side] = jnp.where(outside[side], BIG, strips[side])
        return state, strips

    blank = jnp.full(tile, BIG, jnp.float32)
    state, strips = all_steps(width_x, step, ([blank] * depth, [blank] * 2))
    reach_strip = packed(*[jnp.where(o, BIG, s) for o, s in zip(outside, strips)])

    edges = [[local_strip[x, side] for x in range(width_x)] for side in range(2)]
    halo[...] = halo_columns(*edges).reshape(halo.shape)

    def again(lap, carry):
        x = width_x - 1 - lap
        values = [local[x, z] for z in range(depth)]
        return sweep_step(x, 0, values, local_strip, costs, edge_costs, halo, *carry, None, None)

    back, back_strips = all_steps(width_x, again, ([blank] * depth, [blank] * 2))
    tiles = passages(costs, left_costs[0], right_costs[0], depth)
    strip_total, strip_paths = strip_passages(edge_costs, width_x)

    back_strip = packed(*back_strips)
    reach_strip = jnp.where(sub == 0, shifted_down(back_strip, 3), reach_strip)
    reach_strip = jnp.where(sub == 1, shifted_down(back_strip, 5), reach_strip)
    shared = shared_rows(strip_total, strip_paths)
    count = message.shape[0]
    for p in range(count):
        first = min(p * per, depth - per)
        for k in range(per + 2):
            z = first + k - 1
            message[p, k] = state[z] if 0 <= z < depth else blank
        for k in range(per):
            message[p, per + 2 + k] = back[first + k]
            value = tiles[first + k]
            if k == 0 and first > 0:
                value = jnp.where(sub == 6, jnp.broadcast_to(tiles[first - 1][:1], tile), value)
            if k == 0 and first + per < depth:
                value = jnp.where(sub == 7, jnp.broadcast_to(tiles[first + per][:1], tile), value)
            if per > 1 and k == 1:
                value = jnp.where(sub < 6, value, shared)
            message[p, 2 * per + 2 + k] = value
        message[p, 3 * per + 2] = reach_strip
        message[p, 3 * per + 3] = records
        if per == 1:
            message[p, 3 * per + 4] = shared
        surface = [state[0], state[1], back[0], jnp.where(sub < 6, tiles[0], jnp.broadcast_to(tiles[1][:1], tile))]
        for i, value in enumerate(surface):
            message[p, message.shape[1] - 4 + i] = value


def owner_carries(
    per, depth, place, received, entering, entering_strips, surface_edges, halo,
):
    count = received.shape[0]
    tile = entering.shape[2:]
    lane = iota(tile, 1)
    width_y = tile[1]
    me = place[6]
    blank = jnp.full(tile, BIG, jnp.float32)
    unit = jnp.ones(tile, jnp.float32)
    side = 3 * per + 2

    def rows(device, k, j):
        return jnp.broadcast_to(received[device, 2 * per + 2 + k, j : j + 1, :], tile)

    def total(device, k):
        if k < 0:
            return rows(device, 0, 6)
        return rows(device, k, 0) if k < per else rows(device, 0, 7)

    def further(pair, cost):
        return pair[0] + cost, pair[1]

    shared = [received[d, 2 * per + 3] if per > 1 else received[d, 3 * per + 4] for d in range(count)]
    shared = spread_rows(shared)
    state = [(blank, unit)] * (per + 2)
    strip = (blank, unit)
    first, first_strip = [], []
    for device in range(count):
        first.append([value_of(pair) for pair in state])
        first_strip.append(value_of(strip))
        state = [
            join_pairs((received[device, k], unit), further(state[k], total(device, k - 1))) for k in range(per + 2)
        ]
        strip = join_pairs((received[device, side], unit), further(strip, shared[device][0]))
    own = blank
    for device in range(count):
        own = jnp.where(device == me, first_strip[device], own)
        for k in range(per):
            entering[device, k] = first[device][k + 1]
    entering_strips[0] = own
    group = width_y // 8
    for at in range(0, count, group):
        some = first_strip[at : at + group]
        some = some + [blank] * (group - len(some))
        turned = halo_columns(some, [shifted_down(s, 2) for s in some])
        halo[at // group] = turned.reshape(halo.shape[1:])
        surface_edges[at // group] = turned[: tile[0]]
    low = jnp.minimum(me * per, depth - per)
    edges = [[halo[i, low + k] for k in range(per)] for i in range(halo.shape[0])]
    state = [(blank, unit)] * per
    strip = (blank, unit)
    for device in reversed(range(count)):
        for k in range(per):
            entering[device, per + k] = value_of(state[k])
            u = first[device][k + 1]
            turn = (width_y - 5 - 8 * (device % group)) % width_y
            edge = pltpu.roll(edges[device // group][k], turn, 1)
            values = [received[device, per + 2 + k], u + rows(device, k, 1)]
            values.append(jnp.where(lane == 0, edge, pltpu.roll(u, 1, 1)) + rows(device, k, 2))
            values.append(jnp.where(lane == width_y - 1, edge, pltpu.roll(u, width_y - 1, 1)) + rows(device, k, 3))
            values.append(first[device][k] + rows(device, k, 4))
            values.append(first[device][k + 2] + rows(device, k, 5))
            least, _, amount = softmin(values)
            state[k] = join_pairs((least, amount), further(state[k], total(device, k)))
        u = first_strip[device]
        back = received[device, side]
        back = jnp.where(iota(tile, 0) == 3, pltpu.roll(back, 3, 0), pltpu.roll(back, 5, 0))
        paths = shared[device][1]
        values = [back, u + paths[0], pltpu.roll(u, 1, 0) + paths[1], shifted_down(u, 1) + paths[2]]
        values.append(jnp.where(lane < 8, BIG, pltpu.roll(u, 8, 1)) + paths[3])
        values.append(jnp.where(lane >= width_y - 8, BIG, pltpu.roll(u, width_y - 8, 1)) + paths[4])
        least, _, amount = softmin(values)
        passed = join_pairs((least, amount), further(strip, shared[device][0]))
        strip = [jnp.where(device > me, new, old) for new, old in zip(passed, strip)]
    entering_strips[1] = value_of(strip)


def middle_kernel(
    per, rows_of, place, cell, received, first, first_strip, costs, edge_costs, anisotropy, levels_one, sides,
    halo, shares, slopes, keeps, misfits, edges_own, edges_factor, slopes_one, gains, message,
    entering_strips, surface_edges, block_halo, strip, shares_strip, slopes_strip, keeps_strip, misfits_strip, sums, counts, sums_strip, counts_strip,
):
    owner_carries(per, first.shape[1], place, received, message, entering_strips, surface_edges, block_halo)
    width_x, near, quakes, width_y = levels_one.shape
    tile = (quakes, width_y)
    lane = iota(tile, 1)
    count = received.shape[0]
    base = received.shape[1] - 4
    me = place[6]
    add_records(rows_of, 3 * per + 3, place, cell, received, sums, counts, sums_strip, counts_strip)
    blank = jnp.full(tile, BIG, jnp.float32)
    unit = jnp.ones(tile, jnp.float32)

    def rows(device, j):
        return jnp.broadcast_to(received[device, base + 3, j : j + 1, :], tile)

    state = [(blank, unit)] * near
    into = []
    for device in range(count):
        into.append([value_of(pair) for pair in state])
        state = [
            join_pairs((received[device, base + z], unit), (state[z][0] + rows(device, 6 * z), state[z][1]))
            for z in range(near)
        ]
    carried = [blank] * near
    for device in range(count):
        carried = [jnp.where(device == me, new, old) for new, old in zip(into[device], carried)]
    back = (blank, unit)
    group = width_y // 8
    for device in reversed(range(count)):
        u, deeper = into[device]
        edge = pltpu.roll(surface_edges[device // group], (width_y - 5 - 8 * (device % group)) % width_y, 1)
        values = [received[device, base + 2], u + rows(device, 1), deeper + rows(device, 5)]
        values.append(jnp.where(lane == 0, edge, pltpu.roll(u, 1, 1)) + rows(device, 2))
        values.append(jnp.where(lane == width_y - 1, edge, pltpu.roll(u, width_y - 1, 1)) + rows(device, 3))
        least, _, amount = softmin(values)
        passed = join_pairs((least, amount), (back[0] + rows(device, 0), back[1]))
        back = [jnp.where(device > me, new, old) for new, old in zip(passed, back)]
    back = value_of(back)

    outside = outside_strips(place, tile)
    strips_in = [[s, shifted_down(s, 2)] for s in (entering_strips[0], entering_strips[1])]
    running = [jnp.zeros(tile, jnp.float32)] * (near + 2)
    prior = carried
    close = []
    for x in range(width_x):
        values = []
        for z in range(near):
            cost = row(costs, z, x, tile)
            running[z] = running[z] + cost
            values.append(soft_pair(first[x, z], carried[z] + running[z]))
            keep, slope = split_pair(levels_one[x, z], prior[z] + cost)
            slopes_one[x, z] = slope
            gains[x, z] = slope * row(anisotropy, z, x, tile) + keep * sides[x, z]
        prior = values
        close.append(values)
        for side in range(2):
            running[near + side] = running[near + side] + edge_costs[3 * side, x]
            value = soft_pair(first_strip[x, side], strips_in[0][side] + running[near + side])
            strip[x, side] = jnp.where(outside[side], BIG, value)
    edges = [[strip[x, side] for x in range(width_x)] for side in range(2)]
    halo[...] = halo_columns(*edges).reshape(halo.shape)

    def keep(x, z, level, w, passed):
        for i in range(4):
            shares[i, x] = w[i]
        keeps[x], slopes[x] = split_pair(level, passed)

    def keep_strip(x, level, w, passed, value):
        shares_strip[x] = w
        keeps_strip[x], slopes_strip[x] = split_pair(level, passed)
        tally = pltpu.roll(counts_strip[...], (width_y - 8 * x) % width_y, 1)
        total = pltpu.roll(sums_strip[...], (width_y - 8 * x) % width_y, 1)
        misfits_strip[x] = ADJ_SCALE * (tally * (value * (1.0 / RATE)) - total)

    def step(lap, carry):
        x = width_x - 1 - lap
        state, strips = sweep_step(x, 1, close[x], strip, costs, edge_costs, halo, *carry, keep, keep_strip)
        misfits[x] = ADJ_SCALE * (row_of(counts, x, tile) * (state[0] * (1.0 / RATE)) - sums[x])
        return state, strips

    all_steps(width_x, step, ([back], strips_in[1]))
    zero = jnp.zeros(tile, jnp.float32)
    own, factor, strip_own, strip_factor = zero, unit, zero, unit
    owns, factors = [], []
    sent = [zero, zero]
    for x in range(width_x):
        own = misfits[x] + own
        owns.append(keeps[x] * own)
        factors.append(keeps[x] * factor)
        own, factor = slopes[x] * own, slopes[x] * factor
        strip_own = misfits_strip[x] + strip_own
        through = keeps_strip[x] * shares_strip[x]
        for i, value in enumerate((strip_own, strip_factor)):
            value = pltpu.roll(through * value, 8 * x, 1) if x else through * value
            sent[i] = jnp.where((lane >> 3) == x, value, sent[i])
        strip_own, strip_factor = slopes_strip[x] * strip_own, slopes_strip[x] * strip_factor
    edges_own[...] = end_columns(sent[0]).reshape(edges_own.shape)
    edges_factor[...] = end_columns(sent[1]).reshape(edges_factor.shape)
    chain = [unit] * near
    blocks = [zero] * near
    links = [zero] * 4
    for x in range(width_x):
        entry = entries_of(owns[x], shares, x, edges_own[x])
        for z in range(near):
            chain[z] = chain[z] * slopes_one[x, z]
            blocks[z] = blocks[z] + chain[z] * entry[z]
        for i, path in enumerate(ways_of(factors[x], shares, x, edges_factor[x])):
            links[i] = links[i] + chain[i // 3] * path
    both = jnp.where(iota(tile, 0) < 5, strip_own, pltpu.roll(strip_factor, 2, 0))
    tiles = [own, factor, both] + blocks + chain + links
    for p in range(message.shape[0]):
        for i, value in enumerate(tiles):
            message[p, 2 * per + i] = value


def end_columns(rows):
    wide = rows.shape[1]
    first, last = shifted_down(rows, 3), pltpu.roll(rows, 3, 0)
    return jnp.transpose(jnp.concatenate([first] * (wide // 16) + [last] * (wide // 16), 0))


def ways_of(passed, shares, x, edge):
    lane = iota(passed.shape, 1)
    last = passed.shape[1] - 1
    above = jnp.where(lane == last, edge, pltpu.roll(passed * shares[1, x], last, 1))
    below = jnp.where(lane == 0, edge, pltpu.roll(passed * shares[2, x], 1, 1))
    return passed * shares[0, x], above, below, passed * shares[3, x]


def entries_of(passed, shares, x, edge):
    own, above, below, deeper = ways_of(passed, shares, x, edge)
    return own + above + below, deeper


def add_records(rows_of, tile_of, place, cell, received, sums, counts, sums_strip, counts_strip):
    width_x, quakes, width_y = sums.shape
    last = tile_of
    span_y = place[2]
    lane = iota((quakes, width_y), 1)
    column = iota((width_y, width_y), 0)
    strip_column = iota((8, width_y), 0)
    strip_column = jnp.where(strip_column == 3, -1, jnp.where(strip_column == 4, width_y, -2))
    share = width_y // rows_of
    dims = (((1,), (1,)), ((), ()))
    one_x = iota((width_x, width_y), 0)
    parts = [[], [], []]
    at, at_rows, at_strip = [], [], []
    for chunk in range(cell.shape[0]):
        records = jnp.zeros((quakes, width_y), jnp.float32)
        for part in range(share):
            piece = received[chunk * share + part, last]
            moved = pltpu.roll(piece, part * rows_of, 1) if part else piece
            records = jnp.where(lane // rows_of == part, moved, records)
        cells = cell[chunk : chunk + 1, :]
        station_x = lax.shift_right_logical(cells, place[7]) - place[0]
        station_y = (cells & (span_y - 1)) - place[1]
        at_x = (one_x == jnp.broadcast_to(station_x, one_x.shape)).astype(jnp.float32)
        pieces = [p.astype(jnp.float32) for p in exact_parts(records)]
        for out, piece in zip(parts, pieces):
            spread = [piece * jnp.broadcast_to(at_x[x : x + 1], piece.shape) for x in range(width_x)]
            out.append(jnp.concatenate(spread, 0).astype(jnp.bfloat16))
        at_rows.append(at_x.astype(jnp.bfloat16))
        hit = column == jnp.broadcast_to(station_y, column.shape)
        at.append(hit.astype(jnp.float32).astype(jnp.bfloat16))
        hit = strip_column == jnp.broadcast_to(station_y, strip_column.shape)
        at_strip.append(hit.astype(jnp.float32).astype(jnp.bfloat16))
    at = jnp.concatenate(at, 1)
    at_rows = jnp.concatenate(at_rows, 1)
    at_strip = jnp.concatenate(at_strip, 1)
    parts = [jnp.concatenate(p, 1) for p in parts]

    def product(a, b):
        return lax.dot_general(a, b, dims, preferred_element_type=jnp.float32)

    main = [product(p, at) for p in parts]
    sums[...] = (main[0] + main[1] + main[2]).reshape(sums.shape)
    counts[...] = product(at_rows, at)
    sums_strip[...] = product(at_strip, parts[0]) + product(at_strip, parts[1]) + product(at_strip, parts[2])
    spread = ((iota((width_x, width_y), 1) >> 3) == one_x).astype(jnp.float32).astype(jnp.bfloat16)
    tally = 0.0
    for part in reversed(exact_parts(product(at_strip, at_rows))):
        tally += lax.dot_general(part, spread, (((1,), (0,)), ((), ())), preferred_element_type=jnp.float32)
    counts_strip[...] = tally


def traveltimes(per, first, entering, costs, halo, times, field):
    width_x, depth, quakes, width_y = first.shape
    tile = (quakes, width_y)
    carried = [[entering[z // per, k * per + z % per] for z in range(depth)] for k in range(2)]

    def finish(x, running):
        sums = [running[z] + row(costs, z, x, tile) for z in range(depth)]
        for z in range(depth):
            field[x, z] = soft_pair(first[x, z], carried[0][z] + sums[z])
        return sums

    all_steps(width_x, finish, [jnp.zeros(tile, jnp.float32)] * depth)

    def step(lap, state):
        x = width_x - 1 - lap
        values = [field[x, z] for z in range(depth)]
        state, _ = sweep_step(x, 0, values, None, costs, None, halo, state, None, None, None)
        for z in range(depth):
            times[pl.ds(z * width_x + x, quakes, stride=depth * width_x), :] = state[z] * (1.0 / RATE)
        return state

    all_steps(width_x, step, carried[1])


def last_kernel(
    per, place, received, first, costs, halo, shares, slopes, keeps, misfits, edges_own, edges_factor, slopes_one,
    gains, anisotropy, times, kernel, field, value, copied, entries, top, sent,
):
    traveltimes(per, first, received, costs, halo, value, field)
    copy = pltpu.make_async_copy(value, times, copied)
    copy.start()
    adjoint(
        2 * per, place, received, shares, slopes, keeps, misfits, edges_own, edges_factor, slopes_one, gains, anisotropy,
        kernel, entries, top, sent,
    )
    copy.wait()


def adjoint(
    base, place, received, shares, slopes, keeps, misfits, edges_own, edges_factor, slopes_one, gains, anisotropy, kernel,
    entries, top, sent,
):
    width_x, quakes, width_y = slopes.shape
    tile = (quakes, width_y)
    near = slopes_one.shape[1]
    count = received.shape[0]
    lane = iota(tile, 1)
    last = width_y - 1
    me = place[6]
    zero = jnp.zeros(tile, jnp.float32)
    group = width_y // 8
    state, strip, mine, mine_strip = zero, zero, zero, zero
    carries = []
    for device in range(count):
        carries.append(state)
        mine = jnp.where(device == me, state, mine)
        at = device % group
        moved = pltpu.roll(strip, 8 * at, 1) if at else strip
        sent[device // group] = moved if at == 0 else jnp.where((lane >> 3) == at, moved, sent[device // group])
        both = received[device, base + 2]
        state = received[device, base] + received[device, base + 1] * state
        strip = both + shifted_down(both, 2) * strip
    ends = [end_columns(sent[i]) for i in range(sent.shape[0])]
    state = [zero] * near
    mine_edge = zero
    for device in reversed(range(count)):
        at = 8 * (device % group)
        edge = ends[device // group][at : at + 8]
        mine_edge = jnp.where(device == me, edge, mine_edge)
        carry = carries[device]
        block = [received[device, base + 3 + z] for z in range(near)]
        above = jnp.where(lane == last, edge, pltpu.roll(carry, last, 1))
        below = jnp.where(lane == 0, edge, pltpu.roll(carry, 1, 1))
        link = [received[device, base + 3 + 2 * near + i] for i in range(4)]
        block[0] = block[0] + link[0] * carry + link[1] * above + link[2] * below
        block[1] = block[1] + link[3] * carry
        for z in range(near):
            passed = block[z] + received[device, base + 3 + near + z] * state[z]
            state[z] = jnp.where(device > me, passed, state[z])
    carry = mine
    for x in range(width_x):
        total = misfits[x] + carry
        carry = slopes[x] * total
        passed = keeps[x] * total
        sideways = row(anisotropy, near, x, tile) * (shares[1, x] + shares[2, x])
        sideways = sideways + row(anisotropy, 2 * near, x, tile) * shares[3, x]
        terms = carry * row(anisotropy, 0, x, tile) + passed * sideways
        top[x : x + 1, :] = jnp.sum(terms, axis=0, keepdims=True)
        entry = entries_of(passed, shares, x, edges_own[x] + edges_factor[x] * mine_edge)
        for z in range(near):
            entries[x, z] = entry[z]
    for x in reversed(range(width_x)):
        for z in range(near):
            total = entries[x, z] + state[z]
            state[z] = slopes_one[x, z] * total
            value = jnp.sum(total * gains[x, z], axis=0, keepdims=True)
            if z == 0:
                value = value + top[x : x + 1, :]
            kernel[z, x : x + 1, :] = value
    for z in range(near, kernel.shape[0]):
        kernel[z] = jnp.zeros(kernel.shape[1:], jnp.float32)


def call(kernel, shapes, operands, scratch=(), scalars=0, far=0, last=False, aliases=()):
    many = isinstance(shapes, list)
    shapes = shapes if many else [shapes]
    out = [jax.ShapeDtypeStruct(s, jnp.float32) if last else pltpu.VMEM(s, jnp.float32) for s in shapes]
    result = pl.pallas_call(
        kernel,
        out_shape=out,
        in_specs=[SMEM] * scalars + [FAR] * far + [VMEM] * (len(operands) - scalars - far),
        out_specs=[FAR] * last + [VMEM] * (len(out) - last),
        scratch_shapes=[pltpu.VMEM(s, jnp.float32) if isinstance(s, tuple) else s for s in scratch],
        compiler_params=PARAMS,
        input_output_aliases=dict(aliases),
    )(*operands)
    return result if many else result[0]


def traded(message):
    return lax.all_to_all(message, "gx", 0, 0, tiled=True)


def rotated(value, axis, by):
    count = lax.axis_size(axis)
    return lax.ppermute(value, axis, [(i, (i + by) % count) for i in range(count)])


def body(warm_start, slowness, anisotropy, observed, station_cell, source_cell):
    quakes, depth, width_x, width_y = warm_start.shape
    count_x, count_y = lax.axis_size("gx"), lax.axis_size("gy")
    index_x, index_y = lax.axis_index("gx"), lax.axis_index("gy")
    span_x, span_y = width_x * count_x, width_y * count_y
    near = 2
    per = max(1, depth // count_x)
    tile = (quakes, width_y)
    top = (width_x,) + tile
    close = (width_x, near) + tile
    field = (width_x, depth) + tile
    place = jnp.stack(
        [
            index_x * width_x,
            index_y * width_y,
            jnp.int32(span_y),
            jnp.int32(span_x * span_y),
            (index_y == 0).astype(jnp.int32),
            (index_y == count_y - 1).astype(jnp.int32),
            index_x,
            jnp.int32(span_y.bit_length() - 1),
            index_y,
        ]
    ).astype(jnp.int32)
    anis = anisotropy.reshape(3 * depth, width_x, width_y)
    local_records = observed.shape[1]
    flat = (quakes * depth * width_x, width_y)

    sources = [warm_start.reshape(quakes, depth * width_x, width_y), observed, slowness, anis]
    sources = [pltpu.with_memory_space_constraint(a, pltpu.HBM) for a in [source_cell] + sources]
    start, costs, anis, edge, to_right, to_left, records = call(
        pack_kernel,
        [field, anis.shape, (3 * near, width_x, width_y), (11 * width_x, width_y)]
        + [(6 * width_x + quakes, width_y)] * 2
        + [tile],
        [place] + sources,
        [pltpu.SMEM((quakes,), jnp.int32), (CHUNKS, quakes, depth // CHUNKS * width_x, width_y)]
        + [a.shape for a in sources[2:]]
        + [pltpu.SemaphoreType.DMA((4 + CHUNKS,))],
        scalars=1,
        far=5,
    )
    from_left = rotated(to_right, "gy", 1)
    from_right = rotated(to_left, "gy", -1)
    others = [rotated(records, "gy", by) for by in range(2, count_y - 1)]

    message_shape = (count_x, 3 * per + (8 if per > 1 else 9)) + tile
    first, first_strip, edge_costs, levels_one, sides, message = call(
        functools.partial(first_sweep_kernel, local_records, count_y, per),
        [field, (width_x, 2) + tile, (6,) + top, close, close, message_shape],
        [place, start, edge, records, from_left, from_right, costs, anis] + others,
        [(depth,) + tile, (width_x, 2) + tile],
        scalars=1,
    )
    reach = traded(message)
    chunks = -(-count_x // (width_y // 8))
    halo, *rest, message = call(
        functools.partial(middle_kernel, per, local_records * count_y),
        [(depth,) + tile, (4,) + top] + [top] * 5 + [close, close, (count_x, 2 * per + 7 + 2 * near) + tile],
        [place, station_cell.reshape(-1, width_y), reach, first, first_strip, costs, edge_costs, anis, levels_one, sides],
        [(2,) + tile, (chunks,) + tile, (chunks, depth) + tile, (width_x, 2) + tile]
        + [top] * 5
        + [(width_x, width_y), tile, tile],
        scalars=1,
    )
    times, kernel = call(
        functools.partial(last_kernel, per),
        [flat, (depth, width_x, width_y)],
        [place, traded(message), first, costs, halo] + rest + [anis],
        [field, flat, pltpu.SemaphoreType.DMA, close, (width_x, width_y), (chunks,) + tile],
        scalars=1,
        last=True,
    )
    return (times.reshape(warm_start.shape), kernel)


def solution(mesh):
    return jax.shard_map(
        body,
        mesh=mesh,
        in_specs=(
            P(None, None, "gx", "gy"),
            P(None, "gx", "gy"),
            P(None, None, "gx", "gy"),
            P(None, ("gx", "gy")),
            P(),
            P(),
        ),
        out_specs=(P(None, None, "gx", "gy"), P(None, "gx", "gy")),
        check_vma=False,
    )
```

```python
import functools
import math

import jax
import jax.numpy as jnp
from jax import lax
from jax.experimental import pallas as pl
from jax.experimental.pallas import tpu as pltpu
from jax.sharding import PartitionSpec as P

TAU = 0.05
ADJ_SCALE = 0.1
LOG2E = math.log2(math.e)
RATE = LOG2E / TAU
BIG = 10000.0 * RATE
UNROLL = 8
CHUNKS = 4
VMEM = pl.BlockSpec(memory_space=pltpu.VMEM)
FAR = pl.BlockSpec(memory_space=pl.ANY)
SMEM = pl.BlockSpec(memory_space=pltpu.SMEM)
PARAMS = pltpu.CompilerParams(vmem_limit_bytes=8 * 1024 * 1024)


def softmin(values):
    least = functools.reduce(jnp.minimum, values)
    parts = [jnp.exp2(least - v) for v in values]
    return least, parts, functools.reduce(jnp.add, parts)


def soft_pair(first, second):
    return jnp.minimum(first, second) - LOG2E * jnp.log(1.0 + jnp.exp2(-jnp.abs(first - second)))


def add_pair(least, total, passed):
    low = jnp.minimum(least, passed)
    return low - LOG2E * jnp.log(total * jnp.exp2(low - least) + jnp.exp2(low - passed))


def join_pairs(first, second):
    low = jnp.minimum(first[0], second[0])
    return low, first[1] * jnp.exp2(low - first[0]) + second[1] * jnp.exp2(low - second[0])


def value_of(pair):
    return pair[0] - LOG2E * jnp.log(pair[1])


def split_pair(first, second):
    gap = jnp.exp2(-jnp.abs(first - second))
    share = 1.0 / (1.0 + gap)
    less = gap * share
    nearer = first <= second
    return jnp.where(nearer, share, less), jnp.where(nearer, less, share)


def iota(shape, axis):
    return lax.broadcasted_iota(jnp.int32, shape, axis)


def row(ref, index, x, like):
    return jnp.broadcast_to(ref[index, pl.ds(x, 1), :], like)


def row_of(ref, x, like):
    return jnp.broadcast_to(ref[pl.ds(x, 1), :], like)


def all_steps(count, step, carry):
    for i in range(count):
        carry = step(i, carry)
    return carry


def by_steps(count, step, carry):
    def group(i, carry):
        for j in range(UNROLL):
            carry = step(i * UNROLL + j, carry)
        return carry

    return lax.fori_loop(0, count // UNROLL, group, carry)


def packed(left, right):
    return jnp.where(iota(left.shape, 0) < 5, left, pltpu.roll(right, 2, 0))


def merged(left, right):
    return jnp.where(iota(left.shape, 0) < 4, left, right)


def shifted_down(tile, by):
    return pltpu.roll(tile, tile.shape[0] - by, 0)


def exact_parts(value):
    high = value.astype(jnp.bfloat16).astype(jnp.float32)
    middle = (value - high).astype(jnp.bfloat16).astype(jnp.float32)
    low = value - high - middle
    return [p.astype(jnp.bfloat16) for p in (high, middle, low)]


def pack_kernel(
    place, source_far, warm_far, observed_far, slowness_far, anisotropy_far, stations_far,
    start, costs, near, edge, to_right, to_left, records, stations,
    source, warm, observed, slowness, anisotropy, arrived,
):
    pairs = [(slowness_far, slowness), (anisotropy_far, anisotropy), (observed_far, observed)]
    share = start.shape[1] // CHUNKS
    span = share * start.shape[0]
    pairs += [(warm_far.at[:, pl.ds(i * span, span)], warm.at[i]) for i in range(CHUNKS)]
    pairs += [(stations_far, stations), (source_far, source)]
    copies = [pltpu.make_async_copy(a, b, arrived.at[i]) for i, (a, b) in enumerate(pairs)]
    for copy in copies:
        copy.start()
    width_x, depth, quakes, width_y = start.shape
    tile = (quakes, width_y)
    quake = iota(tile, 0)
    lane = iota(tile, 1)
    span_y = place[2]
    plane = place[3]
    rows = width_x * 8
    wide = (width_x, width_y)
    group = iota(wide, 1) >> 3
    copies[0].wait()
    copies[1].wait()
    native = []
    for k in range(3):
        columns = jnp.zeros(wide, jnp.float32)
        for z in range(depth):
            cost = slowness[z] * anisotropy[k * depth + z] * RATE
            costs[k * depth + z] = cost
            columns = jnp.where(group == z, pltpu.roll(cost, 8 * z + 4, 1), columns)
        edge[rows : rows + width_x, :] = columns
        rows += width_x
        native.append(columns)
        for z in range(near.shape[0] // 3):
            near[k * (near.shape[0] // 3) + z] = anisotropy[k * depth + z]
    early = (iota(wide, 1) & 7) < 4
    at = slice(4 * width_x, 5 * width_x)
    to_right[at, :] = jnp.where(early, native[0], pltpu.roll(native[1], 4, 1))
    to_left[at, :] = jnp.where(early, pltpu.roll(native[1], width_y - 4, 1), native[0])
    at = slice(5 * width_x, 6 * width_x)
    to_right[at, :] = native[2]
    to_left[at, :] = native[2]
    copies[-1].wait()
    cell = jnp.zeros(tile, jnp.int32)
    for e in range(quakes):
        cell = jnp.where(quake == e, source[e], cell)
    cell = cell - (lane + place[0] * span_y + place[1])
    edges = []
    for i in range(CHUNKS):
        copies[3 + i].wait()
        here = warm.at[i].reshape(quakes * share * width_x, width_y)

        chunk = [jnp.zeros(tile, jnp.float32)] * share
        for x in range(width_x):
            mine = (lane >> 3) == x
            for k in range(share):
                value = here[pl.ds(k * width_x + x, quakes, stride=share * width_x), :] * RATE
                value = jnp.where(cell == (i * share + k) * plane + x * span_y, 0.0, value)
                start[x, i * share + k] = value
                chunk[k] = jnp.where(mine, pltpu.roll(value, (8 * x + 4) % width_y, 1), chunk[k])
        edges += chunk
    columns = jnp.transpose(jnp.concatenate(edges, 0))
    edge[: width_x * 8, :] = columns
    low = quake < 4
    for x in range(0, width_x, 2):
        one, two = columns[8 * x : 8 * x + 8], columns[8 * x + 8 : 8 * x + 16]
        to_right[4 * x : 4 * x + 8, :] = jnp.where(low, one, pltpu.roll(two, 4, 0))
        to_left[4 * x : 4 * x + 8, :] = jnp.where(low, pltpu.roll(one, 4, 0), two)
    copies[2].wait()
    copies[-2].wait()
    records[...] = jnp.zeros(tile, jnp.float32)
    records[:, : observed.shape[1]] = observed[...]
    for message in (to_right, to_left):
        message[6 * width_x :, :] = records[...]


def halo_columns(left, right):
    rows = []
    for l, r in zip(left, right):
        rows.append(jnp.where(iota(l.shape, 0) == 4, r, pltpu.roll(l, 2, 0)))
    return jnp.transpose(jnp.concatenate(rows, 0))


def cost_columns(message, width_x, turn):
    pair = message[4 * width_x : 5 * width_x, :]
    return [pair, pltpu.roll(pair, turn, 1), message[5 * width_x : 6 * width_x, :]]


def strip_costs(own, from_left, from_right, out, width_x, depth):
    tile = own.shape[1]
    base = width_x * 8
    lane = iota((8, tile), 1)
    low = (lane & 7) < 4
    mine = (lane & 7) == iota((8, tile), 0)
    spread = ((iota((tile, tile), 0) >> 3) == (iota((tile, tile), 1) >> 3)).astype(jnp.float32)
    spread = spread.astype(jnp.bfloat16)
    for side in range(2):
        for k in range(3):
            rows = []
            for x in range(width_x):
                at = slice(base + k * width_x + x, base + k * width_x + x + 1)
                here = jnp.broadcast_to(own[at, :], lane.shape)
                there = jnp.broadcast_to((from_right if side else from_left)[k][x : x + 1], lane.shape)
                value = jnp.where(low, here, there) if side else jnp.where(low, there, here)
                rows.append(jnp.where(mine, value, 0.0))
            whole = jnp.concatenate(rows, 0)
            total = 0.0
            for part in reversed(exact_parts(whole)):
                total = total + lax.dot_general(
                    part, spread, (((1,), (0,)), ((), ())), preferred_element_type=jnp.float32
                )
            out[3 * side + k] = total.reshape(width_x, 8, tile)


def running_sum(value):
    rows = iota(value.shape, 0)
    by = 1
    while by < value.shape[0]:
        value = value + jnp.where(rows >= by, pltpu.roll(value, by, 0), 0.0)
        by *= 2
    return value


def log_sum(exponents):
    return -LOG2E * jnp.log(functools.reduce(jnp.add, [jnp.exp2(-e) for e in exponents]))


def passages(costs, from_left, from_right, depth):
    width_x, width_y = costs.shape[1:]
    lane = iota((width_x, width_y), 1)
    beside = jnp.where((lane & 7) == 4, running_sum(from_right), pltpu.roll(running_sum(from_left), 2, 1))
    sums = [running_sum(costs[z]) for z in range(depth)]
    sub = iota((8, width_y), 0)
    tiles = []
    for z in range(depth):
        back = sums[z] - costs[z]
        edge = pltpu.roll(beside, width_y - 5 - 8 * z, 1)
        below = jnp.where(lane == 0, edge, pltpu.roll(sums[z], 1, 1))
        above = jnp.where(lane == width_y - 1, edge, pltpu.roll(sums[z], width_y - 1, 1))
        step_y = back + costs[depth + z]
        step_z = back + costs[2 * depth + z]
        paths = [sums[z] + back, below + step_y, above + step_y]
        paths.append(sums[z - 1] + step_z if z > 0 else None)
        paths.append(sums[z + 1] + step_z if z < depth - 1 else None)
        tile = jnp.broadcast_to(sums[z][width_x - 1 :, :], sub.shape)
        for j, path in enumerate(paths):
            if path is None:
                tile = jnp.where(sub == j + 1, BIG, tile)
            else:
                total = jnp.sum(jnp.exp2(-path), axis=0, keepdims=True)
                tile = jnp.where(sub == j + 1, -LOG2E * jnp.log(total), tile)
        tiles.append(tile)
    return tiles


def strip_passages(edge_costs, width_x):
    shape = edge_costs.shape[2:]
    lane = iota(shape, 1)
    sums = jnp.zeros(shape, jnp.float32)
    totals = [jnp.zeros(shape, jnp.float32)] * 5
    for x in range(width_x):
        cost, step_y, step_z = [packed(edge_costs[k, x], edge_costs[3 + k, x]) for k in range(3)]
        back = sums
        sums = sums + cost
        step_y, step_z = step_y + back, step_z + back
        paths = [sums + back, pltpu.roll(sums, 1, 0) + step_y, shifted_down(sums, 1) + step_y]
        paths.append(jnp.where(lane < 8, BIG, pltpu.roll(sums, 8, 1) + step_z))
        paths.append(jnp.where(lane >= shape[1] - 8, BIG, pltpu.roll(sums, shape[1] - 8, 1) + step_z))
        totals = [t + jnp.exp2(-p) for t, p in zip(totals, paths)]
    return sums, [-LOG2E * jnp.log(jnp.maximum(t, 1e-37)) for t in totals]


PLACES = ((2, 0, 16), (4, 16, 16), (5, 32, 16), (7, 48, 16))
BACK_PLACES = ((3, 64, 8), (6, 72, 8))


def shared_tile(reach, back, records):
    lane, sub = iota(reach.shape, 1), iota(reach.shape, 0)
    extra = reach
    for value, places in ((reach, PLACES), (back, BACK_PLACES)):
        for at, low, width in places:
            moved = pltpu.roll(pltpu.roll(value, (2 - at) % 8, 0), low, 1) if low else value
            extra = jnp.where((lane >= low) & (lane < low + width), moved, extra)
    half = reach.shape[1] // 2
    record = jnp.where(lane < half, pltpu.roll(records, 4, 0), pltpu.roll(records, half, 1))
    tile = jnp.where(sub == 0, shifted_down(reach, 3), jnp.where(sub == 1, shifted_down(reach, 5), extra))
    return jnp.where(sub < 4, tile, record)


def unshared_tile(tile):
    sub = iota(tile.shape, 0)
    wide = tile.shape[1]
    reach = jnp.where(sub == 3, pltpu.roll(tile, 3, 0), jnp.where(sub == 6, pltpu.roll(tile, 5, 0), tile))
    for at, low, _ in PLACES[1:]:
        reach = jnp.where(sub == at, pltpu.roll(pltpu.roll(tile, at - 2, 0), wide - low, 1), reach)
    back = [pltpu.roll(pltpu.roll(tile, at - 2, 0), wide - low, 1) for at, low, _ in BACK_PLACES]
    return reach, jnp.where(sub == 3, back[0], back[1])


def shared_rows(total, paths):
    place = iota(total.shape, 1) & 7
    first, second = total, total
    for q in range(6):
        value = pltpu.roll(total, (4 - q) % 8, 0)
        first = jnp.where(place == q, value, first)
    for q, (path, at) in enumerate([(p, r) for p in paths for r in (3, 6)]):
        if q < 2:
            first = jnp.where(place == 6 + q, pltpu.roll(path, (6 - at) % 8, 0), first)
        else:
            second = jnp.where(place == q - 2, pltpu.roll(path, (7 - at) % 8, 0), second)
    return jnp.where(iota(total.shape, 0) == 6, first, second)


def spread_rows(tiles):
    shape = tiles[0].shape
    wide = shape[1]
    sub = iota(shape, 0)
    mine = (iota(shape, 1) & 7) == sub
    spread = ((iota((wide, wide), 0) >> 3) == (iota((wide, wide), 1) >> 3)).astype(jnp.float32)
    spread = spread.astype(jnp.bfloat16)
    rows = [jnp.where(mine, jnp.broadcast_to(t[r : r + 1], shape), 0.0) for t in tiles for r in (6, 7)]
    whole = jnp.concatenate(rows, 0)
    value = 0.0
    for part in reversed(exact_parts(whole)):
        value = value + lax.dot_general(part, spread, (((1,), (0,)), ((), ())), preferred_element_type=jnp.float32)
    out = []
    for i in range(len(tiles)):
        first, second = value[16 * i : 16 * i + 8], value[16 * i + 8 : 16 * i + 16]
        paths = [jnp.where(sub == 3, pltpu.roll(first, 5, 0), pltpu.roll(first, 7, 0))]
        for q in range(4):
            at_three = pltpu.roll(second, (3 - 2 * q) % 8, 0)
            at_six = pltpu.roll(second, (6 - 2 * q - 1) % 8, 0)
            paths.append(jnp.where(sub == 3, at_three, at_six))
        out.append((pltpu.roll(first, 2, 0), paths))
    return out


def sweep_step(x, near, levels, strip, costs, edge_costs, halo, state, strip_state, keep, keep_strip):
    depth = costs.shape[0] // 3
    tile = levels[0].shape
    width_y = tile[1]
    lane = iota(tile, 1)
    out = []
    for z in range(len(state)):
        u = levels[z]
        cost_y = row(costs, depth + z, x, tile)
        cost_z = row(costs, 2 * depth + z, x, tile)
        edge = pltpu.roll(halo[z], width_y - 5 - 8 * x, 1)
        values = [u]
        values.append(jnp.where(lane == 0, edge, pltpu.roll(u, 1, 1)) + cost_y)
        values.append(jnp.where(lane == width_y - 1, edge, pltpu.roll(u, width_y - 1, 1)) + cost_y)
        if z > 0:
            values.append(levels[z - 1] + cost_z)
        if z < depth - 1:
            values.append(levels[z + 1] + cost_z)
        least, parts, total = softmin(values)
        passed = state[z] + row(costs, z, x, tile)
        if z < near:
            scale = 1.0 / total
            keep(x, z, value_of((least, total)), [p * scale for p in parts], passed)
        out.append(add_pair(least, total, passed))
    strips, relaxed, weights, passes = [], [], [], []
    for side in range(2 if strip is not None else 0):
        u = strip[x, side]
        cost_y = edge_costs[3 * side + 1, x]
        cost_z = edge_costs[3 * side + 2, x]
        values = [u, pltpu.roll(u, 1, 0) + cost_y, pltpu.roll(u, 7, 0) + cost_y]
        values.append(jnp.where(lane < 8, BIG, pltpu.roll(u, 8, 1)) + cost_z)
        values.append(jnp.where(lane >= width_y - 8, BIG, pltpu.roll(u, width_y - 8, 1)) + cost_z)
        least, parts, total = softmin(values)
        passes.append(strip_state[side] + edge_costs[3 * side, x])
        strips.append(add_pair(least, total, passes[side]))
        if keep_strip is not None:
            relaxed.append(value_of((least, total)))
            weights.append(parts[2 - side] / total)
    if keep_strip is not None:
        keep_strip(x, merged(*relaxed), merged(*weights), merged(*passes), merged(*strips))
    return out, strips


def outside_strips(place, shape):
    sub = iota(shape, 0)
    return [(place[4] == 1) & (sub < 4), (place[5] == 1) & (sub >= 4)]


def first_sweep_kernel(
    rows_of, count_y, per, place, field, own, mine, from_left, from_right, costs, anisotropy, *rest
):
    others = rest[: count_y - 3]
    local, local_strip, edge_costs, levels, sides, message, halo, strip = rest[count_y - 3 :]
    width_x, depth, quakes, width_y = field.shape
    tile = (quakes, width_y)
    sub = iota(tile, 0)
    low = sub < 4
    near = levels.shape[1]
    last = 6 * width_x
    far = [mine[...], from_left[last:, :]] + [o[...] for o in others] + [from_right[last:, :]]
    records = jnp.zeros(tile, jnp.float32)
    for by, piece in enumerate(far):
        owner = lax.rem(place[8] + count_y - by, count_y)
        records = records + pltpu.roll(piece, owner * rows_of, 1)
    left, right = [], []
    for x in range(width_x):
        at = slice(8 * x, 8 * x + 8)
        two = slice(8 * (x // 2), 8 * (x // 2) + 8)
        before, after = from_left[two, :], from_right[two, :]
        if x % 2:
            before = pltpu.roll(before, 4, 0)
        else:
            after = pltpu.roll(after, 4, 0)
        before = jnp.where(place[4] == 1, BIG, before)
        after = jnp.where(place[5] == 1, BIG, after)
        left.append(jnp.where(low, before, own[at, :]))
        right.append(jnp.where(low, own[at, :], after))
        strip[x, 0] = left[x]
        strip[x, 1] = right[x]
    halo[...] = halo_columns(left, right).reshape(halo.shape)
    left_costs = cost_columns(from_left, width_x, width_y - 4)
    right_costs = cost_columns(from_right, width_x, 4)
    strip_costs(own, left_costs, right_costs, edge_costs, width_x, depth)
    outside = outside_strips(place, tile)

    def keep(x, z, level, w, passed):
        levels[x, z] = level
        vertical = w[3] if z == 0 else w[3] + w[4]
        sideways = row(anisotropy, near + z, x, tile) * (w[1] + w[2])
        sides[x, z] = sideways + row(anisotropy, 2 * near + z, x, tile) * vertical

    def step(x, carry):
        state, strips = sweep_step(x, near, [field[x, z] for z in range(depth)], strip, costs, edge_costs, halo, *carry, keep, None)
        for z in range(depth):
            local[x, z] = state[z]
        for side in range(2):
            local_strip[x, side] = jnp.where(outside[side], BIG, strips[side])
        return state, strips

    blank = jnp.full(tile, BIG, jnp.float32)
    state, strips = all_steps(width_x, step, ([blank] * depth, [blank] * 2))
    reach_strip = packed(*[jnp.where(o, BIG, s) for o, s in zip(outside, strips)])

    edges = [[local_strip[x, side] for x in range(width_x)] for side in range(2)]
    halo[...] = halo_columns(*edges).reshape(halo.shape)

    def again(lap, carry):
        x = width_x - 1 - lap
        values = [local[x, z] for z in range(depth)]
        return sweep_step(x, 0, values, local_strip, costs, edge_costs, halo, *carry, None, None)

    back, back_strips = all_steps(width_x, again, ([blank] * depth, [blank] * 2))
    tiles = passages(costs, left_costs[0], right_costs[0], depth)
    strip_total, strip_paths = strip_passages(edge_costs, width_x)

    strip_tile = shared_tile(reach_strip, packed(*back_strips), records)
    shared = shared_rows(strip_total, strip_paths)
    count = message.shape[0]
    for p in range(count):
        first = min(p * per, depth - per)
        for k in range(per + 2):
            z = first + k - 1
            message[p, k] = state[z] if 0 <= z < depth else blank
        for k in range(per):
            message[p, per + 2 + k] = back[first + k]
            value = tiles[first + k]
            if k == 0 and first > 0:
                value = jnp.where(sub == 6, jnp.broadcast_to(tiles[first - 1][:1], tile), value)
            if k == 0 and first + per < depth:
                value = jnp.where(sub == 7, jnp.broadcast_to(tiles[first + per][:1], tile), value)
            if per > 1 and k == 1:
                value = jnp.where(sub < 6, value, shared)
            message[p, 2 * per + 2 + k] = value
        message[p, 3 * per + 2] = strip_tile
        if per == 1:
            message[p, 3 * per + 3] = shared
        surface = [state[0], state[1], back[0], jnp.where(sub < 6, tiles[0], jnp.broadcast_to(tiles[1][:1], tile))]
        for i, value in enumerate(surface):
            message[p, message.shape[1] - 4 + i] = value


def owner_carries(
    per, depth, place, received, entering, entering_strips, surface_edges, halo,
):
    count = received.shape[0]
    tile = entering.shape[2:]
    lane = iota(tile, 1)
    width_y = tile[1]
    me = place[6]
    blank = jnp.full(tile, BIG, jnp.float32)
    unit = jnp.ones(tile, jnp.float32)
    side = 3 * per + 2

    def rows(device, k, j):
        return jnp.broadcast_to(received[device, 2 * per + 2 + k, j : j + 1, :], tile)

    def total(device, k):
        if k < 0:
            return rows(device, 0, 6)
        return rows(device, k, 0) if k < per else rows(device, 0, 7)

    def further(pair, cost):
        return pair[0] + cost, pair[1]

    shared = [received[d, 2 * per + 3] if per > 1 else received[d, 3 * per + 3] for d in range(count)]
    strips = [unshared_tile(received[d, side]) for d in range(count)]
    shared = spread_rows(shared)
    state = [(blank, unit)] * (per + 2)
    strip = (blank, unit)
    first, first_strip = [], []
    for device in range(count):
        first.append([value_of(pair) for pair in state])
        first_strip.append(value_of(strip))
        state = [
            join_pairs((received[device, k], unit), further(state[k], total(device, k - 1))) for k in range(per + 2)
        ]
        strip = join_pairs((strips[device][0], unit), further(strip, shared[device][0]))
    own = blank
    for device in range(count):
        own = jnp.where(device == me, first_strip[device], own)
        for k in range(per):
            entering[device, k] = first[device][k + 1]
    entering_strips[0] = own
    group = width_y // 8
    for at in range(0, count, group):
        some = first_strip[at : at + group]
        some = some + [blank] * (group - len(some))
        turned = halo_columns(some, [shifted_down(s, 2) for s in some])
        halo[at // group] = turned.reshape(halo.shape[1:])
        surface_edges[at // group] = turned[: tile[0]]
    low = jnp.minimum(me * per, depth - per)
    edges = [[halo[i, low + k] for k in range(per)] for i in range(halo.shape[0])]
    state = [(blank, unit)] * per
    strip = (blank, unit)
    for device in reversed(range(count)):
        for k in range(per):
            entering[device, per + k] = value_of(state[k])
            u = first[device][k + 1]
            turn = (width_y - 5 - 8 * (device % group)) % width_y
            edge = pltpu.roll(edges[device // group][k], turn, 1)
            values = [received[device, per + 2 + k], u + rows(device, k, 1)]
            values.append(jnp.where(lane == 0, edge, pltpu.roll(u, 1, 1)) + rows(device, k, 2))
            values.append(jnp.where(lane == width_y - 1, edge, pltpu.roll(u, width_y - 1, 1)) + rows(device, k, 3))
            values.append(first[device][k] + rows(device, k, 4))
            values.append(first[device][k + 2] + rows(device, k, 5))
            least, _, amount = softmin(values)
            state[k] = join_pairs((least, amount), further(state[k], total(device, k)))
        u = first_strip[device]
        back = strips[device][1]
        paths = shared[device][1]
        values = [back, u + paths[0], pltpu.roll(u, 1, 0) + paths[1], shifted_down(u, 1) + paths[2]]
        values.append(jnp.where(lane < 8, BIG, pltpu.roll(u, 8, 1)) + paths[3])
        values.append(jnp.where(lane >= width_y - 8, BIG, pltpu.roll(u, width_y - 8, 1)) + paths[4])
        least, _, amount = softmin(values)
        passed = join_pairs((least, amount), further(strip, shared[device][0]))
        strip = [jnp.where(device > me, new, old) for new, old in zip(passed, strip)]
    entering_strips[1] = value_of(strip)


def middle_kernel(
    per, rows_of, place, cell, received, first, first_strip, costs, edge_costs, anisotropy, levels_one, sides,
    halo, shares, slopes, keeps, misfits, edges_own, edges_factor, slopes_one, gains, message,
    entering_strips, surface_edges, block_halo, strip, shares_strip, slopes_strip, keeps_strip, misfits_strip, sums, counts, sums_strip, counts_strip,
):
    owner_carries(per, first.shape[1], place, received, message, entering_strips, surface_edges, block_halo)
    width_x, near, quakes, width_y = levels_one.shape
    tile = (quakes, width_y)
    lane = iota(tile, 1)
    count = received.shape[0]
    base = received.shape[1] - 4
    me = place[6]
    add_records(rows_of, 3 * per + 2, place, cell, received, sums, counts, sums_strip, counts_strip)
    blank = jnp.full(tile, BIG, jnp.float32)
    unit = jnp.ones(tile, jnp.float32)

    def rows(device, j):
        return jnp.broadcast_to(received[device, base + 3, j : j + 1, :], tile)

    state = [(blank, unit)] * near
    into = []
    for device in range(count):
        into.append([value_of(pair) for pair in state])
        state = [
            join_pairs((received[device, base + z], unit), (state[z][0] + rows(device, 6 * z), state[z][1]))
            for z in range(near)
        ]
    carried = [blank] * near
    for device in range(count):
        carried = [jnp.where(device == me, new, old) for new, old in zip(into[device], carried)]
    back = (blank, unit)
    group = width_y // 8
    for device in reversed(range(count)):
        u, deeper = into[device]
        edge = pltpu.roll(surface_edges[device // group], (width_y - 5 - 8 * (device % group)) % width_y, 1)
        values = [received[device, base + 2], u + rows(device, 1), deeper + rows(device, 5)]
        values.append(jnp.where(lane == 0, edge, pltpu.roll(u, 1, 1)) + rows(device, 2))
        values.append(jnp.where(lane == width_y - 1, edge, pltpu.roll(u, width_y - 1, 1)) + rows(device, 3))
        least, _, amount = softmin(values)
        passed = join_pairs((least, amount), (back[0] + rows(device, 0), back[1]))
        back = [jnp.where(device > me, new, old) for new, old in zip(passed, back)]
    back = value_of(back)

    outside = outside_strips(place, tile)
    strips_in = [[s, shifted_down(s, 2)] for s in (entering_strips[0], entering_strips[1])]
    running = [jnp.zeros(tile, jnp.float32)] * (near + 2)
    prior = carried
    close = []
    for x in range(width_x):
        values = []
        for z in range(near):
            cost = row(costs, z, x, tile)
            running[z] = running[z] + cost
            values.append(soft_pair(first[x, z], carried[z] + running[z]))
            keep, slope = split_pair(levels_one[x, z], prior[z] + cost)
            slopes_one[x, z] = slope
            gains[x, z] = slope * row(anisotropy, z, x, tile) + keep * sides[x, z]
        prior = values
        close.append(values)
        for side in range(2):
            running[near + side] = running[near + side] + edge_costs[3 * side, x]
            value = soft_pair(first_strip[x, side], strips_in[0][side] + running[near + side])
            strip[x, side] = jnp.where(outside[side], BIG, value)
    edges = [[strip[x, side] for x in range(width_x)] for side in range(2)]
    halo[...] = halo_columns(*edges).reshape(halo.shape)

    def keep(x, z, level, w, passed):
        for i in range(4):
            shares[i, x] = w[i]
        keeps[x], slopes[x] = split_pair(level, passed)

    def keep_strip(x, level, w, passed, value):
        shares_strip[x] = w
        keeps_strip[x], slopes_strip[x] = split_pair(level, passed)
        tally = pltpu.roll(counts_strip[...], (width_y - 8 * x) % width_y, 1)
        total = pltpu.roll(sums_strip[...], (width_y - 8 * x) % width_y, 1)
        misfits_strip[x] = ADJ_SCALE * (tally * (value * (1.0 / RATE)) - total)

    def step(lap, carry):
        x = width_x - 1 - lap
        state, strips = sweep_step(x, 1, close[x], strip, costs, edge_costs, halo, *carry, keep, keep_strip)
        misfits[x] = ADJ_SCALE * (row_of(counts, x, tile) * (state[0] * (1.0 / RATE)) - sums[x])
        return state, strips

    all_steps(width_x, step, ([back], strips_in[1]))
    zero = jnp.zeros(tile, jnp.float32)
    own, factor, strip_own, strip_factor = zero, unit, zero, unit
    owns, factors = [], []
    sent = [zero, zero]
    for x in range(width_x):
        own = misfits[x] + own
        owns.append(keeps[x] * own)
        factors.append(keeps[x] * factor)
        own, factor = slopes[x] * own, slopes[x] * factor
        strip_own = misfits_strip[x] + strip_own
        through = keeps_strip[x] * shares_strip[x]
        for i, value in enumerate((strip_own, strip_factor)):
            value = pltpu.roll(through * value, 8 * x, 1) if x else through * value
            sent[i] = jnp.where((lane >> 3) == x, value, sent[i])
        strip_own, strip_factor = slopes_strip[x] * strip_own, slopes_strip[x] * strip_factor
    edges_own[...] = end_columns(sent[0]).reshape(edges_own.shape)
    edges_factor[...] = end_columns(sent[1]).reshape(edges_factor.shape)
    chain = [unit] * near
    blocks = [zero] * near
    links = [zero] * 4
    for x in range(width_x):
        entry = entries_of(owns[x], shares, x, edges_own[x])
        for z in range(near):
            chain[z] = chain[z] * slopes_one[x, z]
            blocks[z] = blocks[z] + chain[z] * entry[z]
        for i, path in enumerate(ways_of(factors[x], shares, x, edges_factor[x])):
            links[i] = links[i] + chain[i // 3] * path
    both = jnp.where(iota(tile, 0) < 5, strip_own, pltpu.roll(strip_factor, 2, 0))
    tiles = [own, factor, both] + blocks + chain + links
    for p in range(message.shape[0]):
        for i, value in enumerate(tiles):
            message[p, 2 * per + i] = value


def end_columns(rows):
    wide = rows.shape[1]
    first, last = shifted_down(rows, 3), pltpu.roll(rows, 3, 0)
    return jnp.transpose(jnp.concatenate([first] * (wide // 16) + [last] * (wide // 16), 0))


def ways_of(passed, shares, x, edge):
    lane = iota(passed.shape, 1)
    last = passed.shape[1] - 1
    above = jnp.where(lane == last, edge, pltpu.roll(passed * shares[1, x], last, 1))
    below = jnp.where(lane == 0, edge, pltpu.roll(passed * shares[2, x], 1, 1))
    return passed * shares[0, x], above, below, passed * shares[3, x]


def entries_of(passed, shares, x, edge):
    own, above, below, deeper = ways_of(passed, shares, x, edge)
    return own + above + below, deeper


def add_records(rows_of, tile_of, place, cell, received, sums, counts, sums_strip, counts_strip):
    width_x, quakes, width_y = sums.shape
    last = tile_of
    span_y = place[2]
    lane = iota((quakes, width_y), 1)
    column = iota((width_y, width_y), 0)
    strip_column = iota((8, width_y), 0)
    strip_column = jnp.where(strip_column == 3, -1, jnp.where(strip_column == 4, width_y, -2))
    share = width_y // rows_of
    dims = (((1,), (1,)), ((), ()))
    one_x = iota((width_x, width_y), 0)
    parts = [[], [], []]
    at, at_rows, at_strip = [], [], []
    for chunk in range(cell.shape[0]):
        records = jnp.zeros((quakes, width_y), jnp.float32)
        for part in range(share):
            piece = received[chunk * share + part, last]
            piece = jnp.where(iota(piece.shape, 0) < 4, pltpu.roll(piece, 4, 0), pltpu.roll(piece, width_y // 2, 1))
            moved = pltpu.roll(piece, part * rows_of, 1) if part else piece
            records = jnp.where(lane // rows_of == part, moved, records)
        cells = cell[chunk : chunk + 1, :]
        station_x = lax.shift_right_logical(cells, place[7]) - place[0]
        station_y = (cells & (span_y - 1)) - place[1]
        at_x = (one_x == jnp.broadcast_to(station_x, one_x.shape)).astype(jnp.float32)
        pieces = [p.astype(jnp.float32) for p in exact_parts(records)]
        for out, piece in zip(parts, pieces):
            spread = [piece * jnp.broadcast_to(at_x[x : x + 1], piece.shape) for x in range(width_x)]
            out.append(jnp.concatenate(spread, 0).astype(jnp.bfloat16))
        at_rows.append(at_x.astype(jnp.bfloat16))
        hit = column == jnp.broadcast_to(station_y, column.shape)
        at.append(hit.astype(jnp.float32).astype(jnp.bfloat16))
        hit = strip_column == jnp.broadcast_to(station_y, strip_column.shape)
        at_strip.append(hit.astype(jnp.float32).astype(jnp.bfloat16))
    at = jnp.concatenate(at, 1)
    at_rows = jnp.concatenate(at_rows, 1)
    at_strip = jnp.concatenate(at_strip, 1)
    parts = [jnp.concatenate(p, 1) for p in parts]

    def product(a, b):
        return lax.dot_general(a, b, dims, preferred_element_type=jnp.float32)

    main = [product(p, at) for p in parts]
    sums[...] = (main[0] + main[1] + main[2]).reshape(sums.shape)
    counts[...] = product(at_rows, at)
    sums_strip[...] = product(at_strip, parts[0]) + product(at_strip, parts[1]) + product(at_strip, parts[2])
    spread = ((iota((width_x, width_y), 1) >> 3) == one_x).astype(jnp.float32).astype(jnp.bfloat16)
    tally = 0.0
    for part in reversed(exact_parts(product(at_strip, at_rows))):
        tally += lax.dot_general(part, spread, (((1,), (0,)), ((), ())), preferred_element_type=jnp.float32)
    counts_strip[...] = tally


def traveltimes(per, first, entering, costs, halo, times, field):
    width_x, depth, quakes, width_y = first.shape
    tile = (quakes, width_y)
    carried = [[entering[z // per, k * per + z % per] for z in range(depth)] for k in range(2)]

    def finish(x, running):
        sums = [running[z] + row(costs, z, x, tile) for z in range(depth)]
        for z in range(depth):
            field[x, z] = soft_pair(first[x, z], carried[0][z] + sums[z])
        return sums

    all_steps(width_x, finish, [jnp.zeros(tile, jnp.float32)] * depth)

    def step(lap, state):
        x = width_x - 1 - lap
        values = [field[x, z] for z in range(depth)]
        state, _ = sweep_step(x, 0, values, None, costs, None, halo, state, None, None, None)
        for z in range(depth):
            times[pl.ds(z * width_x + x, quakes, stride=depth * width_x), :] = state[z] * (1.0 / RATE)
        return state

    all_steps(width_x, step, carried[1])


def last_kernel(
    per, place, received, first, costs, halo, shares, slopes, keeps, misfits, edges_own, edges_factor, slopes_one,
    gains, anisotropy, times, kernel, field, value, copied, entries, top, sent,
):
    traveltimes(per, first, received, costs, halo, value, field)
    copy = pltpu.make_async_copy(value, times, copied)
    copy.start()
    adjoint(
        2 * per, place, received, shares, slopes, keeps, misfits, edges_own, edges_factor, slopes_one, gains, anisotropy,
        kernel, entries, top, sent,
    )
    copy.wait()


def adjoint(
    base, place, received, shares, slopes, keeps, misfits, edges_own, edges_factor, slopes_one, gains, anisotropy, kernel,
    entries, top, sent,
):
    width_x, quakes, width_y = slopes.shape
    tile = (quakes, width_y)
    near = slopes_one.shape[1]
    count = received.shape[0]
    lane = iota(tile, 1)
    last = width_y - 1
    me = place[6]
    zero = jnp.zeros(tile, jnp.float32)
    group = width_y // 8
    state, strip, mine, mine_strip = zero, zero, zero, zero
    carries = []
    for device in range(count):
        carries.append(state)
        mine = jnp.where(device == me, state, mine)
        at = device % group
        moved = pltpu.roll(strip, 8 * at, 1) if at else strip
        sent[device // group] = moved if at == 0 else jnp.where((lane >> 3) == at, moved, sent[device // group])
        both = received[device, base + 2]
        state = received[device, base] + received[device, base + 1] * state
        strip = both + shifted_down(both, 2) * strip
    ends = [end_columns(sent[i]) for i in range(sent.shape[0])]
    state = [zero] * near
    mine_edge = zero
    for device in reversed(range(count)):
        at = 8 * (device % group)
        edge = ends[device // group][at : at + 8]
        mine_edge = jnp.where(device == me, edge, mine_edge)
        carry = carries[device]
        block = [received[device, base + 3 + z] for z in range(near)]
        above = jnp.where(lane == last, edge, pltpu.roll(carry, last, 1))
        below = jnp.where(lane == 0, edge, pltpu.roll(carry, 1, 1))
        link = [received[device, base + 3 + 2 * near + i] for i in range(4)]
        block[0] = block[0] + link[0] * carry + link[1] * above + link[2] * below
        block[1] = block[1] + link[3] * carry
        for z in range(near):
            passed = block[z] + received[device, base + 3 + near + z] * state[z]
            state[z] = jnp.where(device > me, passed, state[z])
    carry = mine
    for x in range(width_x):
        total = misfits[x] + carry
        carry = slopes[x] * total
        passed = keeps[x] * total
        sideways = row(anisotropy, near, x, tile) * (shares[1, x] + shares[2, x])
        sideways = sideways + row(anisotropy, 2 * near, x, tile) * shares[3, x]
        terms = carry * row(anisotropy, 0, x, tile) + passed * sideways
        top[x : x + 1, :] = jnp.sum(terms, axis=0, keepdims=True)
        entry = entries_of(passed, shares, x, edges_own[x] + edges_factor[x] * mine_edge)
        for z in range(near):
            entries[x, z] = entry[z]
    for x in reversed(range(width_x)):
        for z in range(near):
            total = entries[x, z] + state[z]
            state[z] = slopes_one[x, z] * total
            value = jnp.sum(total * gains[x, z], axis=0, keepdims=True)
            if z == 0:
                value = value + top[x : x + 1, :]
            kernel[z, x : x + 1, :] = value
    for z in range(near, kernel.shape[0]):
        kernel[z] = jnp.zeros(kernel.shape[1:], jnp.float32)


def call(kernel, shapes, operands, scratch=(), scalars=0, far=0, last=False, aliases=()):
    many = isinstance(shapes, list)
    shapes = shapes if many else [shapes]
    held = jax.ShapeDtypeStruct if last else pltpu.VMEM
    out = [held(s, jnp.float32) if isinstance(s, tuple) else s for s in shapes]
    result = pl.pallas_call(
        kernel,
        out_shape=out,
        in_specs=[SMEM] * scalars + [FAR] * far + [VMEM] * (len(operands) - scalars - far),
        out_specs=[FAR] * last + [VMEM] * (len(out) - last),
        scratch_shapes=[pltpu.VMEM(s, jnp.float32) if isinstance(s, tuple) else s for s in scratch],
        compiler_params=PARAMS,
        input_output_aliases=dict(aliases),
    )(*operands)
    return result if many else result[0]


def traded(message):
    return lax.all_to_all(message, "gx", 0, 0, tiled=True)


def rotated(value, axis, by):
    count = lax.axis_size(axis)
    return lax.ppermute(value, axis, [(i, (i + by) % count) for i in range(count)])


def body(warm_start, slowness, anisotropy, observed, station_cell, source_cell):
    quakes, depth, width_x, width_y = warm_start.shape
    count_x, count_y = lax.axis_size("gx"), lax.axis_size("gy")
    index_x, index_y = lax.axis_index("gx"), lax.axis_index("gy")
    span_x, span_y = width_x * count_x, width_y * count_y
    near = 2
    per = max(1, depth // count_x)
    tile = (quakes, width_y)
    top = (width_x,) + tile
    close = (width_x, near) + tile
    field = (width_x, depth) + tile
    place = jnp.stack(
        [
            index_x * width_x,
            index_y * width_y,
            jnp.int32(span_y),
            jnp.int32(span_x * span_y),
            (index_y == 0).astype(jnp.int32),
            (index_y == count_y - 1).astype(jnp.int32),
            index_x,
            jnp.int32(span_y.bit_length() - 1),
            index_y,
        ]
    ).astype(jnp.int32)
    anis = anisotropy.reshape(3 * depth, width_x, width_y)
    local_records = observed.shape[1]
    flat = (quakes * depth * width_x, width_y)

    stations = station_cell.reshape(-1, width_y)
    sources = [warm_start.reshape(quakes, depth * width_x, width_y), observed, slowness, anis, stations]
    sources = [pltpu.with_memory_space_constraint(a, pltpu.HBM) for a in [source_cell] + sources]
    start, costs, anis, edge, to_right, to_left, records, stations = call(
        pack_kernel,
        [field, anis.shape, (3 * near, width_x, width_y), (11 * width_x, width_y)]
        + [(6 * width_x + quakes, width_y)] * 2
        + [tile, pltpu.VMEM(stations.shape, jnp.int32)],
        [place] + sources,
        [pltpu.SMEM((quakes,), jnp.int32), (CHUNKS, quakes, depth // CHUNKS * width_x, width_y)]
        + [a.shape for a in sources[2:5]]
        + [pltpu.SemaphoreType.DMA((5 + CHUNKS,))],
        scalars=1,
        far=6,
    )
    from_left = rotated(to_right, "gy", 1)
    from_right = rotated(to_left, "gy", -1)
    others = [rotated(records, "gy", by) for by in range(2, count_y - 1)]

    message_shape = (count_x, 3 * per + (7 if per > 1 else 8)) + tile
    first, first_strip, edge_costs, levels_one, sides, message = call(
        functools.partial(first_sweep_kernel, local_records, count_y, per),
        [field, (width_x, 2) + tile, (6,) + top, close, close, message_shape],
        [place, start, edge, records, from_left, from_right, costs, anis] + others,
        [(depth,) + tile, (width_x, 2) + tile],
        scalars=1,
    )
    reach = traded(message)
    chunks = -(-count_x // (width_y // 8))
    halo, *rest, message = call(
        functools.partial(middle_kernel, per, local_records * count_y),
        [(depth,) + tile, (4,) + top] + [top] * 5 + [close, close, (count_x, 2 * per + 7 + 2 * near) + tile],
        [place, stations, reach, first, first_strip, costs, edge_costs, anis, levels_one, sides],
        [(2,) + tile, (chunks,) + tile, (chunks, depth) + tile, (width_x, 2) + tile]
        + [top] * 5
        + [(width_x, width_y), tile, tile],
        scalars=1,
    )
    times, kernel = call(
        functools.partial(last_kernel, per),
        [flat, (depth, width_x, width_y)],
        [place, traded(message), first, costs, halo] + rest + [anis],
        [field, flat, pltpu.SemaphoreType.DMA, close, (width_x, width_y), (chunks,) + tile],
        scalars=1,
        last=True,
    )
    return (times.reshape(warm_start.shape), kernel)


def solution(mesh):
    return jax.shard_map(
        body,
        mesh=mesh,
        in_specs=(
            P(None, None, "gx", "gy"),
            P(None, "gx", "gy"),
            P(None, None, "gx", "gy"),
            P(None, ("gx", "gy")),
            P(),
            P(),
        ),
        out_specs=(P(None, None, "gx", "gy"), P(None, "gx", "gy")),
        check_vma=False,
    )
```

```python
import functools
import math

import jax
import jax.numpy as jnp
from jax import lax
from jax.experimental import pallas as pl
from jax.experimental.pallas import tpu as pltpu
from jax.sharding import PartitionSpec as P

TAU = 0.05
ADJ_SCALE = 0.1
LOG2E = math.log2(math.e)
RATE = LOG2E / TAU
BIG = 10000.0 * RATE
UNROLL = 8
CHUNKS = 4
VMEM = pl.BlockSpec(memory_space=pltpu.VMEM)
FAR = pl.BlockSpec(memory_space=pl.ANY)
SMEM = pl.BlockSpec(memory_space=pltpu.SMEM)
PARAMS = pltpu.CompilerParams(vmem_limit_bytes=8 * 1024 * 1024)


def softmin(values):
    least = functools.reduce(jnp.minimum, values)
    parts = [jnp.exp2(least - v) for v in values]
    return least, parts, functools.reduce(jnp.add, parts)


def soft_pair(first, second):
    return jnp.minimum(first, second) - LOG2E * jnp.log(1.0 + jnp.exp2(-jnp.abs(first - second)))


def add_pair(least, total, passed):
    low = jnp.minimum(least, passed)
    return low - LOG2E * jnp.log(total * jnp.exp2(low - least) + jnp.exp2(low - passed))


def join_pairs(first, second):
    low = jnp.minimum(first[0], second[0])
    return low, first[1] * jnp.exp2(low - first[0]) + second[1] * jnp.exp2(low - second[0])


def value_of(pair):
    return pair[0] - LOG2E * jnp.log(pair[1])


def split_pair(first, second):
    gap = jnp.exp2(-jnp.abs(first - second))
    share = 1.0 / (1.0 + gap)
    less = gap * share
    nearer = first <= second
    return jnp.where(nearer, share, less), jnp.where(nearer, less, share)


def iota(shape, axis):
    return lax.broadcasted_iota(jnp.int32, shape, axis)


def row(ref, index, x, like):
    return jnp.broadcast_to(ref[index, pl.ds(x, 1), :], like)


def row_of(ref, x, like):
    return jnp.broadcast_to(ref[pl.ds(x, 1), :], like)


def all_steps(count, step, carry):
    for i in range(count):
        carry = step(i, carry)
    return carry


def by_steps(count, step, carry):
    def group(i, carry):
        for j in range(UNROLL):
            carry = step(i * UNROLL + j, carry)
        return carry

    return lax.fori_loop(0, count // UNROLL, group, carry)


def packed(left, right):
    return jnp.where(iota(left.shape, 0) < 5, left, pltpu.roll(right, 2, 0))


def merged(left, right):
    return jnp.where(iota(left.shape, 0) < 4, left, right)


def shifted_down(tile, by):
    return pltpu.roll(tile, tile.shape[0] - by, 0)


def exact_parts(value):
    high = value.astype(jnp.bfloat16).astype(jnp.float32)
    middle = (value - high).astype(jnp.bfloat16).astype(jnp.float32)
    low = value - high - middle
    return [p.astype(jnp.bfloat16) for p in (high, middle, low)]


def pack_kernel(
    place, source_far, warm_far, observed_far, slowness_far, anisotropy_far, stations_far,
    start, costs, near, edge, to_right, to_left, records, stations,
    source, observed, slowness, anisotropy, arrived,
):
    pairs = [(slowness_far, slowness), (anisotropy_far, anisotropy), (observed_far, observed)]
    pairs += [(stations_far, stations), (source_far, source)]
    depth, width_x, quakes, width_y = start.shape
    share = depth // CHUNKS
    for i in range(CHUNKS):
        levels = pl.ds(i * share, share)
        pairs += [(warm_far.at[e, levels], start.at[levels, :, e, :]) for e in range(quakes)]
    copies = [pltpu.make_async_copy(a, b, arrived.at[i]) for i, (a, b) in enumerate(pairs)]
    for copy in copies:
        copy.start()
    tile = (quakes, width_y)
    quake = iota(tile, 0)
    lane = iota(tile, 1)
    span_y = place[2]
    plane = place[3]
    rows = width_x * 8
    wide = (width_x, width_y)
    group = iota(wide, 1) >> 3
    copies[0].wait()
    copies[1].wait()
    native = []
    for k in range(3):
        columns = jnp.zeros(wide, jnp.float32)
        for z in range(depth):
            cost = slowness[z] * anisotropy[k * depth + z] * RATE
            costs[k * depth + z] = cost
            columns = jnp.where(group == z, pltpu.roll(cost, 8 * z + 4, 1), columns)
        edge[rows : rows + width_x, :] = columns
        rows += width_x
        native.append(columns)
        for z in range(near.shape[0] // 3):
            near[k * (near.shape[0] // 3) + z] = anisotropy[k * depth + z]
    early = (iota(wide, 1) & 7) < 4
    at = slice(4 * width_x, 5 * width_x)
    to_right[at, :] = jnp.where(early, native[0], pltpu.roll(native[1], 4, 1))
    to_left[at, :] = jnp.where(early, pltpu.roll(native[1], width_y - 4, 1), native[0])
    at = slice(5 * width_x, 6 * width_x)
    to_right[at, :] = native[2]
    to_left[at, :] = native[2]
    copies[4].wait()
    cell = jnp.zeros(tile, jnp.int32)
    for e in range(quakes):
        cell = jnp.where(quake == e, source[e], cell)
    cell = cell - (lane + place[0] * span_y + place[1])
    edges = []
    for i in range(CHUNKS):
        for copy in copies[5 + i * quakes : 5 + (i + 1) * quakes]:
            copy.wait()

        chunk = [jnp.zeros(tile, jnp.float32)] * share
        for x in range(width_x):
            mine = (lane >> 3) == x
            for k in range(share):
                value = start[i * share + k, x] * RATE
                value = jnp.where(cell == (i * share + k) * plane + x * span_y, 0.0, value)
                start[i * share + k, x] = value
                chunk[k] = jnp.where(mine, pltpu.roll(value, (8 * x + 4) % width_y, 1), chunk[k])
        edges += chunk
    columns = jnp.transpose(jnp.concatenate(edges, 0))
    edge[: width_x * 8, :] = columns
    low = quake < 4
    for x in range(0, width_x, 2):
        one, two = columns[8 * x : 8 * x + 8], columns[8 * x + 8 : 8 * x + 16]
        to_right[4 * x : 4 * x + 8, :] = jnp.where(low, one, pltpu.roll(two, 4, 0))
        to_left[4 * x : 4 * x + 8, :] = jnp.where(low, pltpu.roll(one, 4, 0), two)
    copies[2].wait()
    copies[3].wait()
    records[...] = jnp.zeros(tile, jnp.float32)
    records[:, : observed.shape[1]] = observed[...]
    for message in (to_right, to_left):
        message[6 * width_x :, :] = records[...]


def halo_columns(left, right):
    rows = []
    for l, r in zip(left, right):
        rows.append(jnp.where(iota(l.shape, 0) == 4, r, pltpu.roll(l, 2, 0)))
    return jnp.transpose(jnp.concatenate(rows, 0))


def cost_columns(message, width_x, turn):
    pair = message[4 * width_x : 5 * width_x, :]
    return [pair, pltpu.roll(pair, turn, 1), message[5 * width_x : 6 * width_x, :]]


def strip_costs(own, from_left, from_right, out, width_x, depth):
    tile = own.shape[1]
    base = width_x * 8
    lane = iota((8, tile), 1)
    low = (lane & 7) < 4
    mine = (lane & 7) == iota((8, tile), 0)
    spread = ((iota((tile, tile), 0) >> 3) == (iota((tile, tile), 1) >> 3)).astype(jnp.float32)
    spread = spread.astype(jnp.bfloat16)
    for side in range(2):
        for k in range(3):
            rows = []
            for x in range(width_x):
                at = slice(base + k * width_x + x, base + k * width_x + x + 1)
                here = jnp.broadcast_to(own[at, :], lane.shape)
                there = jnp.broadcast_to((from_right if side else from_left)[k][x : x + 1], lane.shape)
                value = jnp.where(low, here, there) if side else jnp.where(low, there, here)
                rows.append(jnp.where(mine, value, 0.0))
            whole = jnp.concatenate(rows, 0)
            total = 0.0
            for part in reversed(exact_parts(whole)):
                total = total + lax.dot_general(
                    part, spread, (((1,), (0,)), ((), ())), preferred_element_type=jnp.float32
                )
            out[3 * side + k] = total.reshape(width_x, 8, tile)


def running_sum(value):
    rows = iota(value.shape, 0)
    by = 1
    while by < value.shape[0]:
        value = value + jnp.where(rows >= by, pltpu.roll(value, by, 0), 0.0)
        by *= 2
    return value


def log_sum(exponents):
    return -LOG2E * jnp.log(functools.reduce(jnp.add, [jnp.exp2(-e) for e in exponents]))


def passages(costs, from_left, from_right, depth):
    width_x, width_y = costs.shape[1:]
    lane = iota((width_x, width_y), 1)
    beside = jnp.where((lane & 7) == 4, running_sum(from_right), pltpu.roll(running_sum(from_left), 2, 1))
    sums = [running_sum(costs[z]) for z in range(depth)]
    sub = iota((8, width_y), 0)
    tiles = []
    for z in range(depth):
        back = sums[z] - costs[z]
        edge = pltpu.roll(beside, width_y - 5 - 8 * z, 1)
        below = jnp.where(lane == 0, edge, pltpu.roll(sums[z], 1, 1))
        above = jnp.where(lane == width_y - 1, edge, pltpu.roll(sums[z], width_y - 1, 1))
        step_y = back + costs[depth + z]
        step_z = back + costs[2 * depth + z]
        paths = [sums[z] + back, below + step_y, above + step_y]
        paths.append(sums[z - 1] + step_z if z > 0 else None)
        paths.append(sums[z + 1] + step_z if z < depth - 1 else None)
        tile = jnp.broadcast_to(sums[z][width_x - 1 :, :], sub.shape)
        for j, path in enumerate(paths):
            if path is None:
                tile = jnp.where(sub == j + 1, BIG, tile)
            else:
                total = jnp.sum(jnp.exp2(-path), axis=0, keepdims=True)
                tile = jnp.where(sub == j + 1, -LOG2E * jnp.log(total), tile)
        tiles.append(tile)
    return tiles


def strip_passages(edge_costs, width_x):
    shape = edge_costs.shape[2:]
    lane = iota(shape, 1)
    sums = jnp.zeros(shape, jnp.float32)
    totals = [jnp.zeros(shape, jnp.float32)] * 5
    for x in range(width_x):
        cost, step_y, step_z = [packed(edge_costs[k, x], edge_costs[3 + k, x]) for k in range(3)]
        back = sums
        sums = sums + cost
        step_y, step_z = step_y + back, step_z + back
        paths = [sums + back, pltpu.roll(sums, 1, 0) + step_y, shifted_down(sums, 1) + step_y]
        paths.append(jnp.where(lane < 8, BIG, pltpu.roll(sums, 8, 1) + step_z))
        paths.append(jnp.where(lane >= shape[1] - 8, BIG, pltpu.roll(sums, shape[1] - 8, 1) + step_z))
        totals = [t + jnp.exp2(-p) for t, p in zip(totals, paths)]
    return sums, [-LOG2E * jnp.log(jnp.maximum(t, 1e-37)) for t in totals]


PLACES = ((2, 0, 16), (4, 16, 16), (5, 32, 16), (7, 48, 16))
BACK_PLACES = ((3, 64, 8), (6, 72, 8))


def shared_tile(reach, back, records):
    lane, sub = iota(reach.shape, 1), iota(reach.shape, 0)
    extra = reach
    for value, places in ((reach, PLACES), (back, BACK_PLACES)):
        for at, low, width in places:
            moved = pltpu.roll(pltpu.roll(value, (2 - at) % 8, 0), low, 1) if low else value
            extra = jnp.where((lane >= low) & (lane < low + width), moved, extra)
    half = reach.shape[1] // 2
    record = jnp.where(lane < half, pltpu.roll(records, 4, 0), pltpu.roll(records, half, 1))
    tile = jnp.where(sub == 0, shifted_down(reach, 3), jnp.where(sub == 1, shifted_down(reach, 5), extra))
    return jnp.where(sub < 4, tile, record)


def unshared_tile(tile):
    sub = iota(tile.shape, 0)
    wide = tile.shape[1]
    reach = jnp.where(sub == 3, pltpu.roll(tile, 3, 0), jnp.where(sub == 6, pltpu.roll(tile, 5, 0), tile))
    for at, low, _ in PLACES[1:]:
        reach = jnp.where(sub == at, pltpu.roll(pltpu.roll(tile, at - 2, 0), wide - low, 1), reach)
    back = [pltpu.roll(pltpu.roll(tile, at - 2, 0), wide - low, 1) for at, low, _ in BACK_PLACES]
    return reach, jnp.where(sub == 3, back[0], back[1])


def shared_rows(total, paths):
    place = iota(total.shape, 1) & 7
    first, second = total, total
    for q in range(6):
        value = pltpu.roll(total, (4 - q) % 8, 0)
        first = jnp.where(place == q, value, first)
    for q, (path, at) in enumerate([(p, r) for p in paths for r in (3, 6)]):
        if q < 2:
            first = jnp.where(place == 6 + q, pltpu.roll(path, (6 - at) % 8, 0), first)
        else:
            second = jnp.where(place == q - 2, pltpu.roll(path, (7 - at) % 8, 0), second)
    return jnp.where(iota(total.shape, 0) == 6, first, second)


def spread_rows(tiles):
    shape = tiles[0].shape
    wide = shape[1]
    sub = iota(shape, 0)
    mine = (iota(shape, 1) & 7) == sub
    spread = ((iota((wide, wide), 0) >> 3) == (iota((wide, wide), 1) >> 3)).astype(jnp.float32)
    spread = spread.astype(jnp.bfloat16)
    rows = [jnp.where(mine, jnp.broadcast_to(t[r : r + 1], shape), 0.0) for t in tiles for r in (6, 7)]
    whole = jnp.concatenate(rows, 0)
    value = 0.0
    for part in reversed(exact_parts(whole)):
        value = value + lax.dot_general(part, spread, (((1,), (0,)), ((), ())), preferred_element_type=jnp.float32)
    out = []
    for i in range(len(tiles)):
        first, second = value[16 * i : 16 * i + 8], value[16 * i + 8 : 16 * i + 16]
        paths = [jnp.where(sub == 3, pltpu.roll(first, 5, 0), pltpu.roll(first, 7, 0))]
        for q in range(4):
            at_three = pltpu.roll(second, (3 - 2 * q) % 8, 0)
            at_six = pltpu.roll(second, (6 - 2 * q - 1) % 8, 0)
            paths.append(jnp.where(sub == 3, at_three, at_six))
        out.append((pltpu.roll(first, 2, 0), paths))
    return out


def sweep_step(x, near, levels, strip, costs, edge_costs, halo, state, strip_state, keep, keep_strip):
    depth = costs.shape[0] // 3
    tile = levels[0].shape
    width_y = tile[1]
    lane = iota(tile, 1)
    out = []
    for z in range(len(state)):
        u = levels[z]
        cost_y = row(costs, depth + z, x, tile)
        cost_z = row(costs, 2 * depth + z, x, tile)
        edge = pltpu.roll(halo[z], width_y - 5 - 8 * x, 1)
        values = [u]
        values.append(jnp.where(lane == 0, edge, pltpu.roll(u, 1, 1)) + cost_y)
        values.append(jnp.where(lane == width_y - 1, edge, pltpu.roll(u, width_y - 1, 1)) + cost_y)
        if z > 0:
            values.append(levels[z - 1] + cost_z)
        if z < depth - 1:
            values.append(levels[z + 1] + cost_z)
        least, parts, total = softmin(values)
        passed = state[z] + row(costs, z, x, tile)
        if z < near:
            scale = 1.0 / total
            keep(x, z, value_of((least, total)), [p * scale for p in parts], passed)
        out.append(add_pair(least, total, passed))
    strips, relaxed, weights, passes = [], [], [], []
    for side in range(2 if strip is not None else 0):
        u = strip[x, side]
        cost_y = edge_costs[3 * side + 1, x]
        cost_z = edge_costs[3 * side + 2, x]
        values = [u, pltpu.roll(u, 1, 0) + cost_y, pltpu.roll(u, 7, 0) + cost_y]
        values.append(jnp.where(lane < 8, BIG, pltpu.roll(u, 8, 1)) + cost_z)
        values.append(jnp.where(lane >= width_y - 8, BIG, pltpu.roll(u, width_y - 8, 1)) + cost_z)
        least, parts, total = softmin(values)
        passes.append(strip_state[side] + edge_costs[3 * side, x])
        strips.append(add_pair(least, total, passes[side]))
        if keep_strip is not None:
            relaxed.append(value_of((least, total)))
            weights.append(parts[2 - side] / total)
    if keep_strip is not None:
        keep_strip(x, merged(*relaxed), merged(*weights), merged(*passes), merged(*strips))
    return out, strips


def outside_strips(place, shape):
    sub = iota(shape, 0)
    return [(place[4] == 1) & (sub < 4), (place[5] == 1) & (sub >= 4)]


def first_sweep_kernel(
    rows_of, count_y, per, place, field, own, mine, from_left, from_right, costs, anisotropy, *rest
):
    others = rest[: count_y - 3]
    local, local_strip, edge_costs, levels, sides, message, halo, strip = rest[count_y - 3 :]
    depth, width_x, quakes, width_y = field.shape
    tile = (quakes, width_y)
    sub = iota(tile, 0)
    low = sub < 4
    near = levels.shape[1]
    last = 6 * width_x
    far = [mine[...], from_left[last:, :]] + [o[...] for o in others] + [from_right[last:, :]]
    records = jnp.zeros(tile, jnp.float32)
    for by, piece in enumerate(far):
        owner = lax.rem(place[8] + count_y - by, count_y)
        records = records + pltpu.roll(piece, owner * rows_of, 1)
    left, right = [], []
    for x in range(width_x):
        at = slice(8 * x, 8 * x + 8)
        two = slice(8 * (x // 2), 8 * (x // 2) + 8)
        before, after = from_left[two, :], from_right[two, :]
        if x % 2:
            before = pltpu.roll(before, 4, 0)
        else:
            after = pltpu.roll(after, 4, 0)
        before = jnp.where(place[4] == 1, BIG, before)
        after = jnp.where(place[5] == 1, BIG, after)
        left.append(jnp.where(low, before, own[at, :]))
        right.append(jnp.where(low, own[at, :], after))
        strip[x, 0] = left[x]
        strip[x, 1] = right[x]
    halo[...] = halo_columns(left, right).reshape(halo.shape)
    left_costs = cost_columns(from_left, width_x, width_y - 4)
    right_costs = cost_columns(from_right, width_x, 4)
    strip_costs(own, left_costs, right_costs, edge_costs, width_x, depth)
    outside = outside_strips(place, tile)

    def keep(x, z, level, w, passed):
        levels[x, z] = level
        vertical = w[3] if z == 0 else w[3] + w[4]
        sideways = row(anisotropy, near + z, x, tile) * (w[1] + w[2])
        sides[x, z] = sideways + row(anisotropy, 2 * near + z, x, tile) * vertical

    def step(x, carry):
        state, strips = sweep_step(x, near, [field[z, x] for z in range(depth)], strip, costs, edge_costs, halo, *carry, keep, None)
        for z in range(depth):
            local[x, z] = state[z]
        for side in range(2):
            local_strip[x, side] = jnp.where(outside[side], BIG, strips[side])
        return state, strips

    blank = jnp.full(tile, BIG, jnp.float32)
    state, strips = all_steps(width_x, step, ([blank] * depth, [blank] * 2))
    reach_strip = packed(*[jnp.where(o, BIG, s) for o, s in zip(outside, strips)])

    edges = [[local_strip[x, side] for x in range(width_x)] for side in range(2)]
    halo[...] = halo_columns(*edges).reshape(halo.shape)

    def again(lap, carry):
        x = width_x - 1 - lap
        values = [local[x, z] for z in range(depth)]
        return sweep_step(x, 0, values, local_strip, costs, edge_costs, halo, *carry, None, None)

    back, back_strips = all_steps(width_x, again, ([blank] * depth, [blank] * 2))
    tiles = passages(costs, left_costs[0], right_costs[0], depth)
    strip_total, strip_paths = strip_passages(edge_costs, width_x)

    strip_tile = shared_tile(reach_strip, packed(*back_strips), records)
    shared = shared_rows(strip_total, strip_paths)
    count = message.shape[0]
    for p in range(count):
        first = min(p * per, depth - per)
        for k in range(per + 2):
            z = first + k - 1
            message[p, k] = state[z] if 0 <= z < depth else blank
        for k in range(per):
            message[p, per + 2 + k] = back[first + k]
            value = tiles[first + k]
            if k == 0 and first > 0:
                value = jnp.where(sub == 6, jnp.broadcast_to(tiles[first - 1][:1], tile), value)
            if k == 0 and first + per < depth:
                value = jnp.where(sub == 7, jnp.broadcast_to(tiles[first + per][:1], tile), value)
            if per > 1 and k == 1:
                value = jnp.where(sub < 6, value, shared)
            message[p, 2 * per + 2 + k] = value
        message[p, 3 * per + 2] = strip_tile
        if per == 1:
            message[p, 3 * per + 3] = shared
        surface = [state[0], state[1], back[0], jnp.where(sub < 6, tiles[0], jnp.broadcast_to(tiles[1][:1], tile))]
        for i, value in enumerate(surface):
            message[p, message.shape[1] - 4 + i] = value


def owner_carries(
    per, depth, place, received, entering, entering_strips, surface_edges, halo,
):
    count = received.shape[0]
    tile = entering.shape[2:]
    lane = iota(tile, 1)
    width_y = tile[1]
    me = place[6]
    blank = jnp.full(tile, BIG, jnp.float32)
    unit = jnp.ones(tile, jnp.float32)
    side = 3 * per + 2

    def rows(device, k, j):
        return jnp.broadcast_to(received[device, 2 * per + 2 + k, j : j + 1, :], tile)

    def total(device, k):
        if k < 0:
            return rows(device, 0, 6)
        return rows(device, k, 0) if k < per else rows(device, 0, 7)

    def further(pair, cost):
        return pair[0] + cost, pair[1]

    shared = [received[d, 2 * per + 3] if per > 1 else received[d, 3 * per + 3] for d in range(count)]
    strips = [unshared_tile(received[d, side]) for d in range(count)]
    shared = spread_rows(shared)
    state = [(blank, unit)] * (per + 2)
    strip = (blank, unit)
    first, first_strip = [], []
    for device in range(count):
        first.append([value_of(pair) for pair in state])
        first_strip.append(value_of(strip))
        state = [
            join_pairs((received[device, k], unit), further(state[k], total(device, k - 1))) for k in range(per + 2)
        ]
        strip = join_pairs((strips[device][0], unit), further(strip, shared[device][0]))
    own = blank
    for device in range(count):
        own = jnp.where(device == me, first_strip[device], own)
        for k in range(per):
            entering[device, k] = first[device][k + 1]
    entering_strips[0] = own
    group = width_y // 8
    for at in range(0, count, group):
        some = first_strip[at : at + group]
        some = some + [blank] * (group - len(some))
        turned = halo_columns(some, [shifted_down(s, 2) for s in some])
        halo[at // group] = turned.reshape(halo.shape[1:])
        surface_edges[at // group] = turned[: tile[0]]
    low = jnp.minimum(me * per, depth - per)
    edges = [[halo[i, low + k] for k in range(per)] for i in range(halo.shape[0])]
    state = [(blank, unit)] * per
    strip = (blank, unit)
    for device in reversed(range(count)):
        for k in range(per):
            entering[device, per + k] = value_of(state[k])
            u = first[device][k + 1]
            turn = (width_y - 5 - 8 * (device % group)) % width_y
            edge = pltpu.roll(edges[device // group][k], turn, 1)
            values = [received[device, per + 2 + k], u + rows(device, k, 1)]
            values.append(jnp.where(lane == 0, edge, pltpu.roll(u, 1, 1)) + rows(device, k, 2))
            values.append(jnp.where(lane == width_y - 1, edge, pltpu.roll(u, width_y - 1, 1)) + rows(device, k, 3))
            values.append(first[device][k] + rows(device, k, 4))
            values.append(first[device][k + 2] + rows(device, k, 5))
            least, _, amount = softmin(values)
            state[k] = join_pairs((least, amount), further(state[k], total(device, k)))
        u = first_strip[device]
        back = strips[device][1]
        paths = shared[device][1]
        values = [back, u + paths[0], pltpu.roll(u, 1, 0) + paths[1], shifted_down(u, 1) + paths[2]]
        values.append(jnp.where(lane < 8, BIG, pltpu.roll(u, 8, 1)) + paths[3])
        values.append(jnp.where(lane >= width_y - 8, BIG, pltpu.roll(u, width_y - 8, 1)) + paths[4])
        least, _, amount = softmin(values)
        passed = join_pairs((least, amount), further(strip, shared[device][0]))
        strip = [jnp.where(device > me, new, old) for new, old in zip(passed, strip)]
    entering_strips[1] = value_of(strip)


def middle_kernel(
    per, rows_of, place, cell, received, first, first_strip, costs, edge_costs, anisotropy, levels_one, sides,
    halo, shares, slopes, keeps, misfits, edges_own, edges_factor, slopes_one, gains, message,
    entering_strips, surface_edges, block_halo, strip, shares_strip, slopes_strip, keeps_strip, misfits_strip, sums, counts, sums_strip, counts_strip,
):
    owner_carries(per, first.shape[1], place, received, message, entering_strips, surface_edges, block_halo)
    width_x, near, quakes, width_y = levels_one.shape
    tile = (quakes, width_y)
    lane = iota(tile, 1)
    count = received.shape[0]
    base = received.shape[1] - 4
    me = place[6]
    add_records(rows_of, 3 * per + 2, place, cell, received, sums, counts, sums_strip, counts_strip)
    blank = jnp.full(tile, BIG, jnp.float32)
    unit = jnp.ones(tile, jnp.float32)

    def rows(device, j):
        return jnp.broadcast_to(received[device, base + 3, j : j + 1, :], tile)

    state = [(blank, unit)] * near
    into = []
    for device in range(count):
        into.append([value_of(pair) for pair in state])
        state = [
            join_pairs((received[device, base + z], unit), (state[z][0] + rows(device, 6 * z), state[z][1]))
            for z in range(near)
        ]
    carried = [blank] * near
    for device in range(count):
        carried = [jnp.where(device == me, new, old) for new, old in zip(into[device], carried)]
    back = (blank, unit)
    group = width_y // 8
    for device in reversed(range(count)):
        u, deeper = into[device]
        edge = pltpu.roll(surface_edges[device // group], (width_y - 5 - 8 * (device % group)) % width_y, 1)
        values = [received[device, base + 2], u + rows(device, 1), deeper + rows(device, 5)]
        values.append(jnp.where(lane == 0, edge, pltpu.roll(u, 1, 1)) + rows(device, 2))
        values.append(jnp.where(lane == width_y - 1, edge, pltpu.roll(u, width_y - 1, 1)) + rows(device, 3))
        least, _, amount = softmin(values)
        passed = join_pairs((least, amount), (back[0] + rows(device, 0), back[1]))
        back = [jnp.where(device > me, new, old) for new, old in zip(passed, back)]
    back = value_of(back)

    outside = outside_strips(place, tile)
    strips_in = [[s, shifted_down(s, 2)] for s in (entering_strips[0], entering_strips[1])]
    running = [jnp.zeros(tile, jnp.float32)] * (near + 2)
    prior = carried
    close = []
    for x in range(width_x):
        values = []
        for z in range(near):
            cost = row(costs, z, x, tile)
            running[z] = running[z] + cost
            values.append(soft_pair(first[x, z], carried[z] + running[z]))
            keep, slope = split_pair(levels_one[x, z], prior[z] + cost)
            slopes_one[x, z] = slope
            gains[x, z] = slope * row(anisotropy, z, x, tile) + keep * sides[x, z]
        prior = values
        close.append(values)
        for side in range(2):
            running[near + side] = running[near + side] + edge_costs[3 * side, x]
            value = soft_pair(first_strip[x, side], strips_in[0][side] + running[near + side])
            strip[x, side] = jnp.where(outside[side], BIG, value)
    edges = [[strip[x, side] for x in range(width_x)] for side in range(2)]
    halo[...] = halo_columns(*edges).reshape(halo.shape)

    def keep(x, z, level, w, passed):
        for i in range(4):
            shares[i, x] = w[i]
        keeps[x], slopes[x] = split_pair(level, passed)

    def keep_strip(x, level, w, passed, value):
        shares_strip[x] = w
        keeps_strip[x], slopes_strip[x] = split_pair(level, passed)
        tally = pltpu.roll(counts_strip[...], (width_y - 8 * x) % width_y, 1)
        total = pltpu.roll(sums_strip[...], (width_y - 8 * x) % width_y, 1)
        misfits_strip[x] = ADJ_SCALE * (tally * (value * (1.0 / RATE)) - total)

    def step(lap, carry):
        x = width_x - 1 - lap
        state, strips = sweep_step(x, 1, close[x], strip, costs, edge_costs, halo, *carry, keep, keep_strip)
        misfits[x] = ADJ_SCALE * (row_of(counts, x, tile) * (state[0] * (1.0 / RATE)) - sums[x])
        return state, strips

    all_steps(width_x, step, ([back], strips_in[1]))
    zero = jnp.zeros(tile, jnp.float32)
    own, factor, strip_own, strip_factor = zero, unit, zero, unit
    owns, factors = [], []
    sent = [zero, zero]
    for x in range(width_x):
        own = misfits[x] + own
        owns.append(keeps[x] * own)
        factors.append(keeps[x] * factor)
        own, factor = slopes[x] * own, slopes[x] * factor
        strip_own = misfits_strip[x] + strip_own
        through = keeps_strip[x] * shares_strip[x]
        for i, value in enumerate((strip_own, strip_factor)):
            value = pltpu.roll(through * value, 8 * x, 1) if x else through * value
            sent[i] = jnp.where((lane >> 3) == x, value, sent[i])
        strip_own, strip_factor = slopes_strip[x] * strip_own, slopes_strip[x] * strip_factor
    edges_own[...] = end_columns(sent[0]).reshape(edges_own.shape)
    edges_factor[...] = end_columns(sent[1]).reshape(edges_factor.shape)
    chain = [unit] * near
    blocks = [zero] * near
    links = [zero] * 4
    for x in range(width_x):
        entry = entries_of(owns[x], shares, x, edges_own[x])
        for z in range(near):
            chain[z] = chain[z] * slopes_one[x, z]
            blocks[z] = blocks[z] + chain[z] * entry[z]
        for i, path in enumerate(ways_of(factors[x], shares, x, edges_factor[x])):
            links[i] = links[i] + chain[i // 3] * path
    both = jnp.where(iota(tile, 0) < 5, strip_own, pltpu.roll(strip_factor, 2, 0))
    tiles = [own, factor, both] + blocks + chain + links
    for p in range(message.shape[0]):
        for i, value in enumerate(tiles):
            message[p, 2 * per + i] = value


def end_columns(rows):
    wide = rows.shape[1]
    first, last = shifted_down(rows, 3), pltpu.roll(rows, 3, 0)
    return jnp.transpose(jnp.concatenate([first] * (wide // 16) + [last] * (wide // 16), 0))


def ways_of(passed, shares, x, edge):
    lane = iota(passed.shape, 1)
    last = passed.shape[1] - 1
    above = jnp.where(lane == last, edge, pltpu.roll(passed * shares[1, x], last, 1))
    below = jnp.where(lane == 0, edge, pltpu.roll(passed * shares[2, x], 1, 1))
    return passed * shares[0, x], above, below, passed * shares[3, x]


def entries_of(passed, shares, x, edge):
    own, above, below, deeper = ways_of(passed, shares, x, edge)
    return own + above + below, deeper


def add_records(rows_of, tile_of, place, cell, received, sums, counts, sums_strip, counts_strip):
    width_x, quakes, width_y = sums.shape
    last = tile_of
    span_y = place[2]
    lane = iota((quakes, width_y), 1)
    column = iota((width_y, width_y), 0)
    strip_column = iota((8, width_y), 0)
    strip_column = jnp.where(strip_column == 3, -1, jnp.where(strip_column == 4, width_y, -2))
    share = width_y // rows_of
    dims = (((1,), (1,)), ((), ()))
    one_x = iota((width_x, width_y), 0)
    parts = [[], [], []]
    at, at_rows, at_strip = [], [], []
    for chunk in range(cell.shape[0]):
        records = jnp.zeros((quakes, width_y), jnp.float32)
        for part in range(share):
            piece = received[chunk * share + part, last]
            piece = jnp.where(iota(piece.shape, 0) < 4, pltpu.roll(piece, 4, 0), pltpu.roll(piece, width_y // 2, 1))
            moved = pltpu.roll(piece, part * rows_of, 1) if part else piece
            records = jnp.where(lane // rows_of == part, moved, records)
        cells = cell[chunk : chunk + 1, :]
        station_x = lax.shift_right_logical(cells, place[7]) - place[0]
        station_y = (cells & (span_y - 1)) - place[1]
        at_x = (one_x == jnp.broadcast_to(station_x, one_x.shape)).astype(jnp.float32)
        pieces = [p.astype(jnp.float32) for p in exact_parts(records)]
        for out, piece in zip(parts, pieces):
            spread = [piece * jnp.broadcast_to(at_x[x : x + 1], piece.shape) for x in range(width_x)]
            out.append(jnp.concatenate(spread, 0).astype(jnp.bfloat16))
        at_rows.append(at_x.astype(jnp.bfloat16))
        hit = column == jnp.broadcast_to(station_y, column.shape)
        at.append(hit.astype(jnp.float32).astype(jnp.bfloat16))
        hit = strip_column == jnp.broadcast_to(station_y, strip_column.shape)
        at_strip.append(hit.astype(jnp.float32).astype(jnp.bfloat16))
    at = jnp.concatenate(at, 1)
    at_rows = jnp.concatenate(at_rows, 1)
    at_strip = jnp.concatenate(at_strip, 1)
    parts = [jnp.concatenate(p, 1) for p in parts]

    def product(a, b):
        return lax.dot_general(a, b, dims, preferred_element_type=jnp.float32)

    main = [product(p, at) for p in parts]
    sums[...] = (main[0] + main[1] + main[2]).reshape(sums.shape)
    counts[...] = product(at_rows, at)
    sums_strip[...] = product(at_strip, parts[0]) + product(at_strip, parts[1]) + product(at_strip, parts[2])
    spread = ((iota((width_x, width_y), 1) >> 3) == one_x).astype(jnp.float32).astype(jnp.bfloat16)
    tally = 0.0
    for part in reversed(exact_parts(product(at_strip, at_rows))):
        tally += lax.dot_general(part, spread, (((1,), (0,)), ((), ())), preferred_element_type=jnp.float32)
    counts_strip[...] = tally


def traveltimes(per, first, entering, costs, halo, times, field):
    width_x, depth, quakes, width_y = first.shape
    tile = (quakes, width_y)
    carried = [[entering[z // per, k * per + z % per] for z in range(depth)] for k in range(2)]

    def finish(x, running):
        sums = [running[z] + row(costs, z, x, tile) for z in range(depth)]
        for z in range(depth):
            field[x, z] = soft_pair(first[x, z], carried[0][z] + sums[z])
        return sums

    all_steps(width_x, finish, [jnp.zeros(tile, jnp.float32)] * depth)

    def step(lap, state):
        x = width_x - 1 - lap
        values = [field[x, z] for z in range(depth)]
        state, _ = sweep_step(x, 0, values, None, costs, None, halo, state, None, None, None)
        for z in range(depth):
            times[z, x] = state[z] * (1.0 / RATE)
        return state

    all_steps(width_x, step, carried[1])


def last_kernel(
    per, place, received, first, costs, halo, shares, slopes, keeps, misfits, edges_own, edges_factor, slopes_one,
    gains, anisotropy, times, kernel, field, value, copied, entries, top, sent,
):
    traveltimes(per, first, received, costs, halo, value, field)
    copies = [pltpu.make_async_copy(value.at[:, :, e, :], times.at[e], copied.at[e]) for e in range(times.shape[0])]
    for copy in copies:
        copy.start()
    adjoint(
        2 * per, place, received, shares, slopes, keeps, misfits, edges_own, edges_factor, slopes_one, gains, anisotropy,
        kernel, entries, top, sent,
    )
    for copy in copies:
        copy.wait()


def adjoint(
    base, place, received, shares, slopes, keeps, misfits, edges_own, edges_factor, slopes_one, gains, anisotropy, kernel,
    entries, top, sent,
):
    width_x, quakes, width_y = slopes.shape
    tile = (quakes, width_y)
    near = slopes_one.shape[1]
    count = received.shape[0]
    lane = iota(tile, 1)
    last = width_y - 1
    me = place[6]
    zero = jnp.zeros(tile, jnp.float32)
    group = width_y // 8
    state, strip, mine, mine_strip = zero, zero, zero, zero
    carries = []
    for device in range(count):
        carries.append(state)
        mine = jnp.where(device == me, state, mine)
        at = device % group
        moved = pltpu.roll(strip, 8 * at, 1) if at else strip
        sent[device // group] = moved if at == 0 else jnp.where((lane >> 3) == at, moved, sent[device // group])
        both = received[device, base + 2]
        state = received[device, base] + received[device, base + 1] * state
        strip = both + shifted_down(both, 2) * strip
    ends = [end_columns(sent[i]) for i in range(sent.shape[0])]
    state = [zero] * near
    mine_edge = zero
    for device in reversed(range(count)):
        at = 8 * (device % group)
        edge = ends[device // group][at : at + 8]
        mine_edge = jnp.where(device == me, edge, mine_edge)
        carry = carries[device]
        block = [received[device, base + 3 + z] for z in range(near)]
        above = jnp.where(lane == last, edge, pltpu.roll(carry, last, 1))
        below = jnp.where(lane == 0, edge, pltpu.roll(carry, 1, 1))
        link = [received[device, base + 3 + 2 * near + i] for i in range(4)]
        block[0] = block[0] + link[0] * carry + link[1] * above + link[2] * below
        block[1] = block[1] + link[3] * carry
        for z in range(near):
            passed = block[z] + received[device, base + 3 + near + z] * state[z]
            state[z] = jnp.where(device > me, passed, state[z])
    carry = mine
    for x in range(width_x):
        total = misfits[x] + carry
        carry = slopes[x] * total
        passed = keeps[x] * total
        sideways = row(anisotropy, near, x, tile) * (shares[1, x] + shares[2, x])
        sideways = sideways + row(anisotropy, 2 * near, x, tile) * shares[3, x]
        terms = carry * row(anisotropy, 0, x, tile) + passed * sideways
        top[x : x + 1, :] = jnp.sum(terms, axis=0, keepdims=True)
        entry = entries_of(passed, shares, x, edges_own[x] + edges_factor[x] * mine_edge)
        for z in range(near):
            entries[x, z] = entry[z]
    for x in reversed(range(width_x)):
        for z in range(near):
            total = entries[x, z] + state[z]
            state[z] = slopes_one[x, z] * total
            value = jnp.sum(total * gains[x, z], axis=0, keepdims=True)
            if z == 0:
                value = value + top[x : x + 1, :]
            kernel[z, x : x + 1, :] = value
    for z in range(near, kernel.shape[0]):
        kernel[z] = jnp.zeros(kernel.shape[1:], jnp.float32)


def call(kernel, shapes, operands, scratch=(), scalars=0, far=0, last=False, aliases=()):
    many = isinstance(shapes, list)
    shapes = shapes if many else [shapes]
    held = jax.ShapeDtypeStruct if last else pltpu.VMEM
    out = [held(s, jnp.float32) if isinstance(s, tuple) else s for s in shapes]
    result = pl.pallas_call(
        kernel,
        out_shape=out,
        in_specs=[SMEM] * scalars + [FAR] * far + [VMEM] * (len(operands) - scalars - far),
        out_specs=[FAR] * last + [VMEM] * (len(out) - last),
        scratch_shapes=[pltpu.VMEM(s, jnp.float32) if isinstance(s, tuple) else s for s in scratch],
        compiler_params=PARAMS,
        input_output_aliases=dict(aliases),
    )(*operands)
    return result if many else result[0]


def traded(message):
    return lax.all_to_all(message, "gx", 0, 0, tiled=True)


def rotated(value, axis, by):
    count = lax.axis_size(axis)
    return lax.ppermute(value, axis, [(i, (i + by) % count) for i in range(count)])


def body(warm_start, slowness, anisotropy, observed, station_cell, source_cell):
    quakes, depth, width_x, width_y = warm_start.shape
    count_x, count_y = lax.axis_size("gx"), lax.axis_size("gy")
    index_x, index_y = lax.axis_index("gx"), lax.axis_index("gy")
    span_x, span_y = width_x * count_x, width_y * count_y
    near = 2
    per = max(1, depth // count_x)
    tile = (quakes, width_y)
    top = (width_x,) + tile
    close = (width_x, near) + tile
    field = (width_x, depth) + tile
    place = jnp.stack(
        [
            index_x * width_x,
            index_y * width_y,
            jnp.int32(span_y),
            jnp.int32(span_x * span_y),
            (index_y == 0).astype(jnp.int32),
            (index_y == count_y - 1).astype(jnp.int32),
            index_x,
            jnp.int32(span_y.bit_length() - 1),
            index_y,
        ]
    ).astype(jnp.int32)
    anis = anisotropy.reshape(3 * depth, width_x, width_y)
    local_records = observed.shape[1]

    stations = station_cell.reshape(-1, width_y)
    sources = [warm_start, observed, slowness, anis, stations]
    sources = [pltpu.with_memory_space_constraint(a, pltpu.HBM) for a in [source_cell] + sources]
    start, costs, anis, edge, to_right, to_left, records, stations = call(
        pack_kernel,
        [(depth, width_x) + tile, anis.shape, (3 * near, width_x, width_y), (11 * width_x, width_y)]
        + [(6 * width_x + quakes, width_y)] * 2
        + [tile, pltpu.VMEM(stations.shape, jnp.int32)],
        [place] + sources,
        [pltpu.SMEM((quakes,), jnp.int32)]
        + [a.shape for a in sources[2:5]]
        + [pltpu.SemaphoreType.DMA((5 + CHUNKS * quakes,))],
        scalars=1,
        far=6,
    )
    from_left = rotated(to_right, "gy", 1)
    from_right = rotated(to_left, "gy", -1)
    others = [rotated(records, "gy", by) for by in range(2, count_y - 1)]

    message_shape = (count_x, 3 * per + (7 if per > 1 else 8)) + tile
    first, first_strip, edge_costs, levels_one, sides, message = call(
        functools.partial(first_sweep_kernel, local_records, count_y, per),
        [field, (width_x, 2) + tile, (6,) + top, close, close, message_shape],
        [place, start, edge, records, from_left, from_right, costs, anis] + others,
        [(depth,) + tile, (width_x, 2) + tile],
        scalars=1,
    )
    reach = traded(message)
    chunks = -(-count_x // (width_y // 8))
    halo, *rest, message = call(
        functools.partial(middle_kernel, per, local_records * count_y),
        [(depth,) + tile, (4,) + top] + [top] * 5 + [close, close, (count_x, 2 * per + 7 + 2 * near) + tile],
        [place, stations, reach, first, first_strip, costs, edge_costs, anis, levels_one, sides],
        [(2,) + tile, (chunks,) + tile, (chunks, depth) + tile, (width_x, 2) + tile]
        + [top] * 5
        + [(width_x, width_y), tile, tile],
        scalars=1,
    )
    times, kernel = call(
        functools.partial(last_kernel, per),
        [warm_start.shape, (depth, width_x, width_y)],
        [place, traded(message), first, costs, halo] + rest + [anis],
        [field, (depth, width_x) + tile, pltpu.SemaphoreType.DMA((quakes,)), close, (width_x, width_y), (chunks,) + tile],
        scalars=1,
        last=True,
    )
    return (times, kernel)


def solution(mesh):
    return jax.shard_map(
        body,
        mesh=mesh,
        in_specs=(
            P(None, None, "gx", "gy"),
            P(None, "gx", "gy"),
            P(None, None, "gx", "gy"),
            P(None, ("gx", "gy")),
            P(),
            P(),
        ),
        out_specs=(P(None, None, "gx", "gy"), P(None, "gx", "gy")),
        check_vma=False,
    )
```

```python
import functools
import math

import jax
import jax.numpy as jnp
from jax import lax
from jax.experimental import pallas as pl
from jax.experimental.pallas import tpu as pltpu
from jax.sharding import PartitionSpec as P

TAU = 0.05
ADJ_SCALE = 0.1
LOG2E = math.log2(math.e)
RATE = LOG2E / TAU
BIG = 10000.0 * RATE
CHUNKS = 2
VMEM = pl.BlockSpec(memory_space=pltpu.VMEM)
FAR = pl.BlockSpec(memory_space=pl.ANY)
SMEM = pl.BlockSpec(memory_space=pltpu.SMEM)
PARAMS = pltpu.CompilerParams(vmem_limit_bytes=8 * 1024 * 1024)


def softmin(values):
    least = functools.reduce(jnp.minimum, values)
    parts = [jnp.exp2(least - v) for v in values]
    return least, parts, functools.reduce(jnp.add, parts)


def soft_pair(first, second):
    return jnp.minimum(first, second) - LOG2E * jnp.log(1.0 + jnp.exp2(-jnp.abs(first - second)))


def add_pair(least, total, passed):
    low = jnp.minimum(least, passed)
    return low - LOG2E * jnp.log(total * jnp.exp2(low - least) + jnp.exp2(low - passed))


def join_pairs(first, second):
    low = jnp.minimum(first[0], second[0])
    return low, first[1] * jnp.exp2(low - first[0]) + second[1] * jnp.exp2(low - second[0])


def value_of(pair):
    return pair[0] - LOG2E * jnp.log(pair[1])


def split_pair(first, second):
    gap = jnp.exp2(-jnp.abs(first - second))
    share = 1.0 / (1.0 + gap)
    less = gap * share
    nearer = first <= second
    return jnp.where(nearer, share, less), jnp.where(nearer, less, share)


def iota(shape, axis):
    return lax.broadcasted_iota(jnp.int32, shape, axis)


def row(ref, index, x, like):
    return jnp.broadcast_to(ref[index, pl.ds(x, 1), :], like)


def row_of(ref, x, like):
    return jnp.broadcast_to(ref[pl.ds(x, 1), :], like)


def all_steps(count, step, carry):
    for i in range(count):
        carry = step(i, carry)
    return carry


def packed(left, right):
    return jnp.where(iota(left.shape, 0) < 5, left, pltpu.roll(right, 2, 0))


def merged(left, right):
    return jnp.where(iota(left.shape, 0) < 4, left, right)


def shifted_down(tile, by):
    return pltpu.roll(tile, tile.shape[0] - by, 0)


def exact_parts(value):
    high = value.astype(jnp.bfloat16).astype(jnp.float32)
    middle = (value - high).astype(jnp.bfloat16).astype(jnp.float32)
    low = value - high - middle
    return [p.astype(jnp.bfloat16) for p in (high, middle, low)]


def pack_kernel(
    place, source_far, warm_far, observed_far, slowness_far, anisotropy_far, stations_far,
    start, costs, near, edge, to_right, to_left, records, stations,
    source, observed, slowness, anisotropy, arrived,
):
    pairs = [(slowness_far, slowness), (anisotropy_far, anisotropy), (observed_far, observed)]
    pairs += [(stations_far, stations), (source_far, source)]
    depth, width_x, quakes, width_y = start.shape
    share = depth // CHUNKS
    for i in range(CHUNKS):
        levels = pl.ds(i * share, share)
        pairs += [(warm_far.at[e, levels], start.at[levels, :, e, :]) for e in range(quakes)]
    copies = [pltpu.make_async_copy(a, b, arrived.at[i]) for i, (a, b) in enumerate(pairs)]
    for copy in copies:
        copy.start()
    tile = (quakes, width_y)
    quake = iota(tile, 0)
    lane = iota(tile, 1)
    span_y = place[2]
    plane = place[3]
    rows = width_x * 8
    wide = (width_x, width_y)
    group = iota(wide, 1) >> 3
    copies[0].wait()
    copies[1].wait()
    native = []
    for k in range(3):
        columns = jnp.zeros(wide, jnp.float32)
        for z in range(depth):
            cost = slowness[z] * anisotropy[k * depth + z] * RATE
            costs[k * depth + z] = cost
            columns = jnp.where(group == z, pltpu.roll(cost, 8 * z + 4, 1), columns)
        edge[rows : rows + width_x, :] = columns
        rows += width_x
        native.append(columns)
        for z in range(near.shape[0] // 3):
            near[k * (near.shape[0] // 3) + z] = anisotropy[k * depth + z]
    early = (iota(wide, 1) & 7) < 4
    at = slice(4 * width_x, 5 * width_x)
    to_right[at, :] = jnp.where(early, native[0], pltpu.roll(native[1], 4, 1))
    to_left[at, :] = jnp.where(early, pltpu.roll(native[1], width_y - 4, 1), native[0])
    at = slice(5 * width_x, 6 * width_x)
    to_right[at, :] = native[2]
    to_left[at, :] = native[2]
    copies[4].wait()
    cell = jnp.zeros(tile, jnp.int32)
    for e in range(quakes):
        cell = jnp.where(quake == e, source[e], cell)
    cell = cell - (lane + place[0] * span_y + place[1])
    edges = []
    for i in range(CHUNKS):
        for copy in copies[5 + i * quakes : 5 + (i + 1) * quakes]:
            copy.wait()

        chunk = [jnp.zeros(tile, jnp.float32)] * share
        for x in range(width_x):
            mine = (lane >> 3) == x
            for k in range(share):
                value = start[i * share + k, x] * RATE
                value = jnp.where(cell == (i * share + k) * plane + x * span_y, 0.0, value)
                start[i * share + k, x] = value
                chunk[k] = jnp.where(mine, pltpu.roll(value, (8 * x + 4) % width_y, 1), chunk[k])
        edges += chunk
    columns = jnp.transpose(jnp.concatenate(edges, 0))
    edge[: width_x * 8, :] = columns
    low = quake < 4
    for x in range(0, width_x, 2):
        one, two = columns[8 * x : 8 * x + 8], columns[8 * x + 8 : 8 * x + 16]
        to_right[4 * x : 4 * x + 8, :] = jnp.where(low, one, pltpu.roll(two, 4, 0))
        to_left[4 * x : 4 * x + 8, :] = jnp.where(low, pltpu.roll(one, 4, 0), two)
    copies[2].wait()
    copies[3].wait()
    records[...] = jnp.zeros(tile, jnp.float32)
    records[:, : observed.shape[1]] = observed[...]
    for message in (to_right, to_left):
        message[6 * width_x :, :] = records[...]


def halo_columns(left, right):
    rows = []
    for l, r in zip(left, right):
        rows.append(jnp.where(iota(l.shape, 0) == 4, r, pltpu.roll(l, 2, 0)))
    return jnp.transpose(jnp.concatenate(rows, 0))


def cost_columns(message, width_x, turn):
    pair = message[4 * width_x : 5 * width_x, :]
    return [pair, pltpu.roll(pair, turn, 1), message[5 * width_x : 6 * width_x, :]]


def strip_costs(own, from_left, from_right, out, width_x, depth):
    tile = own.shape[1]
    base = width_x * 8
    lane = iota((8, tile), 1)
    low = (lane & 7) < 4
    mine = (lane & 7) == iota((8, tile), 0)
    spread = ((iota((tile, tile), 0) >> 3) == (iota((tile, tile), 1) >> 3)).astype(jnp.float32)
    spread = spread.astype(jnp.bfloat16)
    for side in range(2):
        for k in range(3):
            rows = []
            for x in range(width_x):
                at = slice(base + k * width_x + x, base + k * width_x + x + 1)
                here = jnp.broadcast_to(own[at, :], lane.shape)
                there = jnp.broadcast_to((from_right if side else from_left)[k][x : x + 1], lane.shape)
                value = jnp.where(low, here, there) if side else jnp.where(low, there, here)
                rows.append(jnp.where(mine, value, 0.0))
            whole = jnp.concatenate(rows, 0)
            total = 0.0
            for part in reversed(exact_parts(whole)):
                total = total + lax.dot_general(
                    part, spread, (((1,), (0,)), ((), ())), preferred_element_type=jnp.float32
                )
            out[3 * side + k] = total.reshape(width_x, 8, tile)


def running_sum(value):
    rows = iota(value.shape, 0)
    by = 1
    while by < value.shape[0]:
        value = value + jnp.where(rows >= by, pltpu.roll(value, by, 0), 0.0)
        by *= 2
    return value


def log_sum(exponents):
    return -LOG2E * jnp.log(functools.reduce(jnp.add, [jnp.exp2(-e) for e in exponents]))


def passages(costs, from_left, from_right, depth):
    width_x, width_y = costs.shape[1:]
    lane = iota((width_x, width_y), 1)
    beside = jnp.where((lane & 7) == 4, running_sum(from_right), pltpu.roll(running_sum(from_left), 2, 1))
    sums = [running_sum(costs[z]) for z in range(depth)]
    sub = iota((8, width_y), 0)
    tiles = []
    for z in range(depth):
        back = sums[z] - costs[z]
        edge = pltpu.roll(beside, width_y - 5 - 8 * z, 1)
        below = jnp.where(lane == 0, edge, pltpu.roll(sums[z], 1, 1))
        above = jnp.where(lane == width_y - 1, edge, pltpu.roll(sums[z], width_y - 1, 1))
        step_y = back + costs[depth + z]
        step_z = back + costs[2 * depth + z]
        paths = [sums[z] + back, below + step_y, above + step_y]
        paths.append(sums[z - 1] + step_z if z > 0 else None)
        paths.append(sums[z + 1] + step_z if z < depth - 1 else None)
        tile = jnp.broadcast_to(sums[z][width_x - 1 :, :], sub.shape)
        for j, path in enumerate(paths):
            if path is None:
                tile = jnp.where(sub == j + 1, BIG, tile)
            else:
                total = jnp.sum(jnp.exp2(-path), axis=0, keepdims=True)
                tile = jnp.where(sub == j + 1, -LOG2E * jnp.log(total), tile)
        tiles.append(tile)
    return tiles


def strip_passages(edge_costs, width_x):
    shape = edge_costs.shape[2:]
    lane = iota(shape, 1)
    sums = jnp.zeros(shape, jnp.float32)
    totals = [jnp.zeros(shape, jnp.float32)] * 5
    for x in range(width_x):
        cost, step_y, step_z = [packed(edge_costs[k, x], edge_costs[3 + k, x]) for k in range(3)]
        back = sums
        sums = sums + cost
        step_y, step_z = step_y + back, step_z + back
        paths = [sums + back, pltpu.roll(sums, 1, 0) + step_y, shifted_down(sums, 1) + step_y]
        paths.append(jnp.where(lane < 8, BIG, pltpu.roll(sums, 8, 1) + step_z))
        paths.append(jnp.where(lane >= shape[1] - 8, BIG, pltpu.roll(sums, shape[1] - 8, 1) + step_z))
        totals = [t + jnp.exp2(-p) for t, p in zip(totals, paths)]
    return sums, [-LOG2E * jnp.log(jnp.maximum(t, 1e-37)) for t in totals]


PLACES = ((2, 0, 16), (4, 16, 16), (5, 32, 16), (7, 48, 16))
BACK_PLACES = ((3, 64, 8), (6, 72, 8))


def shared_tile(reach, back, records):
    lane, sub = iota(reach.shape, 1), iota(reach.shape, 0)
    extra = reach
    for value, places in ((reach, PLACES), (back, BACK_PLACES)):
        for at, low, width in places:
            moved = pltpu.roll(pltpu.roll(value, (2 - at) % 8, 0), low, 1) if low else value
            extra = jnp.where((lane >= low) & (lane < low + width), moved, extra)
    half = reach.shape[1] // 2
    record = jnp.where(lane < half, pltpu.roll(records, 4, 0), pltpu.roll(records, half, 1))
    tile = jnp.where(sub == 0, shifted_down(reach, 3), jnp.where(sub == 1, shifted_down(reach, 5), extra))
    return jnp.where(sub < 4, tile, record)


def unshared_tile(tile):
    sub = iota(tile.shape, 0)
    wide = tile.shape[1]
    reach = jnp.where(sub == 3, pltpu.roll(tile, 3, 0), jnp.where(sub == 6, pltpu.roll(tile, 5, 0), tile))
    for at, low, _ in PLACES[1:]:
        reach = jnp.where(sub == at, pltpu.roll(pltpu.roll(tile, at - 2, 0), wide - low, 1), reach)
    back = [pltpu.roll(pltpu.roll(tile, at - 2, 0), wide - low, 1) for at, low, _ in BACK_PLACES]
    return reach, jnp.where(sub == 3, back[0], back[1])


def shared_rows(total, paths):
    place = iota(total.shape, 1) & 7
    first, second = total, total
    for q in range(6):
        value = pltpu.roll(total, (4 - q) % 8, 0)
        first = jnp.where(place == q, value, first)
    for q, (path, at) in enumerate([(p, r) for p in paths for r in (3, 6)]):
        if q < 2:
            first = jnp.where(place == 6 + q, pltpu.roll(path, (6 - at) % 8, 0), first)
        else:
            second = jnp.where(place == q - 2, pltpu.roll(path, (7 - at) % 8, 0), second)
    return jnp.where(iota(total.shape, 0) == 6, first, second)


def spread_rows(tiles):
    shape = tiles[0].shape
    wide = shape[1]
    sub = iota(shape, 0)
    mine = (iota(shape, 1) & 7) == sub
    spread = ((iota((wide, wide), 0) >> 3) == (iota((wide, wide), 1) >> 3)).astype(jnp.float32)
    spread = spread.astype(jnp.bfloat16)
    rows = [jnp.where(mine, jnp.broadcast_to(t[r : r + 1], shape), 0.0) for t in tiles for r in (6, 7)]
    whole = jnp.concatenate(rows, 0)
    value = 0.0
    for part in reversed(exact_parts(whole)):
        value = value + lax.dot_general(part, spread, (((1,), (0,)), ((), ())), preferred_element_type=jnp.float32)
    out = []
    for i in range(len(tiles)):
        first, second = value[16 * i : 16 * i + 8], value[16 * i + 8 : 16 * i + 16]
        paths = [jnp.where(sub == 3, pltpu.roll(first, 5, 0), pltpu.roll(first, 7, 0))]
        for q in range(4):
            at_three = pltpu.roll(second, (3 - 2 * q) % 8, 0)
            at_six = pltpu.roll(second, (6 - 2 * q - 1) % 8, 0)
            paths.append(jnp.where(sub == 3, at_three, at_six))
        out.append((pltpu.roll(first, 2, 0), paths))
    return out


def sweep_step(x, near, levels, strip, costs, edge_costs, halo, state, strip_state, keep, keep_strip):
    depth = costs.shape[0] // 3
    tile = levels[0].shape
    width_y = tile[1]
    lane = iota(tile, 1)
    out = []
    for z in range(len(state)):
        u = levels[z]
        cost_y = row(costs, depth + z, x, tile)
        cost_z = row(costs, 2 * depth + z, x, tile)
        edge = pltpu.roll(halo[z], width_y - 5 - 8 * x, 1)
        values = [u]
        values.append(jnp.where(lane == 0, edge, pltpu.roll(u, 1, 1)) + cost_y)
        values.append(jnp.where(lane == width_y - 1, edge, pltpu.roll(u, width_y - 1, 1)) + cost_y)
        if z > 0:
            values.append(levels[z - 1] + cost_z)
        if z < depth - 1:
            values.append(levels[z + 1] + cost_z)
        least, parts, total = softmin(values)
        passed = state[z] + row(costs, z, x, tile)
        if z < near:
            scale = 1.0 / total
            keep(x, z, value_of((least, total)), [p * scale for p in parts], passed)
        out.append(add_pair(least, total, passed))
    strips, relaxed, weights, passes = [], [], [], []
    for side in range(2 if strip is not None else 0):
        u = strip[x, side]
        cost_y = edge_costs[3 * side + 1, x]
        cost_z = edge_costs[3 * side + 2, x]
        values = [u, pltpu.roll(u, 1, 0) + cost_y, pltpu.roll(u, 7, 0) + cost_y]
        values.append(jnp.where(lane < 8, BIG, pltpu.roll(u, 8, 1)) + cost_z)
        values.append(jnp.where(lane >= width_y - 8, BIG, pltpu.roll(u, width_y - 8, 1)) + cost_z)
        least, parts, total = softmin(values)
        passes.append(strip_state[side] + edge_costs[3 * side, x])
        strips.append(add_pair(least, total, passes[side]))
        if keep_strip is not None:
            relaxed.append(value_of((least, total)))
            weights.append(parts[2 - side] / total)
    if keep_strip is not None:
        keep_strip(x, merged(*relaxed), merged(*weights), merged(*passes), merged(*strips))
    return out, strips


def outside_strips(place, shape):
    sub = iota(shape, 0)
    return [(place[4] == 1) & (sub < 4), (place[5] == 1) & (sub >= 4)]


def first_sweep_kernel(
    rows_of, count_y, per, place, field, own, mine, from_left, from_right, costs, anisotropy, *rest
):
    others = rest[: count_y - 3]
    local, local_strip, edge_costs, levels, sides, message, halo, strip = rest[count_y - 3 :]
    depth, width_x, quakes, width_y = field.shape
    tile = (quakes, width_y)
    sub = iota(tile, 0)
    low = sub < 4
    near = levels.shape[1]
    last = 6 * width_x
    far = [mine[...], from_left[last:, :]] + [o[...] for o in others] + [from_right[last:, :]]
    records = jnp.zeros(tile, jnp.float32)
    for by, piece in enumerate(far):
        owner = lax.rem(place[8] + count_y - by, count_y)
        records = records + pltpu.roll(piece, owner * rows_of, 1)
    left, right = [], []
    for x in range(width_x):
        at = slice(8 * x, 8 * x + 8)
        two = slice(8 * (x // 2), 8 * (x // 2) + 8)
        before, after = from_left[two, :], from_right[two, :]
        if x % 2:
            before = pltpu.roll(before, 4, 0)
        else:
            after = pltpu.roll(after, 4, 0)
        before = jnp.where(place[4] == 1, BIG, before)
        after = jnp.where(place[5] == 1, BIG, after)
        left.append(jnp.where(low, before, own[at, :]))
        right.append(jnp.where(low, own[at, :], after))
        strip[x, 0] = left[x]
        strip[x, 1] = right[x]
    halo[...] = halo_columns(left, right).reshape(halo.shape)
    left_costs = cost_columns(from_left, width_x, width_y - 4)
    right_costs = cost_columns(from_right, width_x, 4)
    strip_costs(own, left_costs, right_costs, edge_costs, width_x, depth)
    outside = outside_strips(place, tile)

    def keep(x, z, level, w, passed):
        levels[x, z] = level
        vertical = w[3] if z == 0 else w[3] + w[4]
        sideways = row(anisotropy, near + z, x, tile) * (w[1] + w[2])
        sides[x, z] = sideways + row(anisotropy, 2 * near + z, x, tile) * vertical

    def step(x, carry):
        state, strips = sweep_step(x, near, [field[z, x] for z in range(depth)], strip, costs, edge_costs, halo, *carry, keep, None)
        for z in range(depth):
            local[x, z] = state[z]
        for side in range(2):
            local_strip[x, side] = jnp.where(outside[side], BIG, strips[side])
        return state, strips

    blank = jnp.full(tile, BIG, jnp.float32)
    state, strips = all_steps(width_x, step, ([blank] * depth, [blank] * 2))
    reach_strip = packed(*[jnp.where(o, BIG, s) for o, s in zip(outside, strips)])

    edges = [[local_strip[x, side] for x in range(width_x)] for side in range(2)]
    halo[...] = halo_columns(*edges).reshape(halo.shape)

    def again(lap, carry):
        x = width_x - 1 - lap
        values = [local[x, z] for z in range(depth)]
        return sweep_step(x, 0, values, local_strip, costs, edge_costs, halo, *carry, None, None)

    back, back_strips = all_steps(width_x, again, ([blank] * depth, [blank] * 2))
    tiles = passages(costs, left_costs[0], right_costs[0], depth)
    strip_total, strip_paths = strip_passages(edge_costs, width_x)

    strip_tile = shared_tile(reach_strip, packed(*back_strips), records)
    shared = shared_rows(strip_total, strip_paths)
    count = message.shape[0]
    for p in range(count):
        first = min(p * per, depth - per)
        for k in range(per + 2):
            z = first + k - 1
            message[p, k] = state[z] if 0 <= z < depth else blank
        for k in range(per):
            message[p, per + 2 + k] = back[first + k]
            value = tiles[first + k]
            if k == 0 and first > 0:
                value = jnp.where(sub == 6, jnp.broadcast_to(tiles[first - 1][:1], tile), value)
            if k == 0 and first + per < depth:
                value = jnp.where(sub == 7, jnp.broadcast_to(tiles[first + per][:1], tile), value)
            if per > 1 and k == 1:
                value = jnp.where(sub < 6, value, shared)
            message[p, 2 * per + 2 + k] = value
        message[p, 3 * per + 2] = strip_tile
        if per == 1:
            message[p, 3 * per + 3] = shared
        surface = [state[0], state[1], back[0], jnp.where(sub < 6, tiles[0], jnp.broadcast_to(tiles[1][:1], tile))]
        for i, value in enumerate(surface):
            message[p, message.shape[1] - 4 + i] = value


def owner_carries(
    per, depth, place, received, entering, entering_strips, surface_edges, halo,
):
    count = received.shape[0]
    tile = entering.shape[2:]
    lane = iota(tile, 1)
    width_y = tile[1]
    me = place[6]
    blank = jnp.full(tile, BIG, jnp.float32)
    unit = jnp.ones(tile, jnp.float32)
    side = 3 * per + 2

    def rows(device, k, j):
        return jnp.broadcast_to(received[device, 2 * per + 2 + k, j : j + 1, :], tile)

    def total(device, k):
        if k < 0:
            return rows(device, 0, 6)
        return rows(device, k, 0) if k < per else rows(device, 0, 7)

    def further(pair, cost):
        return pair[0] + cost, pair[1]

    shared = [received[d, 2 * per + 3] if per > 1 else received[d, 3 * per + 3] for d in range(count)]
    strips = [unshared_tile(received[d, side]) for d in range(count)]
    shared = spread_rows(shared)
    state = [(blank, unit)] * (per + 2)
    strip = (blank, unit)
    first, first_strip = [], []
    for device in range(count):
        first.append([value_of(pair) for pair in state])
        first_strip.append(value_of(strip))
        state = [
            join_pairs((received[device, k], unit), further(state[k], total(device, k - 1))) for k in range(per + 2)
        ]
        strip = join_pairs((strips[device][0], unit), further(strip, shared[device][0]))
    own = blank
    for device in range(count):
        own = jnp.where(device == me, first_strip[device], own)
        for k in range(per):
            entering[device, k] = first[device][k + 1]
    entering_strips[0] = own
    group = width_y // 8
    for at in range(0, count, group):
        some = first_strip[at : at + group]
        some = some + [blank] * (group - len(some))
        turned = halo_columns(some, [shifted_down(s, 2) for s in some])
        halo[at // group] = turned.reshape(halo.shape[1:])
        surface_edges[at // group] = turned[: tile[0]]
    low = jnp.minimum(me * per, depth - per)
    edges = [[halo[i, low + k] for k in range(per)] for i in range(halo.shape[0])]
    state = [(blank, unit)] * per
    strip = (blank, unit)
    for device in reversed(range(count)):
        for k in range(per):
            entering[device, per + k] = value_of(state[k])
            u = first[device][k + 1]
            turn = (width_y - 5 - 8 * (device % group)) % width_y
            edge = pltpu.roll(edges[device // group][k], turn, 1)
            values = [received[device, per + 2 + k], u + rows(device, k, 1)]
            values.append(jnp.where(lane == 0, edge, pltpu.roll(u, 1, 1)) + rows(device, k, 2))
            values.append(jnp.where(lane == width_y - 1, edge, pltpu.roll(u, width_y - 1, 1)) + rows(device, k, 3))
            values.append(first[device][k] + rows(device, k, 4))
            values.append(first[device][k + 2] + rows(device, k, 5))
            least, _, amount = softmin(values)
            state[k] = join_pairs((least, amount), further(state[k], total(device, k)))
        u = first_strip[device]
        back = strips[device][1]
        paths = shared[device][1]
        values = [back, u + paths[0], pltpu.roll(u, 1, 0) + paths[1], shifted_down(u, 1) + paths[2]]
        values.append(jnp.where(lane < 8, BIG, pltpu.roll(u, 8, 1)) + paths[3])
        values.append(jnp.where(lane >= width_y - 8, BIG, pltpu.roll(u, width_y - 8, 1)) + paths[4])
        least, _, amount = softmin(values)
        passed = join_pairs((least, amount), further(strip, shared[device][0]))
        strip = [jnp.where(device > me, new, old) for new, old in zip(passed, strip)]
    entering_strips[1] = value_of(strip)


def middle_kernel(
    per, rows_of, place, cell, received, first, first_strip, costs, edge_costs, anisotropy, levels_one, sides,
    halo, shares, slopes, keeps, misfits, edges_own, edges_factor, slopes_one, gains, message,
    entering_strips, surface_edges, block_halo, strip, shares_strip, slopes_strip, keeps_strip, misfits_strip, sums, counts, sums_strip, counts_strip,
):
    owner_carries(per, first.shape[1], place, received, message, entering_strips, surface_edges, block_halo)
    width_x, near, quakes, width_y = levels_one.shape
    tile = (quakes, width_y)
    lane = iota(tile, 1)
    count = received.shape[0]
    base = received.shape[1] - 4
    me = place[6]
    add_records(rows_of, 3 * per + 2, place, cell, received, sums, counts, sums_strip, counts_strip)
    blank = jnp.full(tile, BIG, jnp.float32)
    unit = jnp.ones(tile, jnp.float32)

    def rows(device, j):
        return jnp.broadcast_to(received[device, base + 3, j : j + 1, :], tile)

    state = [(blank, unit)] * near
    into = []
    for device in range(count):
        into.append([value_of(pair) for pair in state])
        state = [
            join_pairs((received[device, base + z], unit), (state[z][0] + rows(device, 6 * z), state[z][1]))
            for z in range(near)
        ]
    carried = [blank] * near
    for device in range(count):
        carried = [jnp.where(device == me, new, old) for new, old in zip(into[device], carried)]
    back = (blank, unit)
    group = width_y // 8
    for device in reversed(range(count)):
        u, deeper = into[device]
        edge = pltpu.roll(surface_edges[device // group], (width_y - 5 - 8 * (device % group)) % width_y, 1)
        values = [received[device, base + 2], u + rows(device, 1), deeper + rows(device, 5)]
        values.append(jnp.where(lane == 0, edge, pltpu.roll(u, 1, 1)) + rows(device, 2))
        values.append(jnp.where(lane == width_y - 1, edge, pltpu.roll(u, width_y - 1, 1)) + rows(device, 3))
        least, _, amount = softmin(values)
        passed = join_pairs((least, amount), (back[0] + rows(device, 0), back[1]))
        back = [jnp.where(device > me, new, old) for new, old in zip(passed, back)]
    back = value_of(back)

    outside = outside_strips(place, tile)
    strips_in = [[s, shifted_down(s, 2)] for s in (entering_strips[0], entering_strips[1])]
    running = [jnp.zeros(tile, jnp.float32)] * (near + 2)
    prior = carried
    close = []
    for x in range(width_x):
        values = []
        for z in range(near):
            cost = row(costs, z, x, tile)
            running[z] = running[z] + cost
            values.append(soft_pair(first[x, z], carried[z] + running[z]))
            keep, slope = split_pair(levels_one[x, z], prior[z] + cost)
            slopes_one[x, z] = slope
            gains[x, z] = slope * row(anisotropy, z, x, tile) + keep * sides[x, z]
        prior = values
        close.append(values)
        for side in range(2):
            running[near + side] = running[near + side] + edge_costs[3 * side, x]
            value = soft_pair(first_strip[x, side], strips_in[0][side] + running[near + side])
            strip[x, side] = jnp.where(outside[side], BIG, value)
    edges = [[strip[x, side] for x in range(width_x)] for side in range(2)]
    halo[...] = halo_columns(*edges).reshape(halo.shape)

    def keep(x, z, level, w, passed):
        for i in range(4):
            shares[i, x] = w[i]
        keeps[x], slopes[x] = split_pair(level, passed)

    def keep_strip(x, level, w, passed, value):
        shares_strip[x] = w
        keeps_strip[x], slopes_strip[x] = split_pair(level, passed)
        tally = pltpu.roll(counts_strip[...], (width_y - 8 * x) % width_y, 1)
        total = pltpu.roll(sums_strip[...], (width_y - 8 * x) % width_y, 1)
        misfits_strip[x] = ADJ_SCALE * (tally * (value * (1.0 / RATE)) - total)

    def step(lap, carry):
        x = width_x - 1 - lap
        state, strips = sweep_step(x, 1, close[x], strip, costs, edge_costs, halo, *carry, keep, keep_strip)
        misfits[x] = ADJ_SCALE * (row_of(counts, x, tile) * (state[0] * (1.0 / RATE)) - sums[x])
        return state, strips

    all_steps(width_x, step, ([back], strips_in[1]))
    zero = jnp.zeros(tile, jnp.float32)
    own, factor, strip_own, strip_factor = zero, unit, zero, unit
    owns, factors = [], []
    sent = [zero, zero]
    for x in range(width_x):
        own = misfits[x] + own
        owns.append(keeps[x] * own)
        factors.append(keeps[x] * factor)
        own, factor = slopes[x] * own, slopes[x] * factor
        strip_own = misfits_strip[x] + strip_own
        through = keeps_strip[x] * shares_strip[x]
        for i, value in enumerate((strip_own, strip_factor)):
            value = pltpu.roll(through * value, 8 * x, 1) if x else through * value
            sent[i] = jnp.where((lane >> 3) == x, value, sent[i])
        strip_own, strip_factor = slopes_strip[x] * strip_own, slopes_strip[x] * strip_factor
    edges_own[...] = end_columns(sent[0]).reshape(edges_own.shape)
    edges_factor[...] = end_columns(sent[1]).reshape(edges_factor.shape)
    chain = [unit] * near
    blocks = [zero] * near
    links = [zero] * 4
    for x in range(width_x):
        entry = entries_of(owns[x], shares, x, edges_own[x])
        for z in range(near):
            chain[z] = chain[z] * slopes_one[x, z]
            blocks[z] = blocks[z] + chain[z] * entry[z]
        for i, path in enumerate(ways_of(factors[x], shares, x, edges_factor[x])):
            links[i] = links[i] + chain[i // 3] * path
    both = jnp.where(iota(tile, 0) < 5, strip_own, pltpu.roll(strip_factor, 2, 0))
    tiles = [own, factor, both] + blocks + chain + links
    for p in range(message.shape[0]):
        for i, value in enumerate(tiles):
            message[p, 2 * per + i] = value


def end_columns(rows):
    wide = rows.shape[1]
    first, last = shifted_down(rows, 3), pltpu.roll(rows, 3, 0)
    return jnp.transpose(jnp.concatenate([first] * (wide // 16) + [last] * (wide // 16), 0))


def ways_of(passed, shares, x, edge):
    lane = iota(passed.shape, 1)
    last = passed.shape[1] - 1
    above = jnp.where(lane == last, edge, pltpu.roll(passed * shares[1, x], last, 1))
    below = jnp.where(lane == 0, edge, pltpu.roll(passed * shares[2, x], 1, 1))
    return passed * shares[0, x], above, below, passed * shares[3, x]


def entries_of(passed, shares, x, edge):
    own, above, below, deeper = ways_of(passed, shares, x, edge)
    return own + above + below, deeper


def add_records(rows_of, tile_of, place, cell, received, sums, counts, sums_strip, counts_strip):
    width_x, quakes, width_y = sums.shape
    last = tile_of
    span_y = place[2]
    lane = iota((quakes, width_y), 1)
    column = iota((width_y, width_y), 0)
    strip_column = iota((8, width_y), 0)
    strip_column = jnp.where(strip_column == 3, -1, jnp.where(strip_column == 4, width_y, -2))
    share = width_y // rows_of
    dims = (((1,), (1,)), ((), ()))
    one_x = iota((width_x, width_y), 0)
    parts = [[], [], []]
    at, at_rows, at_strip = [], [], []
    for chunk in range(cell.shape[0]):
        records = jnp.zeros((quakes, width_y), jnp.float32)
        for part in range(share):
            piece = received[chunk * share + part, last]
            piece = jnp.where(iota(piece.shape, 0) < 4, pltpu.roll(piece, 4, 0), pltpu.roll(piece, width_y // 2, 1))
            moved = pltpu.roll(piece, part * rows_of, 1) if part else piece
            records = jnp.where(lane // rows_of == part, moved, records)
        cells = cell[chunk : chunk + 1, :]
        station_x = lax.shift_right_logical(cells, place[7]) - place[0]
        station_y = (cells & (span_y - 1)) - place[1]
        at_x = (one_x == jnp.broadcast_to(station_x, one_x.shape)).astype(jnp.float32)
        pieces = [p.astype(jnp.float32) for p in exact_parts(records)]
        for out, piece in zip(parts, pieces):
            spread = [piece * jnp.broadcast_to(at_x[x : x + 1], piece.shape) for x in range(width_x)]
            out.append(jnp.concatenate(spread, 0).astype(jnp.bfloat16))
        at_rows.append(at_x.astype(jnp.bfloat16))
        hit = column == jnp.broadcast_to(station_y, column.shape)
        at.append(hit.astype(jnp.float32).astype(jnp.bfloat16))
        hit = strip_column == jnp.broadcast_to(station_y, strip_column.shape)
        at_strip.append(hit.astype(jnp.float32).astype(jnp.bfloat16))
    at = jnp.concatenate(at, 1)
    at_rows = jnp.concatenate(at_rows, 1)
    at_strip = jnp.concatenate(at_strip, 1)
    parts = [jnp.concatenate(p, 1) for p in parts]

    def product(a, b):
        return lax.dot_general(a, b, dims, preferred_element_type=jnp.float32)

    main = [product(p, at) for p in parts]
    sums[...] = (main[0] + main[1] + main[2]).reshape(sums.shape)
    counts[...] = product(at_rows, at)
    sums_strip[...] = product(at_strip, parts[0]) + product(at_strip, parts[1]) + product(at_strip, parts[2])
    spread = ((iota((width_x, width_y), 1) >> 3) == one_x).astype(jnp.float32).astype(jnp.bfloat16)
    tally = 0.0
    for part in reversed(exact_parts(product(at_strip, at_rows))):
        tally += lax.dot_general(part, spread, (((1,), (0,)), ((), ())), preferred_element_type=jnp.float32)
    counts_strip[...] = tally


def traveltimes(per, first, entering, costs, halo, times, field):
    width_x, depth, quakes, width_y = first.shape
    tile = (quakes, width_y)
    carried = [[entering[z // per, k * per + z % per] for z in range(depth)] for k in range(2)]

    def finish(x, running):
        sums = [running[z] + row(costs, z, x, tile) for z in range(depth)]
        for z in range(depth):
            field[x, z] = soft_pair(first[x, z], carried[0][z] + sums[z])
        return sums

    all_steps(width_x, finish, [jnp.zeros(tile, jnp.float32)] * depth)

    def step(lap, state):
        x = width_x - 1 - lap
        values = [field[x, z] for z in range(depth)]
        state, _ = sweep_step(x, 0, values, None, costs, None, halo, state, None, None, None)
        for z in range(depth):
            times[z, x] = state[z] * (1.0 / RATE)
        return state

    all_steps(width_x, step, carried[1])


def last_kernel(
    per, place, received, first, costs, halo, shares, slopes, keeps, misfits, edges_own, edges_factor, slopes_one,
    gains, anisotropy, times, kernel, field, value, copied, entries, top, sent,
):
    traveltimes(per, first, received, costs, halo, value, field)
    copies = [pltpu.make_async_copy(value.at[:, :, e, :], times.at[e], copied.at[e]) for e in range(times.shape[0])]
    for copy in copies:
        copy.start()
    adjoint(
        2 * per, place, received, shares, slopes, keeps, misfits, edges_own, edges_factor, slopes_one, gains, anisotropy,
        kernel, entries, top, sent,
    )
    for copy in copies:
        copy.wait()


def adjoint(
    base, place, received, shares, slopes, keeps, misfits, edges_own, edges_factor, slopes_one, gains, anisotropy, kernel,
    entries, top, sent,
):
    width_x, quakes, width_y = slopes.shape
    tile = (quakes, width_y)
    near = slopes_one.shape[1]
    count = received.shape[0]
    lane = iota(tile, 1)
    last = width_y - 1
    me = place[6]
    zero = jnp.zeros(tile, jnp.float32)
    group = width_y // 8
    state, strip, mine, mine_strip = zero, zero, zero, zero
    carries = []
    for device in range(count):
        carries.append(state)
        mine = jnp.where(device == me, state, mine)
        at = device % group
        moved = pltpu.roll(strip, 8 * at, 1) if at else strip
        sent[device // group] = moved if at == 0 else jnp.where((lane >> 3) == at, moved, sent[device // group])
        both = received[device, base + 2]
        state = received[device, base] + received[device, base + 1] * state
        strip = both + shifted_down(both, 2) * strip
    ends = [end_columns(sent[i]) for i in range(sent.shape[0])]
    state = [zero] * near
    mine_edge = zero
    for device in reversed(range(count)):
        at = 8 * (device % group)
        edge = ends[device // group][at : at + 8]
        mine_edge = jnp.where(device == me, edge, mine_edge)
        carry = carries[device]
        block = [received[device, base + 3 + z] for z in range(near)]
        above = jnp.where(lane == last, edge, pltpu.roll(carry, last, 1))
        below = jnp.where(lane == 0, edge, pltpu.roll(carry, 1, 1))
        link = [received[device, base + 3 + 2 * near + i] for i in range(4)]
        block[0] = block[0] + link[0] * carry + link[1] * above + link[2] * below
        block[1] = block[1] + link[3] * carry
        for z in range(near):
            passed = block[z] + received[device, base + 3 + near + z] * state[z]
            state[z] = jnp.where(device > me, passed, state[z])
    carry = mine
    for x in range(width_x):
        total = misfits[x] + carry
        carry = slopes[x] * total
        passed = keeps[x] * total
        sideways = row(anisotropy, near, x, tile) * (shares[1, x] + shares[2, x])
        sideways = sideways + row(anisotropy, 2 * near, x, tile) * shares[3, x]
        terms = carry * row(anisotropy, 0, x, tile) + passed * sideways
        top[x : x + 1, :] = jnp.sum(terms, axis=0, keepdims=True)
        entry = entries_of(passed, shares, x, edges_own[x] + edges_factor[x] * mine_edge)
        for z in range(near):
            entries[x, z] = entry[z]
    for x in reversed(range(width_x)):
        for z in range(near):
            total = entries[x, z] + state[z]
            state[z] = slopes_one[x, z] * total
            value = jnp.sum(total * gains[x, z], axis=0, keepdims=True)
            if z == 0:
                value = value + top[x : x + 1, :]
            kernel[z, x : x + 1, :] = value
    for z in range(near, kernel.shape[0]):
        kernel[z] = jnp.zeros(kernel.shape[1:], jnp.float32)


def call(kernel, shapes, operands, scratch=(), scalars=0, far=0, last=False, aliases=()):
    many = isinstance(shapes, list)
    shapes = shapes if many else [shapes]
    held = jax.ShapeDtypeStruct if last else pltpu.VMEM
    out = [held(s, jnp.float32) if isinstance(s, tuple) else s for s in shapes]
    result = pl.pallas_call(
        kernel,
        out_shape=out,
        in_specs=[SMEM] * scalars + [FAR] * far + [VMEM] * (len(operands) - scalars - far),
        out_specs=[FAR] * last + [VMEM] * (len(out) - last),
        scratch_shapes=[pltpu.VMEM(s, jnp.float32) if isinstance(s, tuple) else s for s in scratch],
        compiler_params=PARAMS,
        input_output_aliases=dict(aliases),
    )(*operands)
    return result if many else result[0]


def traded(message):
    return lax.all_to_all(message, "gx", 0, 0, tiled=True)


def rotated(value, axis, by):
    count = lax.axis_size(axis)
    return lax.ppermute(value, axis, [(i, (i + by) % count) for i in range(count)])


def body(warm_start, slowness, anisotropy, observed, station_cell, source_cell):
    quakes, depth, width_x, width_y = warm_start.shape
    count_x, count_y = lax.axis_size("gx"), lax.axis_size("gy")
    index_x, index_y = lax.axis_index("gx"), lax.axis_index("gy")
    span_x, span_y = width_x * count_x, width_y * count_y
    near = 2
    per = max(1, depth // count_x)
    tile = (quakes, width_y)
    top = (width_x,) + tile
    close = (width_x, near) + tile
    field = (width_x, depth) + tile
    place = jnp.stack(
        [
            index_x * width_x,
            index_y * width_y,
            jnp.int32(span_y),
            jnp.int32(span_x * span_y),
            (index_y == 0).astype(jnp.int32),
            (index_y == count_y - 1).astype(jnp.int32),
            index_x,
            jnp.int32(span_y.bit_length() - 1),
            index_y,
        ]
    ).astype(jnp.int32)
    anis = anisotropy.reshape(3 * depth, width_x, width_y)
    local_records = observed.shape[1]

    stations = station_cell.reshape(-1, width_y)
    sources = [warm_start, observed, slowness, anis, stations]
    sources = [pltpu.with_memory_space_constraint(a, pltpu.HBM) for a in [source_cell] + sources]
    start, costs, anis, edge, to_right, to_left, records, stations = call(
        pack_kernel,
        [(depth, width_x) + tile, anis.shape, (3 * near, width_x, width_y), (11 * width_x, width_y)]
        + [(6 * width_x + quakes, width_y)] * 2
        + [tile, pltpu.VMEM(stations.shape, jnp.int32)],
        [place] + sources,
        [pltpu.SMEM((quakes,), jnp.int32)]
        + [a.shape for a in sources[2:5]]
        + [pltpu.SemaphoreType.DMA((5 + CHUNKS * quakes,))],
        scalars=1,
        far=6,
    )
    from_left = rotated(to_right, "gy", 1)
    from_right = rotated(to_left, "gy", -1)
    others = [rotated(records, "gy", by) for by in range(2, count_y - 1)]

    message_shape = (count_x, 3 * per + (7 if per > 1 else 8)) + tile
    first, first_strip, edge_costs, levels_one, sides, message = call(
        functools.partial(first_sweep_kernel, local_records, count_y, per),
        [field, (width_x, 2) + tile, (6,) + top, close, close, message_shape],
        [place, start, edge, records, from_left, from_right, costs, anis] + others,
        [(depth,) + tile, (width_x, 2) + tile],
        scalars=1,
    )
    reach = traded(message)
    chunks = -(-count_x // (width_y // 8))
    halo, *rest, message = call(
        functools.partial(middle_kernel, per, local_records * count_y),
        [(depth,) + tile, (4,) + top] + [top] * 5 + [close, close, (count_x, 2 * per + 7 + 2 * near) + tile],
        [place, stations, reach, first, first_strip, costs, edge_costs, anis, levels_one, sides],
        [(2,) + tile, (chunks,) + tile, (chunks, depth) + tile, (width_x, 2) + tile]
        + [top] * 5
        + [(width_x, width_y), tile, tile],
        scalars=1,
    )
    times, kernel = call(
        functools.partial(last_kernel, per),
        [warm_start.shape, (depth, width_x, width_y)],
        [place, traded(message), first, costs, halo] + rest + [anis],
        [field, (depth, width_x) + tile, pltpu.SemaphoreType.DMA((quakes,)), close, (width_x, width_y), (chunks,) + tile],
        scalars=1,
        last=True,
    )
    return (times, kernel)


def solution(mesh):
    return jax.shard_map(
        body,
        mesh=mesh,
        in_specs=(
            P(None, None, "gx", "gy"),
            P(None, "gx", "gy"),
            P(None, None, "gx", "gy"),
            P(None, ("gx", "gy")),
            P(),
            P(),
        ),
        out_specs=(P(None, None, "gx", "gy"), P(None, "gx", "gy")),
        check_vma=False,
    )
```
